32 devices in a mesh: grp: 4 (over x, core), tile: 8 (over z, y).
Axes of the slice: x: 2, y: 2, z: 4, core: 2. Of those that a mesh axis runs over, the one named last changes fastest.
Arguments:
- nodes: bfloat16 [32768, 192], P(('grp', 'tile')), may hold values from -6 to 6
- node_ids: int32 [32768], P(('grp', 'tile')), may hold values from 0 to 262143
- node_count: int32 [32], P(('grp', 'tile')), may hold values from 256 to 1024
- pos_weight: float32 [3, 192], replicated, may hold values from -6 to 6
- gain_one: float32 [192], replicated, may hold values from 0.25 to 1.75
- qkv_one: bfloat16 [192, 576], replicated, may hold values from -0.4375 to 0.4375
- out_one: bfloat16 [192, 192], replicated, may hold values from -0.4375 to 0.4375
- gain_two: float32 [192], replicated, may hold values from 0.25 to 1.75
- qkv_two: bfloat16 [192, 576], replicated, may hold values from -0.4375 to 0.4375
- out_two: bfloat16 [192, 192], replicated, may hold values from -0.4375 to 0.4375
- gain_three: float32 [192], replicated, may hold values from 0.25 to 1.75
- w_up: bfloat16 [192, 768], replicated, may hold values from -0.4375 to 0.4375
- w_down: bfloat16 [768, 192], replicated, may hold values from -0.21875 to 0.21875
- vote_slot: int32 [16384], P(('grp', 'tile')), may hold values from 0 to 1023
- vote_owner: int32 [16384, 1], P(('grp', 'tile')), may hold values from 0 to 7; in each aligned block of 512 rows (0 to 511, 512 to 1023, ...) at most 128 rows name the same one
- vote_voxel: int32 [16384], P(('grp', 'tile')), may hold values from 0 to 255
Outputs:
- features_out: float32 [32768, 192], P(('grp', 'tile'))
- voxel_sums: float32 [8192, 192], P(('grp', 'tile'))
The draws below stay inside these ranges and needn't reach their ends.
Inputs may be any that keep to these rules, and one draw needn't show every extreme that they name: `vote_owner`: among the votes of one shard, at most 128 name any one owner; some owner is named by exactly 128.
All inputs are finite; a program needn't handle non-finite values.
Results may differ from the reference program's by a relative error of at most 0.017.
Values may be sent and summed in bfloat16 or wider, within the bound.
No kernel may reach another device: no remote copies, remote signals or barrier semaphores. Data moves between devices by JAX's collectives and lax.ppermute only.
A program may use at most 64 MiB of HBM per device.

```python
import math
import jax
import jax.numpy as jnp
import numpy as np
from jax import lax

C = 192
HEADS = 12
WIN = 32
FF_HID = 768
NODE_DEV = 1024
VOTE_DEV = 512
VOX_DEV = 256
CAP = 128
NODES = 32768
VOTES = 16384
VOXELS = 8192
N_GRP = 4
N_TILE = 8


def place_ends(values, rng, least, high):
    spot = [jax.random.randint(jax.random.fold_in(rng, axis), (), 0, length) for axis, length in enumerate(values.shape)]
    widest = values.shape.index(max(values.shape))
    beside = spot[:widest] + [(spot[widest] + 1) % values.shape[widest]] + spot[widest + 1:]
    return values.at[tuple(spot)].set(least).at[tuple(beside)].set(high)


def steps_of(key, dims, cuts, low, largest):
    def one(dim, parts):
        heights = jax.random.uniform(jax.random.fold_in(jax.random.fold_in(key, 6), dim), (parts,), jnp.float32, low / len(cuts), largest / len(cuts))
        return jnp.repeat(jnp.exp(heights), dims[dim] // parts).reshape((-1,) + (1,) * (len(dims) - dim - 1))

    level = one(*cuts[0])
    for cut in cuts[1:]:
        level = level * one(*cut)
    return level


def routed_block(stream_key, own, number, rows, amount, top, bound, slope):
    order = jax.random.permutation(stream_key, amount)
    packed, common = load_shares(amount, rows * top, bound, slope, True), load_shares(amount, rows * top, bound, slope, False)
    places = jnp.arange(amount)

    def named(sizes, offset_by):
        used = int((sizes > 0).sum())
        fixed = max(1, used // 4)
        moved = fixed + (places - fixed + offset_by * (used - fixed)) % max(1, amount - fixed)
        return jnp.zeros((amount,), jnp.int32).at[order[jnp.where(places < fixed, places, moved)]].set(jnp.asarray(sizes, jnp.int32))

    sizes = jnp.where(number % 4 == 0, named(packed, number // 4), named(common, number - number // 4 - 1))
    mixed = jax.random.permutation(jax.random.fold_in(own, 3), amount)
    source_of, taker = mixed[0:amount // 2 * 2:2], mixed[1:amount // 2 * 2:2]
    slack = jnp.minimum(sizes[source_of] - 1, bound - sizes[taker]) // 2
    slack = jnp.where((source_of == order[0]) | (taker == order[0]) | (sizes[taker] == 0), 0, jnp.maximum(slack, 0))
    moved = jax.random.randint(jax.random.fold_in(own, 4), (amount // 2,), 0, 1 << 20) % (slack + 1)
    sizes = sizes.at[source_of].add(-moved).at[taker].add(moved)
    items = jnp.searchsorted(jnp.cumsum(sizes), jnp.arange(rows * top), side="right").astype(jnp.int32)
    grid = items.reshape(top, rows).T
    grid = grid[jax.random.permutation(jax.random.fold_in(own, 1), rows)]
    offset_by = jax.random.randint(jax.random.fold_in(own, 2), (rows, 1), 0, top)
    return jnp.take_along_axis(grid, (jnp.arange(top)[None, :] + offset_by) % top, axis=1)


def load_shares(number_of, total, most, skew, full):
    portions = [(1 << 20) // math.isqrt(standing ** skew) + 1 for standing in range(1, number_of + 1)]
    largest = most if full else min(most, max(-(-total // number_of), total * portions[0] // sum(portions)))
    least = 1 if total - largest >= number_of - 1 else 0
    given, rest = [largest] + [least] * (number_of - 1), total - largest - least * (number_of - 1)
    while rest > 0:
        movable = [i for i in range(1, number_of) if given[i] < largest] or [i for i in range(1, number_of) if given[i] < most]
        whole, remaining = sum([portions[i] for i in movable]), rest
        for i in movable:
            addition = min(most - given[i], max(1, remaining * portions[i] // whole), rest)
            given[i] = given[i] + addition
            rest = rest - addition
    return np.array(given)


def noise(key, extent, scale, most, cuts=(), kind=jnp.bfloat16):
    values = scale * jax.random.normal(key, extent, jnp.float32)
    if cuts:
        values = values * steps_of(key, extent, cuts, -0.22, 0.18)
    return jnp.clip(values, -most, most).astype(kind)


def setup_inputs(seed: int = 0) -> dict:
    arg_keys = jax.random.split(jax.random.key(seed), 17)
    nodes = noise(arg_keys[0], (NODES, C), 1.0, 6.0, ((0, 32),))
    node_ids = place_ends(jax.random.randint(arg_keys[1], (NODES,), 0, 262144), jax.random.fold_in(arg_keys[1], 1), 0, 262143).astype(jnp.int32)
    node_count = place_ends(jax.random.randint(arg_keys[2], (N_GRP * N_TILE,), NODE_DEV // 4, NODE_DEV + 1), jax.random.fold_in(arg_keys[2], 1), NODE_DEV // 4, NODE_DEV).astype(jnp.int32)
    pos_weight = noise(arg_keys[3], (3, C), 1.0, 6.0, (), jnp.float32)
    gain_one = jnp.clip(1.0 + 0.15 * jax.random.normal(arg_keys[4], (C,), jnp.float32), 0.25, 1.75)
    qkv_one = noise(arg_keys[5], (C, 3 * C), C ** -0.5, 0.4375)
    out_one = noise(arg_keys[6], (C, C), C ** -0.5, 0.4375)
    gain_two = jnp.clip(1.0 + 0.15 * jax.random.normal(arg_keys[7], (C,), jnp.float32), 0.25, 1.75)
    qkv_two = noise(arg_keys[8], (C, 3 * C), C ** -0.5, 0.4375)
    out_two = noise(arg_keys[9], (C, C), C ** -0.5, 0.4375)
    gain_three = jnp.clip(1.0 + 0.15 * jax.random.normal(arg_keys[10], (C,), jnp.float32), 0.25, 1.75)
    w_up = noise(arg_keys[11], (C, FF_HID), C ** -0.5, 0.4375)
    w_down = noise(arg_keys[12], (FF_HID, C), FF_HID ** -0.5, 0.21875)
    vote_slot = place_ends(jax.random.randint(arg_keys[13], (VOTES,), 0, NODE_DEV), jax.random.fold_in(arg_keys[13], 1), 0, NODE_DEV - 1).astype(jnp.int32)
    vote_owner_keys = jax.random.split(jax.random.fold_in(arg_keys[14], 1), VOTES // VOTE_DEV)
    vote_owner_turns = jax.random.permutation(jax.random.fold_in(arg_keys[14], 3), VOTES // VOTE_DEV)
    vote_owner = jax.vmap(lambda own, number: routed_block(jax.random.fold_in(arg_keys[14], 2), own, number, VOTE_DEV, N_TILE, 1, CAP, 2))(vote_owner_keys, vote_owner_turns).reshape((VOTES, 1))
    vote_voxel = place_ends(jax.random.randint(arg_keys[15], (VOTES,), 0, VOX_DEV), jax.random.fold_in(arg_keys[15], 1), 0, VOX_DEV - 1).astype(jnp.int32)
    return {"nodes": nodes, "node_ids": node_ids, "node_count": node_count, "pos_weight": pos_weight, "gain_one": gain_one, "qkv_one": qkv_one, "out_one": out_one, "gain_two": gain_two, "qkv_two": qkv_two, "out_two": out_two, "gain_three": gain_three, "w_up": w_up, "w_down": w_down, "vote_slot": vote_slot, "vote_owner": vote_owner, "vote_voxel": vote_voxel}


def position(node_ids, pos_weight):
    rows = []
    for axis in range(3):
        total = jnp.zeros(node_ids.shape, jnp.int32)
        for level in range(6):
            bit = jnp.bitwise_and(jnp.right_shift(node_ids, 3 * level + axis), 1)
            total = total + bit * 2 ** level
        rows.append(total.astype(jnp.float32) / 64.0 - 0.5)
    coords = jnp.stack(rows, 0)
    return jnp.einsum('an,ac->nc', coords, pos_weight, precision=lax.Precision.HIGHEST)

def normed(x, gain):
    mean = lax.optimization_barrier(jnp.mean(x, -1, keepdims=True))
    var = lax.optimization_barrier(jnp.mean((x - mean) ** 2, -1, keepdims=True))
    return ((x - mean) * lax.rsqrt(var + 1e-05) * gain).astype(jnp.bfloat16)

def attend(windows, keep, gain, w_qkv, w_out):
    xf = windows.astype(jnp.float32)
    count, width, chans = windows.shape
    head_dim = chans // HEADS
    inner = normed(xf, gain)
    qkv = jnp.einsum('nwc,cd->nwd', inner.astype(jnp.float32), w_qkv.astype(jnp.float32)).astype(jnp.bfloat16)
    qkv = qkv.reshape(count, width, 3, HEADS, head_dim).astype(jnp.float32)
    query, keys, values = (qkv[:, :, 0], qkv[:, :, 1], qkv[:, :, 2])
    scores = jnp.einsum('nqhd,nkhd->nhqk', query, keys) * head_dim ** (-0.5)
    scores = scores + ((keep - 1.0) * 1000000000.0)[:, None, None, :]
    probs = jax.nn.softmax(scores, -1).astype(jnp.bfloat16)
    context = jnp.einsum('nhqk,nkhd->nqhd', probs.astype(jnp.float32), values).reshape(count, width, chans)
    context = context.astype(jnp.bfloat16)
    return xf + jnp.einsum('nwc,cd->nwd', context.astype(jnp.float32), w_out.astype(jnp.float32))

def feed(x, gain, w_up, w_down):
    inner = normed(x, gain)
    hidden = jax.nn.gelu(jnp.einsum('nwc,cd->nwd', inner.astype(jnp.float32), w_up.astype(jnp.float32))).astype(jnp.bfloat16)
    return x + jnp.einsum('nwd,dc->nwc', hidden.astype(jnp.float32), w_down.astype(jnp.float32))

def reference(nodes, node_ids, node_count, pos_weight, gain_one, qkv_one, out_one, gain_two, qkv_two, out_two, gain_three, w_up, w_down, vote_slot, vote_owner, vote_voxel):
    shards = N_GRP * N_TILE
    block = NODE_DEV // N_GRP
    run = WIN // N_GRP
    keep = (jnp.arange(NODE_DEV, dtype=jnp.int32)[None, :] < node_count[:, None]).astype(jnp.float32).reshape(-1)
    start = (nodes.astype(jnp.float32) + position(node_ids, pos_weight)).astype(jnp.bfloat16)

    def local(pair):
        return attend(pair[0], pair[1], gain_one, qkv_one, out_one).astype(jnp.bfloat16)
    first = lax.map(local, (start.reshape(shards, NODE_DEV // WIN, WIN, C), keep.reshape(shards, NODE_DEV // WIN, WIN)))

    def arrange(array):
        shaped = array.reshape(N_GRP, N_TILE, N_GRP, block // run, run, -1)
        return shaped.transpose(1, 2, 3, 0, 4, 5).reshape(N_TILE, N_GRP * (block // run), WIN, -1)

    def dilated(pair):
        mixed = attend(pair[0], pair[1][..., 0], gain_two, qkv_two, out_two)
        return feed(mixed, gain_three, w_up, w_down)
    third = lax.map(dilated, (arrange(first), arrange(keep[:, None])))
    third = third.reshape(N_TILE, N_GRP, block // run, N_GRP, run, C).transpose(3, 0, 1, 2, 4, 5).reshape(NODES, C)
    features_out = third.astype(jnp.float32) * keep[:, None]
    index = jnp.arange(VOTES, dtype=jnp.int32)
    shard = index // VOTE_DEV
    global_node = shard * NODE_DEV + vote_slot
    group = shard // N_TILE
    voxel = (group * N_TILE + vote_owner[:, 0]) * VOX_DEV + vote_voxel
    picked = features_out[global_node].astype(jnp.bfloat16).astype(jnp.float32)
    voxel_sums = jax.ops.segment_sum(picked, voxel, num_segments=VOXELS)
    return (features_out, voxel_sums)
```

```python
import functools
import math

import jax
import jax.numpy as jnp
from jax import lax
from jax.experimental import pallas as pl
from jax.experimental.pallas import tpu as pltpu
from jax.sharding import PartitionSpec as P

HEADS = 12
WIN = 32
VOX_DEV = 256
LANES = 128
FLAG = 16384.0
VMEM = 48 * 1024 * 1024
F32 = jnp.float32
BF16 = jnp.bfloat16


def iota(shape, dim):
    return lax.broadcasted_iota(jnp.int32, shape, dim)


def dot(a, b):
    return jnp.dot(a, b, preferred_element_type=F32)


def dot_t(a, b):
    return lax.dot_general(a, b, (((1,), (1,)), ((), ())), preferred_element_type=F32)


def head_order(j, chans):
    size = chans // HEADS
    cut = 8 * size
    high = j - cut
    low_src = (j % 8) * size + j // 8
    high_src = (8 + high % 4) * size + high // 8 + (size // 2) * ((high % 8) // 4)
    return jnp.where(j < cut, low_src, high_src)


def permutation(parts, chans):
    n = parts * chans
    row = iota((n, n), 0)
    src = (row // chans) * chans + head_order(row % chans, chans)
    return (src == iota((n, n), 1)).astype(BF16)


def project_weights(w_qkv, w_out):
    chans = w_out.shape[0]
    qkv_t = dot_t(permutation(3, chans), w_qkv).astype(BF16)
    out_t = dot(permutation(1, chans), w_out).T.astype(BF16)
    return qkv_t, out_t


def norm_t(x, gain):
    inv = 1.0 / x.shape[0]
    mean = jnp.sum(x, 0, keepdims=True) * inv
    cent = x - mean
    var = jnp.sum(cent * cent, 0, keepdims=True) * inv
    return cent * lax.rsqrt(var + 1e-05) * gain


def attend_tiles(q_s, k_s, v_s, s_s, tiles, mask_of, write):
    cut = 2 * q_s.shape[1] // 3

    def one(t, _):
        query = q_s[t]

        def score(key, top):
            prod = query * k_s[key]
            a = jnp.sum(prod[:cut], 0)
            b = jnp.sum(prod[cut:], 0)
            b = b + pltpu.roll(b, 4, 0)
            mask = mask_of(key)
            a = a + mask
            b = b + mask
            s_s[key, 0] = a
            s_s[key, 1] = b
            return jnp.maximum(top[0], a), jnp.maximum(top[1], b)

        low = jnp.full((8, LANES), -3e38, F32)
        top_a, top_b = lax.fori_loop(0, WIN, score, (low, low), unroll=4)

        def gather(key, carry):
            sum_a, sum_b, acc_a, acc_b = carry
            pa = jnp.exp2(s_s[key, 0] - top_a)
            pb = jnp.exp2(s_s[key, 1] - top_b)
            value = v_s[key]
            return (
                sum_a + pa,
                sum_b + pb,
                acc_a + pa[None] * value[:cut],
                acc_b + pb[None] * value[cut:],
            )

        zero = jnp.zeros((8, LANES), F32)
        sum_a, sum_b, acc_a, acc_b = lax.fori_loop(
            0,
            WIN,
            gather,
            (
                zero,
                zero,
                jnp.zeros((cut, 8, LANES), F32),
                jnp.zeros((q_s.shape[1] - cut, 8, LANES), F32),
            ),
            unroll=4,
        )
        ctx = jnp.concatenate([acc_a / sum_a[None], acc_b / sum_b[None]], 0)
        write(t, ctx.reshape(-1, LANES).astype(BF16))
        return 0

    lax.fori_loop(0, tiles, one, 0)


def slot_base(run, unit, r):
    lane = iota((8, LANES), 1)
    rep_at = lane // WIN
    return (lane % 8) * LANES + ((lane // 8) % 4) * WIN + (4 * unit + rep_at) * run + r


def first_kernel(
    run, count_ref, nodes_ref, ids_ref, pos_ref, gain_one_ref, gain_two_ref, qkv_ref, out_ref,
    first_ref, sent_ref, x_s, start_s, n_s, q_s, k_s, v_s, s_s, ctx_s
):
    slots, chans = nodes_ref.shape
    tiles = slots // LANES
    units = tiles // run
    rows8 = chans // 8
    count = count_ref[0]
    qkv_t, out_t = project_weights(qkv_ref[...], out_ref[...])
    cols = jnp.concatenate(
        [pos_ref[...], gain_one_ref[...], gain_two_ref[...], jnp.zeros((3, chans), F32)], 0
    ).T
    left = nodes_ref[...].astype(F32)
    x_s[0] = left[:, :LANES]
    x_s[1, :, : chans - LANES] = left[:, LANES:]
    ids = ids_ref[...]
    ids = jnp.concatenate([ids[:, w * WIN : (w + 1) * WIN] for w in range(4)], 0).T
    ids = jnp.concatenate(
        [
            jnp.concatenate(
                [ids[(4 * u + i) * run : (4 * u + i + 1) * run] for i in range(4)], 1
            )
            for u in range(units)
        ],
        0,
    )
    coords = []
    for axis in range(3):
        total = jnp.zeros(ids.shape, jnp.int32)
        for level in range(6):
            bit = jnp.bitwise_and(jnp.right_shift(ids, 3 * level + axis), 1)
            total = total + bit * 2**level
        coords.append(total.astype(F32) / 64.0 - 0.5)
    eye = (iota((chans, chans), 0) == iota((chans, chans), 1)).astype(BF16)
    for q in range(tiles):
        u, r = q // run, q % run
        halves = [
            jnp.concatenate(
                [
                    x_s[half, pl.ds(w * WIN + (4 * u + i) * run + r, 8, stride=LANES), :]
                    for i in range(4)
                    for w in range(4)
                ],
                0,
            )
            for half in range(2)
        ]
        rows = jnp.concatenate([halves[0], halves[1][:, : chans - LANES]], 1).astype(BF16)
        at = cols[:, 0:1] * coords[0][q : q + 1]
        at = at + cols[:, 1:2] * coords[1][q : q + 1]
        at = at + cols[:, 2:3] * coords[2][q : q + 1]
        start = (dot_t(eye, rows) + at).astype(BF16)
        start_s[:, q * LANES : (q + 1) * LANES] = start
        n_s[:, q * LANES : (q + 1) * LANES] = norm_t(start.astype(F32), cols[:, 3:4]).astype(BF16)
    spread = (
        iota((LANES, 4 * LANES), 0)
        == (iota((LANES, 4 * LANES), 1) // LANES) * WIN + iota((LANES, 4 * LANES), 1) % WIN
    ).astype(BF16)
    scale = (chans // HEADS) ** -0.5 * math.log2(math.e)
    for q in range(tiles):
        u, r = q // run, q % run
        qkv = dot(qkv_t, n_s[:, q * LANES : (q + 1) * LANES])
        q_s[q] = (qkv[:chans] * scale).reshape(rows8, 8, LANES)
        wide = dot(qkv[chans:].astype(BF16), spread)
        for i in range(4):
            p = (4 * u + i) * run + r
            piece = wide[:, i * LANES : (i + 1) * LANES]
            k_s[p] = piece[:chans].reshape(rows8, 8, LANES)
            v_s[p] = piece[chans:].reshape(rows8, 8, LANES)

    lane = iota((8, LANES), 1)
    base = (lane % 8) * LANES + ((lane // 8) % 4) * WIN

    def mask_of(key):
        return jnp.where(base + key < count, 0.0, -1e9).astype(F32)

    def write(t, ctx):
        ctx_s[t] = ctx

    attend_tiles(q_s, k_s, v_s, s_s, tiles, mask_of, write)
    for q in range(tiles):
        u, r = q // run, q % run
        at = slice(q * LANES, (q + 1) * LANES)
        first = (start_s[:, at].astype(F32) + dot(out_t, ctx_s[q])).astype(BF16)
        first_ref[:, at] = first
        normed = norm_t(first.astype(F32), cols[:, 4:5])
        kept = slot_base(run, u, r)[0:1] < count
        head = jnp.where((iota((16, LANES), 0) > 0) | kept, normed[:16], FLAG)
        sent_ref[:, at] = jnp.concatenate([head, normed[16:]], 0).astype(BF16)


def tables_kernel(
    run, cap, qkv_ref, out_ref, up_ref, down_ref, slot_ref, owner_ref, voxel_ref,
    qkv_t_ref, out_t_ref, up_t_ref, down_t_ref, token_ref, label_ref
):
    votes = slot_ref.shape[1]
    codes = token_ref.shape[1]
    owners = codes // cap
    qkv_t_ref[...], out_t_ref[...] = project_weights(qkv_ref[...], out_ref[...])
    up_t_ref[...] = up_ref[...].astype(F32).T.astype(BF16)
    down_t_ref[...] = down_ref[...].astype(F32).T.astype(BF16)
    owner = owner_ref[...]
    hot = owner == iota((owners, votes), 0)
    upto = (iota((votes, votes), 0) <= iota((votes, votes), 1)).astype(BF16)
    rank = jnp.sum(jnp.where(hot, dot(hot.astype(BF16), upto), 0.0), 0, keepdims=True)
    code = owner * cap + rank.astype(jnp.int32) - 1
    member = (code == iota((codes, votes), 0)).astype(BF16)
    slot = slot_ref[...]
    p = slot % WIN
    i = p // run
    token = (
        ((i // 4) * run + p % run) * LANES
        + (i % 4) * WIN
        + ((slot // WIN) % 4) * 8
        + slot // LANES
    )
    row = iota((16, votes), 0)
    facts = jnp.where(
        row == 0,
        token // 32,
        jnp.where(row == 1, token % 32, jnp.where(row == 2, voxel_ref[...], 1)),
    )
    listed = dot_t(facts.astype(F32).astype(BF16), member)
    held = listed[3:4] > 0.5
    token_of = listed[0:1] * 32.0 + listed[1:2]
    token_ref[...] = jnp.where(held, token_of, -1.0).astype(jnp.int32)
    label = jnp.where(held, listed[2:3], -1.0)
    label_ref[...] = jnp.broadcast_to(label, label_ref.shape).astype(BF16)


def second_kernel(
    run, cap, count_ref, all_ref, own_ref, first_ref, gain_ref, qkv_t_ref, out_t_ref, up_t_ref,
    down_t_ref, token_ref, label_ref, feat_ref, votes_ref, q_s, k_s, v_s, m_s, s_s, ctx_s, bf_s, x_s
):
    groups, chans, slots = all_ref.shape
    tiles = slots // LANES
    units = tiles // run
    rows8 = chans // 8
    count = count_ref[0]
    gain = jnp.concatenate([gain_ref[...], jnp.zeros((7, chans), F32)], 0).T[:, 0:1]
    scale = (chans // HEADS) ** -0.5 * math.log2(math.e)

    def clean(block):
        head = block[:16].astype(F32)
        gone = head[0:1] > 0.5 * FLAG
        head = jnp.where((iota(head.shape, 0) == 0) & gone, 0.0, head)
        return jnp.concatenate([head.astype(BF16), block[16:]], 0), gone

    q_t = qkv_t_ref[:chans, :]
    kv_t = qkv_t_ref[chans:, :]
    for u in range(units):
        for r in range(run):
            t = u * run + r
            at = slice(t * LANES, (t + 1) * LANES)
            own, _ = clean(own_ref[:, at])
            q_s[r] = (dot(q_t, own) * scale).reshape(rows8, 8, LANES)
            for g in range(groups):
                block, gone = clean(all_ref[g, :, at])
                kv = dot(kv_t, block)
                k_s[g * run + r] = kv[:chans].reshape(rows8, 8, LANES)
                v_s[g * run + r] = kv[chans:].reshape(rows8, 8, LANES)
                m_s[g * run + r] = jnp.broadcast_to(jnp.where(gone, -1e9, 0.0), (8, LANES))

        def write(t, ctx, u=u):
            ctx_s[u * run + t] = ctx

        attend_tiles(q_s, k_s, v_s, s_s, run, lambda key: m_s[key], write)

    out_t = out_t_ref[...]
    for t in range(tiles):
        u, r = t // run, t % run
        at = slice(t * LANES, (t + 1) * LANES)
        second = first_ref[:, at].astype(F32) + dot(out_t, ctx_s[t])
        inner = norm_t(second, gain).astype(BF16)
        hidden = jax.nn.gelu(dot(up_t_ref[...], inner)).astype(BF16)
        third = second + dot(down_t_ref[...], hidden)
        third = jnp.where(slot_base(run, u, r)[0:1] < count, third, 0.0)
        bf_s[:, at] = third.astype(BF16)
        third = jnp.concatenate([third, jnp.zeros((2 * LANES - chans, LANES), F32)], 0)
        for half in range(2):
            rows = third[half * LANES : (half + 1) * LANES].T
            for i in range(4):
                for w in range(4):
                    x_s[half, pl.ds(w * WIN + (4 * u + i) * run + r, 8, stride=LANES), :] = rows[
                        (i * 4 + w) * 8 : (i * 4 + w + 1) * 8
                    ]
    feat_ref[:, :LANES] = x_s[0]
    feat_ref[:, LANES:] = x_s[1, :, : chans - LANES]
    codes = token_ref.shape[1]
    token = token_ref[...]
    picked = jnp.zeros((chans, codes), F32)
    step = 256
    for at in range(0, slots, step):
        hot = (token == iota((step, codes), 0) + at).astype(BF16)
        picked = picked + dot(bf_s[:, at : at + step], hot)
    picked = picked.astype(BF16)
    for o in range(codes // cap):
        votes_ref[o, :chans, :] = picked[:, o * cap : (o + 1) * cap]
        votes_ref[o, chans:, :] = label_ref[:, o * cap : (o + 1) * cap]


def sums_kernel(got_ref, out_ref):
    sources, rows, cap = got_ref.shape
    chans = out_ref.shape[1]
    total = jnp.zeros(out_ref.shape, F32)
    for s in range(sources):
        label = got_ref[s, chans:, :].astype(F32)[0:1]
        hot = (label == iota((out_ref.shape[0], cap), 0).astype(F32)).astype(BF16)
        total = total + dot_t(hot, got_ref[s, :chans, :])
    out_ref[...] = total


def call(kernel, outs, scratch, flops, in_smem=0, n_in=0):
    specs = [pl.BlockSpec(memory_space=pltpu.SMEM)] * in_smem
    specs += [pl.BlockSpec(memory_space=pltpu.VMEM)] * (n_in - in_smem)
    return pl.pallas_call(
        kernel,
        out_shape=outs,
        in_specs=specs,
        out_specs=[pl.BlockSpec(memory_space=pltpu.VMEM)] * len(outs),
        scratch_shapes=scratch,
        compiler_params=pltpu.CompilerParams(vmem_limit_bytes=VMEM),
        cost_estimate=pl.CostEstimate(flops=flops, bytes_accessed=2 << 20, transcendentals=0),
    )


def body(
    nodes,
    node_ids,
    node_count,
    pos_weight,
    gain_one,
    qkv_one,
    out_one,
    gain_two,
    qkv_two,
    out_two,
    gain_three,
    w_up,
    w_down,
    vote_slot,
    vote_owner,
    vote_voxel,
):
    slots, chans = nodes.shape
    groups, owners = lax.axis_size("grp"), lax.axis_size("tile")
    run = WIN // groups
    votes = vote_slot.shape[0]
    cap = 2 * votes // owners
    codes = owners * cap
    tiles = slots // LANES
    rows8 = chans // 8
    hidden = w_up.shape[1]
    sds = jax.ShapeDtypeStruct

    first, sent = call(
        functools.partial(first_kernel, run),
        [sds((chans, slots), BF16), sds((chans, slots), BF16)],
        [
            pltpu.VMEM((2, slots, LANES), F32),
            pltpu.VMEM((chans, slots), BF16),
            pltpu.VMEM((chans, slots), BF16),
            pltpu.VMEM((tiles, rows8, 8, LANES), F32),
            pltpu.VMEM((WIN, rows8, 8, LANES), F32),
            pltpu.VMEM((WIN, rows8, 8, LANES), F32),
            pltpu.VMEM((WIN, 2, 8, LANES), F32),
            pltpu.VMEM((tiles, chans, LANES), BF16),
        ],
        2_000_000_000,
        in_smem=1,
        n_in=8,
    )(
        node_count,
        nodes,
        node_ids.reshape(slots // LANES, LANES),
        pos_weight,
        gain_one.reshape(1, chans),
        gain_two.reshape(1, chans),
        qkv_one,
        out_one,
    )
    gathered = lax.all_gather(sent, "grp", axis=0, tiled=False)
    qkv_t, out_t, up_t, down_t, token, label = call(
        functools.partial(tables_kernel, run, cap),
        [
            sds((3 * chans, chans), BF16),
            sds((chans, chans), BF16),
            sds((hidden, chans), BF16),
            sds((chans, hidden), BF16),
            sds((1, codes), jnp.int32),
            sds((16, codes), BF16),
        ],
        [],
        2_000_000_000,
        n_in=7,
    )(
        qkv_two,
        out_two,
        w_up,
        w_down,
        vote_slot.reshape(1, votes),
        vote_owner.reshape(1, votes),
        vote_voxel.reshape(1, votes),
    )
    features_out, ballots = call(
        functools.partial(second_kernel, run, cap),
        [sds((slots, chans), F32), sds((owners, chans + 16, cap), BF16)],
        [
            pltpu.VMEM((run, rows8, 8, LANES), F32),
            pltpu.VMEM((WIN, rows8, 8, LANES), F32),
            pltpu.VMEM((WIN, rows8, 8, LANES), F32),
            pltpu.VMEM((WIN, 8, LANES), F32),
            pltpu.VMEM((WIN, 2, 8, LANES), F32),
            pltpu.VMEM((tiles, chans, LANES), BF16),
            pltpu.VMEM((chans, slots), BF16),
            pltpu.VMEM((2, slots, LANES), F32),
        ],
        3_000_000_000,
        in_smem=1,
        n_in=11,
    )(
        node_count,
        gathered,
        sent,
        first,
        gain_three.reshape(1, chans),
        qkv_t,
        out_t,
        up_t,
        down_t,
        token,
        label,
    )
    got = lax.all_to_all(ballots, "tile", split_axis=0, concat_axis=0, tiled=True)
    (voxel_sums,) = call(
        sums_kernel, [sds((VOX_DEV, chans), F32)], [], 200_000_000, n_in=1
    )(got)
    return (features_out, voxel_sums)


def solution(mesh):
    in_specs = (
        P(("grp", "tile"), None),
        P(("grp", "tile")),
        P(("grp", "tile")),
        P(),
        P(),
        P(),
        P(),
        P(),
        P(),
        P(),
        P(),
        P(),
        P(),
        P(("grp", "tile")),
        P(("grp", "tile"), None),
        P(("grp", "tile")),
    )
    out_specs = (P(("grp", "tile"), None), P(("grp", "tile"), None))
    return jax.shard_map(body, mesh=mesh, in_specs=in_specs, out_specs=out_specs, check_vma=False)
```

```python
import functools
import math

import jax
import jax.numpy as jnp
from jax import lax
from jax.experimental import pallas as pl
from jax.experimental.pallas import tpu as pltpu
from jax.sharding import PartitionSpec as P

HEADS = 12
WIN = 32
VOX_DEV = 256
LANES = 128
FLAG = 16384.0
VMEM = 56 * 1024 * 1024
F32 = jnp.float32
BF16 = jnp.bfloat16
LOG2E = math.log2(math.e)


def iota(shape, dim):
    return lax.broadcasted_iota(jnp.int32, shape, dim)


def dot(a, b):
    return jnp.dot(a, b, preferred_element_type=F32)


def dot_t(a, b):
    return lax.dot_general(a, b, (((1,), (1,)), ((), ())), preferred_element_type=F32)


def eye(n):
    return (iota((n, n), 0) == iota((n, n), 1)).astype(BF16)


def transposed(a):
    return dot_t(eye(a.shape[1]), a).astype(BF16)


def tile(t):
    return slice(t * LANES, (t + 1) * LANES)


def head_order(chans):
    size = chans // HEADS
    cut = 8 * size
    j = iota((chans, 1), 0)
    high = j - cut
    low_src = (j % 8) * size + j // 8
    high_src = (8 + high % 4) * size + high // 8 + (size // 2) * ((high % 8) // 4)
    return jnp.where(j < cut, low_src, high_src)


def slot_of_lane(slots, run):
    t = iota((1, slots), 1)
    at, lane = t // LANES, t % LANES
    p = (4 * (at // run) + lane // WIN) * run + at % run
    return (lane % 8) * LANES + ((lane // 8) % 4) * WIN + p


def reorder(slots, run):
    return (iota((slots, slots), 0) == slot_of_lane(slots, run)).astype(BF16)


def norm_t(x, gain):
    inv = 1.0 / x.shape[0]
    mean = jnp.sum(x, 0, keepdims=True) * inv
    cent = x - mean
    var = jnp.sum(cent * cent, 0, keepdims=True) * inv
    return cent * lax.rsqrt(var + 1e-05) * gain


def load_all(pairs, sems):
    copies = [pltpu.make_async_copy(a, b, sems.at[n]) for n, (a, b) in enumerate(pairs)]
    for copy in copies:
        copy.start()
    for copy in copies:
        copy.wait()


def fold8(x, op):
    y = x[0]
    for n in range(1, x.shape[0]):
        y = op(y, x[n])
    for shift in (4, 2, 1):
        y = op(y, pltpu.roll(y, shift, 0))
    return y


def first_kernel(
    run, count_ref, nodes_hbm, ids_hbm, pos_hbm, gain_one_hbm, gain_two_hbm, qkv_hbm, out_hbm,
    first_ref, sent_ref, nodes_ref, ids_ref, pos_ref, gain_one_ref, gain_two_ref, qkv_ref, out_ref,
    sems, q_s, k_s, v_s, ctx_s, n_s
):
    load_all(
        [
            (nodes_hbm, nodes_ref),
            (ids_hbm, ids_ref),
            (pos_hbm, pos_ref),
            (gain_one_hbm, gain_one_ref),
            (gain_two_hbm, gain_two_ref),
            (qkv_hbm, qkv_ref),
            (out_hbm, out_ref),
        ],
        sems,
    )
    chans, slots = nodes_ref.shape
    tiles = slots // LANES
    size = chans // HEADS
    per = LANES // WIN
    count = count_ref[0]
    cols = jnp.concatenate(
        [pos_ref[...], gain_one_ref[...], gain_two_ref[...], jnp.zeros((3, chans), F32)], 0
    ).T
    qkv_t = transposed(qkv_ref[...])
    out_t = transposed(out_ref[...])
    ids = ids_ref[...]
    coords = []
    for axis in range(3):
        total = jnp.zeros(ids.shape, jnp.int32)
        for level in range(6):
            bit = jnp.bitwise_and(jnp.right_shift(ids, 3 * level + axis), 1)
            total = total + bit * 2**level
        coords.append(total.astype(F32) / 64.0 - 0.5)
    side = eye(LANES)
    spread = (
        iota((LANES, per * LANES), 0)
        == (iota((LANES, per * LANES), 1) // LANES) * WIN + iota((LANES, per * LANES), 1) % WIN
    ).astype(BF16)
    row_head = (iota((chans, LANES), 0) // size) % per
    own_head = row_head == iota((chans, LANES), 1) // WIN
    for t in range(tiles):
        at = tile(t)
        where = cols[:, 0:1] * coords[0][:, at]
        where = where + cols[:, 1:2] * coords[1][:, at]
        where = where + cols[:, 2:3] * coords[2][:, at]
        start = (nodes_ref[:, at].astype(F32) + where).astype(BF16)
        nodes_ref[:, at] = start
        normed = norm_t(start.astype(F32), cols[:, 3:4]).astype(BF16)
        n_s[:, at] = normed
        qv = dot(qkv_t, normed)
        q_s[t] = (qv[:chans] * (size**-0.5)).astype(BF16)
        wide = dot(qv[2 * chans :].astype(BF16), spread)
        for w in range(per):
            v_s[t, w] = jnp.where(own_head, wide[:, tile(w)], 0.0).astype(BF16)
        rows = dot_t(side, normed).astype(BF16)
        k_s[t] = dot_t(rows, qkv_t[chans : 2 * chans]).astype(BF16)

    lane_head = iota((WIN, chans), 1) // size
    window = iota((8, LANES), 1) // WIN
    rank = iota((WIN, LANES), 0) + WIN * (iota((WIN, LANES), 1) // WIN)

    def group(t, _):
        query = q_s[t]
        scores = None
        for w in range(per):
            keys = k_s[t, w * WIN : (w + 1) * WIN, :]
            by_head = jnp.concatenate(
                [jnp.where(lane_head == h, keys, jnp.zeros_like(keys)) for h in range(HEADS)], 0
            )
            got = dot(by_head, query).reshape(-1, 8, LANES)
            scores = got if w == 0 else jnp.where(window[None] == w, got, scores)
        mask = jnp.where(rank + t * LANES < count, 0.0, -1e9).astype(F32)
        mask = mask.reshape(WIN // 8, 8, LANES)
        probs, inverse = [], []
        for h in range(HEADS):
            mine = scores[h * (WIN // 8) : (h + 1) * (WIN // 8)] + mask
            top = fold8(mine, jnp.maximum)
            weight = jnp.exp(mine - top[None])
            inverse.append(1.0 / fold8(weight, jnp.add))
            probs.append(weight.reshape(WIN, LANES).astype(BF16))
        half = per * size
        parts = []
        for j in range(HEADS // per):
            weight = jnp.concatenate(probs[j * per : (j + 1) * per], 0)
            ctx = None
            for w in range(per):
                got = dot(v_s[t, w, j * half : (j + 1) * half, :], weight).reshape(-1, 8, LANES)
                ctx = got if w == 0 else jnp.where(window[None] == w, got, ctx)
            for h in range(per):
                block = ctx[h * (size // 8) : (h + 1) * (size // 8)] * inverse[j * per + h][None]
                parts.append(block.reshape(size, LANES))
        ctx_s[t] = jnp.concatenate(parts, 0).astype(BF16)
        return 0

    lax.fori_loop(0, tiles, group, 0, unroll=2)
    for t in range(tiles):
        at = tile(t)
        first = (nodes_ref[:, at].astype(F32) + dot(out_t, ctx_s[t])).astype(BF16)
        first_ref[:, at] = first
        normed = norm_t(first.astype(F32), cols[:, 4:5])
        kept = iota((1, LANES), 1) + t * LANES < count
        head = jnp.where((iota((16, LANES), 0) > 0) | kept, normed[:16], FLAG)
        n_s[:, at] = jnp.concatenate([head, normed[16:]], 0).astype(BF16)
    sent_ref[...] = dot(n_s[...], reorder(slots, run)).astype(BF16)


def tables_kernel(
    run, cap, qkv_hbm, out_hbm, up_hbm, slot_hbm, owner_hbm, voxel_hbm,
    qkv_t_ref, out_t_ref, up_t_ref, hot_ref, order_ref, label_ref,
    qkv_ref, out_ref, up_ref, slot_ref, owner_ref, voxel_ref, sems
):
    load_all(
        [
            (qkv_hbm, qkv_ref),
            (out_hbm, out_ref),
            (up_hbm, up_ref),
            (slot_hbm, slot_ref),
            (owner_hbm, owner_ref),
            (voxel_hbm, voxel_ref),
        ],
        sems,
    )
    votes = slot_ref.shape[1]
    slots, codes = hot_ref.shape
    owners = codes // cap
    chans = out_ref.shape[0]
    src = head_order(chans)
    src = jnp.concatenate([src, src + chans, src + 2 * chans], 0)
    shuffle = (src == iota((3 * chans, 3 * chans), 1)).astype(BF16)
    qkv_t_ref[...] = dot_t(shuffle, qkv_ref[...]).astype(BF16)
    out_t = transposed(out_ref[...])
    out_t_ref[...] = dot_t(out_t, shuffle[:chans, :chans]).astype(BF16)
    up_t_ref[...] = transposed(up_ref[...])
    order_ref[...] = reorder(slots, run)
    owner = jnp.bitwise_xor(owner_ref[...], lax.axis_index("tile"))
    hot = owner == iota((owners, votes), 0)
    upto = (iota((votes, votes), 0) <= iota((votes, votes), 1)).astype(BF16)
    rank = jnp.sum(jnp.where(hot, dot(hot.astype(BF16), upto), 0.0), 0, keepdims=True)
    code = owner * cap + rank.astype(jnp.int32) - 1
    member = (code == iota((codes, votes), 0)).astype(BF16)
    slot = slot_ref[...]
    row = iota((16, votes), 0)
    facts = jnp.where(
        row == 0,
        slot // 32,
        jnp.where(row == 1, slot % 32, jnp.where(row == 2, voxel_ref[...], 1)),
    )
    listed = dot_t(facts.astype(F32).astype(BF16), member)
    held = listed[3:4] > 0.5
    slot_of = jnp.where(held, listed[0:1] * 32.0 + listed[1:2], -1.0).astype(jnp.int32)
    hot_ref[...] = (slot_of == iota((slots, codes), 0)).astype(BF16)
    label = jnp.where(held, listed[2:3], -1.0)
    label_ref[...] = jnp.broadcast_to(label, label_ref.shape).astype(BF16)


def clean(block):
    head = block[:16].astype(F32)
    gone = head[0:1] > 0.5 * FLAG
    head = jnp.where((iota(head.shape, 0) == 0) & gone, 0.0, head)
    return jnp.concatenate([head.astype(BF16), block[16:]], 0), gone


def partial_attend(run, unit, blocks, kv_t, q_s, k_s, v_s, m_s, s_s, top_s, sum_s, acc_s, fresh):
    rows8 = q_s.shape[1]
    chans = 8 * rows8
    cut = 2 * rows8 // 3
    for n, block_ref in enumerate(blocks):
        for r in range(run):
            block, gone = clean(block_ref[:, tile(unit * run + r)])
            kv = dot(kv_t, block)
            k_s[n * run + r] = kv[:chans].reshape(rows8, 8, LANES)
            v_s[n * run + r] = kv[chans:].reshape(rows8, 8, LANES)
            m_s[n * run + r] = jnp.broadcast_to(jnp.where(gone, -1e9, 0.0), (8, LANES))
    keys = len(blocks) * run

    def one(r, _):
        t = unit * run + r
        query = q_s[t]

        def score(key, top):
            prod = query * k_s[key]
            a = jnp.sum(prod[:cut], 0)
            b = jnp.sum(prod[cut:], 0)
            b = b + pltpu.roll(b, 4, 0)
            mask = m_s[key]
            a = a + mask
            b = b + mask
            s_s[key, 0] = a
            s_s[key, 1] = b
            return jnp.maximum(top[0], a), jnp.maximum(top[1], b)

        if fresh:
            low = jnp.full((8, LANES), -3e38, F32)
            old = (low, low)
        else:
            old = (top_s[t, 0], top_s[t, 1])
        top_a, top_b = lax.fori_loop(0, keys, score, old, unroll=4)

        def gather(key, carry):
            sum_a, sum_b, acc_a, acc_b = carry
            pa = jnp.exp2(s_s[key, 0] - top_a)
            pb = jnp.exp2(s_s[key, 1] - top_b)
            value = v_s[key]
            return (
                sum_a + pa,
                sum_b + pb,
                acc_a + pa[None] * value[:cut],
                acc_b + pb[None] * value[cut:],
            )

        if fresh:
            zero = jnp.zeros((8, LANES), F32)
            held = (
                zero,
                zero,
                jnp.zeros((cut, 8, LANES), F32),
                jnp.zeros((rows8 - cut, 8, LANES), F32),
            )
        else:
            fade_a = jnp.exp2(old[0] - top_a)
            fade_b = jnp.exp2(old[1] - top_b)
            acc = acc_s[t]
            held = (
                sum_s[t, 0] * fade_a,
                sum_s[t, 1] * fade_b,
                acc[:cut] * fade_a[None],
                acc[cut:] * fade_b[None],
            )
        sum_a, sum_b, acc_a, acc_b = lax.fori_loop(0, keys, gather, held, unroll=4)
        return t, top_a, top_b, sum_a, sum_b, acc_a, acc_b

    return one


def near_kernel(
    run, own_ref, near_ref, qkv_t_ref, q_ref, top_ref, sum_ref, acc_ref, k_s, v_s, m_s, s_s
):
    chans, slots = own_ref.shape
    tiles = slots // LANES
    scale = (chans // HEADS) ** -0.5 * LOG2E
    q_t = qkv_t_ref[:chans, :]
    for t in range(tiles):
        own, _ = clean(own_ref[:, tile(t)])
        q_ref[t] = (dot(q_t, own) * scale).reshape(chans // 8, 8, LANES)
    for unit in range(tiles // run):
        one = partial_attend(
            run, unit, [own_ref, near_ref], qkv_t_ref[chans:, :], q_ref, k_s, v_s, m_s, s_s,
            None, None, None, True
        )

        def step(r, _, one=one):
            t, top_a, top_b, sum_a, sum_b, acc_a, acc_b = one(r, 0)
            top_ref[t, 0] = top_a
            top_ref[t, 1] = top_b
            sum_ref[t, 0] = sum_a
            sum_ref[t, 1] = sum_b
            acc_ref[t] = jnp.concatenate([acc_a, acc_b], 0)
            return 0

        lax.fori_loop(0, run, step, 0)


def second_kernel(
    run, cap, far, count_ref, *refs
):
    blocks, refs = refs[:far], refs[far:]
    (
        first_ref, q_ref, top_ref, sum_ref, acc_ref, gain_ref, qkv_t_ref, out_t_ref, up_t_ref,
        down_hbm, hot_ref, order_ref, label_ref
    ) = refs[:13]
    chans, slots = first_ref.shape
    codes = hot_ref.shape[1]
    owners = codes // cap
    feat_ref, votes_refs = refs[13], refs[14 : 14 + owners]
    k_s, v_s, m_s, s_s, ctx_s, bf_s, down_ref, sem = refs[14 + owners :]
    load_down = pltpu.make_async_copy(down_hbm, down_ref, sem)
    load_down.start()
    tiles = slots // LANES
    count = count_ref[0]
    for unit in range(tiles // run):
        one = partial_attend(
            run, unit, blocks, qkv_t_ref[chans:, :], q_ref, k_s, v_s, m_s, s_s,
            top_ref, sum_ref, acc_ref, False
        )

        def step(r, _, one=one):
            t, _, _, sum_a, sum_b, acc_a, acc_b = one(r, 0)
            ctx = jnp.concatenate([acc_a / sum_a[None], acc_b / sum_b[None]], 0)
            ctx_s[t] = ctx.reshape(chans, LANES).astype(BF16)
            return 0

        lax.fori_loop(0, run, step, 0)
    ctx = dot_t(
        jnp.concatenate([ctx_s[t] for t in range(tiles)], 1), order_ref[...]
    ).astype(BF16)
    gain = jnp.concatenate([gain_ref[...], jnp.zeros((7, chans), F32)], 0).T[:, 0:1]
    load_down.wait()
    for t in range(tiles):
        at = tile(t)
        second = first_ref[:, at].astype(F32) + dot(out_t_ref[...], ctx[:, at])
        inner = norm_t(second, gain).astype(BF16)
        hidden = jax.nn.gelu(dot(up_t_ref[...], inner)).astype(BF16)
        third = second + dot(down_ref[...], hidden)
        third = jnp.where(iota((1, LANES), 1) + t * LANES < count, third, 0.0)
        feat_ref[:, at] = third
        bf_s[:, at] = third.astype(BF16)
    picked = dot(bf_s[...], hot_ref[...]).astype(BF16)
    for o in range(owners):
        votes_refs[o][:chans, :] = picked[:, o * cap : (o + 1) * cap]
        votes_refs[o][chans:, :] = label_ref[:, o * cap : (o + 1) * cap]


def sums_kernel(*refs):
    got, out_ref = refs[:-1], refs[-1]
    chans, voxels = out_ref.shape
    cap = got[0].shape[1]
    total = jnp.zeros(out_ref.shape, F32)
    for ref in got:
        label = ref[chans:, :].astype(F32)[0:1]
        hot = (label == iota((voxels, cap), 0).astype(F32)).astype(BF16)
        total = total + dot_t(ref[:chans, :], hot)
    out_ref[...] = total


def call(kernel, outs, scratch, flops, spaces):
    return pl.pallas_call(
        kernel,
        out_shape=outs,
        in_specs=[
            pl.BlockSpec(memory_space={"s": pltpu.SMEM, "v": pltpu.VMEM, "a": pl.ANY}[c])
            for c in spaces
        ],
        out_specs=[pl.BlockSpec(memory_space=pltpu.VMEM)] * len(outs),
        scratch_shapes=scratch,
        compiler_params=pltpu.CompilerParams(vmem_limit_bytes=VMEM),
        cost_estimate=pl.CostEstimate(flops=flops, bytes_accessed=2 << 20, transcendentals=0),
    )


def turned(x, axis, bit):
    n = lax.axis_size(axis)
    return lax.ppermute(x, axis, [(i, i ^ bit) for i in range(n)])


def body(
    nodes,
    node_ids,
    node_count,
    pos_weight,
    gain_one,
    qkv_one,
    out_one,
    gain_two,
    qkv_two,
    out_two,
    gain_three,
    w_up,
    w_down,
    vote_slot,
    vote_owner,
    vote_voxel,
):
    slots, chans = nodes.shape
    groups, owners = lax.axis_size("grp"), lax.axis_size("tile")
    run = WIN // groups
    votes = vote_slot.shape[0]
    cap = 2 * votes // owners
    codes = owners * cap
    tiles = slots // LANES
    rows8 = chans // 8
    hidden = w_up.shape[1]
    per = LANES // WIN
    sds = jax.ShapeDtypeStruct
    vmem = pltpu.VMEM
    dma = pltpu.SemaphoreType.DMA

    first, sent = call(
        functools.partial(first_kernel, run),
        [sds((chans, slots), BF16), sds((chans, slots), BF16)],
        [
            vmem((chans, slots), BF16),
            vmem((1, slots), jnp.int32),
            vmem((3, chans), F32),
            vmem((1, chans), F32),
            vmem((1, chans), F32),
            vmem((chans, 3 * chans), BF16),
            vmem((chans, chans), BF16),
            dma((7,)),
            vmem((tiles, chans, LANES), BF16),
            vmem((tiles, LANES, chans), BF16),
            vmem((tiles, per, chans, LANES), BF16),
            vmem((tiles, chans, LANES), BF16),
            vmem((chans, slots), BF16),
        ],
        2_000_000_000,
        "saaaaaaa",
    )(
        node_count,
        nodes.T,
        node_ids.reshape(1, slots),
        pos_weight,
        gain_one.reshape(1, chans),
        gain_two.reshape(1, chans),
        qkv_one,
        out_one,
    )
    near = turned(sent, "grp", 1)
    bit = groups // 2
    far = []
    while bit > 1:
        far += [turned(block, "grp", bit) for block in [sent] + far]
        bit //= 2
    far += [turned(block, "grp", 1) for block in far]
    qkv_t, out_t, up_t, hot, order, label = call(
        functools.partial(tables_kernel, run, cap),
        [
            sds((3 * chans, chans), BF16),
            sds((chans, chans), BF16),
            sds((hidden, chans), BF16),
            sds((slots, codes), BF16),
            sds((slots, slots), BF16),
            sds((16, codes), BF16),
        ],
        [
            vmem((chans, 3 * chans), BF16),
            vmem((chans, chans), BF16),
            vmem((chans, hidden), BF16),
            vmem((1, votes), jnp.int32),
            vmem((1, votes), jnp.int32),
            vmem((1, votes), jnp.int32),
            dma((6,)),
        ],
        2_000_000_000,
        "aaaaaa",
    )(
        qkv_two,
        out_two,
        w_up,
        vote_slot.reshape(1, votes),
        vote_owner.reshape(1, votes),
        vote_voxel.reshape(1, votes),
    )
    state = [
        sds((tiles, rows8, 8, LANES), F32),
        sds((tiles, 2, 8, LANES), F32),
        sds((tiles, 2, 8, LANES), F32),
        sds((tiles, rows8, 8, LANES), F32),
    ]

    def key_scratch(keys):
        return [
            vmem((keys, rows8, 8, LANES), F32),
            vmem((keys, rows8, 8, LANES), F32),
            vmem((keys, 8, LANES), F32),
            vmem((keys, 2, 8, LANES), F32),
        ]

    query, top, total, acc = call(
        functools.partial(near_kernel, run),
        state,
        key_scratch(2 * run),
        3_000_000_000,
        "vvv",
    )(sent, near, qkv_t)
    features_t, *ballots = call(
        functools.partial(second_kernel, run, cap, len(far)),
        [sds((chans, slots), F32)] + [sds((chans + 16, cap), BF16)] * owners,
        key_scratch(len(far) * run)
        + [
            vmem((tiles, chans, LANES), BF16),
            vmem((chans, slots), BF16),
            vmem((chans, hidden), BF16),
            dma,
        ],
        3_000_000_000,
        "s" + "v" * len(far) + "vvvvvvvvvavvv",
    )(
        node_count,
        *far,
        first,
        query,
        top,
        total,
        acc,
        gain_three.reshape(1, chans),
        qkv_t,
        out_t,
        up_t,
        w_down.T,
        hot,
        order,
        label,
    )
    got = [ballots[0]] + [turned(ballots[k], "tile", k) for k in range(owners - 1, 0, -1)]
    (sums_t,) = call(
        sums_kernel, [sds((chans, VOX_DEV), F32)], [], 200_000_000, "v" * owners
    )(*got)
    return (features_t.T, sums_t.T)


def solution(mesh):
    in_specs = (
        P(("grp", "tile"), None),
        P(("grp", "tile")),
        P(("grp", "tile")),
        P(),
        P(),
        P(),
        P(),
        P(),
        P(),
        P(),
        P(),
        P(),
        P(),
        P(("grp", "tile")),
        P(("grp", "tile"), None),
        P(("grp", "tile")),
    )
    out_specs = (P(("grp", "tile"), None), P(("grp", "tile"), None))
    return jax.shard_map(body, mesh=mesh, in_specs=in_specs, out_specs=out_specs, check_vma=False)
```

```python
import functools
import math

import jax
import jax.numpy as jnp
from jax import lax
from jax.experimental import pallas as pl
from jax.experimental.pallas import tpu as pltpu
from jax.sharding import PartitionSpec as P

HEADS = 12
WIN = 32
VOX_DEV = 256
LANES = 128
FLAG = 16384.0
VMEM = 64 * 1024 * 1024 - 65536
F32 = jnp.float32
BF16 = jnp.bfloat16
LOG2E = math.log2(math.e)


def iota(shape, dim):
    return lax.broadcasted_iota(jnp.int32, shape, dim)


def dot(a, b):
    return jnp.dot(a, b, preferred_element_type=F32)


def dot_t(a, b):
    return lax.dot_general(a, b, (((1,), (1,)), ((), ())), preferred_element_type=F32)


def eye(n):
    return (iota((n, n), 0) == iota((n, n), 1)).astype(BF16)


def transposed(a):
    return dot_t(eye(a.shape[1]), a).astype(BF16)


def tile(t):
    return slice(t * LANES, (t + 1) * LANES)


def head_order(chans):
    size = chans // HEADS
    cut = 8 * size
    j = iota((chans, 1), 0)
    high = j - cut
    low_src = (j % 8) * size + j // 8
    high_src = (8 + high % 4) * size + high // 8 + (size // 2) * ((high % 8) // 4)
    return jnp.where(j < cut, low_src, high_src)


def slot_of_lane(slots, run):
    t = iota((1, slots), 1)
    at, lane = t // LANES, t % LANES
    p = (4 * (at // run) + lane // WIN) * run + at % run
    return (lane % 8) * LANES + ((lane // 8) % 4) * WIN + p


def reorder(slots, run):
    return (iota((slots, slots), 0) == slot_of_lane(slots, run)).astype(BF16)


def norm_t(x, gain):
    inv = 1.0 / x.shape[0]
    mean = jnp.sum(x, 0, keepdims=True) * inv
    cent = x - mean
    var = jnp.sum(cent * cent, 0, keepdims=True) * inv
    return cent * lax.rsqrt(var + 1e-05) * gain


def start_all(pairs, sems):
    copies = [pltpu.make_async_copy(a, b, sems.at[n]) for n, (a, b) in enumerate(pairs)]
    for copy in copies:
        copy.start()
    return copies


def wait_all(copies):
    for copy in copies:
        copy.wait()


def fold8(x, op):
    y = x[0]
    for n in range(1, x.shape[0]):
        y = op(y, x[n])
    for shift in (4, 2, 1):
        y = op(y, pltpu.roll(y, shift, 0))
    return y


def first_kernel(
    run, count_ref, nodes_hbm, ids_hbm, pos_hbm, gain_one_hbm, gain_two_hbm, qkv_hbm, out_hbm,
    first_ref, sent_ref, nodes_ref, ids_ref, pos_ref, gain_one_ref, gain_two_ref, qkv_ref, out_ref,
    sems, qkv_s, q_s, k_s, v_s, ctx_s, n_s
):
    loads = start_all(
        [
            (nodes_hbm, nodes_ref),
            (ids_hbm, ids_ref),
            (pos_hbm, pos_ref),
            (gain_one_hbm, gain_one_ref),
            (gain_two_hbm, gain_two_ref),
            (qkv_hbm, qkv_ref),
            (out_hbm, out_ref),
        ],
        sems,
    )
    chans, slots = nodes_ref.shape
    tiles = slots // LANES
    size = chans // HEADS
    per = LANES // WIN
    count = count_ref[0]
    wait_all(loads[:5])
    cols = jnp.concatenate(
        [pos_ref[...], gain_one_ref[...], gain_two_ref[...], jnp.zeros((3, chans), F32)], 0
    ).T
    ids = ids_ref[...]
    start = None
    for axis in range(3):
        total = jnp.zeros(ids.shape, jnp.int32)
        for level in range(6):
            bit = jnp.bitwise_and(jnp.right_shift(ids, 3 * level + axis), 1)
            total = total + bit * 2**level
        term = cols[:, axis : axis + 1] * (total.astype(F32) / 64.0 - 0.5)
        start = term if start is None else start + term
    start = (nodes_ref[...].astype(F32) + start).astype(BF16)
    nodes_ref[...] = start
    n_s[...] = norm_t(start.astype(F32), cols[:, 3:4]).astype(BF16)
    wait_all(loads[5:])
    qkv_t = transposed(qkv_ref[...])
    out_t = transposed(out_ref[...])
    qkv_s[...] = dot(qkv_t, n_s[...]).astype(BF16)
    side = eye(LANES)
    spread = (
        iota((LANES, per * LANES), 0)
        == (iota((LANES, per * LANES), 1) // LANES) * WIN + iota((LANES, per * LANES), 1) % WIN
    ).astype(BF16)
    row_head = (iota((chans, LANES), 0) // size) % per
    own_head = row_head == iota((chans, LANES), 1) // WIN
    for t in range(tiles):
        q_s[t] = qkv_s[:chans, tile(t)] * jnp.asarray(size**-0.5, BF16)
        k_s[t] = dot_t(side, qkv_s[chans : 2 * chans, tile(t)]).astype(BF16)
    for t in range(tiles):
        wide = dot(qkv_s[2 * chans :, tile(t)], spread)
        for w in range(per):
            v_s[t, w] = jnp.where(own_head, wide[:, tile(w)], 0.0).astype(BF16)

    lane_head = iota((WIN, chans), 1) // size
    window = iota((8, LANES), 1) // WIN
    rank = iota((WIN, LANES), 0) + WIN * (iota((WIN, LANES), 1) // WIN)

    def group(t, _):
        query = q_s[t]
        scores = None
        for w in range(per):
            keys = k_s[t, w * WIN : (w + 1) * WIN, :]
            by_head = jnp.concatenate(
                [jnp.where(lane_head == h, keys, jnp.zeros_like(keys)) for h in range(HEADS)], 0
            )
            got = dot(by_head, query).reshape(-1, 8, LANES)
            scores = got if w == 0 else jnp.where(window[None] == w, got, scores)
        mask = jnp.where(rank + t * LANES < count, 0.0, -1e9).astype(F32)
        mask = mask.reshape(WIN // 8, 8, LANES)
        probs, inverse = [], []
        for h in range(HEADS):
            mine = scores[h * (WIN // 8) : (h + 1) * (WIN // 8)] + mask
            top = fold8(mine, jnp.maximum)
            weight = jnp.exp(mine - top[None])
            inverse.append(1.0 / fold8(weight, jnp.add))
            probs.append(weight.reshape(WIN, LANES).astype(BF16))
        half = per * size
        parts = []
        for j in range(HEADS // per):
            weight = jnp.concatenate(probs[j * per : (j + 1) * per], 0)
            ctx = None
            for w in range(per):
                got = dot(v_s[t, w, j * half : (j + 1) * half, :], weight).reshape(-1, 8, LANES)
                ctx = got if w == 0 else jnp.where(window[None] == w, got, ctx)
            for h in range(per):
                block = ctx[h * (size // 8) : (h + 1) * (size // 8)] * inverse[j * per + h][None]
                parts.append(block.reshape(size, LANES))
        ctx_s[t] = jnp.concatenate(parts, 0).astype(BF16)
        return 0

    lax.fori_loop(0, tiles, group, 0, unroll=2)
    ctx = jnp.concatenate([ctx_s[t] for t in range(tiles)], 1)
    first = (nodes_ref[...].astype(F32) + dot(out_t, ctx)).astype(BF16)
    first_ref[...] = first
    normed = norm_t(first.astype(F32), cols[:, 4:5])
    kept = iota((1, slots), 1) < count
    head = jnp.where((iota((16, slots), 0) > 0) | kept, normed[:16], FLAG)
    normed = jnp.concatenate([head, normed[16:]], 0).astype(BF16)
    sent_ref[...] = dot(normed, reorder(slots, run)).astype(BF16)


def tables_kernel(
    run, cap, qkv_hbm, out_hbm, up_hbm, slot_hbm, owner_hbm, voxel_hbm,
    qkv_t_ref, out_t_ref, up_t_ref, hot_ref, order_ref, label_ref,
    qkv_ref, out_ref, up_ref, slot_ref, owner_ref, voxel_ref, sems
):
    loads = start_all(
        [
            (qkv_hbm, qkv_ref),
            (out_hbm, out_ref),
            (up_hbm, up_ref),
            (slot_hbm, slot_ref),
            (owner_hbm, owner_ref),
            (voxel_hbm, voxel_ref),
        ],
        sems,
    )
    wait_all(loads)
    votes = slot_ref.shape[1]
    slots, codes = hot_ref.shape
    owners = codes // cap
    chans = out_ref.shape[0]
    src = head_order(chans)
    src = jnp.concatenate([src, src + chans, src + 2 * chans], 0)
    shuffle = (src == iota((3 * chans, 3 * chans), 1)).astype(BF16)
    qkv_t_ref[...] = dot_t(shuffle, qkv_ref[...]).astype(BF16)
    out_t = transposed(out_ref[...])
    out_t_ref[...] = dot_t(out_t, shuffle[:chans, :chans]).astype(BF16)
    up_t_ref[...] = transposed(up_ref[...])
    order_ref[...] = reorder(slots, run)
    owner = jnp.bitwise_xor(owner_ref[...], lax.axis_index("tile"))
    hot = owner == iota((owners, votes), 0)
    upto = (iota((votes, votes), 0) <= iota((votes, votes), 1)).astype(BF16)
    rank = jnp.sum(jnp.where(hot, dot(hot.astype(BF16), upto), 0.0), 0, keepdims=True)
    code = owner * cap + rank.astype(jnp.int32) - 1
    member = (code == iota((codes, votes), 0)).astype(BF16)
    slot = slot_ref[...]
    row = iota((16, votes), 0)
    facts = jnp.where(
        row == 0,
        slot // 32,
        jnp.where(row == 1, slot % 32, jnp.where(row == 2, voxel_ref[...], 1)),
    )
    listed = dot_t(facts.astype(F32).astype(BF16), member)
    held = listed[3:4] > 0.5
    slot_of = jnp.where(held, listed[0:1] * 32.0 + listed[1:2], -1.0).astype(jnp.int32)
    hot_ref[...] = (slot_of == iota((slots, codes), 0)).astype(BF16)
    label = jnp.where(held, listed[2:3], -1.0)
    label_ref[...] = jnp.broadcast_to(label, label_ref.shape).astype(BF16)


def clean(block):
    head = block[:16].astype(F32)
    gone = head[0:1] > 0.5 * FLAG
    head = jnp.where((iota(head.shape, 0) == 0) & gone, 0.0, head)
    return jnp.concatenate([head.astype(BF16), block[16:]], 0), gone


def fold16(x):
    parts = [x[n] for n in range(x.shape[0])]
    while len(parts) > 1:
        parts = [a + b for a, b in zip(parts[::2], parts[1::2])]
    wide = parts[0].astype(F32)
    return wide[:8] + wide[8:]


def twice(x):
    return jnp.concatenate([x, x], 0).astype(BF16)


def add_keys(blocks, kv_t, k_s, v_s, m_s):
    chans = kv_t.shape[1]
    rows16 = chans // 16
    tiles = k_s.shape[1]
    for n, block in enumerate(blocks):
        block, gone = clean(block)
        kv = dot(kv_t, block).astype(BF16)
        mask = jnp.where(gone, -1e9, 0.0)
        for t in range(tiles):
            k_s[n, t] = kv[:chans, tile(t)].reshape(rows16, 16, LANES)
            v_s[n, t] = kv[chans:, tile(t)].reshape(rows16, 16, LANES)
            m_s[n, t] = jnp.broadcast_to(mask[:, tile(t)], (8, LANES))


def attend_more(t, run, q_s, k_s, v_s, m_s, s_s, old):
    rows16 = q_s.shape[1]
    cut = 2 * rows16 // 3
    blocks = k_s.shape[0]
    keys = blocks * run
    base = (t // run) * run
    query = q_s[t]

    def score(key, top):
        n, at = key // run, base + key % run
        prod = query * k_s[n, at]
        a = fold16(prod[:cut])
        b = fold16(prod[cut:])
        b = b + pltpu.roll(b, 4, 0)
        mask = m_s[n, at]
        a = a * LOG2E + mask
        b = b * LOG2E + mask
        s_s[key, 0] = a
        s_s[key, 1] = b
        return jnp.maximum(top[0], a), jnp.maximum(top[1], b)

    if old is None:
        low = jnp.full((8, LANES), -3e38, F32)
        zero = jnp.zeros((8, LANES), F32)
        top_a, top_b = lax.fori_loop(0, keys, score, (low, low), unroll=4)
        held = (zero, zero, jnp.zeros((cut, 16, LANES), F32),
                jnp.zeros((rows16 - cut, 16, LANES), F32))
    else:
        top, total, acc = old
        top_a, top_b = lax.fori_loop(0, keys, score, (top[0], top[1]), unroll=4)
        fade_a = jnp.exp2(top[0] - top_a)
        fade_b = jnp.exp2(top[1] - top_b)
        both_a = jnp.concatenate([fade_a, fade_a], 0)
        both_b = jnp.concatenate([fade_b, fade_b], 0)
        held = (total[0] * fade_a, total[1] * fade_b, acc[:cut] * both_a[None],
                acc[cut:] * both_b[None])

    def gather(step, carry):
        sum_a, sum_b, acc_a, acc_b = carry
        got_a, got_b = [], []
        for key in range(4):
            key = 4 * step + key
            pa = jnp.exp2(s_s[key, 0] - top_a)
            pb = jnp.exp2(s_s[key, 1] - top_b)
            sum_a = sum_a + pa
            sum_b = sum_b + pb
            value = v_s[key // run, base + key % run]
            got_a.append(twice(pa)[None] * value[:cut])
            got_b.append(twice(pb)[None] * value[cut:])
        acc_a = acc_a + ((got_a[0] + got_a[1]) + (got_a[2] + got_a[3])).astype(F32)
        acc_b = acc_b + ((got_b[0] + got_b[1]) + (got_b[2] + got_b[3])).astype(F32)
        return sum_a, sum_b, acc_a, acc_b

    sum_a, sum_b, acc_a, acc_b = lax.fori_loop(0, keys // 4, gather, held)
    return (top_a, top_b), (sum_a, sum_b), (acc_a, acc_b)


def keep_state(t, state, top_ref, sum_ref, acc_ref):
    top, total, acc = state
    for n in range(2):
        top_ref[t, n] = top[n]
        sum_ref[t, n] = total[n]
    acc_ref[t] = jnp.concatenate(acc, 0)


def near_kernel(
    run, own_ref, near_hbm, qkv_t_ref, q_ref, top_ref, sum_ref, acc_ref,
    near_ref, sem, k_s, v_s, m_s, s_s
):
    load = pltpu.make_async_copy(near_hbm, near_ref, sem)
    load.start()
    chans, slots = own_ref.shape
    tiles = slots // LANES
    scale = (chans // HEADS) ** -0.5
    own, _ = clean(own_ref[...])
    query = (dot(qkv_t_ref[:chans, :], own) * scale).astype(BF16)
    for t in range(tiles):
        q_ref[t] = query[:, tile(t)].reshape(chans // 16, 16, LANES)
    kv_t = qkv_t_ref[chans:, :]
    load.wait()
    add_keys([own_ref[...], near_ref[...]], kv_t, k_s, v_s, m_s)

    def step(t, _):
        state = attend_more(t, run, q_ref, k_s, v_s, m_s, s_s, None)
        keep_state(t, state, top_ref, sum_ref, acc_ref)
        return 0

    lax.fori_loop(0, tiles, step, 0)


def middle_kernel(run, count, *refs):
    blocks, refs = refs[:count], refs[count:]
    q_ref, top_in, sum_in, acc_in, qkv_t_ref, top_ref, sum_ref, acc_ref = refs[:8]
    block_s, sems, k_s, v_s, m_s, s_s = refs[8:]
    wait_all(start_all([(blocks[n], block_s.at[n]) for n in range(count)], sems))
    chans = qkv_t_ref.shape[1]
    add_keys([block_s[n] for n in range(count)], qkv_t_ref[chans:, :], k_s, v_s, m_s)

    def step(t, _):
        old = (top_in[t], sum_in[t], acc_in[t])
        state = attend_more(t, run, q_ref, k_s, v_s, m_s, s_s, old)
        keep_state(t, state, top_ref, sum_ref, acc_ref)
        return 0

    lax.fori_loop(0, q_ref.shape[0], step, 0)


def second_kernel(run, cap, far, count_ref, *refs):
    blocks, refs = refs[:far], refs[far:]
    (
        first_hbm, q_ref, top_in, sum_in, acc_in, gain_ref, qkv_t_ref, out_t_ref, up_t_hbm,
        down_hbm, hot_hbm, order_hbm, label_ref
    ) = refs[:13]
    chans, slots = first_hbm.shape
    codes = hot_hbm.shape[1]
    owners = codes // cap
    feat_ref, votes_refs = refs[13], refs[14 : 14 + owners]
    (
        block_s, sems, k_s, v_s, m_s, s_s, ctx_s, bf_s, first_ref, up_t_ref, down_ref, hot_ref,
        order_ref, late_sems
    ) = refs[14 + owners :]
    loads = start_all([(blocks[n], block_s.at[n]) for n in range(far)], sems)
    late = start_all(
        [
            (order_hbm, order_ref),
            (first_hbm, first_ref),
            (up_t_hbm, up_t_ref),
            (down_hbm, down_ref),
            (hot_hbm, hot_ref),
        ],
        late_sems,
    )
    wait_all(loads)
    tiles = slots // LANES
    count = count_ref[0]
    add_keys([block_s[n] for n in range(far)], qkv_t_ref[chans:, :], k_s, v_s, m_s)

    def step(t, _):
        old = (top_in[t], sum_in[t], acc_in[t])
        _, total, acc = attend_more(t, run, q_ref, k_s, v_s, m_s, s_s, old)
        share = [1.0 / total[n] for n in range(2)]
        ctx = jnp.concatenate(
            [acc[n] * jnp.concatenate([share[n], share[n]], 0)[None] for n in range(2)], 0
        )
        ctx_s[t] = ctx.reshape(chans, LANES).astype(BF16)
        return 0

    lax.fori_loop(0, tiles, step, 0)
    ctx = jnp.concatenate([ctx_s[t] for t in range(tiles)], 1)
    wait_all(late)
    ctx = dot_t(ctx, order_ref[...]).astype(BF16)
    gain = jnp.concatenate([gain_ref[...], jnp.zeros((7, chans), F32)], 0).T[:, 0:1]
    second = first_ref[...].astype(F32) + dot(out_t_ref[...], ctx)
    inner = norm_t(second, gain).astype(BF16)
    kept = iota((1, slots), 1) < count
    wide = 2 * LANES
    cuts = [slice(at, at + wide) for at in range(0, slots, wide)]
    up_t = up_t_ref[...]
    raised = dot(up_t, inner[:, cuts[0]])
    for n, at in enumerate(cuts):
        now = raised
        if n + 1 < len(cuts):
            raised = dot(up_t, inner[:, cuts[n + 1]])
        hidden = jax.nn.gelu(now).astype(BF16)
        third = second[:, at] + dot(down_ref[...], hidden)
        third = jnp.where(kept[:, at], third, 0.0)
        feat_ref[:, at] = third
        bf_s[:, at] = third.astype(BF16)
    picked = dot(bf_s[...], hot_ref[...]).astype(BF16)
    for o in range(owners):
        votes_refs[o][:chans, :] = picked[:, o * cap : (o + 1) * cap]
        votes_refs[o][chans:, :] = label_ref[:, o * cap : (o + 1) * cap]


def sums_kernel(owners, *refs):
    got, out_ref, got_s, sems = refs[:owners], refs[owners], refs[owners + 1], refs[owners + 2]
    wait_all(start_all([(got[n], got_s.at[n]) for n in range(owners)], sems))
    chans, voxels = out_ref.shape
    cap = got_s.shape[2]
    total = jnp.zeros(out_ref.shape, F32)
    for n in range(owners):
        label = got_s[n, chans:, :].astype(F32)[0:1]
        hot = (label == iota((voxels, cap), 0).astype(F32)).astype(BF16)
        total = total + dot_t(got_s[n, :chans, :], hot)
    out_ref[...] = total


def call(kernel, outs, scratch, flops, spaces):
    return pl.pallas_call(
        kernel,
        out_shape=outs,
        in_specs=[
            pl.BlockSpec(memory_space={"s": pltpu.SMEM, "v": pltpu.VMEM, "a": pl.ANY}[c])
            for c in spaces
        ],
        out_specs=[pl.BlockSpec(memory_space=pltpu.VMEM)] * len(outs),
        scratch_shapes=scratch,
        compiler_params=pltpu.CompilerParams(vmem_limit_bytes=VMEM),
        cost_estimate=pl.CostEstimate(flops=flops, bytes_accessed=2 << 20, transcendentals=0),
    )


def turned(x, axis, bit):
    n = lax.axis_size(axis)
    return lax.ppermute(x, axis, [(i, i ^ bit) for i in range(n)])


def body(
    nodes,
    node_ids,
    node_count,
    pos_weight,
    gain_one,
    qkv_one,
    out_one,
    gain_two,
    qkv_two,
    out_two,
    gain_three,
    w_up,
    w_down,
    vote_slot,
    vote_owner,
    vote_voxel,
):
    slots, chans = nodes.shape
    groups, owners = lax.axis_size("grp"), lax.axis_size("tile")
    run = WIN // groups
    votes = vote_slot.shape[0]
    cap = 2 * votes // owners
    codes = owners * cap
    tiles = slots // LANES
    rows16 = chans // 16
    hidden = w_up.shape[1]
    per = LANES // WIN
    sds = jax.ShapeDtypeStruct
    vmem = pltpu.VMEM
    dma = pltpu.SemaphoreType.DMA

    first, sent = call(
        functools.partial(first_kernel, run),
        [sds((chans, slots), BF16), sds((chans, slots), BF16)],
        [
            vmem((chans, slots), BF16),
            vmem((1, slots), jnp.int32),
            vmem((3, chans), F32),
            vmem((1, chans), F32),
            vmem((1, chans), F32),
            vmem((chans, 3 * chans), BF16),
            vmem((chans, chans), BF16),
            dma((7,)),
            vmem((3 * chans, slots), BF16),
            vmem((tiles, chans, LANES), BF16),
            vmem((tiles, LANES, chans), BF16),
            vmem((tiles, per, chans, LANES), BF16),
            vmem((tiles, chans, LANES), BF16),
            vmem((chans, slots), BF16),
        ],
        2_000_000_000,
        "saaaaaaa",
    )(
        node_count,
        nodes.T,
        node_ids.reshape(1, slots),
        pos_weight,
        gain_one.reshape(1, chans),
        gain_two.reshape(1, chans),
        qkv_one,
        out_one,
    )
    near = turned(sent, "grp", 1)
    bit = groups // 2
    mid = []
    while bit > 1:
        mid += [turned(block, "grp", bit) for block in [sent] + mid]
        bit //= 2
    qkv_t, out_t, up_t, hot, order, label = call(
        functools.partial(tables_kernel, run, cap),
        [
            sds((3 * chans, chans), BF16),
            sds((chans, chans), BF16),
            sds((hidden, chans), BF16),
            sds((slots, codes), BF16),
            sds((slots, slots), BF16),
            sds((16, codes), BF16),
        ],
        [
            vmem((chans, 3 * chans), BF16),
            vmem((chans, chans), BF16),
            vmem((chans, hidden), BF16),
            vmem((1, votes), jnp.int32),
            vmem((1, votes), jnp.int32),
            vmem((1, votes), jnp.int32),
            dma((6,)),
        ],
        2_000_000_000,
        "aaaaaa",
    )(
        qkv_two,
        out_two,
        w_up,
        vote_slot.reshape(1, votes),
        vote_owner.reshape(1, votes),
        vote_voxel.reshape(1, votes),
    )
    state = [
        sds((tiles, 2, 8, LANES), F32),
        sds((tiles, 2, 8, LANES), F32),
        sds((tiles, rows16, 16, LANES), F32),
    ]

    def key_scratch(blocks):
        return [
            vmem((blocks, tiles, rows16, 16, LANES), BF16),
            vmem((blocks, tiles, rows16, 16, LANES), BF16),
            vmem((blocks, tiles, 8, LANES), F32),
            vmem((blocks * run, 2, 8, LANES), F32),
        ]

    query, *held = call(
        functools.partial(near_kernel, run),
        [sds((tiles, rows16, 16, LANES), BF16)] + state,
        [vmem((chans, slots), BF16), dma] + key_scratch(2),
        3_000_000_000,
        "vav",
    )(sent, near, qkv_t)
    mid, query = lax.optimization_barrier((mid, query))
    far = [turned(block, "grp", 1) for block in mid]
    held = call(
        functools.partial(middle_kernel, run, len(mid)),
        state,
        [vmem((len(mid), chans, slots), BF16), dma((len(mid),))] + key_scratch(len(mid)),
        2_000_000_000,
        "a" * len(mid) + "vvvvv",
    )(*mid, query, *held, qkv_t)
    features_t, *ballots = call(
        functools.partial(second_kernel, run, cap, len(far)),
        [sds((chans, slots), F32)] + [sds((chans + 16, cap), BF16)] * owners,
        [vmem((len(far), chans, slots), BF16), dma((len(far),))]
        + key_scratch(len(far))
        + [
            vmem((tiles, chans, LANES), BF16),
            vmem((chans, slots), BF16),
            vmem((chans, slots), BF16),
            vmem((hidden, chans), BF16),
            vmem((chans, hidden), BF16),
            vmem((slots, codes), BF16),
            vmem((slots, slots), BF16),
            dma((5,)),
        ],
        3_000_000_000,
        "s" + "a" * len(far) + "avvvvvvvaaaav",
    )(
        node_count,
        *far,
        first,
        query,
        *held,
        gain_three.reshape(1, chans),
        qkv_t,
        out_t,
        up_t,
        w_down.T,
        hot,
        order,
        label,
    )
    got = [ballots[0]] + [turned(ballots[k], "tile", k) for k in range(owners - 1, 0, -1)]
    (sums_t,) = call(
        functools.partial(sums_kernel, owners),
        [sds((chans, VOX_DEV), F32)],
        [vmem((owners, chans + 16, cap), BF16), dma((owners,))],
        200_000_000,
        "a" * owners,
    )(*got)
    return (features_t.T, sums_t.T)


def solution(mesh):
    in_specs = (
        P(("grp", "tile"), None),
        P(("grp", "tile")),
        P(("grp", "tile")),
        P(),
        P(),
        P(),
        P(),
        P(),
        P(),
        P(),
        P(),
        P(),
        P(),
        P(("grp", "tile")),
        P(("grp", "tile"), None),
        P(("grp", "tile")),
    )
    out_specs = (P(("grp", "tile"), None), P(("grp", "tile"), None))
    return jax.shard_map(body, mesh=mesh, in_specs=in_specs, out_specs=out_specs, check_vma=False)
```

```python
import functools
import math

import jax
import jax.numpy as jnp
from jax import lax
from jax.experimental import pallas as pl
from jax.experimental.pallas import tpu as pltpu
from jax.sharding import PartitionSpec as P

HEADS = 12
WIN = 32
VOX_DEV = 256
LANES = 128
FLAG = 16384.0
VMEM = 64 * 1024 * 1024 - 65536
F32 = jnp.float32
BF16 = jnp.bfloat16
LOG2E = math.log2(math.e)


def iota(shape, dim):
    return lax.broadcasted_iota(jnp.int32, shape, dim)


def dot(a, b):
    return jnp.dot(a, b, preferred_element_type=F32)


def dot_t(a, b):
    return lax.dot_general(a, b, (((1,), (1,)), ((), ())), preferred_element_type=F32)


def eye(n):
    return (iota((n, n), 0) == iota((n, n), 1)).astype(BF16)


def transposed(a):
    return a.astype(F32).T.astype(BF16)


def tile(t):
    return slice(t * LANES, (t + 1) * LANES)


def head_order(chans):
    size = chans // HEADS
    cut = 8 * size
    j = iota((chans, 1), 0)
    high = j - cut
    low_src = (j % 8) * size + j // 8
    high_src = (8 + high % 4) * size + high // 8 + (size // 2) * ((high % 8) // 4)
    return jnp.where(j < cut, low_src, high_src)


def slot_of_lane(slots, run):
    t = iota((1, slots), 1)
    at, lane = t // LANES, t % LANES
    p = (4 * (at // run) + lane // WIN) * run + at % run
    return (lane % 8) * LANES + ((lane // 8) % 4) * WIN + p


def place(low, high, blocks):
    base = jnp.where(low == iota((LANES, low.shape[1]), 0), 1.0, 0.0).astype(BF16)
    high = jnp.broadcast_to(high, base.shape).astype(F32).astype(BF16)
    nil = jnp.zeros_like(base)
    parts = [jnp.where(high == jnp.asarray(n, BF16), base, nil) for n in range(blocks)]
    return jnp.concatenate(parts, 0)


def reorder(slots, run):
    slot = slot_of_lane(slots, run)
    return place(slot % LANES, slot // LANES, slots // LANES)


def norm_t(x, gain):
    inv = 1.0 / x.shape[0]
    mean = jnp.sum(x, 0, keepdims=True) * inv
    cent = x - mean
    var = jnp.sum(cent * cent, 0, keepdims=True) * inv
    return cent * lax.rsqrt(var + 1e-05) * gain


def start_all(pairs, sems):
    copies = [pltpu.make_async_copy(a, b, sems.at[n]) for n, (a, b) in enumerate(pairs)]
    for copy in copies:
        copy.start()
    return copies


def wait_all(copies):
    for copy in copies:
        copy.wait()


def fold8(x, op):
    y = x[0]
    for n in range(1, x.shape[0]):
        y = op(y, x[n])
    for shift in (4, 2, 1):
        y = op(y, pltpu.roll(y, shift, 0))
    return y


def first_kernel(
    run, count_ref, nodes_hbm, ids_hbm, pos_hbm, gain_one_hbm, gain_two_hbm, qkv_hbm, out_hbm,
    first_hbm, sent_hbm, nodes_ref, ids_ref, pos_ref, gain_one_ref, gain_two_ref, qkv_ref, out_ref,
    sems, qkv_s, q_s, k_s, v_s, ctx_s, n_s, first_s, stores
):
    loads = start_all(
        [
            (nodes_hbm, nodes_ref),
            (ids_hbm, ids_ref),
            (pos_hbm, pos_ref),
            (gain_one_hbm, gain_one_ref),
            (gain_two_hbm, gain_two_ref),
            (qkv_hbm, qkv_ref),
            (out_hbm, out_ref),
        ],
        sems,
    )
    chans, slots = nodes_ref.shape
    tiles = slots // LANES
    size = chans // HEADS
    per = LANES // WIN
    count = count_ref[0]
    wait_all(loads[:5])
    cols = jnp.concatenate(
        [pos_ref[...], gain_one_ref[...], gain_two_ref[...], jnp.zeros((3, chans), F32)], 0
    ).T
    ids = ids_ref[...]
    start = None
    for axis in range(3):
        total = jnp.zeros(ids.shape, jnp.int32)
        for level in range(6):
            bit = jnp.bitwise_and(jnp.right_shift(ids, 3 * level + axis), 1)
            total = total + bit * 2**level
        term = cols[:, axis : axis + 1] * (total.astype(F32) / 64.0 - 0.5)
        start = term if start is None else start + term
    start = (nodes_ref[...].astype(F32) + start).astype(BF16)
    nodes_ref[...] = start
    n_s[...] = norm_t(start.astype(F32), cols[:, 3:4]).astype(BF16)
    wait_all(loads[5:])
    qkv_t = transposed(qkv_ref[...])
    out_t = transposed(out_ref[...])
    qkv_s[...] = dot(qkv_t, n_s[...]).astype(BF16)
    side = eye(LANES)
    spread = (
        iota((LANES, per * LANES), 0)
        == (iota((LANES, per * LANES), 1) // LANES) * WIN + iota((LANES, per * LANES), 1) % WIN
    ).astype(BF16)
    row_head = (iota((chans, LANES), 0) // size) % per
    own_head = row_head == iota((chans, LANES), 1) // WIN
    for t in range(tiles):
        q_s[t] = qkv_s[:chans, tile(t)] * jnp.asarray(size**-0.5, BF16)
        k_s[t] = dot_t(side, qkv_s[chans : 2 * chans, tile(t)]).astype(BF16)
    for t in range(tiles):
        wide = dot(qkv_s[2 * chans :, tile(t)], spread)
        for w in range(per):
            v_s[t, w] = jnp.where(own_head, wide[:, tile(w)], 0.0).astype(BF16)

    lane_head = iota((WIN, chans), 1) // size
    window = iota((8, LANES), 1) // WIN
    rank = iota((WIN, LANES), 0) + WIN * (iota((WIN, LANES), 1) // WIN)

    def group(t, _):
        query = q_s[t]
        scores = None
        for w in range(per):
            keys = k_s[t, w * WIN : (w + 1) * WIN, :]
            by_head = jnp.concatenate(
                [jnp.where(lane_head == h, keys, jnp.zeros_like(keys)) for h in range(HEADS)], 0
            )
            got = dot(by_head, query).reshape(-1, 8, LANES)
            scores = got if w == 0 else jnp.where(window[None] == w, got, scores)
        mask = jnp.where(rank + t * LANES < count, 0.0, -1e9).astype(F32)
        mask = mask.reshape(WIN // 8, 8, LANES)
        probs, inverse = [], []
        for h in range(HEADS):
            mine = scores[h * (WIN // 8) : (h + 1) * (WIN // 8)] + mask
            top = fold8(mine, jnp.maximum)
            weight = jnp.exp(mine - top[None])
            inverse.append(1.0 / fold8(weight, jnp.add))
            probs.append(weight.reshape(WIN, LANES).astype(BF16))
        half = per * size
        parts = []
        for j in range(HEADS // per):
            weight = jnp.concatenate(probs[j * per : (j + 1) * per], 0)
            ctx = None
            for w in range(per):
                got = dot(v_s[t, w, j * half : (j + 1) * half, :], weight).reshape(-1, 8, LANES)
                ctx = got if w == 0 else jnp.where(window[None] == w, got, ctx)
            for h in range(per):
                block = ctx[h * (size // 8) : (h + 1) * (size // 8)] * inverse[j * per + h][None]
                parts.append(block.reshape(size, LANES))
        ctx_s[t] = jnp.concatenate(parts, 0).astype(BF16)
        return 0

    lax.fori_loop(0, tiles, group, 0, unroll=2)
    ctx = jnp.concatenate([ctx_s[t] for t in range(tiles)], 1)
    first = (nodes_ref[...].astype(F32) + dot(out_t, ctx)).astype(BF16)
    first_s[...] = first
    keep_first = pltpu.make_async_copy(first_s, first_hbm, stores.at[0])
    keep_first.start()
    normed = norm_t(first.astype(F32), cols[:, 4:5])
    kept = iota((1, slots), 1) < count
    head = jnp.where((iota((16, slots), 0) > 0) | kept, normed[:16], FLAG)
    normed = jnp.concatenate([head, normed[16:]], 0).astype(BF16)
    n_s[...] = dot(normed, reorder(slots, run)).astype(BF16)
    send = pltpu.make_async_copy(n_s, sent_hbm, stores.at[1])
    send.start()
    wait_all([keep_first, send])


def tables_kernel(
    cap, qkv_hbm, out_hbm, up_hbm, slot_hbm, owner_hbm, voxel_hbm, weights_hbm, facts_hbm,
    qkv_ref, out_ref, up_ref, slot_ref, owner_ref, voxel_ref, sems, weights_s, facts_s, stores
):
    loads = start_all(
        [
            (qkv_hbm, qkv_ref),
            (out_hbm, out_ref),
            (up_hbm, up_ref),
            (slot_hbm, slot_ref),
            (owner_hbm, owner_ref),
            (voxel_hbm, voxel_ref),
        ],
        sems,
    )
    wait_all(loads)
    votes = slot_ref.shape[1]
    codes = facts_s.shape[1]
    owners = codes // cap
    chans = out_ref.shape[0]
    src = head_order(chans)
    src = jnp.concatenate([src, src + chans, src + 2 * chans], 0)
    shuffle = (src == iota((3 * chans, 3 * chans), 1)).astype(BF16)
    weights_s[: 3 * chans] = dot_t(shuffle, qkv_ref[...]).astype(BF16)
    out_t = dot(shuffle[:chans, :chans], out_ref[...])
    weights_s[3 * chans : 4 * chans] = transposed(out_t)
    weights_s[4 * chans :] = transposed(up_ref[...])
    keep_weights = pltpu.make_async_copy(weights_s, weights_hbm, stores.at[0])
    keep_weights.start()
    owner = owner_ref[...]
    hot = owner == iota((owners, votes), 0)
    upto = (iota((votes, votes), 0) <= iota((votes, votes), 1)).astype(BF16)
    rank = jnp.sum(jnp.where(hot, dot(hot.astype(BF16), upto), 0.0), 0, keepdims=True)
    code = owner * cap + rank.astype(jnp.int32) - 1
    member = place(code % LANES, code // LANES, codes // LANES)
    slot = slot_ref[...]
    row = iota((16, votes), 0)
    facts = jnp.where(
        row == 0,
        voxel_ref[...],
        jnp.where(row == 1, slot // LANES, jnp.where(row == 2, slot % LANES, 1)),
    )
    listed = dot_t(facts.astype(F32).astype(BF16), member)
    facts_s[...] = jnp.where(listed[3:4] > 0.5, listed, -1.0).astype(BF16)
    keep_facts = pltpu.make_async_copy(facts_s, facts_hbm, stores.at[1])
    keep_facts.start()
    wait_all([keep_weights, keep_facts])


def clean(block):
    head = block[:16].astype(F32)
    gone = head[0:1] > 0.5 * FLAG
    head = jnp.where((iota(head.shape, 0) == 0) & gone, 0.0, head)
    return jnp.concatenate([head.astype(BF16), block[16:]], 0), gone


def fold16(x):
    parts = [x[n] for n in range(x.shape[0])]
    while len(parts) > 1:
        parts = [a + b for a, b in zip(parts[::2], parts[1::2])]
    wide = parts[0].astype(F32)
    return wide[:8] + wide[8:]


def twice(x):
    return jnp.concatenate([x, x], 0).astype(BF16)


def add_keys(blocks, kv_t, k_s, v_s, m_s):
    chans = kv_t.shape[1]
    rows16 = chans // 16
    tiles = k_s.shape[1]
    for n, block in enumerate(blocks):
        block, gone = clean(block)
        kv = dot(kv_t, block).astype(BF16)
        mask = jnp.where(gone, -1e9, 0.0)
        for t in range(tiles):
            k_s[n, t] = kv[:chans, tile(t)].reshape(rows16, 16, LANES)
            v_s[n, t] = kv[chans:, tile(t)].reshape(rows16, 16, LANES)
            m_s[n, t] = jnp.broadcast_to(mask[:, tile(t)], (8, LANES))


def attend_more(t, run, q_s, k_s, v_s, m_s, s_s, old):
    rows16 = q_s.shape[1]
    cut = 2 * rows16 // 3
    blocks = k_s.shape[0]
    keys = blocks * run
    base = (t // run) * run
    query = q_s[t]

    def score(key, top):
        n, at = key // run, base + key % run
        prod = query * k_s[n, at]
        a = fold16(prod[:cut])
        b = fold16(prod[cut:])
        b = b + pltpu.roll(b, 4, 0)
        mask = m_s[n, at]
        a = a * LOG2E + mask
        b = b * LOG2E + mask
        s_s[key, 0] = a
        s_s[key, 1] = b
        return jnp.maximum(top[0], a), jnp.maximum(top[1], b)

    if old is None:
        low = jnp.full((8, LANES), -3e38, F32)
        zero = jnp.zeros((8, LANES), F32)
        top_a, top_b = lax.fori_loop(0, keys, score, (low, low), unroll=4)
        held = (zero, zero, jnp.zeros((cut, 16, LANES), F32),
                jnp.zeros((rows16 - cut, 16, LANES), F32))
    else:
        top, total, acc = old
        top_a, top_b = lax.fori_loop(0, keys, score, (top[0], top[1]), unroll=4)
        fade_a = jnp.exp2(top[0] - top_a)
        fade_b = jnp.exp2(top[1] - top_b)
        both_a = jnp.concatenate([fade_a, fade_a], 0)
        both_b = jnp.concatenate([fade_b, fade_b], 0)
        held = (total[0] * fade_a, total[1] * fade_b, acc[:cut] * both_a[None],
                acc[cut:] * both_b[None])

    def gather(step, carry):
        sum_a, sum_b, acc_a, acc_b = carry
        got_a, got_b = [], []
        for key in range(4):
            key = 4 * step + key
            pa = jnp.exp2(s_s[key, 0] - top_a)
            pb = jnp.exp2(s_s[key, 1] - top_b)
            sum_a = sum_a + pa
            sum_b = sum_b + pb
            value = v_s[key // run, base + key % run]
            got_a.append(twice(pa)[None] * value[:cut])
            got_b.append(twice(pb)[None] * value[cut:])
        acc_a = acc_a + ((got_a[0] + got_a[1]) + (got_a[2] + got_a[3])).astype(F32)
        acc_b = acc_b + ((got_b[0] + got_b[1]) + (got_b[2] + got_b[3])).astype(F32)
        return sum_a, sum_b, acc_a, acc_b

    sum_a, sum_b, acc_a, acc_b = lax.fori_loop(0, keys // 4, gather, held)
    return (top_a, top_b), (sum_a, sum_b), (acc_a, acc_b)


def hold(t, state, ends_s, acc_s):
    top, total, acc = state
    for n in range(2):
        ends_s[t, n] = top[n]
        ends_s[t, 2 + n] = total[n]
    acc_s[t] = jnp.concatenate(acc, 0)


def held(t, ends_s, acc_s):
    return (ends_s[t, 0], ends_s[t, 1]), (ends_s[t, 2], ends_s[t, 3]), acc_s[t]


def near_kernel(
    run, own_hbm, near_hbm, weights_hbm, q_hbm, ends_hbm, acc_hbm,
    own_ref, near_ref, qkv_t_ref, sems, q_s, ends_s, acc_s, stores, k_s, v_s, m_s, s_s
):
    chans, slots = own_ref.shape
    loads = start_all(
        [
            (own_hbm, own_ref),
            (weights_hbm.at[pl.ds(0, 3 * chans)], qkv_t_ref),
            (near_hbm, near_ref),
        ],
        sems,
    )
    tiles = slots // LANES
    scale = (chans // HEADS) ** -0.5
    wait_all(loads[:2])
    own, _ = clean(own_ref[...])
    query = (dot(qkv_t_ref[:chans, :], own) * scale).astype(BF16)
    for t in range(tiles):
        q_s[t] = query[:, tile(t)].reshape(chans // 16, 16, LANES)
    keep_q = pltpu.make_async_copy(q_s, q_hbm, stores.at[0])
    keep_q.start()
    wait_all(loads[2:])
    add_keys([own_ref[...], near_ref[...]], qkv_t_ref[chans:, :], k_s, v_s, m_s)

    def step(t, _):
        hold(t, attend_more(t, run, q_s, k_s, v_s, m_s, s_s, None), ends_s, acc_s)
        return 0

    lax.fori_loop(0, tiles, step, 0)
    keep_ends = pltpu.make_async_copy(ends_s, ends_hbm, stores.at[1])
    keep_acc = pltpu.make_async_copy(acc_s, acc_hbm, stores.at[2])
    keep_ends.start()
    keep_acc.start()
    wait_all([keep_q, keep_ends, keep_acc])


def middle_kernel(run, count, *refs):
    blocks, refs = refs[:count], refs[count:]
    q_hbm, ends_hbm, acc_hbm, weights_hbm, ends_out, acc_out = refs[:6]
    block_s, sems, q_s, ends_s, acc_s, kv_t_ref, rest, stores, k_s, v_s, m_s, s_s = refs[6:]
    chans = kv_t_ref.shape[1]
    loads = start_all([(blocks[n], block_s.at[n]) for n in range(count)], sems)
    later = start_all(
        [
            (weights_hbm.at[pl.ds(chans, 2 * chans)], kv_t_ref),
            (q_hbm, q_s),
            (ends_hbm, ends_s),
            (acc_hbm, acc_s),
        ],
        rest,
    )
    wait_all(loads + later[:1])
    add_keys([block_s[n] for n in range(count)], kv_t_ref[...], k_s, v_s, m_s)
    wait_all(later[1:])

    def step(t, _):
        old = held(t, ends_s, acc_s)
        hold(t, attend_more(t, run, q_s, k_s, v_s, m_s, s_s, old), ends_s, acc_s)
        return 0

    lax.fori_loop(0, q_s.shape[0], step, 0)
    wait_all(start_all([(ends_s, ends_out), (acc_s, acc_out)], stores))


def second_kernel(run, cap, far, count_ref, *refs):
    blocks, refs = refs[:far], refs[far:]
    (
        q_hbm, ends_hbm, acc_hbm, weights_hbm, first_hbm, gain_hbm, down_hbm, facts_hbm,
        feat_hbm, votes_hbm
    ) = refs[:10]
    (
        block_s, sems, weights_s, q_s, ends_s, acc_s, first_s, gain_s, down_s, facts_s, rest,
        feat_s, votes_s, stores, k_s, v_s, m_s, s_s, ctx_s, bf_s
    ) = refs[10:]
    loads = start_all([(blocks[n], block_s.at[n]) for n in range(far)], sems)
    later = start_all(
        [
            (weights_hbm, weights_s),
            (q_hbm, q_s),
            (ends_hbm, ends_s),
            (acc_hbm, acc_s),
            (first_hbm, first_s),
            (gain_hbm, gain_s),
            (down_hbm, down_s),
            (facts_hbm, facts_s),
        ],
        rest,
    )
    chans, slots = first_s.shape
    owners = votes_s.shape[0]
    tiles = slots // LANES
    count = count_ref[0]
    wait_all(loads + later[:1])
    add_keys([block_s[n] for n in range(far)], weights_s[chans : 3 * chans], k_s, v_s, m_s)
    wait_all(later[1:])

    def step(t, _):
        old = held(t, ends_s, acc_s)
        _, total, acc = attend_more(t, run, q_s, k_s, v_s, m_s, s_s, old)
        share = [1.0 / total[n] for n in range(2)]
        ctx = jnp.concatenate(
            [acc[n] * jnp.concatenate([share[n], share[n]], 0)[None] for n in range(2)], 0
        )
        ctx_s[t] = ctx.reshape(chans, LANES).astype(BF16)
        return 0

    lax.fori_loop(0, tiles, step, 0)
    ctx = jnp.concatenate([ctx_s[t] for t in range(tiles)], 1)
    ctx = dot_t(ctx, reorder(slots, run)).astype(BF16)
    gain = jnp.concatenate([gain_s[...], jnp.zeros((7, chans), F32)], 0).T[:, 0:1]
    second = first_s[...].astype(F32) + dot(weights_s[3 * chans : 4 * chans], ctx)
    inner = norm_t(second, gain).astype(BF16)
    kept = iota((1, slots), 1) < count
    wide = 2 * LANES
    cuts = [slice(at, at + wide) for at in range(0, slots, wide)]
    up_t = weights_s[4 * chans :]
    raised = dot(up_t, inner[:, cuts[0]])
    for n, at in enumerate(cuts):
        now = raised
        if n + 1 < len(cuts):
            raised = dot(up_t, inner[:, cuts[n + 1]])
        hidden = jax.nn.gelu(now).astype(BF16)
        third = second[:, at] + dot(down_s[...], hidden)
        third = jnp.where(kept[:, at], third, 0.0)
        feat_s[:, at] = third
        bf_s[:, at] = third.astype(BF16)
    keep_feat = pltpu.make_async_copy(feat_s, feat_hbm, stores.at[0])
    keep_feat.start()
    facts = facts_s[...].astype(F32)
    low, high = facts[2:3].astype(jnp.int32), facts[1:2].astype(jnp.int32)
    picked = dot(bf_s[...], place(low, high, tiles)).astype(BF16)
    for o in range(owners):
        votes_s[o, :chans, :] = picked[:, o * cap : (o + 1) * cap]
        votes_s[o, chans:, :] = facts_s[:, o * cap : (o + 1) * cap]
    keep_votes = pltpu.make_async_copy(votes_s, votes_hbm, stores.at[1])
    keep_votes.start()
    wait_all([keep_feat, keep_votes])


def sums_kernel(got_ref, out_ref):
    sources, _, cap = got_ref.shape
    chans, voxels = out_ref.shape
    total = jnp.zeros(out_ref.shape, F32)
    for n in range(sources):
        label = got_ref[n, chans:, :].astype(F32)[0:1]
        hot = (label == iota((voxels, cap), 0).astype(F32)).astype(BF16)
        total = total + dot_t(got_ref[n, :chans, :], hot)
    out_ref[...] = total


def call(kernel, outs, scratch, flops, spaces, out_space=pl.ANY, limit=VMEM):
    return pl.pallas_call(
        kernel,
        out_shape=outs,
        in_specs=[
            pl.BlockSpec(memory_space={"s": pltpu.SMEM, "v": pltpu.VMEM, "a": pl.ANY}[c])
            for c in spaces
        ],
        out_specs=[pl.BlockSpec(memory_space=out_space)] * len(outs),
        scratch_shapes=scratch,
        compiler_params=pltpu.CompilerParams(vmem_limit_bytes=limit),
        cost_estimate=pl.CostEstimate(flops=flops, bytes_accessed=2 << 20, transcendentals=0),
    )


def turned(x, axis, bit):
    n = lax.axis_size(axis)
    return lax.ppermute(x, axis, [(i, i ^ bit) for i in range(n)])


def body(
    nodes,
    node_ids,
    node_count,
    pos_weight,
    gain_one,
    qkv_one,
    out_one,
    gain_two,
    qkv_two,
    out_two,
    gain_three,
    w_up,
    w_down,
    vote_slot,
    vote_owner,
    vote_voxel,
):
    slots, chans = nodes.shape
    groups, owners = lax.axis_size("grp"), lax.axis_size("tile")
    run = WIN // groups
    votes = vote_slot.shape[0]
    cap = 2 * votes // owners
    codes = owners * cap
    tiles = slots // LANES
    rows16 = chans // 16
    hidden = w_up.shape[1]
    per = LANES // WIN
    sds = jax.ShapeDtypeStruct
    vmem = pltpu.VMEM
    dma = pltpu.SemaphoreType.DMA

    first, sent = call(
        functools.partial(first_kernel, run),
        [sds((chans, slots), BF16), sds((chans, slots), BF16)],
        [
            vmem((chans, slots), BF16),
            vmem((1, slots), jnp.int32),
            vmem((3, chans), F32),
            vmem((1, chans), F32),
            vmem((1, chans), F32),
            vmem((chans, 3 * chans), BF16),
            vmem((chans, chans), BF16),
            dma((7,)),
            vmem((3 * chans, slots), BF16),
            vmem((tiles, chans, LANES), BF16),
            vmem((tiles, LANES, chans), BF16),
            vmem((tiles, per, chans, LANES), BF16),
            vmem((tiles, chans, LANES), BF16),
            vmem((chans, slots), BF16),
            vmem((chans, slots), BF16),
            dma((2,)),
        ],
        2_000_000_000,
        "saaaaaaa",
    )(
        node_count,
        nodes.T,
        node_ids.reshape(1, slots),
        pos_weight,
        gain_one.reshape(1, chans),
        gain_two.reshape(1, chans),
        qkv_one,
        out_one,
    )
    near = turned(sent, "grp", 1)
    bit = groups // 2
    mid = []
    while bit > 1:
        mid += [turned(block, "grp", bit) for block in [sent] + mid]
        bit //= 2
    weights, facts = call(
        functools.partial(tables_kernel, cap),
        [sds((4 * chans + hidden, chans), BF16), sds((16, codes), BF16)],
        [
            vmem((chans, 3 * chans), BF16),
            vmem((chans, chans), BF16),
            vmem((chans, hidden), BF16),
            vmem((1, votes), jnp.int32),
            vmem((1, votes), jnp.int32),
            vmem((1, votes), jnp.int32),
            dma((6,)),
            vmem((4 * chans + hidden, chans), BF16),
            vmem((16, codes), BF16),
            dma((2,)),
        ],
        2_000_000_000,
        "aaaaaa",
    )(
        qkv_two,
        out_two,
        w_up,
        vote_slot.reshape(1, votes),
        vote_owner.reshape(1, votes),
        vote_voxel.reshape(1, votes),
    )
    q_like = ((tiles, rows16, 16, LANES), BF16)
    ends_like = ((tiles, 4, 8, LANES), F32)
    acc_like = ((tiles, rows16, 16, LANES), F32)

    def key_scratch(blocks):
        return [
            vmem((blocks, tiles, rows16, 16, LANES), BF16),
            vmem((blocks, tiles, rows16, 16, LANES), BF16),
            vmem((blocks, tiles, 8, LANES), F32),
            vmem((blocks * run, 2, 8, LANES), F32),
        ]

    query, ends, acc = call(
        functools.partial(near_kernel, run),
        [sds(*q_like), sds(*ends_like), sds(*acc_like)],
        [
            vmem((chans, slots), BF16),
            vmem((chans, slots), BF16),
            vmem((3 * chans, chans), BF16),
            dma((3,)),
            vmem(*q_like),
            vmem(*ends_like),
            vmem(*acc_like),
            dma((3,)),
        ]
        + key_scratch(2),
        3_000_000_000,
        "aaa",
    )(sent, near, weights)
    mid, query = lax.optimization_barrier((mid, query))
    far = [turned(block, "grp", 1) for block in mid]
    ends, acc = call(
        functools.partial(middle_kernel, run, len(mid)),
        [sds(*ends_like), sds(*acc_like)],
        [
            vmem((len(mid), chans, slots), BF16),
            dma((len(mid),)),
            vmem(*q_like),
            vmem(*ends_like),
            vmem(*acc_like),
            vmem((2 * chans, chans), BF16),
            dma((4,)),
            dma((2,)),
        ]
        + key_scratch(len(mid)),
        2_000_000_000,
        "a" * len(mid) + "aaaa",
    )(*mid, query, ends, acc, weights)
    features_t, ballots = call(
        functools.partial(second_kernel, run, cap, len(far)),
        [sds((chans, slots), F32), sds((owners, chans + 16, cap), BF16)],
        [
            vmem((len(far), chans, slots), BF16),
            dma((len(far),)),
            vmem((4 * chans + hidden, chans), BF16),
            vmem(*q_like),
            vmem(*ends_like),
            vmem(*acc_like),
            vmem((chans, slots), BF16),
            vmem((1, chans), F32),
            vmem((chans, hidden), BF16),
            vmem((16, codes), BF16),
            dma((8,)),
            vmem((chans, slots), F32),
            vmem((owners, chans + 16, cap), BF16),
            dma((2,)),
        ]
        + key_scratch(len(far))
        + [vmem((tiles, chans, LANES), BF16), vmem((chans, slots), BF16)],
        3_000_000_000,
        "s" + "a" * (len(far) + 8),
    )(
        node_count,
        *far,
        query,
        ends,
        acc,
        weights,
        first,
        gain_three.reshape(1, chans),
        w_down.T,
        facts,
    )
    got = lax.all_to_all(ballots, "tile", split_axis=0, concat_axis=0, tiled=True)
    (sums_t,) = call(
        sums_kernel, [sds((chans, VOX_DEV), F32)], [], 200_000_000, "v", pltpu.VMEM, 16 << 20
    )(got)
    return (features_t.T, sums_t.T)


def solution(mesh):
    in_specs = (
        P(("grp", "tile"), None),
        P(("grp", "tile")),
        P(("grp", "tile")),
        P(),
        P(),
        P(),
        P(),
        P(),
        P(),
        P(),
        P(),
        P(),
        P(),
        P(("grp", "tile")),
        P(("grp", "tile"), None),
        P(("grp", "tile")),
    )
    out_specs = (P(("grp", "tile"), None), P(("grp", "tile"), None))
    return jax.shard_map(body, mesh=mesh, in_specs=in_specs, out_specs=out_specs, check_vma=False)
```

```python
import functools
import math

import jax
import jax.numpy as jnp
from jax import lax
from jax.experimental import pallas as pl
from jax.experimental.pallas import tpu as pltpu
from jax.sharding import PartitionSpec as P

HEADS = 12
WIN = 32
VOX_DEV = 256
LANES = 128
FLAG = 16384.0
VMEM = 64 * 1024 * 1024 - 65536
F32 = jnp.float32
BF16 = jnp.bfloat16
LOG2E = math.log2(math.e)


def iota(shape, dim):
    return lax.broadcasted_iota(jnp.int32, shape, dim)


def dot(a, b):
    return jnp.dot(a, b, preferred_element_type=F32)


def dot_t(a, b):
    return lax.dot_general(a, b, (((1,), (1,)), ((), ())), preferred_element_type=F32)


def eye(n):
    return (iota((n, n), 0) == iota((n, n), 1)).astype(BF16)


def transposed(a):
    return a.astype(F32).T.astype(BF16)


def tile(t):
    return slice(t * LANES, (t + 1) * LANES)


def head_order(chans):
    size = chans // HEADS
    cut = 8 * size
    j = iota((chans, 1), 0)
    high = j - cut
    low_src = (j % 8) * size + j // 8
    high_src = (8 + high % 4) * size + high // 8 + (size // 2) * ((high % 8) // 4)
    return jnp.where(j < cut, low_src, high_src)


def slot_of_lane(slots, run):
    t = iota((1, slots), 1)
    at, lane = t // LANES, t % LANES
    p = (4 * (at // run) + lane // WIN) * run + at % run
    return (lane % 8) * LANES + ((lane // 8) % 4) * WIN + p


def place(low, high, blocks):
    base = jnp.where(low == iota((LANES, low.shape[1]), 0), 1.0, 0.0).astype(BF16)
    high = jnp.broadcast_to(high, base.shape).astype(F32).astype(BF16)
    nil = jnp.zeros_like(base)
    parts = [jnp.where(high == jnp.asarray(n, BF16), base, nil) for n in range(blocks)]
    return jnp.concatenate(parts, 0)


def reorder(slots, run):
    slot = slot_of_lane(slots, run)
    return place(slot % LANES, slot // LANES, slots // LANES)


def norm_t(x, gain):
    inv = 1.0 / x.shape[0]
    mean = jnp.sum(x, 0, keepdims=True) * inv
    cent = x - mean
    var = jnp.sum(cent * cent, 0, keepdims=True) * inv
    return cent * lax.rsqrt(var + 1e-05) * gain


def start_all(pairs, sems):
    copies = [pltpu.make_async_copy(a, b, sems.at[n]) for n, (a, b) in enumerate(pairs)]
    for copy in copies:
        copy.start()
    return copies


def wait_all(copies):
    for copy in copies:
        copy.wait()


def fold8(x, op):
    y = x[0]
    for n in range(1, x.shape[0]):
        y = op(y, x[n])
    for shift in (4, 2, 1):
        y = op(y, pltpu.roll(y, shift, 0))
    return y


def first_kernel(
    run, count_ref, nodes_hbm, ids_hbm, pos_hbm, gain_one_hbm, gain_two_hbm, qkv_hbm, out_hbm,
    first_hbm, sent_hbm, nodes_ref, ids_ref, pos_ref, gain_one_ref, gain_two_ref, qkv_ref, out_ref,
    sems, qkv_s, q_s, k_s, v_s, ctx_s, n_s, first_s, sent_s, stores
):
    loads = start_all(
        [
            (nodes_hbm, nodes_ref),
            (ids_hbm, ids_ref),
            (pos_hbm, pos_ref),
            (gain_one_hbm, gain_one_ref),
            (gain_two_hbm, gain_two_ref),
            (qkv_hbm, qkv_ref),
            (out_hbm, out_ref),
        ],
        sems,
    )
    chans, slots = nodes_ref.shape
    tiles = slots // LANES
    size = chans // HEADS
    per = LANES // WIN
    count = count_ref[0]
    wait_all(loads[:5])
    cols = jnp.concatenate(
        [pos_ref[...], gain_one_ref[...], gain_two_ref[...], jnp.zeros((3, chans), F32)], 0
    ).T
    ids = ids_ref[...]
    coords = []
    for axis in range(3):
        total = jnp.zeros(ids.shape, jnp.int32)
        for level in range(6):
            bit = jnp.bitwise_and(jnp.right_shift(ids, 3 * level + axis), 1)
            total = total + bit * 2**level
        coords.append(total.astype(F32) / 64.0 - 0.5)
    for t in range(tiles):
        at = tile(t)
        start = cols[:, 0:1] * coords[0][:, at]
        for axis in range(1, 3):
            start = start + cols[:, axis : axis + 1] * coords[axis][:, at]
        start = (nodes_ref[:, at].astype(F32) + start).astype(BF16)
        nodes_ref[:, at] = start
        n_s[:, at] = norm_t(start.astype(F32), cols[:, 3:4]).astype(BF16)
    wait_all(loads[5:])
    qkv_t = transposed(qkv_ref[...])
    out_t = transposed(out_ref[...])
    qkv_s[...] = dot(qkv_t, n_s[...]).astype(BF16)
    side = eye(LANES)
    spread = (
        iota((LANES, per * LANES), 0)
        == (iota((LANES, per * LANES), 1) // LANES) * WIN + iota((LANES, per * LANES), 1) % WIN
    ).astype(BF16)
    row_head = (iota((chans, LANES), 0) // size) % per
    own_head = row_head == iota((chans, LANES), 1) // WIN
    for t in range(tiles):
        q_s[t] = qkv_s[:chans, tile(t)] * jnp.asarray(size**-0.5, BF16)
        k_s[t] = dot_t(side, qkv_s[chans : 2 * chans, tile(t)]).astype(BF16)
    for t in range(tiles):
        wide = dot(qkv_s[2 * chans :, tile(t)], spread)
        for w in range(per):
            v_s[t, w] = jnp.where(own_head, wide[:, tile(w)], 0.0).astype(BF16)

    lane_head = iota((WIN, chans), 1) // size
    head_mask = [jnp.where(lane_head == h, 1.0, 0.0).astype(BF16) for h in range(HEADS)]
    window = iota((8, LANES), 1) // WIN
    rank = iota((WIN, LANES), 0) + WIN * (iota((WIN, LANES), 1) // WIN)
    half = per * size

    def by_window(made):
        out = made(0)
        for w in range(1, per):
            out = jnp.where(window[None] == w, made(w), out)
        return out

    def group(t, _):
        query = q_s[t]
        mask = jnp.where(rank + t * LANES < count, 0.0, -1e9).astype(F32)
        mask = mask.reshape(WIN // 8, 8, LANES)

        def scores_of(j):
            def made(w):
                keys = k_s[t, w * WIN : (w + 1) * WIN, :]
                heads = [keys * head_mask[j * per + h] for h in range(per)]
                return dot(jnp.concatenate(heads, 0), query).reshape(-1, 8, LANES)

            return by_window(made)

        parts = []
        coming = scores_of(0)
        for j in range(HEADS // per):
            scores = coming
            if j + 1 < HEADS // per:
                coming = scores_of(j + 1)
            probs, inverse = [], []
            for h in range(per):
                mine = scores[h * (WIN // 8) : (h + 1) * (WIN // 8)] + mask
                top = fold8(mine, jnp.maximum)
                weight = jnp.exp(mine - top[None])
                inverse.append(1.0 / fold8(weight, jnp.add))
                probs.append(weight.reshape(WIN, LANES).astype(BF16))
            weight = jnp.concatenate(probs, 0)
            ctx = by_window(
                lambda w: dot(v_s[t, w, j * half : (j + 1) * half, :], weight).reshape(
                    -1, 8, LANES
                )
            )
            for h in range(per):
                block = ctx[h * (size // 8) : (h + 1) * (size // 8)] * inverse[h][None]
                parts.append(block.reshape(size, LANES))
        ctx_s[t] = jnp.concatenate(parts, 0).astype(BF16)
        return 0

    lax.fori_loop(0, tiles, group, 0, unroll=2)
    ctx = jnp.concatenate([ctx_s[t] for t in range(tiles)], 1)
    moved = dot(out_t, ctx)
    for t in range(tiles):
        at = tile(t)
        first = (nodes_ref[:, at].astype(F32) + moved[:, at]).astype(BF16)
        first_s[:, at] = first
        normed = norm_t(first.astype(F32), cols[:, 4:5])
        kept = iota((1, LANES), 1) + t * LANES < count
        head = jnp.where((iota((16, LANES), 0) > 0) | kept, normed[:16], FLAG)
        n_s[:, at] = jnp.concatenate([head, normed[16:]], 0).astype(BF16)
    keep_first = pltpu.make_async_copy(first_s, first_hbm, stores.at[0])
    keep_first.start()
    sent_s[...] = dot(n_s[...], reorder(slots, run)).astype(BF16)
    send = pltpu.make_async_copy(sent_s, sent_hbm, stores.at[1])
    send.start()
    wait_all([keep_first, send])


def tables_kernel(
    cap, qkv_hbm, out_hbm, up_hbm, slot_hbm, owner_hbm, voxel_hbm, weights_hbm, facts_hbm,
    qkv_ref, out_ref, up_ref, slot_ref, owner_ref, voxel_ref, sems, weights_s, facts_s, stores
):
    loads = start_all(
        [
            (qkv_hbm, qkv_ref),
            (out_hbm, out_ref),
            (up_hbm, up_ref),
            (slot_hbm, slot_ref),
            (owner_hbm, owner_ref),
            (voxel_hbm, voxel_ref),
        ],
        sems,
    )
    wait_all(loads)
    votes = slot_ref.shape[1]
    codes = facts_s.shape[1]
    owners = codes // cap
    chans = out_ref.shape[0]
    src = head_order(chans)
    src = jnp.concatenate([src, src + chans, src + 2 * chans], 0)
    shuffle = (src == iota((3 * chans, 3 * chans), 1)).astype(BF16)
    weights_s[: 3 * chans] = dot_t(shuffle, qkv_ref[...]).astype(BF16)
    out_t = dot(shuffle[:chans, :chans], out_ref[...])
    weights_s[3 * chans : 4 * chans] = transposed(out_t)
    weights_s[4 * chans :] = transposed(up_ref[...])
    keep_weights = pltpu.make_async_copy(weights_s, weights_hbm, stores.at[0])
    keep_weights.start()
    owner = jnp.bitwise_xor(owner_ref[...], lax.axis_index("tile"))
    hot = owner == iota((owners, votes), 0)
    upto = (iota((votes, votes), 0) <= iota((votes, votes), 1)).astype(BF16)
    rank = jnp.sum(jnp.where(hot, dot(hot.astype(BF16), upto), 0.0), 0, keepdims=True)
    code = owner * cap + rank.astype(jnp.int32) - 1
    member = place(code % LANES, code // LANES, codes // LANES)
    slot = slot_ref[...]
    row = iota((16, votes), 0)
    facts = jnp.where(
        row == 0,
        voxel_ref[...],
        jnp.where(row == 1, slot // LANES, jnp.where(row == 2, slot % LANES, 1)),
    )
    listed = dot_t(facts.astype(F32).astype(BF16), member)
    facts_s[...] = jnp.where(listed[3:4] > 0.5, listed, -1.0).astype(BF16)
    keep_facts = pltpu.make_async_copy(facts_s, facts_hbm, stores.at[1])
    keep_facts.start()
    wait_all([keep_weights, keep_facts])


def clean(block):
    head = block[:16].astype(F32)
    gone = head[0:1] > 0.5 * FLAG
    head = jnp.where((iota(head.shape, 0) == 0) & gone, 0.0, head)
    return jnp.concatenate([head.astype(BF16), block[16:]], 0), gone


def fold16(x):
    parts = [x[n] for n in range(x.shape[0])]
    while len(parts) > 1:
        parts = [a + b for a, b in zip(parts[::2], parts[1::2])]
    wide = parts[0].astype(F32)
    return wide[:8] + wide[8:]


def twice(x):
    return jnp.concatenate([x, x], 0).astype(BF16)


def add_keys(blocks, kv_t, k_s, v_s, m_s):
    chans = kv_t.shape[1]
    rows16 = chans // 16
    tiles = k_s.shape[1]
    for n, block in enumerate(blocks):
        block, gone = clean(block)
        kv = dot(kv_t, block).astype(BF16)
        mask = jnp.where(gone, -1e9, 0.0)
        for t in range(tiles):
            k_s[n, t] = kv[:chans, tile(t)].reshape(rows16, 16, LANES)
            v_s[n, t] = kv[chans:, tile(t)].reshape(rows16, 16, LANES)
            m_s[n, t] = jnp.broadcast_to(mask[:, tile(t)], (8, LANES))


def attend_more(t, run, q_s, k_s, v_s, m_s, s_s, old):
    rows16 = q_s.shape[1]
    cut = 2 * rows16 // 3
    blocks = k_s.shape[0]
    keys = blocks * run
    base = (t // run) * run
    query = q_s[t]

    def score(key, top):
        n, at = key // run, base + key % run
        prod = query * k_s[n, at]
        a = fold16(prod[:cut])
        b = fold16(prod[cut:])
        b = b + pltpu.roll(b, 4, 0)
        mask = m_s[n, at]
        a = a * LOG2E + mask
        b = b * LOG2E + mask
        s_s[key, 0] = a
        s_s[key, 1] = b
        return jnp.maximum(top[0], a), jnp.maximum(top[1], b)

    if old is None:
        low = jnp.full((8, LANES), -3e38, F32)
        zero = jnp.zeros((8, LANES), F32)
        top_a, top_b = lax.fori_loop(0, keys, score, (low, low), unroll=4)
        held = (zero, zero, jnp.zeros((cut, 16, LANES), F32),
                jnp.zeros((rows16 - cut, 16, LANES), F32))
    else:
        top, total, acc = old
        top_a, top_b = lax.fori_loop(0, keys, score, (top[0], top[1]), unroll=4)
        fade_a = jnp.exp2(top[0] - top_a)
        fade_b = jnp.exp2(top[1] - top_b)
        both_a = jnp.concatenate([fade_a, fade_a], 0)
        both_b = jnp.concatenate([fade_b, fade_b], 0)
        held = (total[0] * fade_a, total[1] * fade_b, acc[:cut] * both_a[None],
                acc[cut:] * both_b[None])

    def gather(step, carry):
        sum_a, sum_b, acc_a, acc_b = carry
        got_a, got_b = [], []
        for key in range(4):
            key = 4 * step + key
            pa = jnp.exp2(s_s[key, 0] - top_a)
            pb = jnp.exp2(s_s[key, 1] - top_b)
            sum_a = sum_a + pa
            sum_b = sum_b + pb
            value = v_s[key // run, base + key % run]
            got_a.append(twice(pa)[None] * value[:cut])
            got_b.append(twice(pb)[None] * value[cut:])
        acc_a = acc_a + ((got_a[0] + got_a[1]) + (got_a[2] + got_a[3])).astype(F32)
        acc_b = acc_b + ((got_b[0] + got_b[1]) + (got_b[2] + got_b[3])).astype(F32)
        return sum_a, sum_b, acc_a, acc_b

    sum_a, sum_b, acc_a, acc_b = lax.fori_loop(0, keys // 4, gather, held)
    return (top_a, top_b), (sum_a, sum_b), (acc_a, acc_b)


def hold(t, state, ends_s, acc_s):
    top, total, acc = state
    for n in range(2):
        ends_s[t, n] = top[n]
        ends_s[t, 2 + n] = total[n]
    acc_s[t] = jnp.concatenate(acc, 0)


def held(t, ends_s, acc_s):
    return (ends_s[t, 0], ends_s[t, 1]), (ends_s[t, 2], ends_s[t, 3]), acc_s[t]


def near_kernel(
    run, own_hbm, near_hbm, weights_hbm, q_hbm, ends_hbm, acc_hbm,
    own_ref, near_ref, qkv_t_ref, sems, q_s, ends_s, acc_s, stores, k_s, v_s, m_s, s_s
):
    chans, slots = own_ref.shape
    loads = start_all(
        [
            (own_hbm, own_ref),
            (weights_hbm.at[pl.ds(0, 3 * chans)], qkv_t_ref),
            (near_hbm, near_ref),
        ],
        sems,
    )
    tiles = slots // LANES
    scale = (chans // HEADS) ** -0.5
    wait_all(loads[:2])
    own, _ = clean(own_ref[...])
    query = (dot(qkv_t_ref[:chans, :], own) * scale).astype(BF16)
    for t in range(tiles):
        q_s[t] = query[:, tile(t)].reshape(chans // 16, 16, LANES)
    keep_q = pltpu.make_async_copy(q_s, q_hbm, stores.at[0])
    keep_q.start()
    wait_all(loads[2:])
    add_keys([own_ref[...], near_ref[...]], qkv_t_ref[chans:, :], k_s, v_s, m_s)

    def step(t, _):
        hold(t, attend_more(t, run, q_s, k_s, v_s, m_s, s_s, None), ends_s, acc_s)
        return 0

    lax.fori_loop(0, tiles, step, 0)
    keep_ends = pltpu.make_async_copy(ends_s, ends_hbm, stores.at[1])
    keep_acc = pltpu.make_async_copy(acc_s, acc_hbm, stores.at[2])
    keep_ends.start()
    keep_acc.start()
    wait_all([keep_q, keep_ends, keep_acc])


def middle_kernel(run, count, *refs):
    blocks, refs = refs[:count], refs[count:]
    q_hbm, ends_hbm, acc_hbm, weights_hbm, ends_out, acc_out = refs[:6]
    block_s, sems, q_s, ends_s, acc_s, kv_t_ref, rest, stores, k_s, v_s, m_s, s_s = refs[6:]
    chans = kv_t_ref.shape[1]
    loads = start_all([(blocks[n], block_s.at[n]) for n in range(count)], sems)
    later = start_all(
        [
            (weights_hbm.at[pl.ds(chans, 2 * chans)], kv_t_ref),
            (q_hbm, q_s),
            (ends_hbm, ends_s),
            (acc_hbm, acc_s),
        ],
        rest,
    )
    wait_all(loads + later[:1])
    add_keys([block_s[n] for n in range(count)], kv_t_ref[...], k_s, v_s, m_s)
    wait_all(later[1:])

    def step(t, _):
        old = held(t, ends_s, acc_s)
        hold(t, attend_more(t, run, q_s, k_s, v_s, m_s, s_s, old), ends_s, acc_s)
        return 0

    lax.fori_loop(0, q_s.shape[0], step, 0)
    wait_all(start_all([(ends_s, ends_out), (acc_s, acc_out)], stores))


def second_kernel(run, cap, far, owners, count_ref, *refs):
    blocks, refs = refs[:far], refs[far:]
    (
        q_hbm, ends_hbm, acc_hbm, weights_hbm, first_hbm, gain_hbm, down_hbm, facts_hbm, feat_hbm
    ) = refs[:9]
    votes_hbm, refs = refs[9 : 9 + owners], refs[9 + owners :]
    (
        block_s, sems, weights_s, q_s, ends_s, acc_s, first_s, gain_s, down_s, facts_s, rest,
        feat_s, votes_s, stores, k_s, v_s, m_s, s_s, ctx_s, bf_s, inner_s, hidden_s
    ) = refs
    loads = start_all([(blocks[n], block_s.at[n]) for n in range(far)], sems)
    later = start_all(
        [
            (weights_hbm, weights_s),
            (q_hbm, q_s),
            (ends_hbm, ends_s),
            (acc_hbm, acc_s),
            (first_hbm, first_s),
            (gain_hbm, gain_s),
            (down_hbm, down_s),
            (facts_hbm, facts_s),
        ],
        rest,
    )
    chans, slots = first_s.shape
    tiles = slots // LANES
    count = count_ref[0]
    wait_all(loads + later[:1])
    add_keys([block_s[n] for n in range(far)], weights_s[chans : 3 * chans], k_s, v_s, m_s)
    wait_all(later[1:])

    def step(t, _):
        old = held(t, ends_s, acc_s)
        _, total, acc = attend_more(t, run, q_s, k_s, v_s, m_s, s_s, old)
        share = [1.0 / total[n] for n in range(2)]
        ctx = jnp.concatenate(
            [acc[n] * jnp.concatenate([share[n], share[n]], 0)[None] for n in range(2)], 0
        )
        ctx_s[t] = ctx.reshape(chans, LANES).astype(BF16)
        return 0

    lax.fori_loop(0, tiles, step, 0)
    ctx = jnp.concatenate([ctx_s[t] for t in range(tiles)], 1)
    ctx = dot_t(ctx, reorder(slots, run)).astype(BF16)
    gain = jnp.concatenate([gain_s[...], jnp.zeros((7, chans), F32)], 0).T[:, 0:1]
    moved = dot(weights_s[3 * chans : 4 * chans], ctx)
    for t in range(tiles):
        at = tile(t)
        second = first_s[:, at].astype(F32) + moved[:, at]
        feat_s[:, at] = second
        inner_s[:, at] = norm_t(second, gain).astype(BF16)
    kept = iota((1, slots), 1) < count
    wide = 2 * LANES
    part = chans // 2
    for n in range(slots // wide):
        at = slice(n * wide, (n + 1) * wide)
        inner = inner_s[:, at]
        for m in range(down_s.shape[1] // part):
            row = 4 * chans + m * part
            raised = dot(weights_s[row : row + part], inner)
            hidden_s[n % 2, m * part : (m + 1) * part] = jax.nn.gelu(raised).astype(BF16)
        for m in range(chans // part):
            rows = slice(m * part, (m + 1) * part)
            third = feat_s[rows, at] + dot(down_s[rows, :], hidden_s[n % 2])
            third = jnp.where(kept[:, at], third, 0.0)
            feat_s[rows, at] = third
            bf_s[rows, at] = third.astype(BF16)
    keep = [pltpu.make_async_copy(feat_s, feat_hbm, stores.at[owners])]
    keep[0].start()
    facts = facts_s[...].astype(F32)
    low, high = facts[2:3].astype(jnp.int32), facts[1:2].astype(jnp.int32)
    picked = dot(bf_s[...], place(low, high, tiles)).astype(BF16)
    for o in range(owners):
        votes_s[o, :chans, :] = picked[:, o * cap : (o + 1) * cap]
        votes_s[o, chans:, :] = facts_s[:, o * cap : (o + 1) * cap]
        keep.append(pltpu.make_async_copy(votes_s.at[o], votes_hbm[o], stores.at[o]))
        keep[-1].start()
    wait_all(keep)


def sums_kernel(owners, *refs):
    got, out_ref, got_s, sems = refs[:owners], refs[owners], refs[owners + 1], refs[owners + 2]
    loads = start_all([(got[n], got_s.at[n]) for n in range(owners)], sems)
    chans, voxels = out_ref.shape
    cap = got_s.shape[2]
    total = jnp.zeros(out_ref.shape, F32)
    wait_all(loads)
    for n in range(owners):
        label = got_s[n, chans:, :].astype(F32)[0:1]
        hot = (label == iota((voxels, cap), 0).astype(F32)).astype(BF16)
        total = total + dot_t(got_s[n, :chans, :], hot)
    out_ref[...] = total


def call(kernel, outs, scratch, flops, spaces, out_space=pl.ANY):
    return pl.pallas_call(
        kernel,
        out_shape=outs,
        in_specs=[
            pl.BlockSpec(memory_space={"s": pltpu.SMEM, "v": pltpu.VMEM, "a": pl.ANY}[c])
            for c in spaces
        ],
        out_specs=[pl.BlockSpec(memory_space=out_space)] * len(outs),
        scratch_shapes=scratch,
        compiler_params=pltpu.CompilerParams(vmem_limit_bytes=VMEM),
        cost_estimate=pl.CostEstimate(flops=flops, bytes_accessed=2 << 20, transcendentals=0),
    )


def turned(x, axis, bit):
    n = lax.axis_size(axis)
    return lax.ppermute(x, axis, [(i, i ^ bit) for i in range(n)])


def body(
    nodes,
    node_ids,
    node_count,
    pos_weight,
    gain_one,
    qkv_one,
    out_one,
    gain_two,
    qkv_two,
    out_two,
    gain_three,
    w_up,
    w_down,
    vote_slot,
    vote_owner,
    vote_voxel,
):
    slots, chans = nodes.shape
    groups, owners = lax.axis_size("grp"), lax.axis_size("tile")
    run = WIN // groups
    votes = vote_slot.shape[0]
    cap = 2 * votes // owners
    codes = owners * cap
    tiles = slots // LANES
    rows16 = chans // 16
    hidden = w_up.shape[1]
    per = LANES // WIN
    sds = jax.ShapeDtypeStruct
    vmem = pltpu.VMEM
    dma = pltpu.SemaphoreType.DMA

    first, sent = call(
        functools.partial(first_kernel, run),
        [sds((chans, slots), BF16), sds((chans, slots), BF16)],
        [
            vmem((chans, slots), BF16),
            vmem((1, slots), jnp.int32),
            vmem((3, chans), F32),
            vmem((1, chans), F32),
            vmem((1, chans), F32),
            vmem((chans, 3 * chans), BF16),
            vmem((chans, chans), BF16),
            dma((7,)),
            vmem((3 * chans, slots), BF16),
            vmem((tiles, chans, LANES), BF16),
            vmem((tiles, LANES, chans), BF16),
            vmem((tiles, per, chans, LANES), BF16),
            vmem((tiles, chans, LANES), BF16),
            vmem((chans, slots), BF16),
            vmem((chans, slots), BF16),
            vmem((chans, slots), BF16),
            dma((2,)),
        ],
        2_000_000_000,
        "saaaaaaa",
    )(
        node_count,
        nodes.T,
        node_ids.reshape(1, slots),
        pos_weight,
        gain_one.reshape(1, chans),
        gain_two.reshape(1, chans),
        qkv_one,
        out_one,
    )
    near = turned(sent, "grp", 1)
    bit = groups // 2
    mid = []
    while bit > 1:
        mid += [turned(block, "grp", bit) for block in [sent] + mid]
        bit //= 2
    weights, facts = call(
        functools.partial(tables_kernel, cap),
        [sds((4 * chans + hidden, chans), BF16), sds((16, codes), BF16)],
        [
            vmem((chans, 3 * chans), BF16),
            vmem((chans, chans), BF16),
            vmem((chans, hidden), BF16),
            vmem((1, votes), jnp.int32),
            vmem((1, votes), jnp.int32),
            vmem((1, votes), jnp.int32),
            dma((6,)),
            vmem((4 * chans + hidden, chans), BF16),
            vmem((16, codes), BF16),
            dma((2,)),
        ],
        2_000_000_000,
        "aaaaaa",
    )(
        qkv_two,
        out_two,
        w_up,
        vote_slot.reshape(1, votes),
        vote_owner.reshape(1, votes),
        vote_voxel.reshape(1, votes),
    )
    q_like = ((tiles, rows16, 16, LANES), BF16)
    ends_like = ((tiles, 4, 8, LANES), F32)
    acc_like = ((tiles, rows16, 16, LANES), F32)

    def key_scratch(blocks):
        return [
            vmem((blocks, tiles, rows16, 16, LANES), BF16),
            vmem((blocks, tiles, rows16, 16, LANES), BF16),
            vmem((blocks, tiles, 8, LANES), F32),
            vmem((blocks * run, 2, 8, LANES), F32),
        ]

    query, ends, acc = call(
        functools.partial(near_kernel, run),
        [sds(*q_like), sds(*ends_like), sds(*acc_like)],
        [
            vmem((chans, slots), BF16),
            vmem((chans, slots), BF16),
            vmem((3 * chans, chans), BF16),
            dma((3,)),
            vmem(*q_like),
            vmem(*ends_like),
            vmem(*acc_like),
            dma((3,)),
        ]
        + key_scratch(2),
        3_000_000_000,
        "aaa",
    )(sent, near, weights)
    mid, query = lax.optimization_barrier((mid, query))
    far = [turned(block, "grp", 1) for block in mid]
    ends, acc = call(
        functools.partial(middle_kernel, run, len(mid)),
        [sds(*ends_like), sds(*acc_like)],
        [
            vmem((len(mid), chans, slots), BF16),
            dma((len(mid),)),
            vmem(*q_like),
            vmem(*ends_like),
            vmem(*acc_like),
            vmem((2 * chans, chans), BF16),
            dma((4,)),
            dma((2,)),
        ]
        + key_scratch(len(mid)),
        2_000_000_000,
        "a" * len(mid) + "aaaa",
    )(*mid, query, ends, acc, weights)
    features_t, *ballots = call(
        functools.partial(second_kernel, run, cap, len(far), owners),
        [sds((chans, slots), F32)] + [sds((chans + 16, cap), BF16)] * owners,
        [
            vmem((len(far), chans, slots), BF16),
            dma((len(far),)),
            vmem((4 * chans + hidden, chans), BF16),
            vmem(*q_like),
            vmem(*ends_like),
            vmem(*acc_like),
            vmem((chans, slots), BF16),
            vmem((1, chans), F32),
            vmem((chans, hidden), BF16),
            vmem((16, codes), BF16),
            dma((8,)),
            vmem((chans, slots), F32),
            vmem((owners, chans + 16, cap), BF16),
            dma((owners + 1,)),
        ]
        + key_scratch(len(far))
        + [
            vmem((tiles, chans, LANES), BF16),
            vmem((chans, slots), BF16),
            vmem((chans, slots), BF16),
            vmem((2, hidden, 2 * LANES), BF16),
        ],
        3_000_000_000,
        "s" + "a" * (len(far) + 8),
    )(
        node_count,
        *far,
        query,
        ends,
        acc,
        weights,
        first,
        gain_three.reshape(1, chans),
        w_down.T,
        facts,
    )
    got = [ballots[0]] + [turned(ballots[k], "tile", k) for k in range(owners - 1, 0, -1)]
    (sums_t,) = call(
        functools.partial(sums_kernel, owners),
        [sds((chans, VOX_DEV), F32)],
        [vmem((owners, chans + 16, cap), BF16), dma((owners,))],
        200_000_000,
        "a" * owners,
        pltpu.VMEM,
    )(*got)
    return (features_t.T, sums_t.T)


def solution(mesh):
    in_specs = (
        P(("grp", "tile"), None),
        P(("grp", "tile")),
        P(("grp", "tile")),
        P(),
        P(),
        P(),
        P(),
        P(),
        P(),
        P(),
        P(),
        P(),
        P(),
        P(("grp", "tile")),
        P(("grp", "tile"), None),
        P(("grp", "tile")),
    )
    out_specs = (P(("grp", "tile"), None), P(("grp", "tile"), None))
    return jax.shard_map(body, mesh=mesh, in_specs=in_specs, out_specs=out_specs, check_vma=False)
```

```python
import functools
import math

import jax
import jax.numpy as jnp
from jax import lax
from jax.experimental import pallas as pl
from jax.experimental.pallas import tpu as pltpu
from jax.sharding import PartitionSpec as P

HEADS = 12
WIN = 32
VOX_DEV = 256
LANES = 128
FLAG = 16384.0
VMEM = 64 * 1024 * 1024 - 65536
F32 = jnp.float32
BF16 = jnp.bfloat16
LOG2E = math.log2(math.e)


def iota(shape, dim):
    return lax.broadcasted_iota(jnp.int32, shape, dim)


def dot(a, b):
    return jnp.dot(a, b, preferred_element_type=F32)


def dot_t(a, b):
    return lax.dot_general(a, b, (((1,), (1,)), ((), ())), preferred_element_type=F32)


def eye(n):
    return (iota((n, n), 0) == iota((n, n), 1)).astype(BF16)


def transposed(a):
    return a.astype(F32).T.astype(BF16)


def tile(t):
    return slice(t * LANES, (t + 1) * LANES)


def head_order(chans):
    size = chans // HEADS
    cut = 8 * size
    j = iota((chans, 1), 0)
    high = j - cut
    low_src = (j % 8) * size + j // 8
    high_src = (8 + high % 4) * size + high // 8 + (size // 2) * ((high % 8) // 4)
    return jnp.where(j < cut, low_src, high_src)


def within(run):
    lane = iota((1, LANES), 1)
    q, e = lane // 16, lane % 16
    p = (4 * (q // run) + e // 4) * run + q % run
    return ((e % 4) * WIN + p == iota((LANES, LANES), 0)).astype(BF16)


def swap_blocks(tiles):
    tiles = list(tiles)
    block = iota(tiles[0].shape, 1) // 16
    step = len(tiles) // 2
    while step:
        for n in range(len(tiles)):
            if n & step:
                continue
            a, b = tiles[n], tiles[n + step]
            low = block // step % 2 == 0
            tiles[n] = jnp.where(low, a, pltpu.roll(b, 16 * step, 1))
            tiles[n + step] = jnp.where(low, pltpu.roll(a, LANES - 16 * step, 1), b)
        step //= 2
    return tiles


def place(low, high, blocks):
    base = jnp.where(low == iota((LANES, low.shape[1]), 0), 1.0, 0.0).astype(BF16)
    high = jnp.broadcast_to(high, base.shape).astype(F32).astype(BF16)
    nil = jnp.zeros_like(base)
    parts = [jnp.where(high == jnp.asarray(n, BF16), base, nil) for n in range(blocks)]
    return jnp.concatenate(parts, 0)


def norm_t(x, gain):
    inv = 1.0 / x.shape[0]
    mean = jnp.sum(x, 0, keepdims=True) * inv
    cent = x - mean
    var = jnp.sum(cent * cent, 0, keepdims=True) * inv
    return cent * lax.rsqrt(var + 1e-05) * gain


def start_all(pairs, sems):
    copies = [pltpu.make_async_copy(a, b, sems.at[n]) for n, (a, b) in enumerate(pairs)]
    for copy in copies:
        copy.start()
    return copies


def wait_all(copies):
    for copy in copies:
        copy.wait()


def fold8(x, op):
    y = x[0]
    for n in range(1, x.shape[0]):
        y = op(y, x[n])
    for shift in (4, 2, 1):
        y = op(y, pltpu.roll(y, shift, 0))
    return y


def first_kernel(
    run, count_ref, nodes_hbm, ids_hbm, pos_hbm, gain_one_hbm, gain_two_hbm, qkv_hbm, out_hbm,
    first_hbm, sent_hbm, nodes_ref, ids_ref, pos_ref, gain_one_ref, gain_two_ref, qkv_ref, out_ref,
    sems, qkv_s, q_s, k_s, v_s, ctx_s, n_s, first_s, sent_s, stores
):
    loads = start_all(
        [
            (nodes_hbm, nodes_ref),
            (ids_hbm, ids_ref),
            (pos_hbm, pos_ref),
            (gain_one_hbm, gain_one_ref),
            (gain_two_hbm, gain_two_ref),
            (qkv_hbm, qkv_ref),
            (out_hbm, out_ref),
        ],
        sems,
    )
    chans, slots = nodes_ref.shape
    tiles = slots // LANES
    size = chans // HEADS
    per = LANES // WIN
    count = count_ref[0]
    wait_all(loads[:5])
    cols = jnp.concatenate(
        [pos_ref[...], gain_one_ref[...], gain_two_ref[...], jnp.zeros((3, chans), F32)], 0
    ).T
    ids = ids_ref[...]
    coords = []
    for axis in range(3):
        total = jnp.zeros(ids.shape, jnp.int32)
        for level in range(6):
            bit = jnp.bitwise_and(jnp.right_shift(ids, 3 * level + axis), 1)
            total = total + bit * 2**level
        coords.append(total.astype(F32) / 64.0 - 0.5)
    for t in range(tiles):
        at = tile(t)
        start = cols[:, 0:1] * coords[0][:, at]
        for axis in range(1, 3):
            start = start + cols[:, axis : axis + 1] * coords[axis][:, at]
        start = (nodes_ref[:, at].astype(F32) + start).astype(BF16)
        nodes_ref[:, at] = start
        n_s[:, at] = norm_t(start.astype(F32), cols[:, 3:4]).astype(BF16)
    wait_all(loads[5:])
    qkv_t = transposed(qkv_ref[...])
    out_t = transposed(out_ref[...])
    qkv_s[...] = dot(qkv_t, n_s[...]).astype(BF16)
    side = eye(LANES)
    spread = (
        iota((LANES, per * LANES), 0)
        == (iota((LANES, per * LANES), 1) // LANES) * WIN + iota((LANES, per * LANES), 1) % WIN
    ).astype(BF16)
    row_head = (iota((chans, LANES), 0) // size) % per
    own_head = row_head == iota((chans, LANES), 1) // WIN
    even_row = row_head % 2 == 0
    for t in range(tiles):
        query = qkv_s[:chans, tile(t)].astype(F32) * size**-0.5
        q_s[t, :, :LANES] = jnp.where(even_row, query, 0.0).astype(BF16)
        q_s[t, :, LANES:] = jnp.where(even_row, 0.0, query).astype(BF16)
        k_s[t] = dot_t(side, qkv_s[chans : 2 * chans, tile(t)]).astype(BF16)
    for t in range(tiles):
        wide = dot(qkv_s[2 * chans :, tile(t)], spread)
        for w in range(per):
            v_s[t, w] = jnp.where(own_head, wide[:, tile(w)], 0.0).astype(BF16)

    lane_pair = iota((WIN, chans), 1) // (2 * size)
    window = iota((8, LANES), 1) // WIN
    rank = iota((WIN, LANES), 0) + WIN * (iota((WIN, LANES), 1) // WIN)

    def group(t, _):
        query = q_s[t]
        even, odd = None, None
        for w in range(per):
            keys = k_s[t, w * WIN : (w + 1) * WIN, :]
            by_pair = jnp.concatenate(
                [jnp.where(lane_pair == m, keys, jnp.zeros_like(keys)) for m in range(HEADS // 2)],
                0,
            )
            got = dot(by_pair, query)
            left = got[:, :LANES].reshape(-1, 8, LANES)
            right = got[:, LANES:].reshape(-1, 8, LANES)
            even = left if w == 0 else jnp.where(window[None] == w, left, even)
            odd = right if w == 0 else jnp.where(window[None] == w, right, odd)
        mask = jnp.where(rank + t * LANES < count, 0.0, -1e9).astype(F32)
        mask = mask.reshape(WIN // 8, 8, LANES)
        probs, inverse = [], []
        for h in range(HEADS):
            scores = (even, odd)[h % 2]
            mine = scores[h // 2 * (WIN // 8) : (h // 2 + 1) * (WIN // 8)] + mask
            top = fold8(mine, jnp.maximum)
            weight = jnp.exp(mine - top[None])
            inverse.append(1.0 / fold8(weight, jnp.add))
            probs.append(weight.reshape(WIN, LANES).astype(BF16))
        half = per * size
        parts = []
        for j in range(HEADS // per):
            weight = jnp.concatenate(probs[j * per : (j + 1) * per], 0)
            ctx = None
            for w in range(per):
                got = dot(v_s[t, w, j * half : (j + 1) * half, :], weight).reshape(-1, 8, LANES)
                ctx = got if w == 0 else jnp.where(window[None] == w, got, ctx)
            for h in range(per):
                block = ctx[h * (size // 8) : (h + 1) * (size // 8)] * inverse[j * per + h][None]
                parts.append(block.reshape(size, LANES))
        ctx_s[t] = jnp.concatenate(parts, 0).astype(BF16)
        return 0

    lax.fori_loop(0, tiles, group, 0, unroll=2)
    ctx = jnp.concatenate([ctx_s[t] for t in range(tiles)], 1)
    moved = dot(out_t, ctx)
    for t in range(tiles):
        at = tile(t)
        first = (nodes_ref[:, at].astype(F32) + moved[:, at]).astype(BF16)
        first_s[:, at] = first
        normed = norm_t(first.astype(F32), cols[:, 4:5])
        kept = iota((1, LANES), 1) + t * LANES < count
        head = jnp.where((iota((16, LANES), 0) > 0) | kept, normed[:16], FLAG)
        n_s[:, at] = jnp.concatenate([head, normed[16:]], 0).astype(BF16)
    keep_first = pltpu.make_async_copy(first_s, first_hbm, stores.at[0])
    keep_first.start()
    inside = within(run)
    for t, block in enumerate(swap_blocks([dot(n_s[:, tile(t)], inside) for t in range(tiles)])):
        sent_s[:, tile(t)] = block.astype(BF16)
    send = pltpu.make_async_copy(sent_s, sent_hbm, stores.at[1])
    send.start()
    wait_all([keep_first, send])


def tables_kernel(
    cap, qkv_hbm, out_hbm, up_hbm, slot_hbm, owner_hbm, voxel_hbm, weights_hbm, facts_hbm,
    qkv_ref, out_ref, up_ref, slot_ref, owner_ref, voxel_ref, sems, weights_s, facts_s, stores
):
    loads = start_all(
        [
            (qkv_hbm, qkv_ref),
            (out_hbm, out_ref),
            (up_hbm, up_ref),
            (slot_hbm, slot_ref),
            (owner_hbm, owner_ref),
            (voxel_hbm, voxel_ref),
        ],
        sems,
    )
    wait_all(loads)
    votes = slot_ref.shape[1]
    codes = facts_s.shape[1]
    owners = codes // cap
    chans = out_ref.shape[0]
    src = head_order(chans)
    src = jnp.concatenate([src, src + chans, src + 2 * chans], 0)
    shuffle = (src == iota((3 * chans, 3 * chans), 1)).astype(BF16)
    weights_s[: 3 * chans] = dot_t(shuffle, qkv_ref[...]).astype(BF16)
    out_t = dot(shuffle[:chans, :chans], out_ref[...])
    weights_s[3 * chans : 4 * chans] = transposed(out_t)
    weights_s[4 * chans :] = transposed(up_ref[...])
    keep_weights = pltpu.make_async_copy(weights_s, weights_hbm, stores.at[0])
    keep_weights.start()
    owner = jnp.bitwise_xor(owner_ref[...], lax.axis_index("tile"))
    hot = owner == iota((owners, votes), 0)
    upto = (iota((votes, votes), 0) <= iota((votes, votes), 1)).astype(BF16)
    rank = jnp.sum(jnp.where(hot, dot(hot.astype(BF16), upto), 0.0), 0, keepdims=True)
    code = owner * cap + rank.astype(jnp.int32) - 1
    member = place(code % LANES, code // LANES, codes // LANES)
    slot = slot_ref[...]
    row = iota((16, votes), 0)
    facts = jnp.where(
        row == 0,
        voxel_ref[...],
        jnp.where(row == 1, slot // LANES, jnp.where(row == 2, slot % LANES, 1)),
    )
    listed = dot_t(facts.astype(F32).astype(BF16), member)
    facts_s[...] = jnp.where(listed[3:4] > 0.5, listed, -1.0).astype(BF16)
    keep_facts = pltpu.make_async_copy(facts_s, facts_hbm, stores.at[1])
    keep_facts.start()
    wait_all([keep_weights, keep_facts])


def clean(block):
    head = block[:16].astype(F32)
    gone = head[0:1] > 0.5 * FLAG
    head = jnp.where((iota(head.shape, 0) == 0) & gone, 0.0, head)
    return jnp.concatenate([head.astype(BF16), block[16:]], 0), gone


def add_keys(blocks, kv_t, k_s, v_s, m_s):
    chans = kv_t.shape[1]
    tiles = k_s.shape[1]
    for n, block in enumerate(blocks):
        block, gone = clean(block)
        kv = dot(kv_t, block)
        mask = jnp.where(gone, -1e9, 0.0)
        for t in range(tiles):
            k_s[n, t] = kv[:chans, tile(t)].reshape(chans // 8, 8, LANES)
            v_s[n, t] = kv[chans:, tile(t)].reshape(chans // 8, 8, LANES)
            m_s[n, t] = jnp.broadcast_to(mask[:, tile(t)], (8, LANES))


def attend_two(t, run, q_s, k_s, v_s, m_s, s_s, ends_s, acc_s, fresh):
    rows8 = q_s.shape[1]
    cut = 2 * rows8 // 3
    keys = k_s.shape[0] * run
    base = (t // run) * run
    both = range(2)
    query = [[q_s[t + n, i] for i in range(rows8)] for n in both]

    def score(key, top):
        block, at = key // run, base + key % run
        mask = m_s[block, at]
        sums = [[None, None], [None, None]]
        for i in range(rows8):
            part = int(i >= cut)
            row = k_s[block, at, i]
            for n in both:
                term = query[n][i] * row
                held = sums[n][part]
                sums[n][part] = term if held is None else held + term
        tops = []
        for n in both:
            a, b = sums[n]
            b = b + pltpu.roll(b, 4, 0)
            a = a + mask
            b = b + mask
            s_s[key, 2 * n] = a
            s_s[key, 2 * n + 1] = b
            tops += [jnp.maximum(top[2 * n], a), jnp.maximum(top[2 * n + 1], b)]
        return tuple(tops)

    if fresh:
        old = tuple(jnp.full((8, LANES), -3e38, F32) for _ in range(4))
    else:
        old = tuple(ends_s[t + n, part] for n in both for part in both)
    tops = lax.fori_loop(0, keys, score, old, unroll=2)
    if fresh:
        zero = jnp.zeros((8, LANES), F32)
        sums = tuple(zero for _ in range(4))
        accs = tuple(zero for _ in range(2 * rows8))
    else:
        fade = [jnp.exp2(old[n] - tops[n]) for n in range(4)]
        sums = tuple(ends_s[t + n, 2 + part] * fade[2 * n + part] for n in both for part in both)
        accs = tuple(
            acc_s[t + n, i] * fade[2 * n + int(i >= cut)] for n in both for i in range(rows8)
        )

    def gather(key, carry):
        sums, accs = carry
        block, at = key // run, base + key % run
        weight = [jnp.exp2(s_s[key, n] - tops[n]) for n in range(4)]
        accs = list(accs)
        for i in range(rows8):
            row = v_s[block, at, i]
            for n in both:
                at_acc = n * rows8 + i
                accs[at_acc] = accs[at_acc] + weight[2 * n + int(i >= cut)] * row
        return tuple(sums[n] + weight[n] for n in range(4)), tuple(accs)

    sums, accs = lax.fori_loop(0, keys, gather, (sums, accs), unroll=2)
    return tops, sums, accs


def hold_two(t, state, ends_s, acc_s):
    tops, sums, accs = state
    rows8 = acc_s.shape[1]
    for n in range(2):
        for part in range(2):
            ends_s[t + n, part] = tops[2 * n + part]
            ends_s[t + n, 2 + part] = sums[2 * n + part]
        for i in range(rows8):
            acc_s[t + n, i] = accs[n * rows8 + i]


def near_kernel(
    run, own_hbm, near_hbm, weights_hbm, q_hbm, ends_hbm, acc_hbm,
    own_ref, near_ref, qkv_t_ref, sems, q_s, ends_s, acc_s, stores, k_s, v_s, m_s, s_s
):
    chans, slots = own_ref.shape
    loads = start_all(
        [
            (own_hbm, own_ref),
            (weights_hbm.at[pl.ds(0, 3 * chans)], qkv_t_ref),
            (near_hbm, near_ref),
        ],
        sems,
    )
    tiles = slots // LANES
    scale = (chans // HEADS) ** -0.5 * LOG2E
    wait_all(loads[:2])
    own, _ = clean(own_ref[...])
    query = dot(qkv_t_ref[:chans, :], own) * scale
    for t in range(tiles):
        q_s[t] = query[:, tile(t)].reshape(chans // 8, 8, LANES)
    keep_q = pltpu.make_async_copy(q_s, q_hbm, stores.at[0])
    keep_q.start()
    wait_all(loads[2:])
    add_keys([own_ref[...], near_ref[...]], qkv_t_ref[chans:, :], k_s, v_s, m_s)

    def step(n, _):
        t = 2 * n
        state = attend_two(t, run, q_s, k_s, v_s, m_s, s_s, ends_s, acc_s, True)
        hold_two(t, state, ends_s, acc_s)
        return 0

    lax.fori_loop(0, tiles // 2, step, 0)
    keep_ends = pltpu.make_async_copy(ends_s, ends_hbm, stores.at[1])
    keep_acc = pltpu.make_async_copy(acc_s, acc_hbm, stores.at[2])
    keep_ends.start()
    keep_acc.start()
    wait_all([keep_q, keep_ends, keep_acc])


def middle_kernel(run, count, *refs):
    blocks, refs = refs[:count], refs[count:]
    q_hbm, ends_hbm, acc_hbm, weights_hbm, ends_out, acc_out = refs[:6]
    block_s, sems, q_s, ends_s, acc_s, kv_t_ref, rest, stores, k_s, v_s, m_s, s_s = refs[6:]
    chans = kv_t_ref.shape[1]
    loads = start_all([(blocks[n], block_s.at[n]) for n in range(count)], sems)
    later = start_all(
        [
            (weights_hbm.at[pl.ds(chans, 2 * chans)], kv_t_ref),
            (q_hbm, q_s),
            (ends_hbm, ends_s),
            (acc_hbm, acc_s),
        ],
        rest,
    )
    wait_all(loads + later[:1])
    add_keys([block_s[n] for n in range(count)], kv_t_ref[...], k_s, v_s, m_s)
    wait_all(later[1:])

    def step(n, _):
        t = 2 * n
        state = attend_two(t, run, q_s, k_s, v_s, m_s, s_s, ends_s, acc_s, False)
        hold_two(t, state, ends_s, acc_s)
        return 0

    lax.fori_loop(0, q_s.shape[0] // 2, step, 0)
    wait_all(start_all([(ends_s, ends_out), (acc_s, acc_out)], stores))


def second_kernel(run, cap, far, owners, count_ref, *refs):
    blocks, refs = refs[:far], refs[far:]
    (
        q_hbm, ends_hbm, acc_hbm, weights_hbm, first_hbm, gain_hbm, down_hbm, facts_hbm, feat_hbm
    ) = refs[:9]
    votes_hbm, refs = refs[9 : 9 + owners], refs[9 + owners :]
    (
        block_s, sems, weights_s, q_s, ends_s, acc_s, first_s, gain_s, down_s, facts_s, rest,
        feat_s, votes_s, stores, k_s, v_s, m_s, s_s, bf_s, inner_s, hidden_s
    ) = refs
    loads = start_all([(blocks[n], block_s.at[n]) for n in range(far)], sems)
    later = start_all(
        [
            (weights_hbm, weights_s),
            (q_hbm, q_s),
            (ends_hbm, ends_s),
            (acc_hbm, acc_s),
            (first_hbm, first_s),
            (gain_hbm, gain_s),
            (down_hbm, down_s),
            (facts_hbm, facts_s),
        ],
        rest,
    )
    chans, slots = first_s.shape
    tiles = slots // LANES
    count = count_ref[0]
    wait_all(loads + later[:1])
    add_keys([block_s[n] for n in range(far)], weights_s[chans : 3 * chans], k_s, v_s, m_s)
    wait_all(later[1:])

    rows8 = chans // 8

    def step(n, _):
        t = 2 * n
        _, sums, accs = attend_two(t, run, q_s, k_s, v_s, m_s, s_s, ends_s, acc_s, False)
        share = [1.0 / total for total in sums]
        cut = 2 * rows8 // 3
        for n in range(2):
            for i in range(rows8):
                acc_s[t + n, i] = accs[n * rows8 + i] * share[2 * n + int(i >= cut)]
        return 0

    lax.fori_loop(0, tiles // 2, step, 0)
    inside = within(run)
    ctx = swap_blocks([acc_s[t].reshape(chans, LANES) for t in range(tiles)])
    ctx = jnp.concatenate([dot_t(c.astype(BF16), inside).astype(BF16) for c in ctx], 1)
    gain = jnp.concatenate([gain_s[...], jnp.zeros((7, chans), F32)], 0).T[:, 0:1]
    moved = dot(weights_s[3 * chans : 4 * chans], ctx)
    for t in range(tiles):
        at = tile(t)
        second = first_s[:, at].astype(F32) + moved[:, at]
        feat_s[:, at] = second
        inner_s[:, at] = norm_t(second, gain).astype(BF16)
    kept = iota((1, slots), 1) < count
    wide = 2 * LANES
    part = chans // 2
    for n in range(slots // wide):
        at = slice(n * wide, (n + 1) * wide)
        inner = inner_s[:, at]
        for m in range(down_s.shape[1] // part):
            row = 4 * chans + m * part
            raised = dot(weights_s[row : row + part], inner)
            hidden_s[n % 2, m * part : (m + 1) * part] = jax.nn.gelu(raised).astype(BF16)
        for m in range(chans // part):
            rows = slice(m * part, (m + 1) * part)
            third = feat_s[rows, at] + dot(down_s[rows, :], hidden_s[n % 2])
            third = jnp.where(kept[:, at], third, 0.0)
            feat_s[rows, at] = third
            bf_s[rows, at] = third.astype(BF16)
    keep = [pltpu.make_async_copy(feat_s, feat_hbm, stores.at[owners])]
    keep[0].start()
    facts = facts_s[...].astype(F32)
    low, high = facts[2:3].astype(jnp.int32), facts[1:2].astype(jnp.int32)
    picked = dot(bf_s[...], place(low, high, tiles)).astype(BF16)
    for o in range(owners):
        votes_s[o, :chans, :] = picked[:, o * cap : (o + 1) * cap]
        votes_s[o, chans:, :] = facts_s[:, o * cap : (o + 1) * cap]
        keep.append(pltpu.make_async_copy(votes_s.at[o], votes_hbm[o], stores.at[o]))
        keep[-1].start()
    wait_all(keep)


def sums_kernel(owners, *refs):
    got, out_ref, got_s, sems = refs[:owners], refs[owners], refs[owners + 1], refs[owners + 2]
    loads = start_all([(got[n], got_s.at[n]) for n in range(owners)], sems)
    chans, voxels = out_ref.shape
    cap = got_s.shape[2]
    total = jnp.zeros(out_ref.shape, F32)
    wait_all(loads)
    for n in range(owners):
        label = got_s[n, chans:, :].astype(F32)[0:1]
        hot = (label == iota((voxels, cap), 0).astype(F32)).astype(BF16)
        total = total + dot_t(got_s[n, :chans, :], hot)
    out_ref[...] = total


def call(kernel, outs, scratch, flops, spaces, out_space=pl.ANY):
    return pl.pallas_call(
        kernel,
        out_shape=outs,
        in_specs=[
            pl.BlockSpec(memory_space={"s": pltpu.SMEM, "v": pltpu.VMEM, "a": pl.ANY}[c])
            for c in spaces
        ],
        out_specs=[pl.BlockSpec(memory_space=out_space)] * len(outs),
        scratch_shapes=scratch,
        compiler_params=pltpu.CompilerParams(vmem_limit_bytes=VMEM),
        cost_estimate=pl.CostEstimate(flops=flops, bytes_accessed=2 << 20, transcendentals=0),
    )


def turned(x, axis, bit):
    n = lax.axis_size(axis)
    return lax.ppermute(x, axis, [(i, i ^ bit) for i in range(n)])


def body(
    nodes,
    node_ids,
    node_count,
    pos_weight,
    gain_one,
    qkv_one,
    out_one,
    gain_two,
    qkv_two,
    out_two,
    gain_three,
    w_up,
    w_down,
    vote_slot,
    vote_owner,
    vote_voxel,
):
    slots, chans = nodes.shape
    groups, owners = lax.axis_size("grp"), lax.axis_size("tile")
    run = WIN // groups
    votes = vote_slot.shape[0]
    cap = 2 * votes // owners
    codes = owners * cap
    tiles = slots // LANES
    rows8 = chans // 8
    hidden = w_up.shape[1]
    per = LANES // WIN
    sds = jax.ShapeDtypeStruct
    vmem = pltpu.VMEM
    dma = pltpu.SemaphoreType.DMA

    first, sent = call(
        functools.partial(first_kernel, run),
        [sds((chans, slots), BF16), sds((chans, slots), BF16)],
        [
            vmem((chans, slots), BF16),
            vmem((1, slots), jnp.int32),
            vmem((3, chans), F32),
            vmem((1, chans), F32),
            vmem((1, chans), F32),
            vmem((chans, 3 * chans), BF16),
            vmem((chans, chans), BF16),
            dma((7,)),
            vmem((3 * chans, slots), BF16),
            vmem((tiles, chans, 2 * LANES), BF16),
            vmem((tiles, LANES, chans), BF16),
            vmem((tiles, per, chans, LANES), BF16),
            vmem((tiles, chans, LANES), BF16),
            vmem((chans, slots), BF16),
            vmem((chans, slots), BF16),
            vmem((chans, slots), BF16),
            dma((2,)),
        ],
        2_000_000_000,
        "saaaaaaa",
    )(
        node_count,
        nodes.T,
        node_ids.reshape(1, slots),
        pos_weight,
        gain_one.reshape(1, chans),
        gain_two.reshape(1, chans),
        qkv_one,
        out_one,
    )
    near = turned(sent, "grp", 1)
    bit = groups // 2
    mid = []
    while bit > 1:
        mid += [turned(block, "grp", bit) for block in [sent] + mid]
        bit //= 2
    weights, facts = call(
        functools.partial(tables_kernel, cap),
        [sds((4 * chans + hidden, chans), BF16), sds((16, codes), BF16)],
        [
            vmem((chans, 3 * chans), BF16),
            vmem((chans, chans), BF16),
            vmem((chans, hidden), BF16),
            vmem((1, votes), jnp.int32),
            vmem((1, votes), jnp.int32),
            vmem((1, votes), jnp.int32),
            dma((6,)),
            vmem((4 * chans + hidden, chans), BF16),
            vmem((16, codes), BF16),
            dma((2,)),
        ],
        2_000_000_000,
        "aaaaaa",
    )(
        qkv_two,
        out_two,
        w_up,
        vote_slot.reshape(1, votes),
        vote_owner.reshape(1, votes),
        vote_voxel.reshape(1, votes),
    )
    q_like = ((tiles, rows8, 8, LANES), F32)
    ends_like = ((tiles, 4, 8, LANES), F32)
    acc_like = ((tiles, rows8, 8, LANES), F32)

    def key_scratch(blocks):
        return [
            vmem((blocks, tiles, rows8, 8, LANES), F32),
            vmem((blocks, tiles, rows8, 8, LANES), F32),
            vmem((blocks, tiles, 8, LANES), F32),
            vmem((blocks * run, 4, 8, LANES), F32),
        ]

    query, ends, acc = call(
        functools.partial(near_kernel, run),
        [sds(*q_like), sds(*ends_like), sds(*acc_like)],
        [
            vmem((chans, slots), BF16),
            vmem((chans, slots), BF16),
            vmem((3 * chans, chans), BF16),
            dma((3,)),
            vmem(*q_like),
            vmem(*ends_like),
            vmem(*acc_like),
            dma((3,)),
        ]
        + key_scratch(2),
        3_000_000_000,
        "aaa",
    )(sent, near, weights)
    mid, query = lax.optimization_barrier((mid, query))
    far = [turned(block, "grp", 1) for block in mid]
    ends, acc = call(
        functools.partial(middle_kernel, run, len(mid)),
        [sds(*ends_like), sds(*acc_like)],
        [
            vmem((len(mid), chans, slots), BF16),
            dma((len(mid),)),
            vmem(*q_like),
            vmem(*ends_like),
            vmem(*acc_like),
            vmem((2 * chans, chans), BF16),
            dma((4,)),
            dma((2,)),
        ]
        + key_scratch(len(mid)),
        2_000_000_000,
        "a" * len(mid) + "aaaa",
    )(*mid, query, ends, acc, weights)
    features_t, *ballots = call(
        functools.partial(second_kernel, run, cap, len(far), owners),
        [sds((chans, slots), F32)] + [sds((chans + 16, cap), BF16)] * owners,
        [
            vmem((len(far), chans, slots), BF16),
            dma((len(far),)),
            vmem((4 * chans + hidden, chans), BF16),
            vmem(*q_like),
            vmem(*ends_like),
            vmem(*acc_like),
            vmem((chans, slots), BF16),
            vmem((1, chans), F32),
            vmem((chans, hidden), BF16),
            vmem((16, codes), BF16),
            dma((8,)),
            vmem((chans, slots), F32),
            vmem((owners, chans + 16, cap), BF16),
            dma((owners + 1,)),
        ]
        + key_scratch(len(far))
        + [
            vmem((chans, slots), BF16),
            vmem((chans, slots), BF16),
            vmem((2, hidden, 2 * LANES), BF16),
        ],
        3_000_000_000,
        "s" + "a" * (len(far) + 8),
    )(
        node_count,
        *far,
        query,
        ends,
        acc,
        weights,
        first,
        gain_three.reshape(1, chans),
        w_down.T,
        facts,
    )
    got = [ballots[0]] + [turned(ballots[k], "tile", k) for k in range(owners - 1, 0, -1)]
    (sums_t,) = call(
        functools.partial(sums_kernel, owners),
        [sds((chans, VOX_DEV), F32)],
        [vmem((owners, chans + 16, cap), BF16), dma((owners,))],
        200_000_000,
        "a" * owners,
        pltpu.VMEM,
    )(*got)
    return (features_t.T, sums_t.T)


def solution(mesh):
    in_specs = (
        P(("grp", "tile"), None),
        P(("grp", "tile")),
        P(("grp", "tile")),
        P(),
        P(),
        P(),
        P(),
        P(),
        P(),
        P(),
        P(),
        P(),
        P(),
        P(("grp", "tile")),
        P(("grp", "tile"), None),
        P(("grp", "tile")),
    )
    out_specs = (P(("grp", "tile"), None), P(("grp", "tile"), None))
    return jax.shard_map(body, mesh=mesh, in_specs=in_specs, out_specs=out_specs, check_vma=False)
```

```python
import functools
import math

import jax
import jax.numpy as jnp
from jax import lax
from jax.experimental import pallas as pl
from jax.experimental.pallas import tpu as pltpu
from jax.sharding import PartitionSpec as P

HEADS = 12
WIN = 32
VOX_DEV = 256
LANES = 128
FLAG = 16384.0
VMEM = 64 * 1024 * 1024 - 65536
F32 = jnp.float32
BF16 = jnp.bfloat16
LOG2E = math.log2(math.e)


def iota(shape, dim):
    return lax.broadcasted_iota(jnp.int32, shape, dim)


def dot(a, b):
    return jnp.dot(a, b, preferred_element_type=F32)


def dot_t(a, b):
    return lax.dot_general(a, b, (((1,), (1,)), ((), ())), preferred_element_type=F32)


def eye(n):
    return (iota((n, n), 0) == iota((n, n), 1)).astype(BF16)


def transposed(a):
    return a.astype(F32).T.astype(BF16)


def tile(t):
    return slice(t * LANES, (t + 1) * LANES)


def head_order(chans):
    size = chans // HEADS
    cut = 8 * size
    j = iota((chans, 1), 0)
    high = j - cut
    low_src = (j % 8) * size + j // 8
    high_src = (8 + high % 4) * size + high // 8 + (size // 2) * ((high % 8) // 4)
    return jnp.where(j < cut, low_src, high_src)


def within(run):
    lane = iota((1, LANES), 1)
    q, e = lane // 16, lane % 16
    p = (4 * (q // run) + e // 4) * run + q % run
    return ((e % 4) * WIN + p == iota((LANES, LANES), 0)).astype(BF16)


def swap_blocks(tiles):
    tiles = list(tiles)
    block = iota(tiles[0].shape, 1) // 16
    step = len(tiles) // 2
    while step:
        for n in range(len(tiles)):
            if n & step:
                continue
            a, b = tiles[n], tiles[n + step]
            low = block // step % 2 == 0
            tiles[n] = jnp.where(low, a, pltpu.roll(b, 16 * step, 1))
            tiles[n + step] = jnp.where(low, pltpu.roll(a, LANES - 16 * step, 1), b)
        step //= 2
    return tiles


def place(low, high, blocks):
    base = jnp.where(low == iota((LANES, low.shape[1]), 0), 1.0, 0.0).astype(BF16)
    high = jnp.broadcast_to(high, base.shape).astype(F32).astype(BF16)
    nil = jnp.zeros_like(base)
    parts = [jnp.where(high == jnp.asarray(n, BF16), base, nil) for n in range(blocks)]
    return jnp.concatenate(parts, 0)


def norm_t(x, gain):
    inv = 1.0 / x.shape[0]
    mean = jnp.sum(x, 0, keepdims=True) * inv
    cent = x - mean
    var = jnp.sum(cent * cent, 0, keepdims=True) * inv
    return cent * lax.rsqrt(var + 1e-05) * gain


def start_all(pairs, sems):
    copies = [pltpu.make_async_copy(a, b, sems.at[n]) for n, (a, b) in enumerate(pairs)]
    for copy in copies:
        copy.start()
    return copies


def wait_all(copies):
    for copy in copies:
        copy.wait()


def fold8(x, op):
    y = x[0]
    for n in range(1, x.shape[0]):
        y = op(y, x[n])
    for shift in (4, 2, 1):
        y = op(y, pltpu.roll(y, shift, 0))
    return y


def first_kernel(
    run, count_ref, nodes_hbm, ids_hbm, pos_hbm, gain_one_hbm, gain_two_hbm, qkv_hbm, out_hbm,
    first_hbm, sent_hbm, nodes_ref, ids_ref, pos_ref, gain_one_ref, gain_two_ref, qkv_ref, out_ref,
    sems, qkv_s, q_s, k_s, v_s, ctx_s, inner_s, n_s, first_s, sent_s, stores
):
    loads = start_all(
        [
            (nodes_hbm, nodes_ref),
            (ids_hbm, ids_ref),
            (pos_hbm, pos_ref),
            (gain_one_hbm, gain_one_ref),
            (gain_two_hbm, gain_two_ref),
            (qkv_hbm, qkv_ref),
            (out_hbm, out_ref),
        ],
        sems,
    )
    chans, slots = nodes_ref.shape
    tiles = slots // LANES
    size = chans // HEADS
    per = LANES // WIN
    count = count_ref[0]
    wait_all(loads[:5])
    cols = jnp.concatenate(
        [pos_ref[...], gain_one_ref[...], gain_two_ref[...], jnp.zeros((3, chans), F32)], 0
    ).T
    ids = ids_ref[...]
    coords = []
    for axis in range(3):
        total = jnp.zeros(ids.shape, jnp.int32)
        for level in range(6):
            bit = jnp.bitwise_and(jnp.right_shift(ids, 3 * level + axis), 1)
            total = total + bit * 2**level
        coords.append(total.astype(F32) / 64.0 - 0.5)
    for t in range(tiles):
        at = tile(t)
        start = cols[:, 0:1] * coords[0][:, at]
        for axis in range(1, 3):
            start = start + cols[:, axis : axis + 1] * coords[axis][:, at]
        start = (nodes_ref[:, at].astype(F32) + start).astype(BF16)
        nodes_ref[:, at] = start
        inner_s[:, at] = norm_t(start.astype(F32), cols[:, 3:4]).astype(BF16)
    wait_all(loads[5:])
    qkv_t = transposed(qkv_ref[...])
    out_t = transposed(out_ref[...])
    qkv_s[...] = dot(qkv_t, inner_s[...]).astype(BF16)
    side = eye(LANES)
    spread = (
        iota((LANES, per * LANES), 0)
        == (iota((LANES, per * LANES), 1) // LANES) * WIN + iota((LANES, per * LANES), 1) % WIN
    ).astype(BF16)
    row_head = (iota((chans, LANES), 0) // size) % per
    own_head = row_head == iota((chans, LANES), 1) // WIN
    even_row = row_head % 2 == 0
    for t in range(tiles):
        query = qkv_s[:chans, tile(t)].astype(F32) * size**-0.5
        q_s[t, :, :LANES] = jnp.where(even_row, query, 0.0).astype(BF16)
        q_s[t, :, LANES:] = jnp.where(even_row, 0.0, query).astype(BF16)
        k_s[t] = dot_t(side, qkv_s[chans : 2 * chans, tile(t)]).astype(BF16)
    half = per * size
    values = jnp.concatenate([qkv_s[2 * chans :, tile(t)] for t in range(tiles)], 0)
    values = dot(values, spread)
    for t in range(tiles):
        for w in range(per):
            wide = values[t * chans : (t + 1) * chans, tile(w)]
            wide = jnp.where(own_head, wide, 0.0).astype(BF16)
            for j in range(HEADS // per):
                v_s[t, j, w * half : (w + 1) * half] = wide[j * half : (j + 1) * half]

    lane_pair = iota((WIN, chans), 1) // (2 * size)
    window = iota((8, LANES), 1) // WIN
    rank = iota((WIN, LANES), 0) + WIN * (iota((WIN, LANES), 1) // WIN)

    def by_window(blocks):
        out = blocks[0]
        for w in range(1, per):
            out = jnp.where(window[None] == w, blocks[w], out)
        return out

    def group(t, _):
        query = q_s[t]
        by_pair = []
        for w in range(per):
            keys = k_s[t, w * WIN : (w + 1) * WIN, :]
            nil = jnp.zeros_like(keys)
            by_pair += [jnp.where(lane_pair == m, keys, nil) for m in range(HEADS // 2)]
        got = dot(jnp.concatenate(by_pair, 0), query)
        even = by_window(got[:, :LANES].reshape(per, -1, 8, LANES))
        odd = by_window(got[:, LANES:].reshape(per, -1, 8, LANES))
        mask = jnp.where(rank + t * LANES < count, 0.0, -1e9).astype(F32)
        mask = mask.reshape(WIN // 8, 8, LANES)
        probs, inverse = [], []
        for h in range(HEADS):
            scores = (even, odd)[h % 2]
            mine = scores[h // 2 * (WIN // 8) : (h // 2 + 1) * (WIN // 8)] + mask
            top = fold8(mine, jnp.maximum)
            weight = jnp.exp(mine - top[None])
            inverse.append(1.0 / fold8(weight, jnp.add))
            probs.append(weight.reshape(WIN, LANES).astype(BF16))
        parts = []
        for j in range(HEADS // per):
            weight = jnp.concatenate(probs[j * per : (j + 1) * per], 0)
            ctx = by_window(dot(v_s[t, j], weight).reshape(per, -1, 8, LANES))
            for h in range(per):
                block = ctx[h * (size // 8) : (h + 1) * (size // 8)] * inverse[j * per + h][None]
                parts.append(block.reshape(size, LANES))
        ctx_s[t] = jnp.concatenate(parts, 0).astype(BF16)
        return 0

    lax.fori_loop(0, tiles, group, 0, unroll=2)
    ctx = jnp.concatenate([ctx_s[t] for t in range(tiles)], 1)
    moved = dot(out_t, ctx)
    for t in range(tiles):
        at = tile(t)
        first = (nodes_ref[:, at].astype(F32) + moved[:, at]).astype(BF16)
        first_s[:, at] = first
        normed = norm_t(first.astype(F32), cols[:, 4:5])
        kept = iota((1, LANES), 1) + t * LANES < count
        head = jnp.where((iota((16, LANES), 0) > 0) | kept, normed[:16], FLAG)
        n_s[t * chans : (t + 1) * chans] = jnp.concatenate([head, normed[16:]], 0).astype(BF16)
    keep_first = pltpu.make_async_copy(first_s, first_hbm, stores.at[0])
    keep_first.start()
    moved = dot(n_s[...], within(run))
    moved = swap_blocks([moved[t * chans : (t + 1) * chans] for t in range(tiles)])
    for t in range(tiles):
        sent_s[:, tile(t)] = moved[t].astype(BF16)
    send = pltpu.make_async_copy(sent_s, sent_hbm, stores.at[1])
    send.start()
    wait_all([keep_first, send])


def tables_kernel(
    cap, qkv_hbm, out_hbm, up_hbm, slot_hbm, owner_hbm, voxel_hbm, weights_hbm, facts_hbm,
    qkv_ref, out_ref, up_ref, slot_ref, owner_ref, voxel_ref, sems, weights_s, facts_s, stores
):
    loads = start_all(
        [
            (qkv_hbm, qkv_ref),
            (out_hbm, out_ref),
            (up_hbm, up_ref),
            (slot_hbm, slot_ref),
            (owner_hbm, owner_ref),
            (voxel_hbm, voxel_ref),
        ],
        sems,
    )
    wait_all(loads)
    votes = slot_ref.shape[1]
    codes = facts_s.shape[1]
    owners = codes // cap
    chans = out_ref.shape[0]
    src = head_order(chans)
    src = jnp.concatenate([src, src + chans, src + 2 * chans], 0)
    shuffle = (src == iota((3 * chans, 3 * chans), 1)).astype(BF16)
    weights_s[: 3 * chans] = dot_t(shuffle, qkv_ref[...]).astype(BF16)
    out_t = dot(shuffle[:chans, :chans], out_ref[...])
    weights_s[3 * chans : 4 * chans] = transposed(out_t)
    weights_s[4 * chans :] = transposed(up_ref[...])
    keep_weights = pltpu.make_async_copy(weights_s, weights_hbm, stores.at[0])
    keep_weights.start()
    owner = jnp.bitwise_xor(owner_ref[...], lax.axis_index("tile"))
    hot = owner == iota((owners, votes), 0)
    upto = (iota((votes, votes), 0) <= iota((votes, votes), 1)).astype(BF16)
    rank = jnp.sum(jnp.where(hot, dot(hot.astype(BF16), upto), 0.0), 0, keepdims=True)
    code = owner * cap + rank.astype(jnp.int32) - 1
    member = place(code % LANES, code // LANES, codes // LANES)
    slot = slot_ref[...]
    row = iota((16, votes), 0)
    facts = jnp.where(
        row == 0,
        voxel_ref[...],
        jnp.where(row == 1, slot // LANES, jnp.where(row == 2, slot % LANES, 1)),
    )
    listed = dot_t(facts.astype(F32).astype(BF16), member)
    facts_s[...] = jnp.where(listed[3:4] > 0.5, listed, -1.0).astype(BF16)
    keep_facts = pltpu.make_async_copy(facts_s, facts_hbm, stores.at[1])
    keep_facts.start()
    wait_all([keep_weights, keep_facts])


def clean(block):
    head = block[:16].astype(F32)
    gone = head[0:1] > 0.5 * FLAG
    head = jnp.where((iota(head.shape, 0) == 0) & gone, 0.0, head)
    return jnp.concatenate([head.astype(BF16), block[16:]], 0), gone


def add_keys(blocks, kv_t, k_s, v_s, m_s):
    chans = kv_t.shape[1]
    tiles = k_s.shape[1]
    for n, block in enumerate(blocks):
        block, gone = clean(block)
        kv = dot(kv_t, block)
        mask = jnp.where(gone, -1e9, 0.0)
        for t in range(tiles):
            k_s[n, t] = kv[:chans, tile(t)].reshape(chans // 8, 8, LANES)
            v_s[n, t] = kv[chans:, tile(t)].reshape(chans // 8, 8, LANES)
            m_s[n, t] = jnp.broadcast_to(mask[:, tile(t)], (8, LANES))


def attend_two(t, run, q_s, k_s, v_s, m_s, s_s, ends_s, acc_s, fresh):
    rows8 = q_s.shape[1]
    cut = 2 * rows8 // 3
    keys = k_s.shape[0] * run
    base = (t // run) * run
    both = range(2)
    query = [[q_s[t + n, i] for i in range(rows8)] for n in both]

    def score(key, top):
        block, at = key // run, base + key % run
        mask = m_s[block, at]
        sums = [[None, None], [None, None]]
        for i in range(rows8):
            part = int(i >= cut)
            row = k_s[block, at, i]
            for n in both:
                term = query[n][i] * row
                held = sums[n][part]
                sums[n][part] = term if held is None else held + term
        tops = []
        for n in both:
            a, b = sums[n]
            b = b + pltpu.roll(b, 4, 0)
            a = a + mask
            b = b + mask
            s_s[key, 2 * n] = a
            s_s[key, 2 * n + 1] = b
            tops += [jnp.maximum(top[2 * n], a), jnp.maximum(top[2 * n + 1], b)]
        return tuple(tops)

    if fresh:
        old = tuple(jnp.full((8, LANES), -3e38, F32) for _ in range(4))
    else:
        old = tuple(ends_s[t + n, part] for n in both for part in both)
    tops = lax.fori_loop(0, keys, score, old, unroll=2)
    if fresh:
        zero = jnp.zeros((8, LANES), F32)
        sums = tuple(zero for _ in range(4))
        accs = tuple(zero for _ in range(2 * rows8))
    else:
        fade = [jnp.exp2(old[n] - tops[n]) for n in range(4)]
        sums = tuple(ends_s[t + n, 2 + part] * fade[2 * n + part] for n in both for part in both)
        accs = tuple(
            acc_s[t + n, i] * fade[2 * n + int(i >= cut)] for n in both for i in range(rows8)
        )

    def gather(key, carry):
        sums, accs = carry
        block, at = key // run, base + key % run
        weight = [jnp.exp2(s_s[key, n] - tops[n]) for n in range(4)]
        accs = list(accs)
        for i in range(rows8):
            row = v_s[block, at, i]
            for n in both:
                at_acc = n * rows8 + i
                accs[at_acc] = accs[at_acc] + weight[2 * n + int(i >= cut)] * row
        return tuple(sums[n] + weight[n] for n in range(4)), tuple(accs)

    sums, accs = lax.fori_loop(0, keys, gather, (sums, accs), unroll=2)
    return tops, sums, accs


def hold_two(t, state, ends_s, acc_s):
    tops, sums, accs = state
    rows8 = acc_s.shape[1]
    for n in range(2):
        for part in range(2):
            ends_s[t + n, part] = tops[2 * n + part]
            ends_s[t + n, 2 + part] = sums[2 * n + part]
        for i in range(rows8):
            acc_s[t + n, i] = accs[n * rows8 + i]


def near_kernel(
    run, own_hbm, near_hbm, weights_hbm, q_hbm, ends_hbm, acc_hbm,
    own_ref, near_ref, qkv_t_ref, sems, q_s, ends_s, acc_s, stores, k_s, v_s, m_s, s_s
):
    chans, slots = own_ref.shape
    loads = start_all(
        [
            (own_hbm, own_ref),
            (weights_hbm.at[pl.ds(0, 3 * chans)], qkv_t_ref),
            (near_hbm, near_ref),
        ],
        sems,
    )
    tiles = slots // LANES
    scale = (chans // HEADS) ** -0.5 * LOG2E
    wait_all(loads[:2])
    own, _ = clean(own_ref[...])
    query = dot(qkv_t_ref[:chans, :], own) * scale
    for t in range(tiles):
        q_s[t] = query[:, tile(t)].reshape(chans // 8, 8, LANES)
    keep_q = pltpu.make_async_copy(q_s, q_hbm, stores.at[0])
    keep_q.start()
    wait_all(loads[2:])
    add_keys([own_ref[...], near_ref[...]], qkv_t_ref[chans:, :], k_s, v_s, m_s)

    def step(n, _):
        t = 2 * n
        state = attend_two(t, run, q_s, k_s, v_s, m_s, s_s, ends_s, acc_s, True)
        hold_two(t, state, ends_s, acc_s)
        return 0

    lax.fori_loop(0, tiles // 2, step, 0)
    keep_ends = pltpu.make_async_copy(ends_s, ends_hbm, stores.at[1])
    keep_acc = pltpu.make_async_copy(acc_s, acc_hbm, stores.at[2])
    keep_ends.start()
    keep_acc.start()
    wait_all([keep_q, keep_ends, keep_acc])


def middle_kernel(run, count, *refs):
    blocks, refs = refs[:count], refs[count:]
    q_hbm, ends_hbm, acc_hbm, weights_hbm, ends_out, acc_out = refs[:6]
    block_s, sems, q_s, ends_s, acc_s, kv_t_ref, rest, stores, k_s, v_s, m_s, s_s = refs[6:]
    chans = kv_t_ref.shape[1]
    loads = start_all([(blocks[n], block_s.at[n]) for n in range(count)], sems)
    later = start_all(
        [
            (weights_hbm.at[pl.ds(chans, 2 * chans)], kv_t_ref),
            (q_hbm, q_s),
            (ends_hbm, ends_s),
            (acc_hbm, acc_s),
        ],
        rest,
    )
    wait_all(loads + later[:1])
    add_keys([block_s[n] for n in range(count)], kv_t_ref[...], k_s, v_s, m_s)
    wait_all(later[1:])

    def step(n, _):
        t = 2 * n
        state = attend_two(t, run, q_s, k_s, v_s, m_s, s_s, ends_s, acc_s, False)
        hold_two(t, state, ends_s, acc_s)
        return 0

    lax.fori_loop(0, q_s.shape[0] // 2, step, 0)
    wait_all(start_all([(ends_s, ends_out), (acc_s, acc_out)], stores))


def second_kernel(run, cap, far, owners, count_ref, *refs):
    blocks, refs = refs[:far], refs[far:]
    (
        q_hbm, ends_hbm, acc_hbm, weights_hbm, first_hbm, gain_hbm, down_hbm, facts_hbm, feat_hbm
    ) = refs[:9]
    votes_hbm, refs = refs[9 : 9 + owners], refs[9 + owners :]
    (
        block_s, sems, weights_s, q_s, ends_s, acc_s, first_s, gain_s, down_s, facts_s, rest,
        feat_s, votes_s, stores, k_s, v_s, m_s, s_s, bf_s, inner_s
    ) = refs
    loads = start_all([(blocks[n], block_s.at[n]) for n in range(far)], sems)
    later = start_all(
        [
            (weights_hbm, weights_s),
            (q_hbm, q_s),
            (ends_hbm, ends_s),
            (acc_hbm, acc_s),
            (first_hbm, first_s),
            (gain_hbm, gain_s),
            (down_hbm, down_s),
            (facts_hbm, facts_s),
        ],
        rest,
    )
    chans, slots = first_s.shape
    tiles = slots // LANES
    count = count_ref[0]
    wait_all(loads + later[:1])
    add_keys([block_s[n] for n in range(far)], weights_s[chans : 3 * chans], k_s, v_s, m_s)
    wait_all(later[1:])

    rows8 = chans // 8

    def step(n, _):
        t = 2 * n
        _, sums, accs = attend_two(t, run, q_s, k_s, v_s, m_s, s_s, ends_s, acc_s, False)
        share = [1.0 / total for total in sums]
        cut = 2 * rows8 // 3
        for n in range(2):
            for i in range(rows8):
                acc_s[t + n, i] = accs[n * rows8 + i] * share[2 * n + int(i >= cut)]
        return 0

    lax.fori_loop(0, tiles // 2, step, 0)
    ctx = swap_blocks([acc_s[t].reshape(chans, LANES) for t in range(tiles)])
    ctx = dot_t(jnp.concatenate(ctx, 0).astype(BF16), within(run)).astype(BF16)
    ctx = jnp.concatenate([ctx[t * chans : (t + 1) * chans] for t in range(tiles)], 1)
    gain = jnp.concatenate([gain_s[...], jnp.zeros((7, chans), F32)], 0).T[:, 0:1]
    moved = dot(weights_s[3 * chans : 4 * chans], ctx)
    for t in range(tiles):
        at = tile(t)
        second = first_s[:, at].astype(F32) + moved[:, at]
        feat_s[:, at] = second
        inner_s[:, at] = norm_t(second, gain).astype(BF16)
    kept = iota((1, slots), 1) < count
    wide = 2 * LANES
    cuts = [slice(at, at + wide) for at in range(0, slots, wide)]
    up_t = weights_s[4 * chans :]
    raised = dot(up_t, inner_s[:, cuts[0]])
    for n, at in enumerate(cuts):
        now = raised
        if n + 1 < len(cuts):
            raised = dot(up_t, inner_s[:, cuts[n + 1]])
        hidden = jax.nn.gelu(now).astype(BF16)
        third = feat_s[:, at] + dot(down_s[...], hidden)
        third = jnp.where(kept[:, at], third, 0.0)
        feat_s[:, at] = third
        bf_s[:, at] = third.astype(BF16)
    keep = [pltpu.make_async_copy(feat_s, feat_hbm, stores.at[owners])]
    keep[0].start()
    facts = facts_s[...].astype(F32)
    low, high = facts[2:3].astype(jnp.int32), facts[1:2].astype(jnp.int32)
    picked = dot(bf_s[...], place(low, high, tiles)).astype(BF16)
    for o in range(owners):
        votes_s[o, :chans, :] = picked[:, o * cap : (o + 1) * cap]
        votes_s[o, chans:, :] = facts_s[:, o * cap : (o + 1) * cap]
        keep.append(pltpu.make_async_copy(votes_s.at[o], votes_hbm[o], stores.at[o]))
        keep[-1].start()
    wait_all(keep)


def sums_kernel(owners, *refs):
    got, out_ref, got_s, sems = refs[:owners], refs[owners], refs[owners + 1], refs[owners + 2]
    loads = start_all([(got[n], got_s.at[n]) for n in range(owners)], sems)
    chans, voxels = out_ref.shape
    cap = got_s.shape[2]
    total = jnp.zeros(out_ref.shape, F32)
    wait_all(loads)
    for n in range(owners):
        label = got_s[n, chans:, :].astype(F32)[0:1]
        hot = (label == iota((voxels, cap), 0).astype(F32)).astype(BF16)
        total = total + dot_t(got_s[n, :chans, :], hot)
    out_ref[...] = total


def call(kernel, outs, scratch, flops, spaces, out_space=pl.ANY):
    return pl.pallas_call(
        kernel,
        out_shape=outs,
        in_specs=[
            pl.BlockSpec(memory_space={"s": pltpu.SMEM, "v": pltpu.VMEM, "a": pl.ANY}[c])
            for c in spaces
        ],
        out_specs=[pl.BlockSpec(memory_space=out_space)] * len(outs),
        scratch_shapes=scratch,
        compiler_params=pltpu.CompilerParams(vmem_limit_bytes=VMEM),
        cost_estimate=pl.CostEstimate(flops=flops, bytes_accessed=2 << 20, transcendentals=0),
    )


def turned(x, axis, bit):
    n = lax.axis_size(axis)
    return lax.ppermute(x, axis, [(i, i ^ bit) for i in range(n)])


def body(
    nodes,
    node_ids,
    node_count,
    pos_weight,
    gain_one,
    qkv_one,
    out_one,
    gain_two,
    qkv_two,
    out_two,
    gain_three,
    w_up,
    w_down,
    vote_slot,
    vote_owner,
    vote_voxel,
):
    slots, chans = nodes.shape
    groups, owners = lax.axis_size("grp"), lax.axis_size("tile")
    run = WIN // groups
    votes = vote_slot.shape[0]
    cap = 2 * votes // owners
    codes = owners * cap
    tiles = slots // LANES
    rows8 = chans // 8
    hidden = w_up.shape[1]
    per = LANES // WIN
    sds = jax.ShapeDtypeStruct
    vmem = pltpu.VMEM
    dma = pltpu.SemaphoreType.DMA

    first, sent = call(
        functools.partial(first_kernel, run),
        [sds((chans, slots), BF16), sds((chans, slots), BF16)],
        [
            vmem((chans, slots), BF16),
            vmem((1, slots), jnp.int32),
            vmem((3, chans), F32),
            vmem((1, chans), F32),
            vmem((1, chans), F32),
            vmem((chans, 3 * chans), BF16),
            vmem((chans, chans), BF16),
            dma((7,)),
            vmem((3 * chans, slots), BF16),
            vmem((tiles, chans, 2 * LANES), BF16),
            vmem((tiles, LANES, chans), BF16),
            vmem((tiles, HEADS // per, per * per * (chans // HEADS), LANES), BF16),
            vmem((tiles, chans, LANES), BF16),
            vmem((chans, slots), BF16),
            vmem((tiles * chans, LANES), BF16),
            vmem((chans, slots), BF16),
            vmem((chans, slots), BF16),
            dma((2,)),
        ],
        2_000_000_000,
        "saaaaaaa",
    )(
        node_count,
        nodes.T,
        node_ids.reshape(1, slots),
        pos_weight,
        gain_one.reshape(1, chans),
        gain_two.reshape(1, chans),
        qkv_one,
        out_one,
    )
    near = turned(sent, "grp", 1)
    bit = groups // 2
    mid = []
    while bit > 1:
        mid += [turned(block, "grp", bit) for block in [sent] + mid]
        bit //= 2
    weights, facts = call(
        functools.partial(tables_kernel, cap),
        [sds((4 * chans + hidden, chans), BF16), sds((16, codes), BF16)],
        [
            vmem((chans, 3 * chans), BF16),
            vmem((chans, chans), BF16),
            vmem((chans, hidden), BF16),
            vmem((1, votes), jnp.int32),
            vmem((1, votes), jnp.int32),
            vmem((1, votes), jnp.int32),
            dma((6,)),
            vmem((4 * chans + hidden, chans), BF16),
            vmem((16, codes), BF16),
            dma((2,)),
        ],
        2_000_000_000,
        "aaaaaa",
    )(
        qkv_two,
        out_two,
        w_up,
        vote_slot.reshape(1, votes),
        vote_owner.reshape(1, votes),
        vote_voxel.reshape(1, votes),
    )
    q_like = ((tiles, rows8, 8, LANES), F32)
    ends_like = ((tiles, 4, 8, LANES), F32)
    acc_like = ((tiles, rows8, 8, LANES), F32)

    def key_scratch(blocks):
        return [
            vmem((blocks, tiles, rows8, 8, LANES), F32),
            vmem((blocks, tiles, rows8, 8, LANES), F32),
            vmem((blocks, tiles, 8, LANES), F32),
            vmem((blocks * run, 4, 8, LANES), F32),
        ]

    query, ends, acc = call(
        functools.partial(near_kernel, run),
        [sds(*q_like), sds(*ends_like), sds(*acc_like)],
        [
            vmem((chans, slots), BF16),
            vmem((chans, slots), BF16),
            vmem((3 * chans, chans), BF16),
            dma((3,)),
            vmem(*q_like),
            vmem(*ends_like),
            vmem(*acc_like),
            dma((3,)),
        ]
        + key_scratch(2),
        3_000_000_000,
        "aaa",
    )(sent, near, weights)
    mid, query = lax.optimization_barrier((mid, query))
    far = [turned(block, "grp", 1) for block in mid]
    ends, acc = call(
        functools.partial(middle_kernel, run, len(mid)),
        [sds(*ends_like), sds(*acc_like)],
        [
            vmem((len(mid), chans, slots), BF16),
            dma((len(mid),)),
            vmem(*q_like),
            vmem(*ends_like),
            vmem(*acc_like),
            vmem((2 * chans, chans), BF16),
            dma((4,)),
            dma((2,)),
        ]
        + key_scratch(len(mid)),
        2_000_000_000,
        "a" * len(mid) + "aaaa",
    )(*mid, query, ends, acc, weights)
    features_t, *ballots = call(
        functools.partial(second_kernel, run, cap, len(far), owners),
        [sds((chans, slots), F32)] + [sds((chans + 16, cap), BF16)] * owners,
        [
            vmem((len(far), chans, slots), BF16),
            dma((len(far),)),
            vmem((4 * chans + hidden, chans), BF16),
            vmem(*q_like),
            vmem(*ends_like),
            vmem(*acc_like),
            vmem((chans, slots), BF16),
            vmem((1, chans), F32),
            vmem((chans, hidden), BF16),
            vmem((16, codes), BF16),
            dma((8,)),
            vmem((chans, slots), F32),
            vmem((owners, chans + 16, cap), BF16),
            dma((owners + 1,)),
        ]
        + key_scratch(len(far))
        + [
            vmem((chans, slots), BF16),
            vmem((chans, slots), BF16),
        ],
        3_000_000_000,
        "s" + "a" * (len(far) + 8),
    )(
        node_count,
        *far,
        query,
        ends,
        acc,
        weights,
        first,
        gain_three.reshape(1, chans),
        w_down.T,
        facts,
    )
    got = [ballots[0]] + [turned(ballots[k], "tile", k) for k in range(owners - 1, 0, -1)]
    (sums_t,) = call(
        functools.partial(sums_kernel, owners),
        [sds((chans, VOX_DEV), F32)],
        [vmem((owners, chans + 16, cap), BF16), dma((owners,))],
        200_000_000,
        "a" * owners,
        pltpu.VMEM,
    )(*got)
    return (features_t.T, sums_t.T)


def solution(mesh):
    in_specs = (
        P(("grp", "tile"), None),
        P(("grp", "tile")),
        P(("grp", "tile")),
        P(),
        P(),
        P(),
        P(),
        P(),
        P(),
        P(),
        P(),
        P(),
        P(),
        P(("grp", "tile")),
        P(("grp", "tile"), None),
        P(("grp", "tile")),
    )
    out_specs = (P(("grp", "tile"), None), P(("grp", "tile"), None))
    return jax.shard_map(body, mesh=mesh, in_specs=in_specs, out_specs=out_specs, check_vma=False)
```

```python
import functools
import math

import jax
import jax.numpy as jnp
from jax import lax
from jax.experimental import pallas as pl
from jax.experimental.pallas import tpu as pltpu
from jax.sharding import PartitionSpec as P

HEADS = 12
WIN = 32
VOX_DEV = 256
LANES = 128
FLAG = 16384.0
VMEM = 64 * 1024 * 1024 - 65536
ROOMY = 24 * 1024 * 1024
F32 = jnp.float32
BF16 = jnp.bfloat16
LOG2E = math.log2(math.e)


def iota(shape, dim):
    return lax.broadcasted_iota(jnp.int32, shape, dim)


def dot(a, b):
    return jnp.dot(a, b, preferred_element_type=F32)


def dot_t(a, b):
    return lax.dot_general(a, b, (((1,), (1,)), ((), ())), preferred_element_type=F32)


def eye(n):
    return (iota((n, n), 0) == iota((n, n), 1)).astype(BF16)


def transposed(a):
    return a.astype(F32).T.astype(BF16)


def tile(t):
    return slice(t * LANES, (t + 1) * LANES)


def head_order(chans):
    size = chans // HEADS
    cut = 8 * size
    j = iota((chans, 1), 0)
    high = j - cut
    low_src = (j % 8) * size + j // 8
    high_src = (8 + high % 4) * size + high // 8 + (size // 2) * ((high % 8) // 4)
    return jnp.where(j < cut, low_src, high_src)


def within(run):
    lane = iota((1, LANES), 1)
    q, e = lane // 16, lane % 16
    p = (4 * (q // run) + e // 4) * run + q % run
    return ((e % 4) * WIN + p == iota((LANES, LANES), 0)).astype(BF16)


def swap_blocks(tiles):
    tiles = list(tiles)
    block = iota(tiles[0].shape, 1) // 16
    step = len(tiles) // 2
    while step:
        for n in range(len(tiles)):
            if n & step:
                continue
            a, b = tiles[n], tiles[n + step]
            low = block // step % 2 == 0
            tiles[n] = jnp.where(low, a, pltpu.roll(b, 16 * step, 1))
            tiles[n + step] = jnp.where(low, pltpu.roll(a, LANES - 16 * step, 1), b)
        step //= 2
    return tiles


def place(low, high, blocks):
    base = jnp.where(low == iota((LANES, low.shape[1]), 0), 1.0, 0.0).astype(BF16)
    high = jnp.broadcast_to(high, base.shape).astype(F32).astype(BF16)
    nil = jnp.zeros_like(base)
    parts = [jnp.where(high == jnp.asarray(n, BF16), base, nil) for n in range(blocks)]
    return jnp.concatenate(parts, 0)


def norm_t(x, gain):
    inv = 1.0 / x.shape[0]
    mean = jnp.sum(x, 0, keepdims=True) * inv
    cent = x - mean
    var = jnp.sum(cent * cent, 0, keepdims=True) * inv
    return cent * lax.rsqrt(var + 1e-05) * gain


def gelu(x):
    half = 0.5 * x
    scale = math.sqrt(2 / math.pi)
    return half + half * jnp.tanh(x * (scale + (0.044715 * scale) * (x * x)))


def start_all(pairs, sems):
    copies = [pltpu.make_async_copy(a, b, sems.at[n]) for n, (a, b) in enumerate(pairs)]
    for copy in copies:
        copy.start()
    return copies


def wait_all(copies):
    for copy in copies:
        copy.wait()


def fold8(x, op):
    y = x[0]
    for n in range(1, x.shape[0]):
        y = op(y, x[n])
    for shift in (4, 2, 1):
        y = op(y, pltpu.roll(y, shift, 0))
    return y


def first_kernel(
    run, count_ref, nodes_hbm, ids_hbm, pos_hbm, gain_one_hbm, gain_two_hbm, qkv_hbm, out_hbm,
    first_hbm, sent_hbm, nodes_ref, ids_ref, pos_ref, gain_one_ref, gain_two_ref, qkv_ref, out_ref,
    sems, qkv_s, q_s, k_s, v_s, ctx_s, n_s, first_s, sent_s, stores
):
    loads = start_all(
        [
            (nodes_hbm, nodes_ref),
            (ids_hbm, ids_ref),
            (pos_hbm, pos_ref),
            (gain_one_hbm, gain_one_ref),
            (gain_two_hbm, gain_two_ref),
            (qkv_hbm, qkv_ref),
            (out_hbm, out_ref),
        ],
        sems,
    )
    chans, slots = nodes_ref.shape
    tiles = slots // LANES
    size = chans // HEADS
    per = LANES // WIN
    count = count_ref[0]
    wait_all(loads[:5])
    cols = jnp.concatenate(
        [pos_ref[...], gain_one_ref[...], gain_two_ref[...], jnp.zeros((3, chans), F32)], 0
    ).T
    ids = ids_ref[...]
    coords = []
    for axis in range(3):
        total = jnp.zeros(ids.shape, jnp.int32)
        for level in range(6):
            bit = jnp.bitwise_and(jnp.right_shift(ids, 3 * level + axis), 1)
            total = total + bit * 2**level
        coords.append(total.astype(F32) / 64.0 - 0.5)
    for t in range(tiles):
        at = tile(t)
        start = cols[:, 0:1] * coords[0][:, at]
        for axis in range(1, 3):
            start = start + cols[:, axis : axis + 1] * coords[axis][:, at]
        start = (nodes_ref[:, at].astype(F32) + start).astype(BF16)
        nodes_ref[:, at] = start
        n_s[:, at] = norm_t(start.astype(F32), cols[:, 3:4]).astype(BF16)
    wait_all(loads[5:])
    qkv_t = transposed(qkv_ref[...])
    out_t = transposed(out_ref[...])
    qkv_s[...] = dot(qkv_t, n_s[...]).astype(BF16)
    side = eye(LANES)
    spread = (
        iota((LANES, per * LANES), 0)
        == (iota((LANES, per * LANES), 1) // LANES) * WIN + iota((LANES, per * LANES), 1) % WIN
    ).astype(BF16)
    row_head = (iota((chans, LANES), 0) // size) % per
    own_head = row_head == iota((chans, LANES), 1) // WIN
    even_row = row_head % 2 == 0
    for t in range(tiles):
        query = qkv_s[:chans, tile(t)].astype(F32) * size**-0.5
        q_s[t, :, :LANES] = jnp.where(even_row, query, 0.0).astype(BF16)
        q_s[t, :, LANES:] = jnp.where(even_row, 0.0, query).astype(BF16)
        k_s[t] = dot_t(side, qkv_s[chans : 2 * chans, tile(t)]).astype(BF16)
    for t in range(tiles):
        wide = dot(qkv_s[2 * chans :, tile(t)], spread)
        for w in range(per):
            v_s[t, w] = jnp.where(own_head, wide[:, tile(w)], 0.0).astype(BF16)

    lane_pair = iota((WIN, chans), 1) // (2 * size)
    window = iota((8, LANES), 1) // WIN
    rank = iota((WIN, LANES), 0) + WIN * (iota((WIN, LANES), 1) // WIN)

    def group(t, _):
        query = q_s[t]
        even, odd = None, None
        for w in range(per):
            keys = k_s[t, w * WIN : (w + 1) * WIN, :]
            by_pair = jnp.concatenate(
                [jnp.where(lane_pair == m, keys, jnp.zeros_like(keys)) for m in range(HEADS // 2)],
                0,
            )
            got = dot(by_pair, query)
            left = got[:, :LANES].reshape(-1, 8, LANES)
            right = got[:, LANES:].reshape(-1, 8, LANES)
            even = left if w == 0 else jnp.where(window[None] == w, left, even)
            odd = right if w == 0 else jnp.where(window[None] == w, right, odd)
        mask = jnp.where(rank + t * LANES < count, 0.0, -1e9).astype(F32)
        mask = mask.reshape(WIN // 8, 8, LANES)
        probs, inverse = [], []
        for h in range(HEADS):
            scores = (even, odd)[h % 2]
            mine = scores[h // 2 * (WIN // 8) : (h // 2 + 1) * (WIN // 8)] + mask
            top = fold8(mine, jnp.maximum)
            weight = jnp.exp(mine - top[None])
            inverse.append(1.0 / fold8(weight, jnp.add))
            probs.append(weight.reshape(WIN, LANES).astype(BF16))
        half = per * size
        parts = []
        for j in range(HEADS // per):
            weight = jnp.concatenate(probs[j * per : (j + 1) * per], 0)
            ctx = None
            for w in range(per):
                got = dot(v_s[t, w, j * half : (j + 1) * half, :], weight).reshape(-1, 8, LANES)
                ctx = got if w == 0 else jnp.where(window[None] == w, got, ctx)
            for h in range(per):
                block = ctx[h * (size // 8) : (h + 1) * (size // 8)] * inverse[j * per + h][None]
                parts.append(block.reshape(size, LANES))
        ctx_s[t] = jnp.concatenate(parts, 0).astype(BF16)
        return 0

    lax.fori_loop(0, tiles, group, 0, unroll=4)
    ctx = jnp.concatenate([ctx_s[t] for t in range(tiles)], 1)
    moved = dot(out_t, ctx)
    for t in range(tiles):
        at = tile(t)
        first = (nodes_ref[:, at].astype(F32) + moved[:, at]).astype(BF16)
        first_s[:, at] = first
        normed = norm_t(first.astype(F32), cols[:, 4:5])
        kept = iota((1, LANES), 1) + t * LANES < count
        head = jnp.where((iota((16, LANES), 0) > 0) | kept, normed[:16], FLAG)
        n_s[:, at] = jnp.concatenate([head, normed[16:]], 0).astype(BF16)
    keep_first = pltpu.make_async_copy(first_s, first_hbm, stores.at[0])
    keep_first.start()
    inside = within(run)
    for t, block in enumerate(swap_blocks([dot(n_s[:, tile(t)], inside) for t in range(tiles)])):
        sent_s[:, tile(t)] = block.astype(BF16)
    send = pltpu.make_async_copy(sent_s, sent_hbm, stores.at[1])
    send.start()
    wait_all([keep_first, send])


def tables_kernel(
    cap, qkv_hbm, out_hbm, up_hbm, slot_hbm, owner_hbm, voxel_hbm, weights_hbm, facts_hbm,
    qkv_ref, out_ref, up_ref, slot_ref, owner_ref, voxel_ref, sems, weights_s, facts_s, stores
):
    loads = start_all(
        [
            (qkv_hbm, qkv_ref),
            (out_hbm, out_ref),
            (up_hbm, up_ref),
            (slot_hbm, slot_ref),
            (owner_hbm, owner_ref),
            (voxel_hbm, voxel_ref),
        ],
        sems,
    )
    wait_all(loads)
    votes = slot_ref.shape[1]
    codes = facts_s.shape[1]
    owners = codes // cap
    chans = out_ref.shape[0]
    src = head_order(chans)
    src = jnp.concatenate([src, src + chans, src + 2 * chans], 0)
    shuffle = (src == iota((3 * chans, 3 * chans), 1)).astype(BF16)
    weights_s[: 3 * chans] = dot_t(shuffle, qkv_ref[...]).astype(BF16)
    out_t = dot(shuffle[:chans, :chans], out_ref[...])
    weights_s[3 * chans : 4 * chans] = transposed(out_t)
    weights_s[4 * chans :] = transposed(up_ref[...])
    keep_weights = pltpu.make_async_copy(weights_s, weights_hbm, stores.at[0])
    keep_weights.start()
    owner = jnp.bitwise_xor(owner_ref[...], lax.axis_index("tile"))
    hot = owner == iota((owners, votes), 0)
    upto = (iota((votes, votes), 0) <= iota((votes, votes), 1)).astype(BF16)
    rank = jnp.sum(jnp.where(hot, dot(hot.astype(BF16), upto), 0.0), 0, keepdims=True)
    code = owner * cap + rank.astype(jnp.int32) - 1
    member = place(code % LANES, code // LANES, codes // LANES)
    slot = slot_ref[...]
    row = iota((16, votes), 0)
    facts = jnp.where(
        row == 0,
        voxel_ref[...],
        jnp.where(row == 1, slot // LANES, jnp.where(row == 2, slot % LANES, 1)),
    )
    listed = dot_t(facts.astype(F32).astype(BF16), member)
    facts_s[...] = jnp.where(listed[3:4] > 0.5, listed, -1.0).astype(BF16)
    keep_facts = pltpu.make_async_copy(facts_s, facts_hbm, stores.at[1])
    keep_facts.start()
    wait_all([keep_weights, keep_facts])


def clean(block):
    head = block[:16].astype(F32)
    gone = head[0:1] > 0.5 * FLAG
    head = jnp.where((iota(head.shape, 0) == 0) & gone, 0.0, head)
    return jnp.concatenate([head.astype(BF16), block[16:]], 0), gone


def add_keys(blocks, kv_t, k_s, v_s, m_s):
    chans = kv_t.shape[1]
    tiles = k_s.shape[1]
    for n, block in enumerate(blocks):
        block, gone = clean(block)
        kv = dot(kv_t, block)
        mask = jnp.where(gone, -1e9, 0.0)
        for t in range(tiles):
            k_s[n, t] = kv[:chans, tile(t)].reshape(chans // 8, 8, LANES)
            v_s[n, t] = kv[chans:, tile(t)].reshape(chans // 8, 8, LANES)
            m_s[n, t] = jnp.broadcast_to(mask[:, tile(t)], (8, LANES))


def attend_two(t, run, q_s, k_s, v_s, m_s, s_s, state_s, fresh):
    rows8 = q_s.shape[1]
    cut = 2 * rows8 // 3
    keys = k_s.shape[0] * run
    base = (t // run) * run
    both = range(2)
    query = [[q_s[t + n, i] for i in range(rows8)] for n in both]

    def score(key, top):
        block, at = key // run, base + key % run
        mask = m_s[block, at]
        sums = [[None, None], [None, None]]
        for i in range(rows8):
            part = int(i >= cut)
            row = k_s[block, at, i]
            for n in both:
                term = query[n][i] * row
                held = sums[n][part]
                sums[n][part] = term if held is None else held + term
        tops = []
        for n in both:
            a, b = sums[n]
            b = b + pltpu.roll(b, 4, 0)
            a = a + mask
            b = b + mask
            s_s[key, 2 * n] = a
            s_s[key, 2 * n + 1] = b
            tops += [jnp.maximum(top[2 * n], a), jnp.maximum(top[2 * n + 1], b)]
        return tuple(tops)

    if fresh:
        old = tuple(jnp.full((8, LANES), -3e38, F32) for _ in range(4))
    else:
        old = tuple(state_s[t + n, rows8 + part] for n in both for part in both)
    tops = lax.fori_loop(0, keys, score, old, unroll=2)
    if fresh:
        zero = jnp.zeros((8, LANES), F32)
        sums = tuple(zero for _ in range(4))
        accs = tuple(zero for _ in range(2 * rows8))
    else:
        fade = [jnp.exp2(old[n] - tops[n]) for n in range(4)]
        sums = tuple(
            state_s[t + n, rows8 + 2 + part] * fade[2 * n + part] for n in both for part in both
        )
        accs = tuple(
            state_s[t + n, i] * fade[2 * n + int(i >= cut)] for n in both for i in range(rows8)
        )

    def gather(key, carry):
        sums, accs = carry
        block, at = key // run, base + key % run
        weight = [jnp.exp2(s_s[key, n] - tops[n]) for n in range(4)]
        accs = list(accs)
        for i in range(rows8):
            row = v_s[block, at, i]
            for n in both:
                at_acc = n * rows8 + i
                accs[at_acc] = accs[at_acc] + weight[2 * n + int(i >= cut)] * row
        return tuple(sums[n] + weight[n] for n in range(4)), tuple(accs)

    sums, accs = lax.fori_loop(0, keys, gather, (sums, accs), unroll=2)
    return tops, sums, accs


def store_pair(n, state_s, state_hbm, stores):
    pair = pl.ds(2 * n, 2)
    return pltpu.make_async_copy(state_s.at[pair], state_hbm.at[pair], stores.at[n])


def hold_two(n, state, state_s, state_hbm, stores):
    tops, sums, accs = state
    rows8 = len(accs) // 2
    for m in range(2):
        for i in range(rows8):
            state_s[2 * n + m, i] = accs[m * rows8 + i]
        for part in range(2):
            state_s[2 * n + m, rows8 + part] = tops[2 * m + part]
            state_s[2 * n + m, rows8 + 2 + part] = sums[2 * m + part]
    store_pair(n, state_s, state_hbm, stores).start()


def near_kernel(
    run, own_ref, near_ref, weights_hbm, q_hbm, state_hbm,
    qkv_t_ref, sems, q_s, state_s, stores, k_s, v_s, m_s, s_s
):
    chans, slots = own_ref.shape
    loads = start_all([(weights_hbm.at[pl.ds(0, 3 * chans)], qkv_t_ref)], sems)
    tiles = slots // LANES
    scale = (chans // HEADS) ** -0.5 * LOG2E
    wait_all(loads)
    own, _ = clean(own_ref[...])
    query = dot(qkv_t_ref[:chans, :], own) * scale
    for t in range(tiles):
        q_s[t] = query[:, tile(t)].reshape(chans // 8, 8, LANES)
    pairs = tiles // 2
    keep_q = pltpu.make_async_copy(q_s, q_hbm, stores.at[pairs])
    keep_q.start()
    add_keys([own_ref[...], near_ref[...]], qkv_t_ref[chans:, :], k_s, v_s, m_s)

    def step(n, _):
        state = attend_two(2 * n, run, q_s, k_s, v_s, m_s, s_s, state_s, True)
        hold_two(n, state, state_s, state_hbm, stores)
        return 0

    lax.fori_loop(0, pairs, step, 0)
    wait_all([keep_q] + [store_pair(n, state_s, state_hbm, stores) for n in range(pairs)])


def middle_kernel(run, count, *refs):
    blocks, refs = refs[:count], refs[count:]
    q_hbm, state_in, weights_hbm, state_hbm = refs[:4]
    q_s, state_s, kv_t_ref, rest, stores, k_s, v_s, m_s, s_s = refs[4:]
    chans = kv_t_ref.shape[1]
    pairs = q_s.shape[0] // 2
    later = start_all(
        [
            (weights_hbm.at[pl.ds(chans, 2 * chans)], kv_t_ref),
            (q_hbm, q_s),
            (state_in, state_s),
        ],
        rest,
    )
    wait_all(later[:1])
    add_keys([block[...] for block in blocks], kv_t_ref[...], k_s, v_s, m_s)
    wait_all(later[1:])

    def step(n, _):
        state = attend_two(2 * n, run, q_s, k_s, v_s, m_s, s_s, state_s, False)
        hold_two(n, state, state_s, state_hbm, stores)
        return 0

    lax.fori_loop(0, pairs, step, 0)
    wait_all([store_pair(n, state_s, state_hbm, stores) for n in range(pairs)])


def second_kernel(run, cap, far, owners, count_ref, *refs):
    blocks, refs = refs[:far], refs[far:]
    (
        q_hbm, state_hbm, weights_hbm, first_hbm, gain_hbm, down_hbm, facts_hbm, feat_hbm
    ) = refs[:8]
    votes_hbm, refs = refs[8 : 8 + owners], refs[8 + owners :]
    (
        weights_s, q_s, state_s, first_s, gain_s, down_s, facts_s, rest,
        feat_s, votes_s, stores, k_s, v_s, m_s, s_s, bf_s, inner_s
    ) = refs
    later = start_all(
        [
            (weights_hbm, weights_s),
            (q_hbm, q_s),
            (state_hbm, state_s),
            (first_hbm, first_s),
            (gain_hbm, gain_s),
            (down_hbm, down_s),
            (facts_hbm, facts_s),
        ],
        rest,
    )
    chans, slots = first_s.shape
    tiles = slots // LANES
    count = count_ref[0]
    wait_all(later[:1])
    add_keys([block[...] for block in blocks], weights_s[chans : 3 * chans], k_s, v_s, m_s)
    wait_all(later[1:])

    rows8 = chans // 8

    def step(n, _):
        t = 2 * n
        _, sums, accs = attend_two(t, run, q_s, k_s, v_s, m_s, s_s, state_s, False)
        share = [1.0 / total for total in sums]
        cut = 2 * rows8 // 3
        for n in range(2):
            for i in range(rows8):
                state_s[t + n, i] = accs[n * rows8 + i] * share[2 * n + int(i >= cut)]
        return 0

    lax.fori_loop(0, tiles // 2, step, 0)
    ctx = swap_blocks([state_s[t, :rows8].reshape(chans, LANES) for t in range(tiles)])
    ctx = dot_t(jnp.concatenate(ctx, 0).astype(BF16), within(run)).astype(BF16)
    ctx = jnp.concatenate([ctx[t * chans : (t + 1) * chans] for t in range(tiles)], 1)
    gain = jnp.concatenate([gain_s[...], jnp.zeros((7, chans), F32)], 0).T[:, 0:1]
    moved = dot(weights_s[3 * chans : 4 * chans], ctx)
    for t in range(tiles):
        at = tile(t)
        second = first_s[:, at].astype(F32) + moved[:, at]
        feat_s[:, at] = second
        inner_s[:, at] = norm_t(second, gain).astype(BF16)
    kept = iota((1, slots), 1) < count
    wide = 2 * LANES
    cuts = [slice(at, at + wide) for at in range(0, slots, wide)]
    up_t = weights_s[4 * chans :]
    raised = dot(up_t, inner_s[:, cuts[0]])
    for n, at in enumerate(cuts):
        now = raised
        if n + 1 < len(cuts):
            raised = dot(up_t, inner_s[:, cuts[n + 1]])
        hidden = gelu(now).astype(BF16)
        third = feat_s[:, at] + dot(down_s[...], hidden)
        third = jnp.where(kept[:, at], third, 0.0)
        feat_s[:, at] = third
        bf_s[:, at] = third.astype(BF16)
    keep = [pltpu.make_async_copy(feat_s, feat_hbm, stores.at[owners])]
    keep[0].start()
    facts = facts_s[...].astype(F32)
    low, high = facts[2:3].astype(jnp.int32), facts[1:2].astype(jnp.int32)
    picked = dot(bf_s[...], place(low, high, tiles)).astype(BF16)
    for o in range(owners):
        votes_s[o, :chans, :] = picked[:, o * cap : (o + 1) * cap]
        votes_s[o, chans:, :] = facts_s[:, o * cap : (o + 1) * cap]
        keep.append(pltpu.make_async_copy(votes_s.at[o], votes_hbm[o], stores.at[o]))
        keep[-1].start()
    wait_all(keep)


def sums_kernel(own_hbm, *refs):
    got, out_ref, own_ref, sem = refs[:-3], refs[-3], refs[-2], refs[-1]
    load = pltpu.make_async_copy(own_hbm, own_ref, sem)
    load.start()
    chans, voxels = out_ref.shape
    cap = own_ref.shape[1]
    total = jnp.zeros(out_ref.shape, F32)
    for ref in got + (own_ref,):
        if ref is own_ref:
            load.wait()
        label = ref[chans:, :].astype(F32)[0:1]
        hot = (label == iota((voxels, cap), 0).astype(F32)).astype(BF16)
        total = total + dot_t(ref[:chans, :], hot)
    out_ref[...] = total


def call(kernel, outs, scratch, flops, spaces, out_space=pl.ANY, limit=VMEM):
    return pl.pallas_call(
        kernel,
        out_shape=outs,
        in_specs=[
            pl.BlockSpec(memory_space={"s": pltpu.SMEM, "v": pltpu.VMEM, "a": pl.ANY}[c])
            for c in spaces
        ],
        out_specs=[pl.BlockSpec(memory_space=out_space)] * len(outs),
        scratch_shapes=scratch,
        compiler_params=pltpu.CompilerParams(vmem_limit_bytes=limit),
        cost_estimate=pl.CostEstimate(flops=flops, bytes_accessed=2 << 20, transcendentals=0),
    )


def turned(x, axis, bit):
    n = lax.axis_size(axis)
    return lax.ppermute(x, axis, [(i, i ^ bit) for i in range(n)])


def body(
    nodes,
    node_ids,
    node_count,
    pos_weight,
    gain_one,
    qkv_one,
    out_one,
    gain_two,
    qkv_two,
    out_two,
    gain_three,
    w_up,
    w_down,
    vote_slot,
    vote_owner,
    vote_voxel,
):
    slots, chans = nodes.shape
    groups, owners = lax.axis_size("grp"), lax.axis_size("tile")
    run = WIN // groups
    votes = vote_slot.shape[0]
    cap = 2 * votes // owners
    codes = owners * cap
    tiles = slots // LANES
    rows8 = chans // 8
    hidden = w_up.shape[1]
    per = LANES // WIN
    sds = jax.ShapeDtypeStruct
    vmem = pltpu.VMEM
    dma = pltpu.SemaphoreType.DMA

    first, sent = call(
        functools.partial(first_kernel, run),
        [sds((chans, slots), BF16), sds((chans, slots), BF16)],
        [
            vmem((chans, slots), BF16),
            vmem((1, slots), jnp.int32),
            vmem((3, chans), F32),
            vmem((1, chans), F32),
            vmem((1, chans), F32),
            vmem((chans, 3 * chans), BF16),
            vmem((chans, chans), BF16),
            dma((7,)),
            vmem((3 * chans, slots), BF16),
            vmem((tiles, chans, 2 * LANES), BF16),
            vmem((tiles, LANES, chans), BF16),
            vmem((tiles, per, chans, LANES), BF16),
            vmem((tiles, chans, LANES), BF16),
            vmem((chans, slots), BF16),
            vmem((chans, slots), BF16),
            vmem((chans, slots), BF16),
            dma((2,)),
        ],
        2_000_000_000,
        "saaaaaaa",
    )(
        node_count,
        nodes.T,
        node_ids.reshape(1, slots),
        pos_weight,
        gain_one.reshape(1, chans),
        gain_two.reshape(1, chans),
        qkv_one,
        out_one,
    )
    bit = groups // 2
    mid = []
    while bit > 1:
        mid += [turned(block, "grp", bit) for block in [sent] + mid]
        bit //= 2
    near = turned(sent, "grp", 1)
    weights, facts = call(
        functools.partial(tables_kernel, cap),
        [sds((4 * chans + hidden, chans), BF16), sds((16, codes), BF16)],
        [
            vmem((chans, 3 * chans), BF16),
            vmem((chans, chans), BF16),
            vmem((chans, hidden), BF16),
            vmem((1, votes), jnp.int32),
            vmem((1, votes), jnp.int32),
            vmem((1, votes), jnp.int32),
            dma((6,)),
            vmem((4 * chans + hidden, chans), BF16),
            vmem((16, codes), BF16),
            dma((2,)),
        ],
        2_000_000_000,
        "aaaaaa",
        limit=ROOMY,
    )(
        qkv_two,
        out_two,
        w_up,
        vote_slot.reshape(1, votes),
        vote_owner.reshape(1, votes),
        vote_voxel.reshape(1, votes),
    )
    q_like = ((tiles, rows8, 8, LANES), F32)
    state_like = ((tiles, rows8 + 4, 8, LANES), F32)

    def key_scratch(blocks):
        return [
            vmem((blocks, tiles, rows8, 8, LANES), F32),
            vmem((blocks, tiles, rows8, 8, LANES), F32),
            vmem((blocks, tiles, 8, LANES), F32),
            vmem((blocks * run, 4, 8, LANES), F32),
        ]

    query, state = call(
        functools.partial(near_kernel, run),
        [sds(*q_like), sds(*state_like)],
        [
            vmem((3 * chans, chans), BF16),
            dma((1,)),
            vmem(*q_like),
            vmem(*state_like),
            dma((tiles // 2 + 1,)),
        ]
        + key_scratch(2),
        3_000_000_000,
        "vva",
        limit=ROOMY,
    )(sent, near, weights)
    mid, query = lax.optimization_barrier((mid, query))
    far = [turned(block, "grp", 1) for block in mid]
    (state,) = call(
        functools.partial(middle_kernel, run, len(mid)),
        [sds(*state_like)],
        [
            vmem(*q_like),
            vmem(*state_like),
            vmem((2 * chans, chans), BF16),
            dma((3,)),
            dma((tiles // 2,)),
        ]
        + key_scratch(len(mid)),
        2_000_000_000,
        "v" * len(mid) + "aaa",
        limit=ROOMY,
    )(*mid, query, state, weights)
    features_t, *ballots = call(
        functools.partial(second_kernel, run, cap, len(far), owners),
        [sds((chans, slots), F32)] + [sds((chans + 16, cap), BF16)] * owners,
        [
            vmem((4 * chans + hidden, chans), BF16),
            vmem(*q_like),
            vmem(*state_like),
            vmem((chans, slots), BF16),
            vmem((1, chans), F32),
            vmem((chans, hidden), BF16),
            vmem((16, codes), BF16),
            dma((7,)),
            vmem((chans, slots), F32),
            vmem((owners, chans + 16, cap), BF16),
            dma((owners + 1,)),
        ]
        + key_scratch(len(far))
        + [
            vmem((chans, slots), BF16),
            vmem((chans, slots), BF16),
        ],
        3_000_000_000,
        "s" + "v" * len(far) + "a" * 7,
        limit=ROOMY,
    )(
        node_count,
        *far,
        query,
        state,
        weights,
        first,
        gain_three.reshape(1, chans),
        w_down.T,
        facts,
    )
    got = [ballots[0]] + [turned(ballots[k], "tile", k) for k in [1] + list(range(owners - 1, 1, -1))]
    (sums_t,) = call(
        sums_kernel,
        [sds((chans, VOX_DEV), F32)],
        [vmem((chans + 16, cap), BF16), dma],
        200_000_000,
        "a" + "v" * (owners - 1),
        pltpu.VMEM,
        ROOMY,
    )(*got)
    return (features_t.T, sums_t.T)


def solution(mesh):
    in_specs = (
        P(("grp", "tile"), None),
        P(("grp", "tile")),
        P(("grp", "tile")),
        P(),
        P(),
        P(),
        P(),
        P(),
        P(),
        P(),
        P(),
        P(),
        P(),
        P(("grp", "tile")),
        P(("grp", "tile"), None),
        P(("grp", "tile")),
    )
    out_specs = (P(("grp", "tile"), None), P(("grp", "tile"), None))
    return jax.shard_map(body, mesh=mesh, in_specs=in_specs, out_specs=out_specs, check_vma=False)
```

```python
import functools
import math

import jax
import jax.numpy as jnp
from jax import lax
from jax.experimental import pallas as pl
from jax.experimental.pallas import tpu as pltpu
from jax.sharding import PartitionSpec as P

HEADS = 12
WIN = 32
VOX_DEV = 256
LANES = 128
FLAG = 16384.0
VMEM = 64 * 1024 * 1024 - 65536
ROOMY = 24 * 1024 * 1024
F32 = jnp.float32
BF16 = jnp.bfloat16
LOG2E = math.log2(math.e)


def iota(shape, dim):
    return lax.broadcasted_iota(jnp.int32, shape, dim)


def dot(a, b):
    return jnp.dot(a, b, preferred_element_type=F32)


def dot_t(a, b):
    return lax.dot_general(a, b, (((1,), (1,)), ((), ())), preferred_element_type=F32)


def eye(n):
    return (iota((n, n), 0) == iota((n, n), 1)).astype(BF16)


def transposed(a):
    return a.astype(F32).T.astype(BF16)


def tile(t):
    return slice(t * LANES, (t + 1) * LANES)


def head_order(chans):
    size = chans // HEADS
    cut = 8 * size
    j = iota((chans, 1), 0)
    high = j - cut
    low_src = (j % 8) * size + j // 8
    high_src = (8 + high % 4) * size + high // 8 + (size // 2) * ((high % 8) // 4)
    return jnp.where(j < cut, low_src, high_src)


def within(run):
    lane = iota((1, LANES), 1)
    q, e = lane // 16, lane % 16
    p = (4 * (q // run) + e // 4) * run + q % run
    return ((e % 4) * WIN + p == iota((LANES, LANES), 0)).astype(BF16)


def swap_blocks(tiles):
    tiles = list(tiles)
    block = iota(tiles[0].shape, 1) // 16
    step = len(tiles) // 2
    while step:
        for n in range(len(tiles)):
            if n & step:
                continue
            a, b = tiles[n], tiles[n + step]
            low = block // step % 2 == 0
            tiles[n] = jnp.where(low, a, pltpu.roll(b, 16 * step, 1))
            tiles[n + step] = jnp.where(low, pltpu.roll(a, LANES - 16 * step, 1), b)
        step //= 2
    return tiles


def place(low, high, blocks):
    base = jnp.where(low == iota((LANES, low.shape[1]), 0), 1.0, 0.0).astype(BF16)
    high = jnp.broadcast_to(high, base.shape).astype(F32).astype(BF16)
    nil = jnp.zeros_like(base)
    parts = [jnp.where(high == jnp.asarray(n, BF16), base, nil) for n in range(blocks)]
    return jnp.concatenate(parts, 0)


def norm_t(x, gain):
    inv = 1.0 / x.shape[0]
    mean = jnp.sum(x, 0, keepdims=True) * inv
    cent = x - mean
    var = jnp.sum(cent * cent, 0, keepdims=True) * inv
    return cent * lax.rsqrt(var + 1e-05) * gain


def gelu(x):
    half = 0.5 * x
    scale = math.sqrt(2 / math.pi)
    return half + half * jnp.tanh(x * (scale + (0.044715 * scale) * (x * x)))


def start_all(pairs, sems):
    copies = [pltpu.make_async_copy(a, b, sems.at[n]) for n, (a, b) in enumerate(pairs)]
    for copy in copies:
        copy.start()
    return copies


def wait_all(copies):
    for copy in copies:
        copy.wait()


def fold8(x, op):
    y = x[0]
    for n in range(1, x.shape[0]):
        y = op(y, x[n])
    for shift in (4, 2, 1):
        y = op(y, pltpu.roll(y, shift, 0))
    return y


def first_kernel(
    run, count_ref, nodes_hbm, ids_hbm, pos_hbm, gain_one_hbm, gain_two_hbm, qkv_hbm, out_hbm,
    first_hbm, sent_hbm, nodes_ref, ids_ref, pos_ref, gain_one_ref, gain_two_ref, qkv_ref, out_ref,
    sems, qkv_s, q_s, k_s, v_s, ctx_s, n_s, first_s, sent_s, stores
):
    loads = start_all(
        [
            (nodes_hbm, nodes_ref),
            (ids_hbm, ids_ref),
            (pos_hbm, pos_ref),
            (gain_one_hbm, gain_one_ref),
            (gain_two_hbm, gain_two_ref),
            (qkv_hbm, qkv_ref),
            (out_hbm, out_ref),
        ],
        sems,
    )
    chans, slots = nodes_ref.shape
    tiles = slots // LANES
    size = chans // HEADS
    per = LANES // WIN
    count = count_ref[0]
    wait_all(loads[:5])
    cols = jnp.concatenate(
        [pos_ref[...], gain_one_ref[...], gain_two_ref[...], jnp.zeros((3, chans), F32)], 0
    ).T
    ids = ids_ref[...]
    coords = []
    for axis in range(3):
        total = jnp.zeros(ids.shape, jnp.int32)
        for level in range(6):
            bit = jnp.bitwise_and(jnp.right_shift(ids, 3 * level + axis), 1)
            total = total + bit * 2**level
        coords.append(total.astype(F32) / 64.0 - 0.5)
    for t in range(tiles):
        at = tile(t)
        start = cols[:, 0:1] * coords[0][:, at]
        for axis in range(1, 3):
            start = start + cols[:, axis : axis + 1] * coords[axis][:, at]
        start = (nodes_ref[:, at].astype(F32) + start).astype(BF16)
        nodes_ref[:, at] = start
        n_s[:, at] = norm_t(start.astype(F32), cols[:, 3:4]).astype(BF16)
    wait_all(loads[5:])
    qkv_t = transposed(qkv_ref[...])
    out_t = transposed(out_ref[...])
    qkv_s[...] = dot(qkv_t, n_s[...]).astype(BF16)
    side = eye(LANES)
    row_head = iota((chans, LANES), 0) // size
    even_row = row_head % 2 == 0
    for t in range(tiles):
        query = qkv_s[:chans, tile(t)].astype(F32) * size**-0.5
        q_s[t, :, :LANES] = jnp.where(even_row, query, 0.0).astype(BF16)
        q_s[t, :, LANES:] = jnp.where(even_row, 0.0, query).astype(BF16)
        k_s[t] = dot_t(side, qkv_s[chans : 2 * chans, tile(t)]).astype(BF16)
        v_s[t] = qkv_s[2 * chans :, tile(t)]

    lane_pair = iota((WIN, chans), 1) // (2 * size)
    window = iota((8, LANES), 1) // WIN
    wide_window = iota((WIN, LANES), 1) // WIN
    rank = iota((WIN, LANES), 0) + WIN * (iota((WIN, LANES), 1) // WIN)

    def group(t, _):
        query = q_s[t]
        even, odd = None, None
        for w in range(per):
            keys = k_s[t, w * WIN : (w + 1) * WIN, :]
            by_pair = jnp.concatenate(
                [jnp.where(lane_pair == m, keys, jnp.zeros_like(keys)) for m in range(HEADS // 2)],
                0,
            )
            got = dot(by_pair, query)
            left = got[:, :LANES].reshape(-1, 8, LANES)
            right = got[:, LANES:].reshape(-1, 8, LANES)
            even = left if w == 0 else jnp.where(window[None] == w, left, even)
            odd = right if w == 0 else jnp.where(window[None] == w, right, odd)
        mask = jnp.where(rank + t * LANES < count, 0.0, -1e9).astype(F32)
        mask = mask.reshape(WIN // 8, 8, LANES)
        probs, inverse = [], []
        for h in range(HEADS):
            scores = (even, odd)[h % 2]
            mine = scores[h // 2 * (WIN // 8) : (h // 2 + 1) * (WIN // 8)] + mask
            top = fold8(mine, jnp.maximum)
            weight = jnp.exp(mine - top[None])
            inverse.append(1.0 / fold8(weight, jnp.add))
            probs.append(weight.reshape(WIN, LANES).astype(BF16))
        parts = []
        for m in range(HEADS // 2):
            both = []
            for h in (2 * m, 2 * m + 1):
                nil = jnp.zeros_like(probs[h])
                both.append(
                    jnp.concatenate(
                        [jnp.where(wide_window == w, probs[h], nil) for w in range(per)], 0
                    )
                )
            rows = slice(2 * m * size, 2 * (m + 1) * size)
            got = dot(v_s[t, rows, :], jnp.concatenate(both, 1))
            for n in range(2):
                block = got[n * size : (n + 1) * size, tile(n)].reshape(-1, 8, LANES)
                block = block * inverse[2 * m + n][None]
                parts.append(block.reshape(size, LANES))
        ctx_s[t] = jnp.concatenate(parts, 0).astype(BF16)
        return 0

    lax.fori_loop(0, tiles, group, 0, unroll=4)
    ctx = jnp.concatenate([ctx_s[t] for t in range(tiles)], 1)
    moved = dot(out_t, ctx)
    for t in range(tiles):
        at = tile(t)
        first = (nodes_ref[:, at].astype(F32) + moved[:, at]).astype(BF16)
        first_s[:, at] = first
        normed = norm_t(first.astype(F32), cols[:, 4:5])
        kept = iota((1, LANES), 1) + t * LANES < count
        head = jnp.where((iota((16, LANES), 0) > 0) | kept, normed[:16], FLAG)
        n_s[:, at] = jnp.concatenate([head, normed[16:]], 0).astype(BF16)
    keep_first = pltpu.make_async_copy(first_s, first_hbm, stores.at[0])
    keep_first.start()
    inside = within(run)
    for t, block in enumerate(swap_blocks([dot(n_s[:, tile(t)], inside) for t in range(tiles)])):
        sent_s[:, tile(t)] = block.astype(BF16)
    send = pltpu.make_async_copy(sent_s, sent_hbm, stores.at[1])
    send.start()
    wait_all([keep_first, send])


def tables_kernel(
    cap, qkv_hbm, out_hbm, up_hbm, slot_hbm, owner_hbm, voxel_hbm, gain_hbm, weights_s, facts_s,
    gain_s, qkv_ref, out_ref, up_ref, slot_ref, owner_ref, voxel_ref, gain_ref, sems
):
    loads = start_all(
        [
            (qkv_hbm, qkv_ref),
            (out_hbm, out_ref),
            (up_hbm, up_ref),
            (slot_hbm, slot_ref),
            (owner_hbm, owner_ref),
            (voxel_hbm, voxel_ref),
            (gain_hbm, gain_ref),
        ],
        sems,
    )
    wait_all(loads)
    gain = jnp.concatenate([gain_ref[...], jnp.zeros((7, gain_ref.shape[1]), F32)], 0)
    gain_s[...] = jnp.broadcast_to(gain.T[:, 0:1], gain_s.shape)
    votes = slot_ref.shape[1]
    codes = facts_s.shape[1]
    owners = codes // cap
    chans = out_ref.shape[0]
    src = head_order(chans)
    src = jnp.concatenate([src, src + chans, src + 2 * chans], 0)
    shuffle = (src == iota((3 * chans, 3 * chans), 1)).astype(BF16)
    weights_s[: 3 * chans] = dot_t(shuffle, qkv_ref[...]).astype(BF16)
    out_t = dot(shuffle[:chans, :chans], out_ref[...])
    weights_s[3 * chans : 4 * chans] = transposed(out_t)
    weights_s[4 * chans :] = transposed(up_ref[...])
    owner = jnp.bitwise_xor(owner_ref[...], lax.axis_index("tile"))
    hot = owner == iota((owners, votes), 0)
    upto = (iota((votes, votes), 0) <= iota((votes, votes), 1)).astype(BF16)
    rank = jnp.sum(jnp.where(hot, dot(hot.astype(BF16), upto), 0.0), 0, keepdims=True)
    code = owner * cap + rank.astype(jnp.int32) - 1
    member = place(code % LANES, code // LANES, codes // LANES)
    slot = slot_ref[...]
    row = iota((16, votes), 0)
    facts = jnp.where(
        row == 0,
        voxel_ref[...],
        jnp.where(row == 1, slot // LANES, jnp.where(row == 2, slot % LANES, 1)),
    )
    listed = dot_t(facts.astype(F32).astype(BF16), member)
    facts_s[...] = jnp.where(listed[3:4] > 0.5, listed, -1.0).astype(BF16)


def clean(block):
    head = block[:16].astype(F32)
    gone = head[0:1] > 0.5 * FLAG
    head = jnp.where((iota(head.shape, 0) == 0) & gone, 0.0, head)
    return jnp.concatenate([head.astype(BF16), block[16:]], 0), gone


def add_keys(blocks, kv_t, k_s, v_s, m_s):
    chans = kv_t.shape[1]
    tiles = k_s.shape[1]
    for n, block in enumerate(blocks):
        block, gone = clean(block)
        kv = dot(kv_t, block)
        mask = jnp.where(gone, -1e9, 0.0)
        for t in range(tiles):
            k_s[n, t] = kv[:chans, tile(t)].reshape(chans // 8, 8, LANES)
            v_s[n, t] = kv[chans:, tile(t)].reshape(chans // 8, 8, LANES)
            m_s[n, t] = jnp.broadcast_to(mask[:, tile(t)], (8, LANES))


def attend_two(t, run, q_s, k_s, v_s, m_s, s_s, state_s, fresh):
    rows8 = q_s.shape[1]
    cut = 2 * rows8 // 3
    keys = k_s.shape[0] * run
    base = (t // run) * run
    both = range(2)
    query = [[q_s[t + n, i] for i in range(rows8)] for n in both]

    def score(key, top):
        block, at = key // run, base + key % run
        mask = m_s[block, at]
        sums = [[None, None], [None, None]]
        for i in range(rows8):
            part = int(i >= cut)
            row = k_s[block, at, i]
            for n in both:
                term = query[n][i] * row
                held = sums[n][part]
                sums[n][part] = term if held is None else held + term
        tops = []
        for n in both:
            a, b = sums[n]
            b = b + pltpu.roll(b, 4, 0)
            a = a + mask
            b = b + mask
            s_s[key, 2 * n] = a
            s_s[key, 2 * n + 1] = b
            tops += [jnp.maximum(top[2 * n], a), jnp.maximum(top[2 * n + 1], b)]
        return tuple(tops)

    if fresh:
        old = tuple(jnp.full((8, LANES), -3e38, F32) for _ in range(4))
    else:
        old = tuple(state_s[t + n, rows8 + part] for n in both for part in both)
    tops = lax.fori_loop(0, keys, score, old, unroll=2)
    if fresh:
        zero = jnp.zeros((8, LANES), F32)
        sums = tuple(zero for _ in range(4))
        accs = tuple(zero for _ in range(2 * rows8))
    else:
        fade = [jnp.exp2(old[n] - tops[n]) for n in range(4)]
        sums = tuple(
            state_s[t + n, rows8 + 2 + part] * fade[2 * n + part] for n in both for part in both
        )
        accs = tuple(
            state_s[t + n, i] * fade[2 * n + int(i >= cut)] for n in both for i in range(rows8)
        )

    def gather(key, carry):
        sums, accs = carry
        block, at = key // run, base + key % run
        weight = [jnp.exp2(s_s[key, n] - tops[n]) for n in range(4)]
        accs = list(accs)
        for i in range(rows8):
            row = v_s[block, at, i]
            for n in both:
                at_acc = n * rows8 + i
                accs[at_acc] = accs[at_acc] + weight[2 * n + int(i >= cut)] * row
        return tuple(sums[n] + weight[n] for n in range(4)), tuple(accs)

    sums, accs = lax.fori_loop(0, keys, gather, (sums, accs), unroll=2)
    return tops, sums, accs


def hold_two(n, state, state_s):
    tops, sums, accs = state
    rows8 = len(accs) // 2
    for m in range(2):
        for i in range(rows8):
            state_s[2 * n + m, i] = accs[m * rows8 + i]
        for part in range(2):
            state_s[2 * n + m, rows8 + part] = tops[2 * m + part]
            state_s[2 * n + m, rows8 + 2 + part] = sums[2 * m + part]


def near_kernel(run, own_ref, near_ref, weights_ref, q_s, state_s, k_s, v_s, m_s, s_s):
    chans, slots = own_ref.shape
    tiles = slots // LANES
    scale = (chans // HEADS) ** -0.5 * LOG2E
    own, _ = clean(own_ref[...])
    query = dot(weights_ref[:chans, :], own) * scale
    for t in range(tiles):
        q_s[t] = query[:, tile(t)].reshape(chans // 8, 8, LANES)
    add_keys([own_ref[...], near_ref[...]], weights_ref[chans : 3 * chans, :], k_s, v_s, m_s)

    def step(n, _):
        hold_two(n, attend_two(2 * n, run, q_s, k_s, v_s, m_s, s_s, state_s, True), state_s)
        return 0

    lax.fori_loop(0, tiles // 2, step, 0)


def middle_kernel(run, count, *refs):
    blocks, refs = refs[:count], refs[count:]
    q_s, old_s, weights_ref, state_s, k_s, v_s, m_s, s_s = refs
    chans = weights_ref.shape[1]
    kv_t = weights_ref[chans : 3 * chans, :]
    add_keys([block[...] for block in blocks], kv_t, k_s, v_s, m_s)

    def step(n, _):
        hold_two(n, attend_two(2 * n, run, q_s, k_s, v_s, m_s, s_s, old_s, False), state_s)
        return 0

    lax.fori_loop(0, q_s.shape[0] // 2, step, 0)


def second_kernel(run, cap, far, owners, count_ref, *refs):
    blocks, refs = refs[:far], refs[far:]
    q_s, state_s, weights_s, first_s, gain_s, down_s, facts_s, feat_hbm = refs[:8]
    votes_s, refs = refs[8 : 8 + owners], refs[8 + owners :]
    feat_s, store, k_s, v_s, m_s, s_s, ctx_s, bf_s, inner_s = refs
    chans, slots = first_s.shape
    tiles = slots // LANES
    count = count_ref[0]
    add_keys([block[...] for block in blocks], weights_s[chans : 3 * chans], k_s, v_s, m_s)
    rows8 = chans // 8

    def step(n, _):
        t = 2 * n
        _, sums, accs = attend_two(t, run, q_s, k_s, v_s, m_s, s_s, state_s, False)
        share = [1.0 / total for total in sums]
        cut = 2 * rows8 // 3
        for n in range(2):
            for i in range(rows8):
                ctx_s[t + n, i] = accs[n * rows8 + i] * share[2 * n + int(i >= cut)]
        return 0

    lax.fori_loop(0, tiles // 2, step, 0)
    ctx = swap_blocks([ctx_s[t].reshape(chans, LANES) for t in range(tiles)])
    ctx = dot_t(jnp.concatenate(ctx, 0).astype(BF16), within(run)).astype(BF16)
    ctx = jnp.concatenate([ctx[t * chans : (t + 1) * chans] for t in range(tiles)], 1)
    gain = gain_s[...]
    moved = dot(weights_s[3 * chans : 4 * chans], ctx)
    for t in range(tiles):
        at = tile(t)
        second = first_s[:, at].astype(F32) + moved[:, at]
        feat_s[:, at] = second
        inner_s[:, at] = norm_t(second, gain).astype(BF16)
    kept = iota((1, slots), 1) < count
    wide = 2 * LANES
    cuts = [slice(at, at + wide) for at in range(0, slots, wide)]
    up_t = weights_s[4 * chans :]
    raised = dot(up_t, inner_s[:, cuts[0]])
    for n, at in enumerate(cuts):
        now = raised
        if n + 1 < len(cuts):
            raised = dot(up_t, inner_s[:, cuts[n + 1]])
        hidden = gelu(now).astype(BF16)
        third = feat_s[:, at] + dot(down_s[...], hidden)
        third = jnp.where(kept[:, at], third, 0.0)
        feat_s[:, at] = third
        bf_s[:, at] = third.astype(BF16)
    keep = pltpu.make_async_copy(feat_s, feat_hbm, store)
    keep.start()
    facts = facts_s[...].astype(F32)
    low, high = facts[2:3].astype(jnp.int32), facts[1:2].astype(jnp.int32)
    picked = dot(bf_s[...], place(low, high, tiles)).astype(BF16)
    for o in range(owners):
        votes_s[o][:chans, :] = picked[:, o * cap : (o + 1) * cap]
        votes_s[o][chans:, :] = facts_s[:, o * cap : (o + 1) * cap]
    keep.wait()


def sums_kernel(*refs):
    got, out_ref = refs[:-1], refs[-1]
    chans, voxels = out_ref.shape
    cap = got[0].shape[1]
    total = jnp.zeros(out_ref.shape, F32)
    for ref in got:
        label = ref[chans:, :].astype(F32)[0:1]
        hot = (label == iota((voxels, cap), 0).astype(F32)).astype(BF16)
        total = total + dot_t(ref[:chans, :], hot)
    out_ref[...] = total


def call(kernel, outs, scratch, flops, spaces, out_spaces, limit=VMEM):
    place_of = {"s": pltpu.SMEM, "v": pltpu.VMEM, "a": pl.ANY}
    return pl.pallas_call(
        kernel,
        out_shape=outs,
        in_specs=[pl.BlockSpec(memory_space=place_of[c]) for c in spaces],
        out_specs=[pl.BlockSpec(memory_space=place_of[c]) for c in out_spaces],
        scratch_shapes=scratch,
        compiler_params=pltpu.CompilerParams(vmem_limit_bytes=limit),
        cost_estimate=pl.CostEstimate(flops=flops, bytes_accessed=2 << 20, transcendentals=0),
    )


def turned(x, axis, bit):
    n = lax.axis_size(axis)
    return lax.ppermute(x, axis, [(i, i ^ bit) for i in range(n)])


def body(
    nodes,
    node_ids,
    node_count,
    pos_weight,
    gain_one,
    qkv_one,
    out_one,
    gain_two,
    qkv_two,
    out_two,
    gain_three,
    w_up,
    w_down,
    vote_slot,
    vote_owner,
    vote_voxel,
):
    slots, chans = nodes.shape
    groups, owners = lax.axis_size("grp"), lax.axis_size("tile")
    run = WIN // groups
    votes = vote_slot.shape[0]
    cap = 2 * votes // owners
    codes = owners * cap
    tiles = slots // LANES
    rows8 = chans // 8
    hidden = w_up.shape[1]
    per = LANES // WIN
    sds = jax.ShapeDtypeStruct
    vmem = pltpu.VMEM
    dma = pltpu.SemaphoreType.DMA

    first, sent = call(
        functools.partial(first_kernel, run),
        [sds((chans, slots), BF16), sds((chans, slots), BF16)],
        [
            vmem((chans, slots), BF16),
            vmem((1, slots), jnp.int32),
            vmem((3, chans), F32),
            vmem((1, chans), F32),
            vmem((1, chans), F32),
            vmem((chans, 3 * chans), BF16),
            vmem((chans, chans), BF16),
            dma((7,)),
            vmem((3 * chans, slots), BF16),
            vmem((tiles, chans, 2 * LANES), BF16),
            vmem((tiles, LANES, chans), BF16),
            vmem((tiles, chans, LANES), BF16),
            vmem((tiles, chans, LANES), BF16),
            vmem((chans, slots), BF16),
            vmem((chans, slots), BF16),
            vmem((chans, slots), BF16),
            dma((2,)),
        ],
        2_000_000_000,
        "saaaaaaa",
        "aa",
    )(
        node_count,
        nodes.T,
        node_ids.reshape(1, slots),
        pos_weight,
        gain_one.reshape(1, chans),
        gain_two.reshape(1, chans),
        qkv_one,
        out_one,
    )
    bit = groups // 2
    mid = []
    while bit > 1:
        mid += [turned(block, "grp", bit) for block in [sent] + mid]
        bit //= 2
    near = turned(sent, "grp", 1)
    weights, facts, gain = call(
        functools.partial(tables_kernel, cap),
        [
            sds((4 * chans + hidden, chans), BF16),
            sds((16, codes), BF16),
            sds((chans, LANES), F32),
        ],
        [
            vmem((chans, 3 * chans), BF16),
            vmem((chans, chans), BF16),
            vmem((chans, hidden), BF16),
            vmem((1, votes), jnp.int32),
            vmem((1, votes), jnp.int32),
            vmem((1, votes), jnp.int32),
            vmem((1, chans), F32),
            dma((7,)),
        ],
        2_000_000_000,
        "aaaaaaa",
        "vvv",
        limit=ROOMY,
    )(
        qkv_two,
        out_two,
        w_up,
        vote_slot.reshape(1, votes),
        vote_owner.reshape(1, votes),
        vote_voxel.reshape(1, votes),
        gain_three.reshape(1, chans),
    )
    q_like = ((tiles, rows8, 8, LANES), F32)
    state_like = ((tiles, rows8 + 4, 8, LANES), F32)

    def key_scratch(blocks):
        return [
            vmem((blocks, tiles, rows8, 8, LANES), F32),
            vmem((blocks, tiles, rows8, 8, LANES), F32),
            vmem((blocks, tiles, 8, LANES), F32),
            vmem((blocks * run, 4, 8, LANES), F32),
        ]

    query, state = call(
        functools.partial(near_kernel, run),
        [sds(*q_like), sds(*state_like)],
        key_scratch(2),
        3_000_000_000,
        "vvv",
        "vv",
        limit=ROOMY,
    )(sent, near, weights)
    mid, query = lax.optimization_barrier((mid, query))
    far = [turned(block, "grp", 1) for block in mid]
    (state,) = call(
        functools.partial(middle_kernel, run, len(mid)),
        [sds(*state_like)],
        key_scratch(len(mid)),
        2_000_000_000,
        "v" * len(mid) + "vvv",
        "v",
        limit=ROOMY,
    )(*mid, query, state, weights)
    features_t, *ballots = call(
        functools.partial(second_kernel, run, cap, len(far), owners),
        [sds((chans, slots), F32)] + [sds((chans + 16, cap), BF16)] * owners,
        [vmem((chans, slots), F32), dma]
        + key_scratch(len(far))
        + [vmem(*q_like), vmem((chans, slots), BF16), vmem((chans, slots), BF16)],
        3_000_000_000,
        "s" + "v" * (len(far) + 7),
        "a" + "v" * owners,
        limit=ROOMY,
    )(
        node_count,
        *far,
        query,
        state,
        weights,
        first,
        gain,
        w_down.T,
        facts,
    )
    got = [ballots[0]] + [turned(ballots[k], "tile", k) for k in [1] + list(range(owners - 1, 1, -1))]
    (sums_t,) = call(
        sums_kernel,
        [sds((chans, VOX_DEV), F32)],
        [],
        200_000_000,
        "v" * owners,
        "v",
        limit=ROOMY,
    )(*got)
    return (features_t.T, sums_t.T)


def solution(mesh):
    in_specs = (
        P(("grp", "tile"), None),
        P(("grp", "tile")),
        P(("grp", "tile")),
        P(),
        P(),
        P(),
        P(),
        P(),
        P(),
        P(),
        P(),
        P(),
        P(),
        P(("grp", "tile")),
        P(("grp", "tile"), None),
        P(("grp", "tile")),
    )
    out_specs = (P(("grp", "tile"), None), P(("grp", "tile"), None))
    return jax.shard_map(body, mesh=mesh, in_specs=in_specs, out_specs=out_specs, check_vma=False)
```

```python
import functools
import math

import jax
import jax.numpy as jnp
from jax import lax
from jax.experimental import pallas as pl
from jax.experimental.pallas import tpu as pltpu
from jax.sharding import PartitionSpec as P

HEADS = 12
WIN = 32
VOX_DEV = 256
LANES = 128
FLAG = 16384.0
VMEM = 64 * 1024 * 1024 - 65536
TIGHT = VMEM - 2 * 1024 * 1024
ROOMY = 24 * 1024 * 1024
F32 = jnp.float32
BF16 = jnp.bfloat16
LOG2E = math.log2(math.e)


def iota(shape, dim):
    return lax.broadcasted_iota(jnp.int32, shape, dim)


def dot(a, b):
    return jnp.dot(a, b, preferred_element_type=F32)


def dot_t(a, b):
    return lax.dot_general(a, b, (((1,), (1,)), ((), ())), preferred_element_type=F32)


def eye(n):
    return (iota((n, n), 0) == iota((n, n), 1)).astype(BF16)


def transposed(a):
    return a.astype(F32).T.astype(BF16)


def tile(t):
    return slice(t * LANES, (t + 1) * LANES)


def head_order(chans):
    size = chans // HEADS
    cut = 8 * size
    j = iota((chans, 1), 0)
    high = j - cut
    low_src = (j % 8) * size + j // 8
    high_src = (8 + high % 4) * size + high // 8 + (size // 2) * ((high % 8) // 4)
    return jnp.where(j < cut, low_src, high_src)


def within(run):
    lane = iota((1, LANES), 1)
    q, e = lane // 16, lane % 16
    p = (4 * (q // run) + e // 4) * run + q % run
    return ((e % 4) * WIN + p == iota((LANES, LANES), 0)).astype(BF16)


def swap_blocks(tiles):
    tiles = list(tiles)
    block = iota(tiles[0].shape, 1) // 16
    step = len(tiles) // 2
    while step:
        for n in range(len(tiles)):
            if n & step:
                continue
            a, b = tiles[n], tiles[n + step]
            low = block // step % 2 == 0
            tiles[n] = jnp.where(low, a, pltpu.roll(b, 16 * step, 1))
            tiles[n + step] = jnp.where(low, pltpu.roll(a, LANES - 16 * step, 1), b)
        step //= 2
    return tiles


def place(low, high, blocks):
    base = jnp.where(low == iota((LANES, low.shape[1]), 0), 1.0, 0.0).astype(BF16)
    high = jnp.broadcast_to(high, base.shape).astype(F32).astype(BF16)
    nil = jnp.zeros_like(base)
    parts = [jnp.where(high == jnp.asarray(n, BF16), base, nil) for n in range(blocks)]
    return jnp.concatenate(parts, 0)


def norm_t(x, gain):
    inv = 1.0 / x.shape[0]
    mean = jnp.sum(x, 0, keepdims=True) * inv
    cent = x - mean
    var = jnp.sum(cent * cent, 0, keepdims=True) * inv
    return cent * lax.rsqrt(var + 1e-05) * gain


def gelu(x):
    half = 0.5 * x
    scale = math.sqrt(2 / math.pi)
    return half + half * jnp.tanh(x * (scale + (0.044715 * scale) * (x * x)))


def start_all(pairs, sems):
    copies = [pltpu.make_async_copy(a, b, sems.at[n]) for n, (a, b) in enumerate(pairs)]
    for copy in copies:
        copy.start()
    return copies


def wait_all(copies):
    for copy in copies:
        copy.wait()


def fold8(x, op):
    y = x[0]
    for n in range(1, x.shape[0]):
        y = op(y, x[n])
    for shift in (4, 2, 1):
        y = op(y, pltpu.roll(y, shift, 0))
    return y


def first_kernel(
    run, count_ref, nodes_hbm, ids_hbm, pos_hbm, gain_one_hbm, gain_two_hbm, qkv_hbm, out_hbm,
    first_hbm, sent_hbm, nodes_ref, ids_ref, pos_ref, gain_one_ref, gain_two_ref, qkv_ref, out_ref,
    sems, qkv_s, q_s, k_s, v_s, ctx_s, n_s, first_s, sent_s, stores
):
    loads = start_all(
        [
            (nodes_hbm, nodes_ref),
            (ids_hbm, ids_ref),
            (pos_hbm, pos_ref),
            (gain_one_hbm, gain_one_ref),
            (gain_two_hbm, gain_two_ref),
            (qkv_hbm, qkv_ref),
            (out_hbm, out_ref),
        ],
        sems,
    )
    chans, slots = nodes_ref.shape
    tiles = slots // LANES
    size = chans // HEADS
    per = LANES // WIN
    count = count_ref[0]
    wait_all(loads)
    cols = jnp.concatenate(
        [pos_ref[...], gain_one_ref[...], gain_two_ref[...], jnp.zeros((3, chans), F32)], 0
    ).T
    ids = ids_ref[...]
    coords = []
    for axis in range(3):
        total = jnp.zeros(ids.shape, jnp.int32)
        for level in range(6):
            bit = jnp.bitwise_and(jnp.right_shift(ids, 3 * level + axis), 1)
            total = total + bit * 2**level
        coords.append(total.astype(F32) / 64.0 - 0.5)
    for t in range(tiles):
        at = tile(t)
        start = cols[:, 0:1] * coords[0][:, at]
        for axis in range(1, 3):
            start = start + cols[:, axis : axis + 1] * coords[axis][:, at]
        start = (nodes_ref[:, at].astype(F32) + start).astype(BF16)
        nodes_ref[:, at] = start
        n_s[:, at] = norm_t(start.astype(F32), cols[:, 3:4]).astype(BF16)
    qkv_t = transposed(qkv_ref[...])
    out_t = transposed(out_ref[...])
    qkv_s[...] = dot(qkv_t, n_s[...]).astype(BF16)
    side = eye(LANES)
    row_head = iota((chans, LANES), 0) // size
    even_row = row_head % 2 == 0
    for t in range(tiles):
        query = qkv_s[:chans, tile(t)].astype(F32) * size**-0.5
        q_s[t, :, :LANES] = jnp.where(even_row, query, 0.0).astype(BF16)
        q_s[t, :, LANES:] = jnp.where(even_row, 0.0, query).astype(BF16)
        k_s[t] = dot_t(side, qkv_s[chans : 2 * chans, tile(t)]).astype(BF16)
        v_s[t] = qkv_s[2 * chans :, tile(t)]

    lane_pair = iota((WIN, chans), 1) // (2 * size)
    window = iota((8, LANES), 1) // WIN
    wide_window = iota((WIN, LANES), 1) // WIN
    rank = iota((WIN, LANES), 0) + WIN * (iota((WIN, LANES), 1) // WIN)

    def group(t, _):
        query = q_s[t]
        even, odd = None, None
        for w in range(per):
            keys = k_s[t, w * WIN : (w + 1) * WIN, :]
            by_pair = jnp.concatenate(
                [jnp.where(lane_pair == m, keys, jnp.zeros_like(keys)) for m in range(HEADS // 2)],
                0,
            )
            got = dot(by_pair, query)
            left = got[:, :LANES].reshape(-1, 8, LANES)
            right = got[:, LANES:].reshape(-1, 8, LANES)
            even = left if w == 0 else jnp.where(window[None] == w, left, even)
            odd = right if w == 0 else jnp.where(window[None] == w, right, odd)
        mask = jnp.where(rank + t * LANES < count, 0.0, -1e9).astype(F32)
        mask = mask.reshape(WIN // 8, 8, LANES)
        probs, inverse = [], []
        for h in range(HEADS):
            scores = (even, odd)[h % 2]
            mine = scores[h // 2 * (WIN // 8) : (h // 2 + 1) * (WIN // 8)] + mask
            top = fold8(mine, jnp.maximum)
            weight = jnp.exp(mine - top[None])
            inverse.append(1.0 / fold8(weight, jnp.add))
            probs.append(weight.reshape(WIN, LANES).astype(BF16))
        parts = []
        for m in range(HEADS // 2):
            both = []
            for h in (2 * m, 2 * m + 1):
                nil = jnp.zeros_like(probs[h])
                both.append(
                    jnp.concatenate(
                        [jnp.where(wide_window == w, probs[h], nil) for w in range(per)], 0
                    )
                )
            rows = slice(2 * m * size, 2 * (m + 1) * size)
            got = dot(v_s[t, rows, :], jnp.concatenate(both, 1))
            for n in range(2):
                block = got[n * size : (n + 1) * size, tile(n)].reshape(-1, 8, LANES)
                block = block * inverse[2 * m + n][None]
                parts.append(block.reshape(size, LANES))
        ctx_s[t] = jnp.concatenate(parts, 0).astype(BF16)
        return 0

    lax.fori_loop(0, tiles, group, 0, unroll=4)
    ctx = jnp.concatenate([ctx_s[t] for t in range(tiles)], 1)
    moved = dot(out_t, ctx)
    for t in range(tiles):
        at = tile(t)
        first = (nodes_ref[:, at].astype(F32) + moved[:, at]).astype(BF16)
        first_s[:, at] = first
        normed = norm_t(first.astype(F32), cols[:, 4:5])
        kept = iota((1, LANES), 1) + t * LANES < count
        head = jnp.where((iota((16, LANES), 0) > 0) | kept, normed[:16], FLAG)
        n_s[:, at] = jnp.concatenate([head, normed[16:]], 0).astype(BF16)
    keep_first = pltpu.make_async_copy(first_s, first_hbm, stores.at[0])
    keep_first.start()
    inside = within(run)
    for t, block in enumerate(swap_blocks([dot(n_s[:, tile(t)], inside) for t in range(tiles)])):
        sent_s[:, tile(t)] = block.astype(BF16)
    send = pltpu.make_async_copy(sent_s, sent_hbm, stores.at[1])
    send.start()
    wait_all([keep_first, send])


def tables_kernel(
    cap, qkv_hbm, out_hbm, up_hbm, slot_hbm, owner_hbm, voxel_hbm, gain_hbm, weights_s, facts_s,
    gain_s, qkv_ref, out_ref, up_ref, slot_ref, owner_ref, voxel_ref, gain_ref, sems
):
    loads = start_all(
        [
            (qkv_hbm, qkv_ref),
            (out_hbm, out_ref),
            (up_hbm, up_ref),
            (slot_hbm, slot_ref),
            (owner_hbm, owner_ref),
            (voxel_hbm, voxel_ref),
            (gain_hbm, gain_ref),
        ],
        sems,
    )
    wait_all(loads)
    gain = jnp.concatenate([gain_ref[...], jnp.zeros((7, gain_ref.shape[1]), F32)], 0)
    gain_s[...] = jnp.broadcast_to(gain.T[:, 0:1], gain_s.shape)
    votes = slot_ref.shape[1]
    codes = facts_s.shape[1]
    owners = codes // cap
    chans = out_ref.shape[0]
    src = head_order(chans)
    src = jnp.concatenate([src, src + chans, src + 2 * chans], 0)
    shuffle = (src == iota((3 * chans, 3 * chans), 1)).astype(BF16)
    weights_s[: 3 * chans] = dot_t(shuffle, qkv_ref[...]).astype(BF16)
    out_t = dot(shuffle[:chans, :chans], out_ref[...])
    weights_s[3 * chans : 4 * chans] = transposed(out_t)
    weights_s[4 * chans :] = transposed(up_ref[...])
    owner = jnp.bitwise_xor(owner_ref[...], lax.axis_index("tile"))
    hot = owner == iota((owners, votes), 0)
    upto = (iota((votes, votes), 0) <= iota((votes, votes), 1)).astype(BF16)
    rank = jnp.sum(jnp.where(hot, dot(hot.astype(BF16), upto), 0.0), 0, keepdims=True)
    code = owner * cap + rank.astype(jnp.int32) - 1
    member = place(code % LANES, code // LANES, codes // LANES)
    slot = slot_ref[...]
    row = iota((16, votes), 0)
    facts = jnp.where(
        row == 0,
        voxel_ref[...],
        jnp.where(row == 1, slot // LANES, jnp.where(row == 2, slot % LANES, 1)),
    )
    listed = dot_t(facts.astype(F32).astype(BF16), member)
    facts_s[...] = jnp.where(listed[3:4] > 0.5, listed, -1.0).astype(BF16)


def clean(block):
    head = block[:16].astype(F32)
    gone = head[0:1] > 0.5 * FLAG
    head = jnp.where((iota(head.shape, 0) == 0) & gone, 0.0, head)
    return jnp.concatenate([head.astype(BF16), block[16:]], 0), gone


def add_keys(blocks, kv_t, k_s, v_s, m_s):
    chans = kv_t.shape[1]
    tiles = k_s.shape[1]
    for n, block in enumerate(blocks):
        block, gone = clean(block)
        kv = dot(kv_t, block)
        mask = jnp.where(gone, -1e9, 0.0)
        for t in range(tiles):
            k_s[n, t] = kv[:chans, tile(t)].reshape(chans // 8, 8, LANES)
            v_s[n, t] = kv[chans:, tile(t)].reshape(chans // 8, 8, LANES)
            m_s[n, t] = jnp.broadcast_to(mask[:, tile(t)], (8, LANES))


def attend_two(t, run, q_s, k_s, v_s, m_s, s_s, state_s, fresh):
    rows8 = q_s.shape[1]
    cut = 2 * rows8 // 3
    keys = k_s.shape[0] * run
    base = (t // run) * run
    both = range(2)
    query = [[q_s[t + n, i] for i in range(rows8)] for n in both]

    def score(key, top):
        block, at = key // run, base + key % run
        mask = m_s[block, at]
        sums = [[None, None], [None, None]]
        for i in range(rows8):
            part = int(i >= cut)
            row = k_s[block, at, i]
            for n in both:
                term = query[n][i] * row
                held = sums[n][part]
                sums[n][part] = term if held is None else held + term
        tops = []
        for n in both:
            a, b = sums[n]
            b = b + pltpu.roll(b, 4, 0)
            a = a + mask
            b = b + mask
            s_s[key, 2 * n] = a
            s_s[key, 2 * n + 1] = b
            tops += [jnp.maximum(top[2 * n], a), jnp.maximum(top[2 * n + 1], b)]
        return tuple(tops)

    if fresh:
        old = tuple(jnp.full((8, LANES), -3e38, F32) for _ in range(4))
    else:
        old = tuple(state_s[t + n, rows8 + part] for n in both for part in both)
    tops = lax.fori_loop(0, keys, score, old, unroll=2)
    if fresh:
        zero = jnp.zeros((8, LANES), F32)
        sums = tuple(zero for _ in range(4))
        accs = tuple(zero for _ in range(2 * rows8))
    else:
        fade = [jnp.exp2(old[n] - tops[n]) for n in range(4)]
        sums = tuple(
            state_s[t + n, rows8 + 2 + part] * fade[2 * n + part] for n in both for part in both
        )
        accs = tuple(
            state_s[t + n, i] * fade[2 * n + int(i >= cut)] for n in both for i in range(rows8)
        )

    def gather(key, carry):
        sums, accs = carry
        block, at = key // run, base + key % run
        weight = [jnp.exp2(s_s[key, n] - tops[n]) for n in range(4)]
        accs = list(accs)
        for i in range(rows8):
            row = v_s[block, at, i]
            for n in both:
                at_acc = n * rows8 + i
                accs[at_acc] = accs[at_acc] + weight[2 * n + int(i >= cut)] * row
        return tuple(sums[n] + weight[n] for n in range(4)), tuple(accs)

    sums, accs = lax.fori_loop(0, keys, gather, (sums, accs), unroll=2)
    return tops, sums, accs


def hold_two(n, state, state_s):
    tops, sums, accs = state
    rows8 = len(accs) // 2
    for m in range(2):
        for i in range(rows8):
            state_s[2 * n + m, i] = accs[m * rows8 + i]
        for part in range(2):
            state_s[2 * n + m, rows8 + part] = tops[2 * m + part]
            state_s[2 * n + m, rows8 + 2 + part] = sums[2 * m + part]


def near_kernel(run, own_ref, near_ref, weights_ref, q_s, state_s, k_s, v_s, m_s, s_s):
    chans, slots = own_ref.shape
    tiles = slots // LANES
    scale = (chans // HEADS) ** -0.5 * LOG2E
    own, _ = clean(own_ref[...])
    query = dot(weights_ref[:chans, :], own) * scale
    for t in range(tiles):
        q_s[t] = query[:, tile(t)].reshape(chans // 8, 8, LANES)
    add_keys([own_ref[...], near_ref[...]], weights_ref[chans : 3 * chans, :], k_s, v_s, m_s)

    def step(n, _):
        hold_two(n, attend_two(2 * n, run, q_s, k_s, v_s, m_s, s_s, state_s, True), state_s)
        return 0

    lax.fori_loop(0, tiles // 2, step, 0)


def middle_kernel(run, count, *refs):
    blocks, refs = refs[:count], refs[count:]
    q_s, old_s, weights_ref, state_s, k_s, v_s, m_s, s_s = refs
    chans = weights_ref.shape[1]
    kv_t = weights_ref[chans : 3 * chans, :]
    add_keys([block[...] for block in blocks], kv_t, k_s, v_s, m_s)

    def step(n, _):
        hold_two(n, attend_two(2 * n, run, q_s, k_s, v_s, m_s, s_s, old_s, False), state_s)
        return 0

    lax.fori_loop(0, q_s.shape[0] // 2, step, 0)


def second_kernel(run, cap, far, owners, count_ref, *refs):
    blocks, refs = refs[:far], refs[far:]
    q_s, state_s, weights_s, first_s, gain_s, down_s, facts_s, feat_hbm = refs[:8]
    votes_s, refs = refs[8 : 8 + owners], refs[8 + owners :]
    feat_s, store, k_s, v_s, m_s, s_s, ctx_s, bf_s, inner_s = refs
    chans, slots = first_s.shape
    tiles = slots // LANES
    count = count_ref[0]
    add_keys([block[...] for block in blocks], weights_s[chans : 3 * chans], k_s, v_s, m_s)
    rows8 = chans // 8

    def step(n, _):
        t = 2 * n
        _, sums, accs = attend_two(t, run, q_s, k_s, v_s, m_s, s_s, state_s, False)
        share = [1.0 / total for total in sums]
        cut = 2 * rows8 // 3
        for n in range(2):
            for i in range(rows8):
                ctx_s[t + n, i] = accs[n * rows8 + i] * share[2 * n + int(i >= cut)]
        return 0

    lax.fori_loop(0, tiles // 2, step, 0)
    ctx = swap_blocks([ctx_s[t].reshape(chans, LANES) for t in range(tiles)])
    ctx = dot_t(jnp.concatenate(ctx, 0).astype(BF16), within(run)).astype(BF16)
    ctx = jnp.concatenate([ctx[t * chans : (t + 1) * chans] for t in range(tiles)], 1)
    gain = gain_s[...]
    moved = dot(weights_s[3 * chans : 4 * chans], ctx)
    for t in range(tiles):
        at = tile(t)
        second = first_s[:, at].astype(F32) + moved[:, at]
        feat_s[:, at] = second
        inner_s[:, at] = norm_t(second, gain).astype(BF16)
    kept = iota((1, slots), 1) < count
    wide = 2 * LANES
    cuts = [slice(at, at + wide) for at in range(0, slots, wide)]
    up_t = weights_s[4 * chans :]
    raised = dot(up_t, inner_s[:, cuts[0]])
    for n, at in enumerate(cuts):
        now = raised
        if n + 1 < len(cuts):
            raised = dot(up_t, inner_s[:, cuts[n + 1]])
        hidden = gelu(now).astype(BF16)
        third = feat_s[:, at] + dot(down_s[...], hidden)
        third = jnp.where(kept[:, at], third, 0.0)
        feat_s[:, at] = third
        bf_s[:, at] = third.astype(BF16)
    keep = pltpu.make_async_copy(feat_s, feat_hbm, store)
    keep.start()
    facts = facts_s[...].astype(F32)
    low, high = facts[2:3].astype(jnp.int32), facts[1:2].astype(jnp.int32)
    picked = dot(bf_s[...], place(low, high, tiles)).astype(BF16)
    for o in range(owners):
        votes_s[o][:chans, :] = picked[:, o * cap : (o + 1) * cap]
        votes_s[o][chans:, :] = facts_s[:, o * cap : (o + 1) * cap]
    keep.wait()


def summed(blocks, chans, voxels):
    cap = blocks[0].shape[1]
    total = jnp.zeros((chans, voxels), F32)
    for ref in blocks:
        label = ref[chans:, :].astype(F32)[0:1]
        hot = (label == iota((voxels, cap), 0).astype(F32)).astype(BF16)
        total = total + dot_t(ref[:chans, :], hot)
    return total


def proxy_kernel(*refs):
    refs[-1][...] = summed(refs[:-1], *refs[-1].shape).astype(BF16)


def sums_kernel(*refs):
    got, other_ref, out_ref = refs[:-2], refs[-2], refs[-1]
    out_ref[...] = summed(got, *out_ref.shape) + other_ref[...].astype(F32)


def call(kernel, outs, scratch, flops, spaces, out_spaces, limit=VMEM):
    place_of = {"s": pltpu.SMEM, "v": pltpu.VMEM, "a": pl.ANY}
    return pl.pallas_call(
        kernel,
        out_shape=outs,
        in_specs=[pl.BlockSpec(memory_space=place_of[c]) for c in spaces],
        out_specs=[pl.BlockSpec(memory_space=place_of[c]) for c in out_spaces],
        scratch_shapes=scratch,
        compiler_params=pltpu.CompilerParams(vmem_limit_bytes=limit),
        cost_estimate=pl.CostEstimate(flops=flops, bytes_accessed=2 << 20, transcendentals=0),
    )


def turned(x, axis, bit):
    n = lax.axis_size(axis)
    return lax.ppermute(x, axis, [(i, i ^ bit) for i in range(n)])


def body(
    nodes,
    node_ids,
    node_count,
    pos_weight,
    gain_one,
    qkv_one,
    out_one,
    gain_two,
    qkv_two,
    out_two,
    gain_three,
    w_up,
    w_down,
    vote_slot,
    vote_owner,
    vote_voxel,
):
    slots, chans = nodes.shape
    groups, owners = lax.axis_size("grp"), lax.axis_size("tile")
    run = WIN // groups
    votes = vote_slot.shape[0]
    cap = 2 * votes // owners
    codes = owners * cap
    tiles = slots // LANES
    rows8 = chans // 8
    hidden = w_up.shape[1]
    per = LANES // WIN
    sds = jax.ShapeDtypeStruct
    vmem = pltpu.VMEM
    dma = pltpu.SemaphoreType.DMA

    first, sent = call(
        functools.partial(first_kernel, run),
        [sds((chans, slots), BF16), sds((chans, slots), BF16)],
        [
            vmem((chans, slots), BF16),
            vmem((1, slots), jnp.int32),
            vmem((3, chans), F32),
            vmem((1, chans), F32),
            vmem((1, chans), F32),
            vmem((chans, 3 * chans), BF16),
            vmem((chans, chans), BF16),
            dma((7,)),
            vmem((3 * chans, slots), BF16),
            vmem((tiles, chans, 2 * LANES), BF16),
            vmem((tiles, LANES, chans), BF16),
            vmem((tiles, chans, LANES), BF16),
            vmem((tiles, chans, LANES), BF16),
            vmem((chans, slots), BF16),
            vmem((chans, slots), BF16),
            vmem((chans, slots), BF16),
            dma((2,)),
        ],
        2_000_000_000,
        "saaaaaaa",
        "aa",
    )(
        node_count,
        nodes.T,
        node_ids.reshape(1, slots),
        pos_weight,
        gain_one.reshape(1, chans),
        gain_two.reshape(1, chans),
        qkv_one,
        out_one,
    )
    bit = groups // 2
    mid = []
    while bit > 1:
        mid += [turned(block, "grp", bit) for block in [sent] + mid]
        bit //= 2
    near = turned(sent, "grp", 1)
    weights, facts, gain = call(
        functools.partial(tables_kernel, cap),
        [
            sds((4 * chans + hidden, chans), BF16),
            sds((16, codes), BF16),
            sds((chans, LANES), F32),
        ],
        [
            vmem((chans, 3 * chans), BF16),
            vmem((chans, chans), BF16),
            vmem((chans, hidden), BF16),
            vmem((1, votes), jnp.int32),
            vmem((1, votes), jnp.int32),
            vmem((1, votes), jnp.int32),
            vmem((1, chans), F32),
            dma((7,)),
        ],
        2_000_000_000,
        "aaaaaaa",
        "vvv",
        limit=TIGHT,
    )(
        qkv_two,
        out_two,
        w_up,
        vote_slot.reshape(1, votes),
        vote_owner.reshape(1, votes),
        vote_voxel.reshape(1, votes),
        gain_three.reshape(1, chans),
    )
    q_like = ((tiles, rows8, 8, LANES), F32)
    state_like = ((tiles, rows8 + 4, 8, LANES), F32)

    def key_scratch(blocks):
        return [
            vmem((blocks, tiles, rows8, 8, LANES), F32),
            vmem((blocks, tiles, rows8, 8, LANES), F32),
            vmem((blocks, tiles, 8, LANES), F32),
            vmem((blocks * run, 4, 8, LANES), F32),
        ]

    query, state = call(
        functools.partial(near_kernel, run),
        [sds(*q_like), sds(*state_like)],
        key_scratch(2),
        3_000_000_000,
        "vvv",
        "vv",
        limit=ROOMY,
    )(sent, near, weights)
    mid, query = lax.optimization_barrier((mid, query))
    far = [turned(block, "grp", 1) for block in mid]
    (state,) = call(
        functools.partial(middle_kernel, run, len(mid)),
        [sds(*state_like)],
        key_scratch(len(mid)),
        2_000_000_000,
        "v" * len(mid) + "vvv",
        "v",
        limit=ROOMY,
    )(*mid, query, state, weights)
    features_t, *ballots = call(
        functools.partial(second_kernel, run, cap, len(far), owners),
        [sds((chans, slots), F32)] + [sds((chans + 16, cap), BF16)] * owners,
        [vmem((chans, slots), F32), dma]
        + key_scratch(len(far))
        + [vmem(*q_like), vmem((chans, slots), BF16), vmem((chans, slots), BF16)],
        3_000_000_000,
        "s" + "v" * (len(far) + 7),
        "a" + "v" * owners,
        limit=ROOMY,
    )(
        node_count,
        *far,
        query,
        state,
        weights,
        first,
        gain,
        w_down.T,
        facts,
    )
    half = owners // 2
    passed = [ballots[half]] + [turned(ballots[half + k], "tile", k) for k in range(1, half)]
    direct = [ballots[0]] + [turned(ballots[k], "tile", k) for k in range(1, half)]
    (partial,) = call(
        proxy_kernel,
        [sds((chans, VOX_DEV), BF16)],
        [],
        200_000_000,
        "v" * half,
        "v",
        limit=ROOMY,
    )(*passed)
    (sums_t,) = call(
        sums_kernel,
        [sds((chans, VOX_DEV), F32)],
        [],
        200_000_000,
        "v" * (half + 1),
        "v",
        limit=ROOMY,
    )(*direct, turned(partial, "tile", half))
    return (features_t.T, sums_t.T)


def solution(mesh):
    in_specs = (
        P(("grp", "tile"), None),
        P(("grp", "tile")),
        P(("grp", "tile")),
        P(),
        P(),
        P(),
        P(),
        P(),
        P(),
        P(),
        P(),
        P(),
        P(),
        P(("grp", "tile")),
        P(("grp", "tile"), None),
        P(("grp", "tile")),
    )
    out_specs = (P(("grp", "tile"), None), P(("grp", "tile"), None))
    return jax.shard_map(body, mesh=mesh, in_specs=in_specs, out_specs=out_specs, check_vma=False)
```

```python
import functools
import math

import jax
import jax.numpy as jnp
from jax import lax
from jax.experimental import pallas as pl
from jax.experimental.pallas import tpu as pltpu
from jax.sharding import PartitionSpec as P

HEADS = 12
WIN = 32
VOX_DEV = 256
LANES = 128
FLAG = 16384.0
PARTS = 2
VMEM = 64 * 1024 * 1024 - 65536
TIGHT = VMEM - 2 * 1024 * 1024
ROOMY = 24 * 1024 * 1024
F32 = jnp.float32
BF16 = jnp.bfloat16
LOG2E = math.log2(math.e)


def iota(shape, dim):
    return lax.broadcasted_iota(jnp.int32, shape, dim)


def dot(a, b):
    return jnp.dot(a, b, preferred_element_type=F32)


def dot_t(a, b):
    return lax.dot_general(a, b, (((1,), (1,)), ((), ())), preferred_element_type=F32)


def eye(n):
    return (iota((n, n), 0) == iota((n, n), 1)).astype(BF16)


def transposed(a):
    return a.astype(F32).T.astype(BF16)


def tile(t):
    return slice(t * LANES, (t + 1) * LANES)


def head_order(chans):
    size = chans // HEADS
    cut = 8 * size
    j = iota((chans, 1), 0)
    high = j - cut
    low_src = (j % 8) * size + j // 8
    high_src = (8 + high % 4) * size + high // 8 + (size // 2) * ((high % 8) // 4)
    return jnp.where(j < cut, low_src, high_src)


def within(run):
    lane = iota((1, LANES), 1)
    q, e = lane // 16, lane % 16
    p = (4 * (q // run) + e // 4) * run + q % run
    return ((e % 4) * WIN + p == iota((LANES, LANES), 0)).astype(BF16)


def swap_blocks(tiles):
    tiles = list(tiles)
    block = iota(tiles[0].shape, 1) // 16
    step = len(tiles) // 2
    while step:
        for n in range(len(tiles)):
            if n & step:
                continue
            a, b = tiles[n], tiles[n + step]
            low = block // step % 2 == 0
            tiles[n] = jnp.where(low, a, pltpu.roll(b, 16 * step, 1))
            tiles[n + step] = jnp.where(low, pltpu.roll(a, LANES - 16 * step, 1), b)
        step //= 2
    return tiles


def place(low, high, blocks):
    base = jnp.where(low == iota((LANES, low.shape[1]), 0), 1.0, 0.0).astype(BF16)
    high = jnp.broadcast_to(high, base.shape).astype(F32).astype(BF16)
    nil = jnp.zeros_like(base)
    parts = [jnp.where(high == jnp.asarray(n, BF16), base, nil) for n in range(blocks)]
    return jnp.concatenate(parts, 0)


def norm_t(x, gain):
    inv = 1.0 / x.shape[0]
    mean = jnp.sum(x, 0, keepdims=True) * inv
    cent = x - mean
    var = jnp.sum(cent * cent, 0, keepdims=True) * inv
    return cent * lax.rsqrt(var + 1e-05) * gain


def gelu(x):
    half = 0.5 * x
    scale = math.sqrt(2 / math.pi)
    return half + half * jnp.tanh(x * (scale + (0.044715 * scale) * (x * x)))


def start_all(pairs, sems):
    copies = [pltpu.make_async_copy(a, b, sems.at[n]) for n, (a, b) in enumerate(pairs)]
    for copy in copies:
        copy.start()
    return copies


def wait_all(copies):
    for copy in copies:
        copy.wait()


def fold8(x, op):
    y = x[0]
    for n in range(1, x.shape[0]):
        y = op(y, x[n])
    for shift in (4, 2, 1):
        y = op(y, pltpu.roll(y, shift, 0))
    return y


def first_kernel(
    run, count_ref, nodes_hbm, ids_hbm, pos_hbm, gain_one_hbm, gain_two_hbm, qkv_hbm, out_hbm,
    first_hbm, *refs
):
    sent_hbm, refs = refs[:PARTS], refs[PARTS:]
    (
        nodes_ref, ids_ref, pos_ref, gain_one_ref, gain_two_ref, qkv_ref, out_ref, sems, qkv_s, q_s,
        k_s, v_s, ctx_s, n_s, first_s, sent_s, stores
    ) = refs
    loads = start_all(
        [
            (nodes_hbm, nodes_ref),
            (ids_hbm, ids_ref),
            (pos_hbm, pos_ref),
            (gain_one_hbm, gain_one_ref),
            (gain_two_hbm, gain_two_ref),
            (qkv_hbm, qkv_ref),
            (out_hbm, out_ref),
        ],
        sems,
    )
    chans, slots = nodes_ref.shape
    tiles = slots // LANES
    size = chans // HEADS
    per = LANES // WIN
    count = count_ref[0]
    wait_all(loads)
    cols = jnp.concatenate(
        [pos_ref[...], gain_one_ref[...], gain_two_ref[...], jnp.zeros((3, chans), F32)], 0
    ).T
    ids = ids_ref[...]
    coords = []
    for axis in range(3):
        total = jnp.zeros(ids.shape, jnp.int32)
        for level in range(6):
            bit = jnp.bitwise_and(jnp.right_shift(ids, 3 * level + axis), 1)
            total = total + bit * 2**level
        coords.append(total.astype(F32) / 64.0 - 0.5)
    for t in range(tiles):
        at = tile(t)
        start = cols[:, 0:1] * coords[0][:, at]
        for axis in range(1, 3):
            start = start + cols[:, axis : axis + 1] * coords[axis][:, at]
        start = (nodes_ref[:, at].astype(F32) + start).astype(BF16)
        nodes_ref[:, at] = start
        n_s[:, at] = norm_t(start.astype(F32), cols[:, 3:4]).astype(BF16)
    qkv_t = transposed(qkv_ref[...])
    out_t = transposed(out_ref[...])
    qkv_s[...] = dot(qkv_t, n_s[...]).astype(BF16)
    side = eye(LANES)
    row_head = iota((chans, LANES), 0) // size
    even_row = row_head % 2 == 0
    for t in range(tiles):
        query = qkv_s[:chans, tile(t)].astype(F32) * size**-0.5
        q_s[t, :, :LANES] = jnp.where(even_row, query, 0.0).astype(BF16)
        q_s[t, :, LANES:] = jnp.where(even_row, 0.0, query).astype(BF16)
        k_s[t] = dot_t(side, qkv_s[chans : 2 * chans, tile(t)]).astype(BF16)
        v_s[t] = qkv_s[2 * chans :, tile(t)]

    lane_pair = iota((WIN, chans), 1) // (2 * size)
    window = iota((8, LANES), 1) // WIN
    wide_window = iota((WIN, LANES), 1) // WIN
    rank = iota((WIN, LANES), 0) + WIN * (iota((WIN, LANES), 1) // WIN)

    def group(t, _):
        query = q_s[t]
        even, odd = None, None
        for w in range(per):
            keys = k_s[t, w * WIN : (w + 1) * WIN, :]
            by_pair = jnp.concatenate(
                [jnp.where(lane_pair == m, keys, jnp.zeros_like(keys)) for m in range(HEADS // 2)],
                0,
            )
            got = dot(by_pair, query)
            left = got[:, :LANES].reshape(-1, 8, LANES)
            right = got[:, LANES:].reshape(-1, 8, LANES)
            even = left if w == 0 else jnp.where(window[None] == w, left, even)
            odd = right if w == 0 else jnp.where(window[None] == w, right, odd)
        mask = jnp.where(rank + t * LANES < count, 0.0, -1e9).astype(F32)
        mask = mask.reshape(WIN // 8, 8, LANES)
        probs, inverse = [], []
        for h in range(HEADS):
            scores = (even, odd)[h % 2]
            mine = scores[h // 2 * (WIN // 8) : (h // 2 + 1) * (WIN // 8)] + mask
            top = fold8(mine, jnp.maximum)
            weight = jnp.exp(mine - top[None])
            inverse.append(1.0 / fold8(weight, jnp.add))
            probs.append(weight.reshape(WIN, LANES).astype(BF16))
        parts = []
        for m in range(HEADS // 2):
            both = []
            for h in (2 * m, 2 * m + 1):
                nil = jnp.zeros_like(probs[h])
                both.append(
                    jnp.concatenate(
                        [jnp.where(wide_window == w, probs[h], nil) for w in range(per)], 0
                    )
                )
            rows = slice(2 * m * size, 2 * (m + 1) * size)
            got = dot(v_s[t, rows, :], jnp.concatenate(both, 1))
            for n in range(2):
                block = got[n * size : (n + 1) * size, tile(n)].reshape(-1, 8, LANES)
                block = block * inverse[2 * m + n][None]
                parts.append(block.reshape(size, LANES))
        ctx_s[t] = jnp.concatenate(parts, 0).astype(BF16)
        return 0

    lax.fori_loop(0, tiles, group, 0, unroll=4)
    ctx = jnp.concatenate([ctx_s[t] for t in range(tiles)], 1)
    moved = dot(out_t, ctx)
    for t in range(tiles):
        at = tile(t)
        first = (nodes_ref[:, at].astype(F32) + moved[:, at]).astype(BF16)
        first_s[:, at] = first
        normed = norm_t(first.astype(F32), cols[:, 4:5])
        kept = iota((1, LANES), 1) + t * LANES < count
        head = jnp.where((iota((16, LANES), 0) > 0) | kept, normed[:16], FLAG)
        n_s[:, at] = jnp.concatenate([head, normed[16:]], 0).astype(BF16)
    keep_first = pltpu.make_async_copy(first_s, first_hbm, stores.at[0])
    keep_first.start()
    inside = within(run)
    for t, block in enumerate(swap_blocks([dot(n_s[:, tile(t)], inside) for t in range(tiles)])):
        sent_s[t * PARTS // tiles, :, tile(t % (tiles // PARTS))] = block.astype(BF16)
    send = [
        pltpu.make_async_copy(sent_s.at[n], sent_hbm[n], stores.at[1 + n]) for n in range(PARTS)
    ]
    for copy in send:
        copy.start()
    wait_all([keep_first] + send)


def tables_kernel(
    cap, qkv_hbm, out_hbm, up_hbm, slot_hbm, owner_hbm, voxel_hbm, gain_hbm, weights_s, facts_s,
    gain_s, qkv_ref, out_ref, up_ref, slot_ref, owner_ref, voxel_ref, gain_ref, sems
):
    loads = start_all(
        [
            (qkv_hbm, qkv_ref),
            (out_hbm, out_ref),
            (up_hbm, up_ref),
            (slot_hbm, slot_ref),
            (owner_hbm, owner_ref),
            (voxel_hbm, voxel_ref),
            (gain_hbm, gain_ref),
        ],
        sems,
    )
    wait_all(loads)
    gain = jnp.concatenate([gain_ref[...], jnp.zeros((7, gain_ref.shape[1]), F32)], 0)
    gain_s[...] = jnp.broadcast_to(gain.T[:, 0:1], gain_s.shape)
    votes = slot_ref.shape[1]
    codes = facts_s.shape[1]
    owners = codes // cap
    chans = out_ref.shape[0]
    src = head_order(chans)
    src = jnp.concatenate([src, src + chans, src + 2 * chans], 0)
    shuffle = (src == iota((3 * chans, 3 * chans), 1)).astype(BF16)
    weights_s[: 3 * chans] = dot_t(shuffle, qkv_ref[...]).astype(BF16)
    out_t = dot(shuffle[:chans, :chans], out_ref[...])
    weights_s[3 * chans : 4 * chans] = transposed(out_t)
    weights_s[4 * chans :] = transposed(up_ref[...])
    owner = jnp.bitwise_xor(owner_ref[...], lax.axis_index("tile"))
    hot = owner == iota((owners, votes), 0)
    upto = (iota((votes, votes), 0) <= iota((votes, votes), 1)).astype(BF16)
    rank = jnp.sum(jnp.where(hot, dot(hot.astype(BF16), upto), 0.0), 0, keepdims=True)
    code = owner * cap + rank.astype(jnp.int32) - 1
    member = place(code % LANES, code // LANES, codes // LANES)
    slot = slot_ref[...]
    row = iota((16, votes), 0)
    facts = jnp.where(
        row == 0,
        voxel_ref[...],
        jnp.where(row == 1, slot // LANES, jnp.where(row == 2, slot % LANES, 1)),
    )
    listed = dot_t(facts.astype(F32).astype(BF16), member)
    facts_s[...] = jnp.where(listed[3:4] > 0.5, listed, -1.0).astype(BF16)


def clean(block):
    head = block[:16].astype(F32)
    gone = head[0:1] > 0.5 * FLAG
    head = jnp.where((iota(head.shape, 0) == 0) & gone, 0.0, head)
    return jnp.concatenate([head.astype(BF16), block[16:]], 0), gone


def add_keys(blocks, kv_t, k_s, v_s, m_s):
    chans = kv_t.shape[1]
    tiles = k_s.shape[1] // PARTS
    for n, part in enumerate(blocks):
        block, gone = clean(part[...])
        kv = dot(kv_t, block)
        mask = jnp.where(gone, -1e9, 0.0)
        n, start = n // PARTS, n % PARTS * tiles
        for t in range(tiles):
            k_s[n, start + t] = kv[:chans, tile(t)].reshape(chans // 8, 8, LANES)
            v_s[n, start + t] = kv[chans:, tile(t)].reshape(chans // 8, 8, LANES)
            m_s[n, start + t] = jnp.broadcast_to(mask[:, tile(t)], (8, LANES))


def attend_two(t, run, q_s, k_s, v_s, m_s, s_s, state_s, fresh):
    rows8 = q_s.shape[1]
    cut = 2 * rows8 // 3
    keys = k_s.shape[0] * run
    base = (t // run) * run
    both = range(2)
    query = [[q_s[t + n, i] for i in range(rows8)] for n in both]

    def score(key, top):
        block, at = key // run, base + key % run
        mask = m_s[block, at]
        sums = [[None, None], [None, None]]
        for i in range(rows8):
            part = int(i >= cut)
            row = k_s[block, at, i]
            for n in both:
                term = query[n][i] * row
                held = sums[n][part]
                sums[n][part] = term if held is None else held + term
        tops = []
        for n in both:
            a, b = sums[n]
            b = b + pltpu.roll(b, 4, 0)
            a = a + mask
            b = b + mask
            s_s[key, 2 * n] = a
            s_s[key, 2 * n + 1] = b
            tops += [jnp.maximum(top[2 * n], a), jnp.maximum(top[2 * n + 1], b)]
        return tuple(tops)

    if fresh:
        old = tuple(jnp.full((8, LANES), -3e38, F32) for _ in range(4))
    else:
        old = tuple(state_s[t + n, rows8 + part] for n in both for part in both)
    tops = lax.fori_loop(0, keys, score, old, unroll=2)
    if fresh:
        zero = jnp.zeros((8, LANES), F32)
        sums = tuple(zero for _ in range(4))
        accs = tuple(zero for _ in range(2 * rows8))
    else:
        fade = [jnp.exp2(old[n] - tops[n]) for n in range(4)]
        sums = tuple(
            state_s[t + n, rows8 + 2 + part] * fade[2 * n + part] for n in both for part in both
        )
        accs = tuple(
            state_s[t + n, i] * fade[2 * n + int(i >= cut)] for n in both for i in range(rows8)
        )

    def gather(key, carry):
        sums, accs = carry
        block, at = key // run, base + key % run
        weight = [jnp.exp2(s_s[key, n] - tops[n]) for n in range(4)]
        accs = list(accs)
        for i in range(rows8):
            row = v_s[block, at, i]
            for n in both:
                at_acc = n * rows8 + i
                accs[at_acc] = accs[at_acc] + weight[2 * n + int(i >= cut)] * row
        return tuple(sums[n] + weight[n] for n in range(4)), tuple(accs)

    sums, accs = lax.fori_loop(0, keys, gather, (sums, accs), unroll=2)
    return tops, sums, accs


def hold_two(n, state, state_s):
    tops, sums, accs = state
    rows8 = len(accs) // 2
    for m in range(2):
        for i in range(rows8):
            state_s[2 * n + m, i] = accs[m * rows8 + i]
        for part in range(2):
            state_s[2 * n + m, rows8 + part] = tops[2 * m + part]
            state_s[2 * n + m, rows8 + 2 + part] = sums[2 * m + part]


def near_kernel(run, *refs):
    blocks, refs = refs[: 2 * PARTS], refs[2 * PARTS :]
    weights_ref, q_s, state_s, k_s, v_s, m_s, s_s = refs
    chans = weights_ref.shape[1]
    tiles = q_s.shape[0]
    scale = (chans // HEADS) ** -0.5 * LOG2E
    for n in range(PARTS):
        own, _ = clean(blocks[n][...])
        query = dot(weights_ref[:chans, :], own) * scale
        for t in range(tiles // PARTS):
            q_s[n * tiles // PARTS + t] = query[:, tile(t)].reshape(chans // 8, 8, LANES)
    add_keys(blocks, weights_ref[chans : 3 * chans, :], k_s, v_s, m_s)

    def step(n, _):
        hold_two(n, attend_two(2 * n, run, q_s, k_s, v_s, m_s, s_s, state_s, True), state_s)
        return 0

    lax.fori_loop(0, tiles // 2, step, 0)


def middle_kernel(run, count, *refs):
    blocks, refs = refs[:count], refs[count:]
    q_s, old_s, weights_ref, state_s, k_s, v_s, m_s, s_s = refs
    chans = weights_ref.shape[1]
    kv_t = weights_ref[chans : 3 * chans, :]
    add_keys(blocks, kv_t, k_s, v_s, m_s)

    def step(n, _):
        hold_two(n, attend_two(2 * n, run, q_s, k_s, v_s, m_s, s_s, old_s, False), state_s)
        return 0

    lax.fori_loop(0, q_s.shape[0] // 2, step, 0)


def second_kernel(run, cap, far, owners, count_ref, *refs):
    blocks, refs = refs[:far], refs[far:]
    q_s, state_s, weights_s, first_s, gain_s, down_s, facts_s, feat_hbm = refs[:8]
    votes_s, refs = refs[8 : 8 + owners], refs[8 + owners :]
    feat_s, store, k_s, v_s, m_s, s_s, ctx_s, bf_s, inner_s = refs
    chans, slots = first_s.shape
    tiles = slots // LANES
    count = count_ref[0]
    add_keys(blocks, weights_s[chans : 3 * chans], k_s, v_s, m_s)
    rows8 = chans // 8

    def step(n, _):
        t = 2 * n
        _, sums, accs = attend_two(t, run, q_s, k_s, v_s, m_s, s_s, state_s, False)
        share = [1.0 / total for total in sums]
        cut = 2 * rows8 // 3
        for n in range(2):
            for i in range(rows8):
                ctx_s[t + n, i] = accs[n * rows8 + i] * share[2 * n + int(i >= cut)]
        return 0

    lax.fori_loop(0, tiles // 2, step, 0)
    ctx = swap_blocks([ctx_s[t].reshape(chans, LANES) for t in range(tiles)])
    ctx = dot_t(jnp.concatenate(ctx, 0).astype(BF16), within(run)).astype(BF16)
    ctx = jnp.concatenate([ctx[t * chans : (t + 1) * chans] for t in range(tiles)], 1)
    gain = gain_s[...]
    moved = dot(weights_s[3 * chans : 4 * chans], ctx)
    for t in range(tiles):
        at = tile(t)
        second = first_s[:, at].astype(F32) + moved[:, at]
        feat_s[:, at] = second
        inner_s[:, at] = norm_t(second, gain).astype(BF16)
    kept = iota((1, slots), 1) < count
    wide = 2 * LANES
    cuts = [slice(at, at + wide) for at in range(0, slots, wide)]
    up_t = weights_s[4 * chans :]
    raised = dot(up_t, inner_s[:, cuts[0]])
    for n, at in enumerate(cuts):
        now = raised
        if n + 1 < len(cuts):
            raised = dot(up_t, inner_s[:, cuts[n + 1]])
        hidden = gelu(now).astype(BF16)
        third = feat_s[:, at] + dot(down_s[...], hidden)
        third = jnp.where(kept[:, at], third, 0.0)
        feat_s[:, at] = third
        bf_s[:, at] = third.astype(BF16)
    keep = pltpu.make_async_copy(feat_s, feat_hbm, store)
    keep.start()
    facts = facts_s[...].astype(F32)
    low, high = facts[2:3].astype(jnp.int32), facts[1:2].astype(jnp.int32)
    picked = dot(bf_s[...], place(low, high, tiles)).astype(BF16)
    for o in range(owners):
        votes_s[o][:chans, :] = picked[:, o * cap : (o + 1) * cap]
        votes_s[o][chans:, :] = facts_s[:, o * cap : (o + 1) * cap]
    keep.wait()


def sums_kernel(*refs):
    got, out_ref = refs[:-1], refs[-1]
    chans, voxels = out_ref.shape
    cap = got[0].shape[1]
    total = jnp.zeros(out_ref.shape, F32)
    for ref in got:
        label = ref[chans:, :].astype(F32)[0:1]
        hot = (label == iota((voxels, cap), 0).astype(F32)).astype(BF16)
        total = total + dot_t(ref[:chans, :], hot)
    out_ref[...] = total


def call(kernel, outs, scratch, flops, spaces, out_spaces, limit=VMEM):
    place_of = {"s": pltpu.SMEM, "v": pltpu.VMEM, "a": pl.ANY}
    return pl.pallas_call(
        kernel,
        out_shape=outs,
        in_specs=[pl.BlockSpec(memory_space=place_of[c]) for c in spaces],
        out_specs=[pl.BlockSpec(memory_space=place_of[c]) for c in out_spaces],
        scratch_shapes=scratch,
        compiler_params=pltpu.CompilerParams(vmem_limit_bytes=limit),
        cost_estimate=pl.CostEstimate(flops=flops, bytes_accessed=2 << 20, transcendentals=0),
    )


def turned(x, axis, bit):
    n = lax.axis_size(axis)
    return lax.ppermute(x, axis, [(i, i ^ bit) for i in range(n)])


def body(
    nodes,
    node_ids,
    node_count,
    pos_weight,
    gain_one,
    qkv_one,
    out_one,
    gain_two,
    qkv_two,
    out_two,
    gain_three,
    w_up,
    w_down,
    vote_slot,
    vote_owner,
    vote_voxel,
):
    slots, chans = nodes.shape
    groups, owners = lax.axis_size("grp"), lax.axis_size("tile")
    run = WIN // groups
    votes = vote_slot.shape[0]
    cap = 2 * votes // owners
    codes = owners * cap
    tiles = slots // LANES
    rows8 = chans // 8
    hidden = w_up.shape[1]
    per = LANES // WIN
    sds = jax.ShapeDtypeStruct
    vmem = pltpu.VMEM
    dma = pltpu.SemaphoreType.DMA

    first, *sent = call(
        functools.partial(first_kernel, run),
        [sds((chans, slots), BF16)] + [sds((chans, slots // PARTS), BF16)] * PARTS,
        [
            vmem((chans, slots), BF16),
            vmem((1, slots), jnp.int32),
            vmem((3, chans), F32),
            vmem((1, chans), F32),
            vmem((1, chans), F32),
            vmem((chans, 3 * chans), BF16),
            vmem((chans, chans), BF16),
            dma((7,)),
            vmem((3 * chans, slots), BF16),
            vmem((tiles, chans, 2 * LANES), BF16),
            vmem((tiles, LANES, chans), BF16),
            vmem((tiles, chans, LANES), BF16),
            vmem((tiles, chans, LANES), BF16),
            vmem((chans, slots), BF16),
            vmem((chans, slots), BF16),
            vmem((PARTS, chans, slots // PARTS), BF16),
            dma((1 + PARTS,)),
        ],
        2_000_000_000,
        "saaaaaaa",
        "a" * (1 + PARTS),
    )(
        node_count,
        nodes.T,
        node_ids.reshape(1, slots),
        pos_weight,
        gain_one.reshape(1, chans),
        gain_two.reshape(1, chans),
        qkv_one,
        out_one,
    )
    bit = groups // 2
    mid = []
    while bit > 1:
        mid += [turned(part, "grp", bit) for part in sent + mid]
        bit //= 2
    near = [turned(part, "grp", 1) for part in sent]
    weights, facts, gain = call(
        functools.partial(tables_kernel, cap),
        [
            sds((4 * chans + hidden, chans), BF16),
            sds((16, codes), BF16),
            sds((chans, LANES), F32),
        ],
        [
            vmem((chans, 3 * chans), BF16),
            vmem((chans, chans), BF16),
            vmem((chans, hidden), BF16),
            vmem((1, votes), jnp.int32),
            vmem((1, votes), jnp.int32),
            vmem((1, votes), jnp.int32),
            vmem((1, chans), F32),
            dma((7,)),
        ],
        2_000_000_000,
        "aaaaaaa",
        "vvv",
        limit=TIGHT,
    )(
        qkv_two,
        out_two,
        w_up,
        vote_slot.reshape(1, votes),
        vote_owner.reshape(1, votes),
        vote_voxel.reshape(1, votes),
        gain_three.reshape(1, chans),
    )
    q_like = ((tiles, rows8, 8, LANES), F32)
    state_like = ((tiles, rows8 + 4, 8, LANES), F32)

    def key_scratch(blocks):
        return [
            vmem((blocks, tiles, rows8, 8, LANES), F32),
            vmem((blocks, tiles, rows8, 8, LANES), F32),
            vmem((blocks, tiles, 8, LANES), F32),
            vmem((blocks * run, 4, 8, LANES), F32),
        ]

    query, state = call(
        functools.partial(near_kernel, run),
        [sds(*q_like), sds(*state_like)],
        key_scratch(2),
        3_000_000_000,
        "v" * (2 * PARTS + 1),
        "vv",
        limit=ROOMY,
    )(*sent, *near, weights)
    mid, query = lax.optimization_barrier((mid, query))
    far = [turned(part, "grp", 1) for part in mid]
    (state,) = call(
        functools.partial(middle_kernel, run, len(mid)),
        [sds(*state_like)],
        key_scratch(len(mid) // PARTS),
        2_000_000_000,
        "v" * len(mid) + "vvv",
        "v",
        limit=ROOMY,
    )(*mid, query, state, weights)
    features_t, *ballots = call(
        functools.partial(second_kernel, run, cap, len(far), owners),
        [sds((chans, slots), F32)] + [sds((chans + 16, cap), BF16)] * owners,
        [vmem((chans, slots), F32), dma]
        + key_scratch(len(far) // PARTS)
        + [vmem(*q_like), vmem((chans, slots), BF16), vmem((chans, slots), BF16)],
        3_000_000_000,
        "s" + "v" * (len(far) + 7),
        "a" + "v" * owners,
        limit=ROOMY,
    )(
        node_count,
        *far,
        query,
        state,
        weights,
        first,
        gain,
        w_down.T,
        facts,
    )
    got = [ballots[0]] + [turned(ballots[k], "tile", k) for k in [1] + list(range(owners - 1, 1, -1))]
    (sums_t,) = call(
        sums_kernel,
        [sds((chans, VOX_DEV), F32)],
        [],
        200_000_000,
        "v" * owners,
        "v",
        limit=ROOMY,
    )(*got)
    return (features_t.T, sums_t.T)


def solution(mesh):
    in_specs = (
        P(("grp", "tile"), None),
        P(("grp", "tile")),
        P(("grp", "tile")),
        P(),
        P(),
        P(),
        P(),
        P(),
        P(),
        P(),
        P(),
        P(),
        P(),
        P(("grp", "tile")),
        P(("grp", "tile"), None),
        P(("grp", "tile")),
    )
    out_specs = (P(("grp", "tile"), None), P(("grp", "tile"), None))
    return jax.shard_map(body, mesh=mesh, in_specs=in_specs, out_specs=out_specs, check_vma=False)
```

```python
import functools
import math

import jax
import jax.numpy as jnp
from jax import lax
from jax.experimental import pallas as pl
from jax.experimental.pallas import tpu as pltpu
from jax.sharding import PartitionSpec as P

HEADS = 12
WIN = 32
VOX_DEV = 256
LANES = 128
FLAG = 16384.0
VMEM = 64 * 1024 * 1024 - 65536
TIGHT = VMEM - 2 * 1024 * 1024
ROOMY = 24 * 1024 * 1024
F32 = jnp.float32
BF16 = jnp.bfloat16
LOG2E = math.log2(math.e)


def iota(shape, dim):
    return lax.broadcasted_iota(jnp.int32, shape, dim)


def dot(a, b):
    return jnp.dot(a, b, preferred_element_type=F32)


def dot_t(a, b):
    return lax.dot_general(a, b, (((1,), (1,)), ((), ())), preferred_element_type=F32)


def eye(n):
    return (iota((n, n), 0) == iota((n, n), 1)).astype(BF16)


def transposed(a):
    return a.astype(F32).T.astype(BF16)


def tile(t):
    return slice(t * LANES, (t + 1) * LANES)


def head_order(chans):
    size = chans // HEADS
    cut = 8 * size
    j = iota((chans, 1), 0)
    high = j - cut
    low_src = (j % 8) * size + j // 8
    high_src = (8 + high % 4) * size + high // 8 + (size // 2) * ((high % 8) // 4)
    return jnp.where(j < cut, low_src, high_src)


def within(run):
    lane = iota((1, LANES), 1)
    q, e = lane // 16, lane % 16
    p = (4 * (q // run) + e // 4) * run + q % run
    return ((e % 4) * WIN + p == iota((LANES, LANES), 0)).astype(BF16)


def swap_blocks(tiles):
    tiles = list(tiles)
    block = iota(tiles[0].shape, 1) // 16
    step = len(tiles) // 2
    while step:
        for n in range(len(tiles)):
            if n & step:
                continue
            a, b = tiles[n], tiles[n + step]
            low = block // step % 2 == 0
            tiles[n] = jnp.where(low, a, pltpu.roll(b, 16 * step, 1))
            tiles[n + step] = jnp.where(low, pltpu.roll(a, LANES - 16 * step, 1), b)
        step //= 2
    return tiles


def place(low, high, blocks):
    base = jnp.where(low == iota((LANES, low.shape[1]), 0), 1.0, 0.0).astype(BF16)
    high = jnp.broadcast_to(high, base.shape).astype(F32).astype(BF16)
    nil = jnp.zeros_like(base)
    parts = [jnp.where(high == jnp.asarray(n, BF16), base, nil) for n in range(blocks)]
    return jnp.concatenate(parts, 0)


def norm_t(x, gain):
    inv = 1.0 / x.shape[0]
    mean = jnp.sum(x, 0, keepdims=True) * inv
    cent = x - mean
    var = jnp.sum(cent * cent, 0, keepdims=True) * inv
    return cent * lax.rsqrt(var + 1e-05) * gain


def gelu(x):
    half = 0.5 * x
    scale = math.sqrt(2 / math.pi)
    return half + half * jnp.tanh(x * (scale + (0.044715 * scale) * (x * x)))


def start_all(pairs, sems):
    copies = [pltpu.make_async_copy(a, b, sems.at[n]) for n, (a, b) in enumerate(pairs)]
    for copy in copies:
        copy.start()
    return copies


def wait_all(copies):
    for copy in copies:
        copy.wait()


def fold8(x, op):
    y = x[0]
    for n in range(1, x.shape[0]):
        y = op(y, x[n])
    for shift in (4, 2, 1):
        y = op(y, pltpu.roll(y, shift, 0))
    return y


def first_kernel(
    run, count_ref, nodes_hbm, ids_hbm, pos_hbm, gain_one_hbm, gain_two_hbm, qkv_hbm, out_hbm,
    first_hbm, sent_hbm, nodes_ref, ids_ref, pos_ref, gain_one_ref, gain_two_ref, qkv_ref, out_ref,
    sems, qkv_s, q_s, k_s, v_s, ctx_s, n_s, first_s, sent_s, stores
):
    loads = start_all(
        [
            (nodes_hbm, nodes_ref),
            (ids_hbm, ids_ref),
            (pos_hbm, pos_ref),
            (gain_one_hbm, gain_one_ref),
            (gain_two_hbm, gain_two_ref),
            (qkv_hbm, qkv_ref),
            (out_hbm, out_ref),
        ],
        sems,
    )
    chans, slots = nodes_ref.shape
    tiles = slots // LANES
    size = chans // HEADS
    per = LANES // WIN
    count = count_ref[0]
    wait_all(loads)
    cols = jnp.concatenate(
        [pos_ref[...], gain_one_ref[...], gain_two_ref[...], jnp.zeros((3, chans), F32)], 0
    ).T
    ids = ids_ref[...]
    coords = []
    for axis in range(3):
        total = jnp.zeros(ids.shape, jnp.int32)
        for level in range(6):
            bit = jnp.bitwise_and(jnp.right_shift(ids, 3 * level + axis), 1)
            total = total + bit * 2**level
        coords.append(total.astype(F32) / 64.0 - 0.5)
    for t in range(tiles):
        at = tile(t)
        start = cols[:, 0:1] * coords[0][:, at]
        for axis in range(1, 3):
            start = start + cols[:, axis : axis + 1] * coords[axis][:, at]
        start = (nodes_ref[:, at].astype(F32) + start).astype(BF16)
        nodes_ref[:, at] = start
        n_s[:, at] = norm_t(start.astype(F32), cols[:, 3:4]).astype(BF16)
    qkv_t = transposed(qkv_ref[...])
    out_t = transposed(out_ref[...])
    qkv_s[...] = dot(qkv_t, n_s[...]).astype(BF16)
    side = eye(LANES)
    row_head = iota((chans, LANES), 0) // size
    even_row = row_head % 2 == 0
    for t in range(tiles):
        query = qkv_s[:chans, tile(t)].astype(F32) * size**-0.5
        q_s[t, :, :LANES] = jnp.where(even_row, query, 0.0).astype(BF16)
        q_s[t, :, LANES:] = jnp.where(even_row, 0.0, query).astype(BF16)
        k_s[t] = dot_t(side, qkv_s[chans : 2 * chans, tile(t)]).astype(BF16)
        v_s[t] = qkv_s[2 * chans :, tile(t)]

    lane_pair = iota((WIN, chans), 1) // (2 * size)
    window = iota((8, LANES), 1) // WIN
    wide_window = iota((WIN, LANES), 1) // WIN
    rank = iota((WIN, LANES), 0) + WIN * (iota((WIN, LANES), 1) // WIN)

    def group(t, _):
        query = q_s[t]
        even, odd = None, None
        for w in range(per):
            keys = k_s[t, w * WIN : (w + 1) * WIN, :]
            by_pair = jnp.concatenate(
                [jnp.where(lane_pair == m, keys, jnp.zeros_like(keys)) for m in range(HEADS // 2)],
                0,
            )
            got = dot(by_pair, query)
            left = got[:, :LANES].reshape(-1, 8, LANES)
            right = got[:, LANES:].reshape(-1, 8, LANES)
            even = left if w == 0 else jnp.where(window[None] == w, left, even)
            odd = right if w == 0 else jnp.where(window[None] == w, right, odd)
        mask = jnp.where(rank + t * LANES < count, 0.0, -1e9).astype(F32)
        mask = mask.reshape(WIN // 8, 8, LANES)
        probs, inverse = [], []
        for h in range(HEADS):
            scores = (even, odd)[h % 2]
            mine = scores[h // 2 * (WIN // 8) : (h // 2 + 1) * (WIN // 8)] + mask
            top = fold8(mine, jnp.maximum)
            weight = jnp.exp(mine - top[None])
            inverse.append(1.0 / fold8(weight, jnp.add))
            probs.append(weight.reshape(WIN, LANES).astype(BF16))
        parts = []
        for m in range(HEADS // 2):
            both = []
            for h in (2 * m, 2 * m + 1):
                nil = jnp.zeros_like(probs[h])
                both.append(
                    jnp.concatenate(
                        [jnp.where(wide_window == w, probs[h], nil) for w in range(per)], 0
                    )
                )
            rows = slice(2 * m * size, 2 * (m + 1) * size)
            got = dot(v_s[t, rows, :], jnp.concatenate(both, 1))
            for n in range(2):
                block = got[n * size : (n + 1) * size, tile(n)].reshape(-1, 8, LANES)
                block = block * inverse[2 * m + n][None]
                parts.append(block.reshape(size, LANES))
        ctx_s[t] = jnp.concatenate(parts, 0).astype(BF16)
        return 0

    lax.fori_loop(0, tiles, group, 0, unroll=8)
    ctx = jnp.concatenate([ctx_s[t] for t in range(tiles)], 1)
    moved = dot(out_t, ctx)
    for t in range(tiles):
        at = tile(t)
        first = (nodes_ref[:, at].astype(F32) + moved[:, at]).astype(BF16)
        first_s[:, at] = first
        normed = norm_t(first.astype(F32), cols[:, 4:5])
        kept = iota((1, LANES), 1) + t * LANES < count
        head = jnp.where((iota((16, LANES), 0) > 0) | kept, normed[:16], FLAG)
        n_s[:, at] = jnp.concatenate([head, normed[16:]], 0).astype(BF16)
    keep_first = pltpu.make_async_copy(first_s, first_hbm, stores.at[0])
    keep_first.start()
    inside = within(run)
    for t, block in enumerate(swap_blocks([dot(n_s[:, tile(t)], inside) for t in range(tiles)])):
        sent_s[:, tile(t)] = block.astype(BF16)
    send = pltpu.make_async_copy(sent_s, sent_hbm, stores.at[1])
    send.start()
    wait_all([keep_first, send])


def tables_kernel(
    cap, qkv_hbm, out_hbm, up_hbm, slot_hbm, owner_hbm, voxel_hbm, gain_hbm, weights_s, facts_s,
    gain_s, qkv_ref, out_ref, up_ref, slot_ref, owner_ref, voxel_ref, gain_ref, sems
):
    loads = start_all(
        [
            (qkv_hbm, qkv_ref),
            (out_hbm, out_ref),
            (up_hbm, up_ref),
            (slot_hbm, slot_ref),
            (owner_hbm, owner_ref),
            (voxel_hbm, voxel_ref),
            (gain_hbm, gain_ref),
        ],
        sems,
    )
    wait_all(loads)
    gain = jnp.concatenate([gain_ref[...], jnp.zeros((7, gain_ref.shape[1]), F32)], 0)
    gain_s[...] = jnp.broadcast_to(gain.T[:, 0:1], gain_s.shape)
    votes = slot_ref.shape[1]
    codes = facts_s.shape[1]
    owners = codes // cap
    chans = out_ref.shape[0]
    src = head_order(chans)
    src = jnp.concatenate([src, src + chans, src + 2 * chans], 0)
    shuffle = (src == iota((3 * chans, 3 * chans), 1)).astype(BF16)
    weights_s[: 3 * chans] = dot_t(shuffle, qkv_ref[...]).astype(BF16)
    out_t = dot(shuffle[:chans, :chans], out_ref[...])
    weights_s[3 * chans : 4 * chans] = transposed(out_t)
    weights_s[4 * chans :] = transposed(up_ref[...])
    owner = jnp.bitwise_xor(owner_ref[...], lax.axis_index("tile"))
    hot = owner == iota((owners, votes), 0)
    upto = (iota((votes, votes), 0) <= iota((votes, votes), 1)).astype(BF16)
    rank = jnp.sum(jnp.where(hot, dot(hot.astype(BF16), upto), 0.0), 0, keepdims=True)
    code = owner * cap + rank.astype(jnp.int32) - 1
    member = place(code % LANES, code // LANES, codes // LANES)
    slot = slot_ref[...]
    row = iota((16, votes), 0)
    facts = jnp.where(
        row == 0,
        voxel_ref[...],
        jnp.where(row == 1, slot // LANES, jnp.where(row == 2, slot % LANES, 1)),
    )
    listed = dot_t(facts.astype(F32).astype(BF16), member)
    facts_s[...] = jnp.where(listed[3:4] > 0.5, listed, -1.0).astype(BF16)


def clean(block):
    head = block[:16].astype(F32)
    gone = head[0:1] > 0.5 * FLAG
    head = jnp.where((iota(head.shape, 0) == 0) & gone, 0.0, head)
    return jnp.concatenate([head.astype(BF16), block[16:]], 0), gone


def add_keys(blocks, kv_t, k_s, v_s, m_s):
    chans = kv_t.shape[1]
    tiles = k_s.shape[1]
    for n, block in enumerate(blocks):
        block, gone = clean(block)
        kv = dot(kv_t, block)
        mask = jnp.where(gone, -1e9, 0.0)
        for t in range(tiles):
            k_s[n, t] = kv[:chans, tile(t)].reshape(chans // 8, 8, LANES)
            v_s[n, t] = kv[chans:, tile(t)].reshape(chans // 8, 8, LANES)
            m_s[n, t] = jnp.broadcast_to(mask[:, tile(t)], (8, LANES))


def attend_two(t, run, q_s, k_s, v_s, m_s, s_s, state_s, fresh):
    rows8 = q_s.shape[1]
    cut = 2 * rows8 // 3
    keys = k_s.shape[0] * run
    base = (t // run) * run
    both = range(2)
    query = [[q_s[t + n, i] for i in range(rows8)] for n in both]

    def score(key, top):
        block, at = key // run, base + key % run
        mask = m_s[block, at]
        sums = [[None, None], [None, None]]
        for i in range(rows8):
            part = int(i >= cut)
            row = k_s[block, at, i]
            for n in both:
                term = query[n][i] * row
                held = sums[n][part]
                sums[n][part] = term if held is None else held + term
        tops = []
        for n in both:
            a, b = sums[n]
            b = b + pltpu.roll(b, 4, 0)
            a = a + mask
            b = b + mask
            s_s[key, 2 * n] = a
            s_s[key, 2 * n + 1] = b
            tops += [jnp.maximum(top[2 * n], a), jnp.maximum(top[2 * n + 1], b)]
        return tuple(tops)

    if fresh:
        old = tuple(jnp.full((8, LANES), -3e38, F32) for _ in range(4))
    else:
        old = tuple(state_s[t + n, rows8 + part] for n in both for part in both)
    tops = lax.fori_loop(0, keys, score, old, unroll=4)
    if fresh:
        zero = jnp.zeros((8, LANES), F32)
        sums = tuple(zero for _ in range(4))
        accs = tuple(zero for _ in range(2 * rows8))
    else:
        fade = [jnp.exp2(old[n] - tops[n]) for n in range(4)]
        sums = tuple(
            state_s[t + n, rows8 + 2 + part] * fade[2 * n + part] for n in both for part in both
        )
        accs = tuple(
            state_s[t + n, i] * fade[2 * n + int(i >= cut)] for n in both for i in range(rows8)
        )

    def gather(key, carry):
        sums, accs = carry
        block, at = key // run, base + key % run
        weight = [jnp.exp2(s_s[key, n] - tops[n]) for n in range(4)]
        accs = list(accs)
        for i in range(rows8):
            row = v_s[block, at, i]
            for n in both:
                at_acc = n * rows8 + i
                accs[at_acc] = accs[at_acc] + weight[2 * n + int(i >= cut)] * row
        return tuple(sums[n] + weight[n] for n in range(4)), tuple(accs)

    sums, accs = lax.fori_loop(0, keys, gather, (sums, accs), unroll=4)
    return tops, sums, accs


def hold_two(n, state, state_s):
    tops, sums, accs = state
    rows8 = len(accs) // 2
    for m in range(2):
        for i in range(rows8):
            state_s[2 * n + m, i] = accs[m * rows8 + i]
        for part in range(2):
            state_s[2 * n + m, rows8 + part] = tops[2 * m + part]
            state_s[2 * n + m, rows8 + 2 + part] = sums[2 * m + part]


def near_kernel(run, own_ref, near_ref, weights_ref, q_s, state_s, k_s, v_s, m_s, s_s):
    chans, slots = own_ref.shape
    tiles = slots // LANES
    scale = (chans // HEADS) ** -0.5 * LOG2E
    own, _ = clean(own_ref[...])
    query = dot(weights_ref[:chans, :], own) * scale
    for t in range(tiles):
        q_s[t] = query[:, tile(t)].reshape(chans // 8, 8, LANES)
    add_keys([own_ref[...], near_ref[...]], weights_ref[chans : 3 * chans, :], k_s, v_s, m_s)

    def step(n, _):
        hold_two(n, attend_two(2 * n, run, q_s, k_s, v_s, m_s, s_s, state_s, True), state_s)
        return 0

    lax.fori_loop(0, tiles // 2, step, 0)


def middle_kernel(run, count, *refs):
    blocks, refs = refs[:count], refs[count:]
    q_s, old_s, weights_ref, state_s, k_s, v_s, m_s, s_s = refs
    chans = weights_ref.shape[1]
    kv_t = weights_ref[chans : 3 * chans, :]
    add_keys([block[...] for block in blocks], kv_t, k_s, v_s, m_s)

    def step(n, _):
        hold_two(n, attend_two(2 * n, run, q_s, k_s, v_s, m_s, s_s, old_s, False), state_s)
        return 0

    lax.fori_loop(0, q_s.shape[0] // 2, step, 0)


def second_kernel(run, cap, far, owners, count_ref, *refs):
    blocks, refs = refs[:far], refs[far:]
    q_s, state_s, weights_s, first_s, gain_s, down_s, facts_s, feat_hbm = refs[:8]
    votes_s, refs = refs[8 : 8 + owners], refs[8 + owners :]
    feat_s, store, k_s, v_s, m_s, s_s, ctx_s, bf_s, inner_s = refs
    chans, slots = first_s.shape
    tiles = slots // LANES
    count = count_ref[0]
    add_keys([block[...] for block in blocks], weights_s[chans : 3 * chans], k_s, v_s, m_s)
    rows8 = chans // 8

    def step(n, _):
        t = 2 * n
        _, sums, accs = attend_two(t, run, q_s, k_s, v_s, m_s, s_s, state_s, False)
        share = [1.0 / total for total in sums]
        cut = 2 * rows8 // 3
        for n in range(2):
            for i in range(rows8):
                ctx_s[t + n, i] = accs[n * rows8 + i] * share[2 * n + int(i >= cut)]
        return 0

    lax.fori_loop(0, tiles // 2, step, 0)
    ctx = swap_blocks([ctx_s[t].reshape(chans, LANES) for t in range(tiles)])
    ctx = dot_t(jnp.concatenate(ctx, 0).astype(BF16), within(run)).astype(BF16)
    ctx = jnp.concatenate([ctx[t * chans : (t + 1) * chans] for t in range(tiles)], 1)
    gain = gain_s[...]
    moved = dot(weights_s[3 * chans : 4 * chans], ctx)
    for t in range(tiles):
        at = tile(t)
        second = first_s[:, at].astype(F32) + moved[:, at]
        feat_s[:, at] = second
        inner_s[:, at] = norm_t(second, gain).astype(BF16)
    kept = iota((1, slots), 1) < count
    wide = 2 * LANES
    cuts = [slice(at, at + wide) for at in range(0, slots, wide)]
    up_t = weights_s[4 * chans :]
    raised = dot(up_t, inner_s[:, cuts[0]])
    for n, at in enumerate(cuts):
        now = raised
        if n + 1 < len(cuts):
            raised = dot(up_t, inner_s[:, cuts[n + 1]])
        hidden = gelu(now).astype(BF16)
        third = feat_s[:, at] + dot(down_s[...], hidden)
        third = jnp.where(kept[:, at], third, 0.0)
        feat_s[:, at] = third
        bf_s[:, at] = third.astype(BF16)
    keep = pltpu.make_async_copy(feat_s, feat_hbm, store)
    keep.start()
    facts = facts_s[...].astype(F32)
    low, high = facts[2:3].astype(jnp.int32), facts[1:2].astype(jnp.int32)
    picked = dot(bf_s[...], place(low, high, tiles)).astype(BF16)
    for o in range(owners):
        at = slice(o * cap, (o + 1) * cap)
        votes_s[o][...] = jnp.concatenate([picked[:, at], facts_s[:8, at]], 0)
    keep.wait()


def sums_kernel(*refs):
    got, out_ref = refs[:-1], refs[-1]
    chans, voxels = out_ref.shape
    cap = got[0].shape[1]
    total = jnp.zeros(out_ref.shape, F32)
    for ref in got:
        ballot = ref[...]
        label = ballot[chans:].astype(F32)[0:1]
        hot = (label == iota((voxels, cap), 0).astype(F32)).astype(BF16)
        total = total + dot_t(ballot[:chans], hot)
    out_ref[...] = total


def call(kernel, outs, scratch, flops, spaces, out_spaces, limit=VMEM):
    place_of = {"s": pltpu.SMEM, "v": pltpu.VMEM, "a": pl.ANY}
    return pl.pallas_call(
        kernel,
        out_shape=outs,
        in_specs=[pl.BlockSpec(memory_space=place_of[c]) for c in spaces],
        out_specs=[pl.BlockSpec(memory_space=place_of[c]) for c in out_spaces],
        scratch_shapes=scratch,
        compiler_params=pltpu.CompilerParams(vmem_limit_bytes=limit),
        cost_estimate=pl.CostEstimate(flops=flops, bytes_accessed=2 << 20, transcendentals=0),
    )


def turned(x, axis, bit):
    n = lax.axis_size(axis)
    return lax.ppermute(x, axis, [(i, i ^ bit) for i in range(n)])


def body(
    nodes,
    node_ids,
    node_count,
    pos_weight,
    gain_one,
    qkv_one,
    out_one,
    gain_two,
    qkv_two,
    out_two,
    gain_three,
    w_up,
    w_down,
    vote_slot,
    vote_owner,
    vote_voxel,
):
    slots, chans = nodes.shape
    groups, owners = lax.axis_size("grp"), lax.axis_size("tile")
    run = WIN // groups
    votes = vote_slot.shape[0]
    cap = 2 * votes // owners
    codes = owners * cap
    tiles = slots // LANES
    rows8 = chans // 8
    hidden = w_up.shape[1]
    per = LANES // WIN
    sds = jax.ShapeDtypeStruct
    vmem = pltpu.VMEM
    dma = pltpu.SemaphoreType.DMA

    first, sent = call(
        functools.partial(first_kernel, run),
        [sds((chans, slots), BF16), sds((chans, slots), BF16)],
        [
            vmem((chans, slots), BF16),
            vmem((1, slots), jnp.int32),
            vmem((3, chans), F32),
            vmem((1, chans), F32),
            vmem((1, chans), F32),
            vmem((chans, 3 * chans), BF16),
            vmem((chans, chans), BF16),
            dma((7,)),
            vmem((3 * chans, slots), BF16),
            vmem((tiles, chans, 2 * LANES), BF16),
            vmem((tiles, LANES, chans), BF16),
            vmem((tiles, chans, LANES), BF16),
            vmem((tiles, chans, LANES), BF16),
            vmem((chans, slots), BF16),
            vmem((chans, slots), BF16),
            vmem((chans, slots), BF16),
            dma((2,)),
        ],
        2_000_000_000,
        "saaaaaaa",
        "aa",
    )(
        node_count,
        nodes.T,
        node_ids.reshape(1, slots),
        pos_weight,
        gain_one.reshape(1, chans),
        gain_two.reshape(1, chans),
        qkv_one,
        out_one,
    )
    bit = groups // 2
    mid = []
    while bit > 1:
        mid += [turned(block, "grp", bit) for block in [sent] + mid]
        bit //= 2
    near = turned(sent, "grp", 1)
    weights, facts, gain = call(
        functools.partial(tables_kernel, cap),
        [
            sds((4 * chans + hidden, chans), BF16),
            sds((16, codes), BF16),
            sds((chans, LANES), F32),
        ],
        [
            vmem((chans, 3 * chans), BF16),
            vmem((chans, chans), BF16),
            vmem((chans, hidden), BF16),
            vmem((1, votes), jnp.int32),
            vmem((1, votes), jnp.int32),
            vmem((1, votes), jnp.int32),
            vmem((1, chans), F32),
            dma((7,)),
        ],
        2_000_000_000,
        "aaaaaaa",
        "vvv",
        limit=TIGHT,
    )(
        qkv_two,
        out_two,
        w_up,
        vote_slot.reshape(1, votes),
        vote_owner.reshape(1, votes),
        vote_voxel.reshape(1, votes),
        gain_three.reshape(1, chans),
    )
    q_like = ((tiles, rows8, 8, LANES), F32)
    state_like = ((tiles, rows8 + 4, 8, LANES), F32)

    def key_scratch(blocks):
        return [
            vmem((blocks, tiles, rows8, 8, LANES), F32),
            vmem((blocks, tiles, rows8, 8, LANES), F32),
            vmem((blocks, tiles, 8, LANES), F32),
            vmem((blocks * run, 4, 8, LANES), F32),
        ]

    query, state = call(
        functools.partial(near_kernel, run),
        [sds(*q_like), sds(*state_like)],
        key_scratch(2),
        3_000_000_000,
        "vvv",
        "vv",
        limit=ROOMY,
    )(sent, near, weights)
    mid, query = lax.optimization_barrier((mid, query))
    far = [turned(block, "grp", 1) for block in mid]
    (state,) = call(
        functools.partial(middle_kernel, run, len(mid)),
        [sds(*state_like)],
        key_scratch(len(mid)),
        2_000_000_000,
        "v" * len(mid) + "vvv",
        "v",
        limit=ROOMY,
    )(*mid, query, state, weights)
    features_t, *ballots = call(
        functools.partial(second_kernel, run, cap, len(far), owners),
        [sds((chans, slots), F32)] + [sds((chans + 8, cap), BF16)] * owners,
        [vmem((chans, slots), F32), dma]
        + key_scratch(len(far))
        + [vmem(*q_like), vmem((chans, slots), BF16), vmem((chans, slots), BF16)],
        3_000_000_000,
        "s" + "v" * (len(far) + 7),
        "a" + "v" * owners,
        limit=ROOMY,
    )(
        node_count,
        *far,
        query,
        state,
        weights,
        first,
        gain,
        w_down.T,
        facts,
    )
    got = [ballots[0]] + [turned(ballots[k], "tile", k) for k in [1] + list(range(owners - 1, 1, -1))]
    (sums_t,) = call(
        sums_kernel,
        [sds((chans, VOX_DEV), F32)],
        [],
        200_000_000,
        "v" * owners,
        "v",
        limit=ROOMY,
    )(*got)
    return (features_t.T, sums_t.T)


def solution(mesh):
    in_specs = (
        P(("grp", "tile"), None),
        P(("grp", "tile")),
        P(("grp", "tile")),
        P(),
        P(),
        P(),
        P(),
        P(),
        P(),
        P(),
        P(),
        P(),
        P(),
        P(("grp", "tile")),
        P(("grp", "tile"), None),
        P(("grp", "tile")),
    )
    out_specs = (P(("grp", "tile"), None), P(("grp", "tile"), None))
    return jax.shard_map(body, mesh=mesh, in_specs=in_specs, out_specs=out_specs, check_vma=False)
```

```python
import functools
import math

import jax
import jax.numpy as jnp
from jax import lax
from jax.experimental import pallas as pl
from jax.experimental.pallas import tpu as pltpu
from jax.sharding import PartitionSpec as P

HEADS = 12
WIN = 32
VOX_DEV = 256
LANES = 128
FLAG = 16384.0
VMEM = 64 * 1024 * 1024 - 65536
TIGHT = VMEM - 2 * 1024 * 1024
ROOMY = 24 * 1024 * 1024
F32 = jnp.float32
BF16 = jnp.bfloat16
LOG2E = math.log2(math.e)


def iota(shape, dim):
    return lax.broadcasted_iota(jnp.int32, shape, dim)


def dot(a, b):
    return jnp.dot(a, b, preferred_element_type=F32)


def dot_t(a, b):
    return lax.dot_general(a, b, (((1,), (1,)), ((), ())), preferred_element_type=F32)


def eye(n):
    return (iota((n, n), 0) == iota((n, n), 1)).astype(BF16)


def transposed(a):
    return a.astype(F32).T.astype(BF16)


def tile(t):
    return slice(t * LANES, (t + 1) * LANES)


def head_order(chans):
    size = chans // HEADS
    cut = 8 * size
    j = iota((chans, 1), 0)
    high = j - cut
    low_src = (j % 8) * size + j // 8
    high_src = (8 + high % 4) * size + high // 8 + (size // 2) * ((high % 8) // 4)
    return jnp.where(j < cut, low_src, high_src)


def within(run):
    lane = iota((1, LANES), 1)
    q, e = lane // 16, lane % 16
    p = (4 * (q // run) + e // 4) * run + q % run
    return ((e % 4) * WIN + p == iota((LANES, LANES), 0)).astype(BF16)


def swap_blocks(tiles):
    tiles = list(tiles)
    block = iota(tiles[0].shape, 1) // 16
    step = len(tiles) // 2
    while step:
        for n in range(len(tiles)):
            if n & step:
                continue
            a, b = tiles[n], tiles[n + step]
            low = block // step % 2 == 0
            tiles[n] = jnp.where(low, a, pltpu.roll(b, 16 * step, 1))
            tiles[n + step] = jnp.where(low, pltpu.roll(a, LANES - 16 * step, 1), b)
        step //= 2
    return tiles


def place(low, high, blocks):
    base = jnp.where(low == iota((LANES, low.shape[1]), 0), 1.0, 0.0).astype(BF16)
    high = jnp.broadcast_to(high, base.shape).astype(F32).astype(BF16)
    nil = jnp.zeros_like(base)
    parts = [jnp.where(high == jnp.asarray(n, BF16), base, nil) for n in range(blocks)]
    return jnp.concatenate(parts, 0)


def norm_t(x, gain):
    inv = 1.0 / x.shape[0]
    mean = jnp.sum(x, 0, keepdims=True) * inv
    cent = x - mean
    var = jnp.sum(cent * cent, 0, keepdims=True) * inv
    return cent * lax.rsqrt(var + 1e-05) * gain


def gelu(x):
    half = 0.5 * x
    scale = math.sqrt(2 / math.pi)
    return half + half * jnp.tanh(x * (scale + (0.044715 * scale) * (x * x)))


def start_all(pairs, sems):
    copies = [pltpu.make_async_copy(a, b, sems.at[n]) for n, (a, b) in enumerate(pairs)]
    for copy in copies:
        copy.start()
    return copies


def wait_all(copies):
    for copy in copies:
        copy.wait()


def fold8(x, op):
    y = x[0]
    for n in range(1, x.shape[0]):
        y = op(y, x[n])
    for shift in (4, 2, 1):
        y = op(y, pltpu.roll(y, shift, 0))
    return y


def first_kernel(
    run, count_ref, nodes_hbm, ids_hbm, pos_hbm, gain_one_hbm, gain_two_hbm, qkv_hbm, out_hbm,
    first_hbm, sent_hbm, nodes_ref, ids_ref, pos_ref, gain_one_ref, gain_two_ref, qkv_ref, out_ref,
    sems, qkv_s, q_s, k_s, v_s, ctx_s, n_s, first_s, sent_s, stores
):
    loads = start_all(
        [
            (nodes_hbm, nodes_ref),
            (ids_hbm, ids_ref),
            (pos_hbm, pos_ref),
            (gain_one_hbm, gain_one_ref),
            (gain_two_hbm, gain_two_ref),
            (qkv_hbm, qkv_ref),
            (out_hbm, out_ref),
        ],
        sems,
    )
    chans, slots = nodes_ref.shape
    tiles = slots // LANES
    size = chans // HEADS
    per = LANES // WIN
    count = count_ref[0]
    wait_all(loads)
    cols = jnp.concatenate(
        [pos_ref[...], gain_one_ref[...], gain_two_ref[...], jnp.zeros((3, chans), F32)], 0
    ).T
    ids = ids_ref[...]
    coords = []
    for axis in range(3):
        total = jnp.zeros(ids.shape, jnp.int32)
        for level in range(6):
            bit = jnp.bitwise_and(jnp.right_shift(ids, 3 * level + axis), 1)
            total = total + bit * 2**level
        coords.append(total.astype(F32) / 64.0 - 0.5)
    for t in range(tiles):
        at = tile(t)
        start = cols[:, 0:1] * coords[0][:, at]
        for axis in range(1, 3):
            start = start + cols[:, axis : axis + 1] * coords[axis][:, at]
        start = (nodes_ref[:, at].astype(F32) + start).astype(BF16)
        nodes_ref[:, at] = start
        n_s[:, at] = norm_t(start.astype(F32), cols[:, 3:4]).astype(BF16)
    qkv_t = transposed(qkv_ref[...])
    out_t = transposed(out_ref[...])
    qkv_s[...] = dot(qkv_t, n_s[...]).astype(BF16)
    side = eye(LANES)
    row_head = iota((chans, LANES), 0) // size
    even_row = row_head % 2 == 0
    for t in range(tiles):
        query = qkv_s[:chans, tile(t)].astype(F32) * size**-0.5
        q_s[t, :, :LANES] = jnp.where(even_row, query, 0.0).astype(BF16)
        q_s[t, :, LANES:] = jnp.where(even_row, 0.0, query).astype(BF16)
        k_s[t] = dot_t(side, qkv_s[chans : 2 * chans, tile(t)]).astype(BF16)
        v_s[t] = qkv_s[2 * chans :, tile(t)]

    lane_pair = iota((WIN, chans), 1) // (2 * size)
    window = iota((8, LANES), 1) // WIN
    wide_window = iota((WIN, LANES), 1) // WIN
    rank = iota((WIN, LANES), 0) + WIN * (iota((WIN, LANES), 1) // WIN)

    def group(t, _):
        query = q_s[t]
        even, odd = None, None
        for w in range(per):
            keys = k_s[t, w * WIN : (w + 1) * WIN, :]
            by_pair = jnp.concatenate(
                [jnp.where(lane_pair == m, keys, jnp.zeros_like(keys)) for m in range(HEADS // 2)],
                0,
            )
            got = dot(by_pair, query)
            left = got[:, :LANES].reshape(-1, 8, LANES)
            right = got[:, LANES:].reshape(-1, 8, LANES)
            even = left if w == 0 else jnp.where(window[None] == w, left, even)
            odd = right if w == 0 else jnp.where(window[None] == w, right, odd)
        mask = jnp.where(rank + t * LANES < count, 0.0, -1e9).astype(F32)
        mask = mask.reshape(WIN // 8, 8, LANES)
        probs, inverse = [], []
        for h in range(HEADS):
            scores = (even, odd)[h % 2]
            mine = scores[h // 2 * (WIN // 8) : (h // 2 + 1) * (WIN // 8)] + mask
            top = fold8(mine, jnp.maximum)
            weight = jnp.exp(mine - top[None])
            inverse.append(1.0 / fold8(weight, jnp.add))
            probs.append(weight.reshape(WIN, LANES).astype(BF16))
        parts = []
        for m in range(HEADS // 2):
            both = []
            for h in (2 * m, 2 * m + 1):
                nil = jnp.zeros_like(probs[h])
                both.append(
                    jnp.concatenate(
                        [jnp.where(wide_window == w, probs[h], nil) for w in range(per)], 0
                    )
                )
            rows = slice(2 * m * size, 2 * (m + 1) * size)
            got = dot(v_s[t, rows, :], jnp.concatenate(both, 1))
            for n in range(2):
                block = got[n * size : (n + 1) * size, tile(n)].reshape(-1, 8, LANES)
                block = block * inverse[2 * m + n][None]
                parts.append(block.reshape(size, LANES))
        ctx_s[t] = jnp.concatenate(parts, 0).astype(BF16)
        return 0

    lax.fori_loop(0, tiles, group, 0, unroll=8)
    ctx = jnp.concatenate([ctx_s[t] for t in range(tiles)], 1)
    moved = dot(out_t, ctx)
    for t in range(tiles):
        at = tile(t)
        first = (nodes_ref[:, at].astype(F32) + moved[:, at]).astype(BF16)
        first_s[:, at] = first
        normed = norm_t(first.astype(F32), cols[:, 4:5])
        kept = iota((1, LANES), 1) + t * LANES < count
        head = jnp.where((iota((16, LANES), 0) > 0) | kept, normed[:16], FLAG)
        n_s[:, at] = jnp.concatenate([head, normed[16:]], 0).astype(BF16)
    keep_first = pltpu.make_async_copy(first_s, first_hbm, stores.at[0])
    keep_first.start()
    inside = within(run)
    for t, block in enumerate(swap_blocks([dot(n_s[:, tile(t)], inside) for t in range(tiles)])):
        sent_s[:, tile(t)] = block.astype(BF16)
    send = pltpu.make_async_copy(sent_s, sent_hbm, stores.at[1])
    send.start()
    wait_all([keep_first, send])


def tables_kernel(
    cap, qkv_hbm, out_hbm, up_hbm, slot_hbm, owner_hbm, voxel_hbm, gain_hbm, weights_s, facts_s,
    gain_s, qkv_ref, out_ref, up_ref, slot_ref, owner_ref, voxel_ref, gain_ref, sems
):
    loads = start_all(
        [
            (qkv_hbm, qkv_ref),
            (out_hbm, out_ref),
            (up_hbm, up_ref),
            (slot_hbm, slot_ref),
            (owner_hbm, owner_ref),
            (voxel_hbm, voxel_ref),
            (gain_hbm, gain_ref),
        ],
        sems,
    )
    wait_all(loads)
    gain = jnp.concatenate([gain_ref[...], jnp.zeros((7, gain_ref.shape[1]), F32)], 0)
    gain_s[...] = jnp.broadcast_to(gain.T[:, 0:1], gain_s.shape)
    votes = slot_ref.shape[1]
    codes = facts_s.shape[1]
    owners = codes // cap
    chans = out_ref.shape[0]
    src = head_order(chans)
    src = jnp.concatenate([src, src + chans, src + 2 * chans], 0)
    shuffle = (src == iota((3 * chans, 3 * chans), 1)).astype(BF16)
    weights_s[: 3 * chans] = dot_t(shuffle, qkv_ref[...]).astype(BF16)
    out_t = dot(shuffle[:chans, :chans], out_ref[...])
    weights_s[3 * chans : 4 * chans] = transposed(out_t)
    weights_s[4 * chans :] = transposed(up_ref[...])
    owner = jnp.bitwise_xor(owner_ref[...], lax.axis_index("tile"))
    hot = owner == iota((owners, votes), 0)
    upto = (iota((votes, votes), 0) <= iota((votes, votes), 1)).astype(BF16)
    rank = jnp.sum(jnp.where(hot, dot(hot.astype(BF16), upto), 0.0), 0, keepdims=True)
    code = owner * cap + rank.astype(jnp.int32) - 1
    member = place(code % LANES, code // LANES, codes // LANES)
    slot = slot_ref[...]
    row = iota((16, votes), 0)
    facts = jnp.where(
        row == 0,
        voxel_ref[...],
        jnp.where(row == 1, slot // LANES, jnp.where(row == 2, slot % LANES, 1)),
    )
    listed = dot_t(facts.astype(F32).astype(BF16), member)
    facts_s[...] = jnp.where(listed[3:4] > 0.5, listed, -1.0).astype(BF16)


def clean(block):
    head = block[:16].astype(F32)
    gone = head[0:1] > 0.5 * FLAG
    head = jnp.where((iota(head.shape, 0) == 0) & gone, 0.0, head)
    return jnp.concatenate([head.astype(BF16), block[16:]], 0), gone


def add_keys(blocks, kv_t, k_s, v_s, m_s):
    chans = kv_t.shape[1]
    tiles = k_s.shape[1]
    for n, block in enumerate(blocks):
        block, gone = clean(block)
        kv = dot(kv_t, block)
        mask = jnp.where(gone, -1e9, 0.0)
        for t in range(tiles):
            k_s[n, t] = kv[:chans, tile(t)].reshape(chans // 8, 8, LANES)
            v_s[n, t] = kv[chans:, tile(t)].reshape(chans // 8, 8, LANES)
            m_s[n, t] = jnp.broadcast_to(mask[:, tile(t)], (8, LANES))


def attend_two(t, run, q_s, k_s, v_s, m_s, s_s, state_s, fresh):
    rows8 = q_s.shape[1]
    cut = 2 * rows8 // 3
    keys = k_s.shape[0] * run
    base = (t // run) * run
    both = range(2)
    query = [[q_s[t + n, i] for i in range(rows8)] for n in both]

    def score(key, top):
        block, at = key // run, base + key % run
        mask = m_s[block, at]
        sums = [[None, None], [None, None]]
        for i in range(rows8):
            part = int(i >= cut)
            row = k_s[block, at, i]
            for n in both:
                term = query[n][i] * row
                held = sums[n][part]
                sums[n][part] = term if held is None else held + term
        tops = []
        for n in both:
            a, b = sums[n]
            b = b + pltpu.roll(b, 4, 0)
            a = a + mask
            b = b + mask
            s_s[key, 2 * n] = a
            s_s[key, 2 * n + 1] = b
            tops += [jnp.maximum(top[2 * n], a), jnp.maximum(top[2 * n + 1], b)]
        return tuple(tops)

    if fresh:
        old = tuple(jnp.full((8, LANES), -3e38, F32) for _ in range(4))
    else:
        old = tuple(state_s[t + n, rows8 + part] for n in both for part in both)
    tops = lax.fori_loop(0, keys, score, old, unroll=8)
    if fresh:
        zero = jnp.zeros((8, LANES), F32)
        sums = tuple(zero for _ in range(4))
        accs = tuple(zero for _ in range(2 * rows8))
    else:
        fade = [jnp.exp2(old[n] - tops[n]) for n in range(4)]
        sums = tuple(
            state_s[t + n, rows8 + 2 + part] * fade[2 * n + part] for n in both for part in both
        )
        accs = tuple(
            state_s[t + n, i] * fade[2 * n + int(i >= cut)] for n in both for i in range(rows8)
        )

    def gather(key, carry):
        sums, accs = carry
        block, at = key // run, base + key % run
        weight = [jnp.exp2(s_s[key, n] - tops[n]) for n in range(4)]
        accs = list(accs)
        for i in range(rows8):
            row = v_s[block, at, i]
            for n in both:
                at_acc = n * rows8 + i
                accs[at_acc] = accs[at_acc] + weight[2 * n + int(i >= cut)] * row
        return tuple(sums[n] + weight[n] for n in range(4)), tuple(accs)

    sums, accs = lax.fori_loop(0, keys, gather, (sums, accs), unroll=8)
    return tops, sums, accs


def hold_two(n, state, state_s):
    tops, sums, accs = state
    rows8 = len(accs) // 2
    for m in range(2):
        for i in range(rows8):
            state_s[2 * n + m, i] = accs[m * rows8 + i]
        for part in range(2):
            state_s[2 * n + m, rows8 + part] = tops[2 * m + part]
            state_s[2 * n + m, rows8 + 2 + part] = sums[2 * m + part]


def near_kernel(run, own_ref, near_ref, weights_ref, q_s, state_s, k_s, v_s, m_s, s_s):
    chans, slots = own_ref.shape
    tiles = slots // LANES
    scale = (chans // HEADS) ** -0.5 * LOG2E
    own, _ = clean(own_ref[...])
    query = dot(weights_ref[:chans, :], own) * scale
    for t in range(tiles):
        q_s[t] = query[:, tile(t)].reshape(chans // 8, 8, LANES)
    add_keys([own_ref[...], near_ref[...]], weights_ref[chans : 3 * chans, :], k_s, v_s, m_s)

    def step(n, _):
        hold_two(n, attend_two(2 * n, run, q_s, k_s, v_s, m_s, s_s, state_s, True), state_s)
        return 0

    lax.fori_loop(0, tiles // 2, step, 0)


def middle_kernel(run, count, *refs):
    blocks, refs = refs[:count], refs[count:]
    q_s, old_s, weights_ref, state_s, k_s, v_s, m_s, s_s = refs
    chans = weights_ref.shape[1]
    kv_t = weights_ref[chans : 3 * chans, :]
    add_keys([block[...] for block in blocks], kv_t, k_s, v_s, m_s)

    def step(n, _):
        hold_two(n, attend_two(2 * n, run, q_s, k_s, v_s, m_s, s_s, old_s, False), state_s)
        return 0

    lax.fori_loop(0, q_s.shape[0] // 2, step, 0)


def second_kernel(run, cap, far, owners, count_ref, *refs):
    blocks, refs = refs[:far], refs[far:]
    q_s, state_s, weights_s, first_s, gain_s, down_s, facts_s, feat_hbm = refs[:8]
    votes_s, refs = refs[8 : 8 + owners // 2], refs[8 + owners // 2 :]
    feat_s, store, k_s, v_s, m_s, s_s, ctx_s, bf_s, inner_s = refs
    chans, slots = first_s.shape
    tiles = slots // LANES
    count = count_ref[0]
    add_keys([block[...] for block in blocks], weights_s[chans : 3 * chans], k_s, v_s, m_s)
    rows8 = chans // 8

    def step(n, _):
        t = 2 * n
        _, sums, accs = attend_two(t, run, q_s, k_s, v_s, m_s, s_s, state_s, False)
        share = [1.0 / total for total in sums]
        cut = 2 * rows8 // 3
        for n in range(2):
            for i in range(rows8):
                ctx_s[t + n, i] = accs[n * rows8 + i] * share[2 * n + int(i >= cut)]
        return 0

    lax.fori_loop(0, tiles // 2, step, 0)
    ctx = swap_blocks([ctx_s[t].reshape(chans, LANES) for t in range(tiles)])
    ctx = dot_t(jnp.concatenate(ctx, 0).astype(BF16), within(run)).astype(BF16)
    ctx = jnp.concatenate([ctx[t * chans : (t + 1) * chans] for t in range(tiles)], 1)
    gain = gain_s[...]
    moved = dot(weights_s[3 * chans : 4 * chans], ctx)
    for t in range(tiles):
        at = tile(t)
        second = first_s[:, at].astype(F32) + moved[:, at]
        feat_s[:, at] = second
        inner_s[:, at] = norm_t(second, gain).astype(BF16)
    kept = iota((1, slots), 1) < count
    wide = 2 * LANES
    cuts = [slice(at, at + wide) for at in range(0, slots, wide)]
    up_t = weights_s[4 * chans :]
    raised = dot(up_t, inner_s[:, cuts[0]])
    for n, at in enumerate(cuts):
        now = raised
        if n + 1 < len(cuts):
            raised = dot(up_t, inner_s[:, cuts[n + 1]])
        hidden = gelu(now).astype(BF16)
        third = feat_s[:, at] + dot(down_s[...], hidden)
        third = jnp.where(kept[:, at], third, 0.0)
        feat_s[:, at] = third
        bf_s[:, at] = third.astype(BF16)
    keep = pltpu.make_async_copy(feat_s, feat_hbm, store)
    keep.start()
    facts = facts_s[...].astype(F32)
    low, high = facts[2:3].astype(jnp.int32), facts[1:2].astype(jnp.int32)
    picked = dot(bf_s[...], place(low, high, tiles)).astype(BF16)
    for o in range(owners):
        at = slice(o * cap, (o + 1) * cap)
        ballot = jnp.concatenate([picked[:, at], facts_s[:8, at]], 0)
        votes_s[o % len(votes_s)][o // len(votes_s)] = ballot
    keep.wait()


def sums_kernel(*refs):
    ballots, outs = refs[:-2], refs[-2:]
    cap = ballots[0].shape[2]
    for kind, out_ref in enumerate(outs):
        chans, voxels = out_ref.shape
        total = jnp.zeros(out_ref.shape, F32)
        for ref in ballots:
            ballot = ref[kind]
            label = ballot[chans:].astype(F32)[0:1]
            hot = (label == iota((voxels, cap), 0).astype(F32)).astype(BF16)
            total = total + dot_t(ballot[:chans], hot)
        out_ref[...] = total.astype(out_ref.dtype)


def total_kernel(here_ref, there_ref, out_ref):
    out_ref[...] = here_ref[...] + there_ref[...].astype(F32)


def call(kernel, outs, scratch, flops, spaces, out_spaces, limit=VMEM):
    place_of = {"s": pltpu.SMEM, "v": pltpu.VMEM, "a": pl.ANY}
    return pl.pallas_call(
        kernel,
        out_shape=outs,
        in_specs=[pl.BlockSpec(memory_space=place_of[c]) for c in spaces],
        out_specs=[pl.BlockSpec(memory_space=place_of[c]) for c in out_spaces],
        scratch_shapes=scratch,
        compiler_params=pltpu.CompilerParams(vmem_limit_bytes=limit),
        cost_estimate=pl.CostEstimate(flops=flops, bytes_accessed=2 << 20, transcendentals=0),
    )


def turned(x, axis, bit):
    n = lax.axis_size(axis)
    return lax.ppermute(x, axis, [(i, i ^ bit) for i in range(n)])


def body(
    nodes,
    node_ids,
    node_count,
    pos_weight,
    gain_one,
    qkv_one,
    out_one,
    gain_two,
    qkv_two,
    out_two,
    gain_three,
    w_up,
    w_down,
    vote_slot,
    vote_owner,
    vote_voxel,
):
    slots, chans = nodes.shape
    groups, owners = lax.axis_size("grp"), lax.axis_size("tile")
    run = WIN // groups
    votes = vote_slot.shape[0]
    cap = 2 * votes // owners
    codes = owners * cap
    tiles = slots // LANES
    rows8 = chans // 8
    hidden = w_up.shape[1]
    per = LANES // WIN
    sds = jax.ShapeDtypeStruct
    vmem = pltpu.VMEM
    dma = pltpu.SemaphoreType.DMA

    first, sent = call(
        functools.partial(first_kernel, run),
        [sds((chans, slots), BF16), sds((chans, slots), BF16)],
        [
            vmem((chans, slots), BF16),
            vmem((1, slots), jnp.int32),
            vmem((3, chans), F32),
            vmem((1, chans), F32),
            vmem((1, chans), F32),
            vmem((chans, 3 * chans), BF16),
            vmem((chans, chans), BF16),
            dma((7,)),
            vmem((3 * chans, slots), BF16),
            vmem((tiles, chans, 2 * LANES), BF16),
            vmem((tiles, LANES, chans), BF16),
            vmem((tiles, chans, LANES), BF16),
            vmem((tiles, chans, LANES), BF16),
            vmem((chans, slots), BF16),
            vmem((chans, slots), BF16),
            vmem((chans, slots), BF16),
            dma((2,)),
        ],
        2_000_000_000,
        "saaaaaaa",
        "aa",
    )(
        node_count,
        nodes.T,
        node_ids.reshape(1, slots),
        pos_weight,
        gain_one.reshape(1, chans),
        gain_two.reshape(1, chans),
        qkv_one,
        out_one,
    )
    bit = groups // 2
    mid = []
    while bit > 1:
        mid += [turned(block, "grp", bit) for block in [sent] + mid]
        bit //= 2
    near = turned(sent, "grp", 1)
    weights, facts, gain = call(
        functools.partial(tables_kernel, cap),
        [
            sds((4 * chans + hidden, chans), BF16),
            sds((16, codes), BF16),
            sds((chans, LANES), F32),
        ],
        [
            vmem((chans, 3 * chans), BF16),
            vmem((chans, chans), BF16),
            vmem((chans, hidden), BF16),
            vmem((1, votes), jnp.int32),
            vmem((1, votes), jnp.int32),
            vmem((1, votes), jnp.int32),
            vmem((1, chans), F32),
            dma((7,)),
        ],
        2_000_000_000,
        "aaaaaaa",
        "vvv",
        limit=TIGHT,
    )(
        qkv_two,
        out_two,
        w_up,
        vote_slot.reshape(1, votes),
        vote_owner.reshape(1, votes),
        vote_voxel.reshape(1, votes),
        gain_three.reshape(1, chans),
    )
    q_like = ((tiles, rows8, 8, LANES), F32)
    state_like = ((tiles, rows8 + 4, 8, LANES), F32)

    def key_scratch(blocks):
        return [
            vmem((blocks, tiles, rows8, 8, LANES), F32),
            vmem((blocks, tiles, rows8, 8, LANES), F32),
            vmem((blocks, tiles, 8, LANES), F32),
            vmem((blocks * run, 4, 8, LANES), F32),
        ]

    query, state = call(
        functools.partial(near_kernel, run),
        [sds(*q_like), sds(*state_like)],
        key_scratch(2),
        3_000_000_000,
        "vvv",
        "vv",
        limit=ROOMY,
    )(sent, near, weights)
    mid, query = lax.optimization_barrier((mid, query))
    far = [turned(block, "grp", 1) for block in mid]
    (state,) = call(
        functools.partial(middle_kernel, run, len(mid)),
        [sds(*state_like)],
        key_scratch(len(mid)),
        2_000_000_000,
        "v" * len(mid) + "vvv",
        "v",
        limit=ROOMY,
    )(*mid, query, state, weights)
    features_t, *ballots = call(
        functools.partial(second_kernel, run, cap, len(far), owners),
        [sds((chans, slots), F32)] + [sds((2, chans + 8, cap), BF16)] * (owners // 2),
        [vmem((chans, slots), F32), dma]
        + key_scratch(len(far))
        + [vmem(*q_like), vmem((chans, slots), BF16), vmem((chans, slots), BF16)],
        3_000_000_000,
        "s" + "v" * (len(far) + 7),
        "a" + "v" * (owners // 2),
        limit=ROOMY,
    )(
        node_count,
        *far,
        query,
        state,
        weights,
        first,
        gain,
        w_down.T,
        facts,
    )
    half = owners // 2
    got = [ballots[0]] + [turned(ballots[k], "tile", k) for k in range(1, half)]
    here, there = call(
        sums_kernel,
        [sds((chans, VOX_DEV), F32), sds((chans, VOX_DEV), BF16)],
        [],
        200_000_000,
        "v" * half,
        "vv",
        limit=ROOMY,
    )(*got)
    (sums_t,) = call(
        total_kernel, [sds((chans, VOX_DEV), F32)], [], 1_000_000, "vv", "v", limit=ROOMY
    )(here, turned(there, "tile", half))
    return (features_t.T, sums_t.T)


def solution(mesh):
    in_specs = (
        P(("grp", "tile"), None),
        P(("grp", "tile")),
        P(("grp", "tile")),
        P(),
        P(),
        P(),
        P(),
        P(),
        P(),
        P(),
        P(),
        P(),
        P(),
        P(("grp", "tile")),
        P(("grp", "tile"), None),
        P(("grp", "tile")),
    )
    out_specs = (P(("grp", "tile"), None), P(("grp", "tile"), None))
    return jax.shard_map(body, mesh=mesh, in_specs=in_specs, out_specs=out_specs, check_vma=False)
```

```python
import functools
import math

import jax
import jax.numpy as jnp
from jax import lax
from jax.experimental import pallas as pl
from jax.experimental.pallas import tpu as pltpu
from jax.sharding import PartitionSpec as P

HEADS = 12
WIN = 32
VOX_DEV = 256
LANES = 128
FLAG = 16384.0
VMEM = 64 * 1024 * 1024 - 65536
TIGHT = VMEM - 2 * 1024 * 1024
ROOMY = 24 * 1024 * 1024
F32 = jnp.float32
BF16 = jnp.bfloat16
LOG2E = math.log2(math.e)


def iota(shape, dim):
    return lax.broadcasted_iota(jnp.int32, shape, dim)


def dot(a, b):
    return jnp.dot(a, b, preferred_element_type=F32)


def dot_t(a, b):
    return lax.dot_general(a, b, (((1,), (1,)), ((), ())), preferred_element_type=F32)


def eye(n):
    return (iota((n, n), 0) == iota((n, n), 1)).astype(BF16)


def transposed(a):
    return a.astype(F32).T.astype(BF16)


def tile(t):
    return slice(t * LANES, (t + 1) * LANES)


def head_order(chans):
    size = chans // HEADS
    cut = 8 * size
    j = iota((chans, 1), 0)
    high = j - cut
    low_src = (j % 8) * size + j // 8
    high_src = (8 + high % 4) * size + high // 8 + (size // 2) * ((high % 8) // 4)
    return jnp.where(j < cut, low_src, high_src)


def within(run):
    lane = iota((1, LANES), 1)
    q, e = lane // 16, lane % 16
    p = (4 * (q // run) + e // 4) * run + q % run
    return ((e % 4) * WIN + p == iota((LANES, LANES), 0)).astype(BF16)


def swap_blocks(tiles):
    tiles = list(tiles)
    block = iota(tiles[0].shape, 1) // 16
    step = len(tiles) // 2
    while step:
        for n in range(len(tiles)):
            if n & step:
                continue
            a, b = tiles[n], tiles[n + step]
            low = block // step % 2 == 0
            tiles[n] = jnp.where(low, a, pltpu.roll(b, 16 * step, 1))
            tiles[n + step] = jnp.where(low, pltpu.roll(a, LANES - 16 * step, 1), b)
        step //= 2
    return tiles


def place(low, high, blocks):
    base = jnp.where(low == iota((LANES, low.shape[1]), 0), 1.0, 0.0).astype(BF16)
    high = jnp.broadcast_to(high, base.shape).astype(F32).astype(BF16)
    nil = jnp.zeros_like(base)
    parts = [jnp.where(high == jnp.asarray(n, BF16), base, nil) for n in range(blocks)]
    return jnp.concatenate(parts, 0)


def norm_t(x, gain):
    inv = 1.0 / x.shape[0]
    mean = jnp.sum(x, 0, keepdims=True) * inv
    cent = x - mean
    var = jnp.sum(cent * cent, 0, keepdims=True) * inv
    return cent * lax.rsqrt(var + 1e-05) * gain


def gelu(x):
    half = 0.5 * x
    scale = math.sqrt(2 / math.pi)
    return half + half * jnp.tanh(x * (scale + (0.044715 * scale) * (x * x)))


def start_all(pairs, sems):
    copies = [pltpu.make_async_copy(a, b, sems.at[n]) for n, (a, b) in enumerate(pairs)]
    for copy in copies:
        copy.start()
    return copies


def wait_all(copies):
    for copy in copies:
        copy.wait()


def fold8(x, op):
    y = x[0]
    for n in range(1, x.shape[0]):
        y = op(y, x[n])
    for shift in (4, 2, 1):
        y = op(y, pltpu.roll(y, shift, 0))
    return y


def first_kernel(
    run, count_ref, nodes_hbm, ids_hbm, pos_hbm, gain_one_hbm, gain_two_hbm, qkv_hbm, out_hbm,
    first_hbm, sent_hbm, nodes_ref, ids_ref, pos_ref, gain_one_ref, gain_two_ref, qkv_ref, out_ref,
    sems, qkv_s, q_s, k_s, v_s, n_s, first_s, sent_s, stores
):
    loads = start_all(
        [
            (nodes_hbm, nodes_ref),
            (ids_hbm, ids_ref),
            (pos_hbm, pos_ref),
            (gain_one_hbm, gain_one_ref),
            (gain_two_hbm, gain_two_ref),
            (qkv_hbm, qkv_ref),
            (out_hbm, out_ref),
        ],
        sems,
    )
    chans, slots = nodes_ref.shape
    tiles = slots // LANES
    size = chans // HEADS
    per = LANES // WIN
    count = count_ref[0]
    wait_all(loads)
    cols = jnp.concatenate(
        [pos_ref[...], gain_one_ref[...], gain_two_ref[...], jnp.zeros((3, chans), F32)], 0
    ).T
    ids = ids_ref[...]
    coords = []
    for axis in range(3):
        total = jnp.zeros(ids.shape, jnp.int32)
        for level in range(6):
            bit = jnp.bitwise_and(jnp.right_shift(ids, 3 * level + axis), 1)
            total = total + bit * 2**level
        coords.append(total.astype(F32) / 64.0 - 0.5)
    for t in range(tiles):
        at = tile(t)
        start = cols[:, 0:1] * coords[0][:, at]
        for axis in range(1, 3):
            start = start + cols[:, axis : axis + 1] * coords[axis][:, at]
        start = (nodes_ref[:, at].astype(F32) + start).astype(BF16)
        nodes_ref[:, at] = start
        n_s[:, at] = norm_t(start.astype(F32), cols[:, 3:4]).astype(BF16)
    qkv_t = transposed(qkv_ref[...])
    out_t = transposed(out_ref[...])
    qkv_s[...] = dot(qkv_t, n_s[...]).astype(BF16)
    side = eye(LANES)
    row_head = iota((chans, LANES), 0) // size
    even_row = row_head % 2 == 0
    for t in range(tiles):
        query = qkv_s[:chans, tile(t)].astype(F32) * size**-0.5
        q_s[t, :, :LANES] = jnp.where(even_row, query, 0.0).astype(BF16)
        q_s[t, :, LANES:] = jnp.where(even_row, 0.0, query).astype(BF16)
        k_s[t] = dot_t(side, qkv_s[chans : 2 * chans, tile(t)]).astype(BF16)
        v_s[t] = qkv_s[2 * chans :, tile(t)]

    lane_pair = iota((WIN, chans), 1) // (2 * size)
    window = iota((8, LANES), 1) // WIN
    wide_window = iota((WIN, LANES), 1) // WIN
    rank = iota((WIN, LANES), 0) + WIN * (iota((WIN, LANES), 1) // WIN)

    def group(t):
        query = q_s[t]
        even, odd = None, None
        for w in range(per):
            keys = k_s[t, w * WIN : (w + 1) * WIN, :]
            by_pair = jnp.concatenate(
                [jnp.where(lane_pair == m, keys, jnp.zeros_like(keys)) for m in range(HEADS // 2)],
                0,
            )
            got = dot(by_pair, query)
            left = got[:, :LANES].reshape(-1, 8, LANES)
            right = got[:, LANES:].reshape(-1, 8, LANES)
            even = left if w == 0 else jnp.where(window[None] == w, left, even)
            odd = right if w == 0 else jnp.where(window[None] == w, right, odd)
        mask = jnp.where(rank + t * LANES < count, 0.0, -1e9).astype(F32)
        mask = mask.reshape(WIN // 8, 8, LANES)
        probs, inverse = [], []
        for h in range(HEADS):
            scores = (even, odd)[h % 2]
            mine = scores[h // 2 * (WIN // 8) : (h // 2 + 1) * (WIN // 8)] + mask
            top = fold8(mine, jnp.maximum)
            weight = jnp.exp(mine - top[None])
            inverse.append(1.0 / fold8(weight, jnp.add))
            probs.append(weight.reshape(WIN, LANES).astype(BF16))
        parts = []
        for m in range(HEADS // 2):
            both = []
            for h in (2 * m, 2 * m + 1):
                nil = jnp.zeros_like(probs[h])
                both.append(
                    jnp.concatenate(
                        [jnp.where(wide_window == w, probs[h], nil) for w in range(per)], 0
                    )
                )
            rows = slice(2 * m * size, 2 * (m + 1) * size)
            got = dot(v_s[t, rows, :], jnp.concatenate(both, 1))
            for n in range(2):
                block = got[n * size : (n + 1) * size, tile(n)].reshape(-1, 8, LANES)
                block = block * inverse[2 * m + n][None]
                parts.append(block.reshape(size, LANES))
        return jnp.concatenate(parts, 0).astype(BF16)

    inside = within(run)
    placed = []
    for t in range(tiles):
        at = tile(t)
        first = (nodes_ref[:, at].astype(F32) + dot(out_t, group(t))).astype(BF16)
        first_s[:, at] = first
        normed = norm_t(first.astype(F32), cols[:, 4:5])
        kept = iota((1, LANES), 1) + t * LANES < count
        head = jnp.where((iota((16, LANES), 0) > 0) | kept, normed[:16], FLAG)
        placed.append(dot(jnp.concatenate([head, normed[16:]], 0).astype(BF16), inside))
    keep_first = pltpu.make_async_copy(first_s, first_hbm, stores.at[0])
    keep_first.start()
    for t, block in enumerate(swap_blocks(placed)):
        sent_s[:, tile(t)] = block.astype(BF16)
    send = pltpu.make_async_copy(sent_s, sent_hbm, stores.at[1])
    send.start()
    wait_all([keep_first, send])


def tables_kernel(
    cap, qkv_hbm, out_hbm, up_hbm, slot_hbm, owner_hbm, voxel_hbm, gain_hbm, weights_s, facts_s,
    gain_s, hot_s, qkv_ref, out_ref, up_ref, slot_ref, owner_ref, voxel_ref, gain_ref, sems
):
    loads = start_all(
        [
            (qkv_hbm, qkv_ref),
            (out_hbm, out_ref),
            (up_hbm, up_ref),
            (slot_hbm, slot_ref),
            (owner_hbm, owner_ref),
            (voxel_hbm, voxel_ref),
            (gain_hbm, gain_ref),
        ],
        sems,
    )
    wait_all(loads)
    gain = jnp.concatenate([gain_ref[...], jnp.zeros((7, gain_ref.shape[1]), F32)], 0)
    gain_s[...] = jnp.broadcast_to(gain.T[:, 0:1], gain_s.shape)
    votes = slot_ref.shape[1]
    codes = facts_s.shape[1]
    owners = codes // cap
    chans = out_ref.shape[0]
    src = head_order(chans)
    src = jnp.concatenate([src, src + chans, src + 2 * chans], 0)
    shuffle = (src == iota((3 * chans, 3 * chans), 1)).astype(BF16)
    weights_s[: 3 * chans] = dot_t(shuffle, qkv_ref[...]).astype(BF16)
    out_t = dot(shuffle[:chans, :chans], out_ref[...])
    weights_s[3 * chans : 4 * chans] = transposed(out_t)
    weights_s[4 * chans :] = transposed(up_ref[...])
    owner = jnp.bitwise_xor(owner_ref[...], lax.axis_index("tile"))
    hot = owner == iota((owners, votes), 0)
    upto = (iota((votes, votes), 0) <= iota((votes, votes), 1)).astype(BF16)
    rank = jnp.sum(jnp.where(hot, dot(hot.astype(BF16), upto), 0.0), 0, keepdims=True)
    code = owner * cap + rank.astype(jnp.int32) - 1
    member = place(code % LANES, code // LANES, codes // LANES)
    slot = slot_ref[...]
    row = iota((16, votes), 0)
    facts = jnp.where(
        row == 0,
        voxel_ref[...],
        jnp.where(row == 1, slot // LANES, jnp.where(row == 2, slot % LANES, 1)),
    )
    listed = dot_t(facts.astype(F32).astype(BF16), member)
    facts = jnp.where(listed[3:4] > 0.5, listed, -1.0)
    facts_s[...] = facts.astype(BF16)
    low, high = facts[2:3].astype(jnp.int32), facts[1:2].astype(jnp.int32)
    hot_s[...] = place(low, high, hot_s.shape[0] // LANES)


def clean(block):
    head = block[:16].astype(F32)
    gone = head[0:1] > 0.5 * FLAG
    head = jnp.where((iota(head.shape, 0) == 0) & gone, 0.0, head)
    return jnp.concatenate([head.astype(BF16), block[16:]], 0), gone


def add_keys(blocks, kv_t, k_s, v_s, m_s):
    chans = kv_t.shape[1]
    tiles = k_s.shape[1]
    for n, block in enumerate(blocks):
        block, gone = clean(block)
        kv = dot(kv_t, block)
        mask = jnp.where(gone, -1e9, 0.0)
        for t in range(tiles):
            k_s[n, t] = kv[:chans, tile(t)].reshape(chans // 8, 8, LANES)
            v_s[n, t] = kv[chans:, tile(t)].reshape(chans // 8, 8, LANES)
            m_s[n, t] = jnp.broadcast_to(mask[:, tile(t)], (8, LANES))


def attend_two(t, run, q_s, k_s, v_s, m_s, s_s, state_s, fresh):
    rows8 = q_s.shape[1]
    cut = 2 * rows8 // 3
    keys = k_s.shape[0] * run
    base = (t // run) * run
    both = range(2)
    query = [[q_s[t + n, i] for i in range(rows8)] for n in both]

    def score(key, top):
        block, at = key // run, base + key % run
        mask = m_s[block, at]
        sums = [[None, None], [None, None]]
        for i in range(rows8):
            part = int(i >= cut)
            row = k_s[block, at, i]
            for n in both:
                term = query[n][i] * row
                held = sums[n][part]
                sums[n][part] = term if held is None else held + term
        tops = []
        for n in both:
            a, b = sums[n]
            b = b + pltpu.roll(b, 4, 0)
            a = a + mask
            b = b + mask
            s_s[key, 2 * n] = a
            s_s[key, 2 * n + 1] = b
            tops += [jnp.maximum(top[2 * n], a), jnp.maximum(top[2 * n + 1], b)]
        return tuple(tops)

    if fresh:
        old = tuple(jnp.full((8, LANES), -3e38, F32) for _ in range(4))
    else:
        old = tuple(state_s[t + n, rows8 + part] for n in both for part in both)
    tops = lax.fori_loop(0, keys, score, old, unroll=8)
    if fresh:
        zero = jnp.zeros((8, LANES), F32)
        sums = tuple(zero for _ in range(4))
        accs = tuple(zero for _ in range(2 * rows8))
    else:
        fade = [jnp.exp2(old[n] - tops[n]) for n in range(4)]
        sums = tuple(
            state_s[t + n, rows8 + 2 + part] * fade[2 * n + part] for n in both for part in both
        )
        accs = tuple(
            state_s[t + n, i] * fade[2 * n + int(i >= cut)] for n in both for i in range(rows8)
        )

    def gather(key, carry):
        sums, accs = carry
        block, at = key // run, base + key % run
        weight = [jnp.exp2(s_s[key, n] - tops[n]) for n in range(4)]
        accs = list(accs)
        for i in range(rows8):
            row = v_s[block, at, i]
            for n in both:
                at_acc = n * rows8 + i
                accs[at_acc] = accs[at_acc] + weight[2 * n + int(i >= cut)] * row
        return tuple(sums[n] + weight[n] for n in range(4)), tuple(accs)

    sums, accs = lax.fori_loop(0, keys, gather, (sums, accs), unroll=8)
    return tops, sums, accs


def hold_two(n, state, state_s):
    tops, sums, accs = state
    rows8 = len(accs) // 2
    for m in range(2):
        for i in range(rows8):
            state_s[2 * n + m, i] = accs[m * rows8 + i]
        for part in range(2):
            state_s[2 * n + m, rows8 + part] = tops[2 * m + part]
            state_s[2 * n + m, rows8 + 2 + part] = sums[2 * m + part]


def near_kernel(run, own_ref, near_ref, weights_ref, q_s, state_s, k_s, v_s, m_s, s_s):
    chans, slots = own_ref.shape
    tiles = slots // LANES
    scale = (chans // HEADS) ** -0.5 * LOG2E
    own, _ = clean(own_ref[...])
    query = dot(weights_ref[:chans, :], own) * scale
    for t in range(tiles):
        q_s[t] = query[:, tile(t)].reshape(chans // 8, 8, LANES)
    add_keys([own_ref[...], near_ref[...]], weights_ref[chans : 3 * chans, :], k_s, v_s, m_s)

    def step(n, _):
        hold_two(n, attend_two(2 * n, run, q_s, k_s, v_s, m_s, s_s, state_s, True), state_s)
        return 0

    lax.fori_loop(0, tiles // 2, step, 0)


def middle_kernel(run, count, *refs):
    blocks, refs = refs[:count], refs[count:]
    q_s, old_s, weights_ref, state_s, k_s, v_s, m_s, s_s = refs
    chans = weights_ref.shape[1]
    kv_t = weights_ref[chans : 3 * chans, :]
    add_keys([block[...] for block in blocks], kv_t, k_s, v_s, m_s)

    def step(n, _):
        hold_two(n, attend_two(2 * n, run, q_s, k_s, v_s, m_s, s_s, old_s, False), state_s)
        return 0

    lax.fori_loop(0, q_s.shape[0] // 2, step, 0)


def second_kernel(run, cap, far, owners, count_ref, *refs):
    blocks, refs = refs[:far], refs[far:]
    q_s, state_s, weights_s, first_s, gain_s, down_s, facts_s, hot_s, feat_hbm = refs[:9]
    votes_s, refs = refs[9 : 9 + owners // 2], refs[9 + owners // 2 :]
    feat_s, store, k_s, v_s, m_s, s_s, ctx_s, bf_s = refs
    chans, slots = first_s.shape
    tiles = slots // LANES
    count = count_ref[0]
    add_keys([block[...] for block in blocks], weights_s[chans : 3 * chans], k_s, v_s, m_s)
    rows8 = chans // 8

    def step(n, _):
        t = 2 * n
        _, sums, accs = attend_two(t, run, q_s, k_s, v_s, m_s, s_s, state_s, False)
        share = [1.0 / total for total in sums]
        cut = 2 * rows8 // 3
        for n in range(2):
            for i in range(rows8):
                ctx_s[t + n, i] = accs[n * rows8 + i] * share[2 * n + int(i >= cut)]
        return 0

    lax.fori_loop(0, tiles // 2, step, 0)
    ctx = swap_blocks([ctx_s[t].reshape(chans, LANES) for t in range(tiles)])
    ctx = dot_t(jnp.concatenate(ctx, 0).astype(BF16), within(run)).astype(BF16)
    ctx = jnp.concatenate([ctx[t * chans : (t + 1) * chans] for t in range(tiles)], 1)
    gain = gain_s[...]
    kept = iota((1, slots), 1) < count
    wide = 2 * LANES
    cuts = [slice(at, at + wide) for at in range(0, slots, wide)]
    out_t, up_t = weights_s[3 * chans : 4 * chans], weights_s[4 * chans :]

    def raise_chunk(at):
        moved = dot(out_t, ctx[:, at])
        inner = []
        for n in range(wide // LANES):
            lanes = slice(at.start + n * LANES, at.start + (n + 1) * LANES)
            second = first_s[:, lanes].astype(F32) + moved[:, tile(n)]
            feat_s[:, lanes] = second
            inner.append(norm_t(second, gain).astype(BF16))
        return dot(up_t, jnp.concatenate(inner, 1))

    raised = raise_chunk(cuts[0])
    for n, at in enumerate(cuts):
        now = raised
        if n + 1 < len(cuts):
            raised = raise_chunk(cuts[n + 1])
        hidden = gelu(now).astype(BF16)
        third = feat_s[:, at] + dot(down_s[...], hidden)
        third = jnp.where(kept[:, at], third, 0.0)
        feat_s[:, at] = third
        bf_s[:, at] = third.astype(BF16)
    keep = pltpu.make_async_copy(feat_s, feat_hbm, store)
    keep.start()
    picked = dot(bf_s[...], hot_s[...]).astype(BF16)
    for o in range(owners):
        at = slice(o * cap, (o + 1) * cap)
        ballot = jnp.concatenate([picked[:, at], facts_s[:8, at]], 0)
        votes_s[o % len(votes_s)][o // len(votes_s)] = ballot
    keep.wait()


def sums_kernel(*refs):
    ballots, outs = refs[:-2], refs[-2:]
    cap = ballots[0].shape[2]
    for kind, out_ref in enumerate(outs):
        chans, voxels = out_ref.shape
        total = jnp.zeros(out_ref.shape, F32)
        for ref in ballots:
            ballot = ref[kind]
            label = ballot[chans:].astype(F32)[0:1]
            hot = (label == iota((voxels, cap), 0).astype(F32)).astype(BF16)
            total = total + dot_t(ballot[:chans], hot)
        out_ref[...] = total.astype(out_ref.dtype)


def total_kernel(here_ref, there_ref, out_ref):
    out_ref[...] = here_ref[...] + there_ref[...].astype(F32)


def call(kernel, outs, scratch, flops, spaces, out_spaces, limit=VMEM):
    place_of = {"s": pltpu.SMEM, "v": pltpu.VMEM, "a": pl.ANY}
    return pl.pallas_call(
        kernel,
        out_shape=outs,
        in_specs=[pl.BlockSpec(memory_space=place_of[c]) for c in spaces],
        out_specs=[pl.BlockSpec(memory_space=place_of[c]) for c in out_spaces],
        scratch_shapes=scratch,
        compiler_params=pltpu.CompilerParams(vmem_limit_bytes=limit),
        cost_estimate=pl.CostEstimate(flops=flops, bytes_accessed=2 << 20, transcendentals=0),
    )


def turned(x, axis, bit):
    n = lax.axis_size(axis)
    return lax.ppermute(x, axis, [(i, i ^ bit) for i in range(n)])


def body(
    nodes,
    node_ids,
    node_count,
    pos_weight,
    gain_one,
    qkv_one,
    out_one,
    gain_two,
    qkv_two,
    out_two,
    gain_three,
    w_up,
    w_down,
    vote_slot,
    vote_owner,
    vote_voxel,
):
    slots, chans = nodes.shape
    groups, owners = lax.axis_size("grp"), lax.axis_size("tile")
    run = WIN // groups
    votes = vote_slot.shape[0]
    cap = 2 * votes // owners
    codes = owners * cap
    tiles = slots // LANES
    rows8 = chans // 8
    hidden = w_up.shape[1]
    per = LANES // WIN
    sds = jax.ShapeDtypeStruct
    vmem = pltpu.VMEM
    dma = pltpu.SemaphoreType.DMA

    first, sent = call(
        functools.partial(first_kernel, run),
        [sds((chans, slots), BF16), sds((chans, slots), BF16)],
        [
            vmem((chans, slots), BF16),
            vmem((1, slots), jnp.int32),
            vmem((3, chans), F32),
            vmem((1, chans), F32),
            vmem((1, chans), F32),
            vmem((chans, 3 * chans), BF16),
            vmem((chans, chans), BF16),
            dma((7,)),
            vmem((3 * chans, slots), BF16),
            vmem((tiles, chans, 2 * LANES), BF16),
            vmem((tiles, LANES, chans), BF16),
            vmem((tiles, chans, LANES), BF16),
            vmem((chans, slots), BF16),
            vmem((chans, slots), BF16),
            vmem((chans, slots), BF16),
            dma((2,)),
        ],
        2_000_000_000,
        "saaaaaaa",
        "aa",
    )(
        node_count,
        nodes.T,
        node_ids.reshape(1, slots),
        pos_weight,
        gain_one.reshape(1, chans),
        gain_two.reshape(1, chans),
        qkv_one,
        out_one,
    )
    bit = groups // 2
    mid = []
    while bit > 1:
        mid += [turned(block, "grp", bit) for block in [sent] + mid]
        bit //= 2
    near = turned(sent, "grp", 1)
    weights, facts, gain, hot = call(
        functools.partial(tables_kernel, cap),
        [
            sds((4 * chans + hidden, chans), BF16),
            sds((16, codes), BF16),
            sds((chans, LANES), F32),
            sds((slots, codes), BF16),
        ],
        [
            vmem((chans, 3 * chans), BF16),
            vmem((chans, chans), BF16),
            vmem((chans, hidden), BF16),
            vmem((1, votes), jnp.int32),
            vmem((1, votes), jnp.int32),
            vmem((1, votes), jnp.int32),
            vmem((1, chans), F32),
            dma((7,)),
        ],
        2_000_000_000,
        "aaaaaaa",
        "vvvv",
        limit=TIGHT,
    )(
        qkv_two,
        out_two,
        w_up,
        vote_slot.reshape(1, votes),
        vote_owner.reshape(1, votes),
        vote_voxel.reshape(1, votes),
        gain_three.reshape(1, chans),
    )
    q_like = ((tiles, rows8, 8, LANES), F32)
    state_like = ((tiles, rows8 + 4, 8, LANES), F32)

    def key_scratch(blocks):
        return [
            vmem((blocks, tiles, rows8, 8, LANES), F32),
            vmem((blocks, tiles, rows8, 8, LANES), F32),
            vmem((blocks, tiles, 8, LANES), F32),
            vmem((blocks * run, 4, 8, LANES), F32),
        ]

    query, state = call(
        functools.partial(near_kernel, run),
        [sds(*q_like), sds(*state_like)],
        key_scratch(2),
        3_000_000_000,
        "vvv",
        "vv",
        limit=ROOMY,
    )(sent, near, weights)
    mid, query = lax.optimization_barrier((mid, query))
    far = [turned(block, "grp", 1) for block in mid]
    (state,) = call(
        functools.partial(middle_kernel, run, len(mid)),
        [sds(*state_like)],
        key_scratch(len(mid)),
        2_000_000_000,
        "v" * len(mid) + "vvv",
        "v",
        limit=ROOMY,
    )(*mid, query, state, weights)
    features_t, *ballots = call(
        functools.partial(second_kernel, run, cap, len(far), owners),
        [sds((chans, slots), F32)] + [sds((2, chans + 8, cap), BF16)] * (owners // 2),
        [vmem((chans, slots), F32), dma]
        + key_scratch(len(far))
        + [vmem(*q_like), vmem((chans, slots), BF16)],
        3_000_000_000,
        "s" + "v" * (len(far) + 8),
        "a" + "v" * (owners // 2),
        limit=ROOMY,
    )(
        node_count,
        *far,
        query,
        state,
        weights,
        first,
        gain,
        w_down.T,
        facts,
        hot,
    )
    half = owners // 2
    got = [ballots[0]] + [turned(ballots[k], "tile", k) for k in range(1, half)]
    here, there = call(
        sums_kernel,
        [sds((chans, VOX_DEV), F32), sds((chans, VOX_DEV), BF16)],
        [],
        200_000_000,
        "v" * half,
        "vv",
        limit=ROOMY,
    )(*got)
    (sums_t,) = call(
        total_kernel, [sds((chans, VOX_DEV), F32)], [], 1_000_000, "vv", "v", limit=ROOMY
    )(here, turned(there, "tile", half))
    return (features_t.T, sums_t.T)


def solution(mesh):
    in_specs = (
        P(("grp", "tile"), None),
        P(("grp", "tile")),
        P(("grp", "tile")),
        P(),
        P(),
        P(),
        P(),
        P(),
        P(),
        P(),
        P(),
        P(),
        P(),
        P(("grp", "tile")),
        P(("grp", "tile"), None),
        P(("grp", "tile")),
    )
    out_specs = (P(("grp", "tile"), None), P(("grp", "tile"), None))
    return jax.shard_map(body, mesh=mesh, in_specs=in_specs, out_specs=out_specs, check_vma=False)
```

```python
import functools
import math

import jax
import jax.numpy as jnp
from jax import lax
from jax.experimental import pallas as pl
from jax.experimental.pallas import tpu as pltpu
from jax.sharding import PartitionSpec as P

HEADS = 12
WIN = 32
VOX_DEV = 256
LANES = 128
FLAG = 16384.0
VMEM = 64 * 1024 * 1024 - 65536
TIGHT = VMEM - 2 * 1024 * 1024
ROOMY = 24 * 1024 * 1024
F32 = jnp.float32
BF16 = jnp.bfloat16
LOG2E = math.log2(math.e)


def iota(shape, dim):
    return lax.broadcasted_iota(jnp.int32, shape, dim)


def dot(a, b):
    return jnp.dot(a, b, preferred_element_type=F32)


def dot_t(a, b):
    return lax.dot_general(a, b, (((1,), (1,)), ((), ())), preferred_element_type=F32)


def eye(n):
    return (iota((n, n), 0) == iota((n, n), 1)).astype(BF16)


def transposed(a):
    return a.astype(F32).T.astype(BF16)


def tile(t):
    return slice(t * LANES, (t + 1) * LANES)


def head_order(chans):
    size = chans // HEADS
    cut = 8 * size
    j = iota((chans, 1), 0)
    high = j - cut
    low_src = (j % 8) * size + j // 8
    high_src = (8 + high % 4) * size + high // 8 + (size // 2) * ((high % 8) // 4)
    return jnp.where(j < cut, low_src, high_src)


def within(run):
    lane = iota((1, LANES), 1)
    q, e = lane // 16, lane % 16
    p = (4 * (q // run) + e // 4) * run + q % run
    return ((e % 4) * WIN + p == iota((LANES, LANES), 0)).astype(BF16)


def swap_blocks(tiles):
    tiles = list(tiles)
    block = iota(tiles[0].shape, 1) // 16
    step = len(tiles) // 2
    while step:
        for n in range(len(tiles)):
            if n & step:
                continue
            a, b = tiles[n], tiles[n + step]
            low = block // step % 2 == 0
            tiles[n] = jnp.where(low, a, pltpu.roll(b, 16 * step, 1))
            tiles[n + step] = jnp.where(low, pltpu.roll(a, LANES - 16 * step, 1), b)
        step //= 2
    return tiles


def place(low, high, blocks):
    base = jnp.where(low == iota((LANES, low.shape[1]), 0), 1.0, 0.0).astype(BF16)
    high = jnp.broadcast_to(high, base.shape).astype(F32).astype(BF16)
    nil = jnp.zeros_like(base)
    parts = [jnp.where(high == jnp.asarray(n, BF16), base, nil) for n in range(blocks)]
    return jnp.concatenate(parts, 0)


def norm_t(x, gain):
    inv = 1.0 / x.shape[0]
    mean = jnp.sum(x, 0, keepdims=True) * inv
    cent = x - mean
    var = jnp.sum(cent * cent, 0, keepdims=True) * inv
    return cent * lax.rsqrt(var + 1e-05) * gain


def gelu(x):
    half = 0.5 * x
    scale = math.sqrt(2 / math.pi)
    return half + half * jnp.tanh(x * (scale + (0.044715 * scale) * (x * x)))


def start_all(pairs, sems):
    copies = [pltpu.make_async_copy(a, b, sems.at[n]) for n, (a, b) in enumerate(pairs)]
    for copy in copies:
        copy.start()
    return copies


def wait_all(copies):
    for copy in copies:
        copy.wait()


def fold8(x, op):
    y = x[0]
    for n in range(1, x.shape[0]):
        y = op(y, x[n])
    for shift in (4, 2, 1):
        y = op(y, pltpu.roll(y, shift, 0))
    return y


def first_kernel(
    run, count_ref, nodes_hbm, ids_hbm, pos_hbm, gain_one_hbm, gain_two_hbm, qkv_hbm, out_hbm,
    first_hbm, sent_hbm, nodes_ref, ids_ref, pos_ref, gain_one_ref, gain_two_ref, qkv_ref, out_ref,
    sems, qkv_s, q_s, k_s, v_s, ctx_s, n_s, stack_s, first_s, sent_s, stores
):
    loads = start_all(
        [
            (nodes_hbm, nodes_ref),
            (ids_hbm, ids_ref),
            (pos_hbm, pos_ref),
            (gain_one_hbm, gain_one_ref),
            (gain_two_hbm, gain_two_ref),
            (qkv_hbm, qkv_ref),
            (out_hbm, out_ref),
        ],
        sems,
    )
    chans, slots = nodes_ref.shape
    tiles = slots // LANES
    size = chans // HEADS
    per = LANES // WIN
    count = count_ref[0]
    wait_all(loads)
    cols = jnp.concatenate(
        [pos_ref[...], gain_one_ref[...], gain_two_ref[...], jnp.zeros((3, chans), F32)], 0
    ).T
    ids = ids_ref[...]
    coords = []
    for axis in range(3):
        total = jnp.zeros(ids.shape, jnp.int32)
        for level in range(6):
            bit = jnp.bitwise_and(jnp.right_shift(ids, 3 * level + axis), 1)
            total = total + bit * 2**level
        coords.append(total.astype(F32) / 64.0 - 0.5)
    for t in range(tiles):
        at = tile(t)
        start = cols[:, 0:1] * coords[0][:, at]
        for axis in range(1, 3):
            start = start + cols[:, axis : axis + 1] * coords[axis][:, at]
        start = (nodes_ref[:, at].astype(F32) + start).astype(BF16)
        nodes_ref[:, at] = start
        n_s[:, at] = norm_t(start.astype(F32), cols[:, 3:4]).astype(BF16)
    qkv_t = transposed(qkv_ref[...])
    out_t = transposed(out_ref[...])
    qkv_s[...] = dot(qkv_t, n_s[...]).astype(BF16)
    side = eye(2 * LANES)
    row_head = iota((chans, LANES), 0) // size
    even_row = row_head % 2 == 0
    for t in range(tiles):
        query = qkv_s[:chans, tile(t)].astype(F32) * size**-0.5
        q_s[t, :, :LANES] = jnp.where(even_row, query, 0.0).astype(BF16)
        q_s[t, :, LANES:] = jnp.where(even_row, 0.0, query).astype(BF16)
        v_s[t] = qkv_s[2 * chans :, tile(t)]
    for t in range(0, tiles, 2):
        keys = qkv_s[chans : 2 * chans, t * LANES : (t + 2) * LANES]
        rows = dot_t(side, keys).astype(BF16)
        k_s[t] = rows[:LANES]
        k_s[t + 1] = rows[LANES:]

    lane_pair = iota((WIN, chans), 1) // (2 * size)
    window = iota((8, LANES), 1) // WIN
    wide_window = iota((WIN, LANES), 1) // WIN
    rank = iota((WIN, LANES), 0) + WIN * (iota((WIN, LANES), 1) // WIN)

    def group(t, _):
        query = q_s[t]
        even, odd = None, None
        for w in range(per):
            keys = k_s[t, w * WIN : (w + 1) * WIN, :]
            by_pair = jnp.concatenate(
                [jnp.where(lane_pair == m, keys, jnp.zeros_like(keys)) for m in range(HEADS // 2)],
                0,
            )
            got = dot(by_pair, query)
            left = got[:, :LANES].reshape(-1, 8, LANES)
            right = got[:, LANES:].reshape(-1, 8, LANES)
            even = left if w == 0 else jnp.where(window[None] == w, left, even)
            odd = right if w == 0 else jnp.where(window[None] == w, right, odd)
        mask = jnp.where(rank + t * LANES < count, 0.0, -1e9).astype(F32)
        mask = mask.reshape(WIN // 8, 8, LANES)
        probs, inverse = [], []
        for h in range(HEADS):
            scores = (even, odd)[h % 2]
            mine = scores[h // 2 * (WIN // 8) : (h // 2 + 1) * (WIN // 8)] + mask
            top = fold8(mine, jnp.maximum)
            weight = jnp.exp(mine - top[None])
            inverse.append(1.0 / fold8(weight, jnp.add))
            probs.append(weight.reshape(WIN, LANES).astype(BF16))
        parts = []
        for m in range(HEADS // 2):
            both = []
            for h in (2 * m, 2 * m + 1):
                nil = jnp.zeros_like(probs[h])
                both.append(
                    jnp.concatenate(
                        [jnp.where(wide_window == w, probs[h], nil) for w in range(per)], 0
                    )
                )
            rows = slice(2 * m * size, 2 * (m + 1) * size)
            got = dot(v_s[t, rows, :], jnp.concatenate(both, 1))
            for n in range(2):
                block = got[n * size : (n + 1) * size, tile(n)].reshape(-1, 8, LANES)
                block = block * inverse[2 * m + n][None]
                parts.append(block.reshape(size, LANES))
        ctx_s[t] = jnp.concatenate(parts, 0).astype(BF16)
        return 0

    lax.fori_loop(0, tiles, group, 0, unroll=8)
    ctx = jnp.concatenate([ctx_s[t] for t in range(tiles)], 1)
    moved = dot(out_t, ctx)
    for t in range(tiles):
        at = tile(t)
        first = (nodes_ref[:, at].astype(F32) + moved[:, at]).astype(BF16)
        first_s[:, at] = first
        normed = norm_t(first.astype(F32), cols[:, 4:5])
        kept = iota((1, LANES), 1) + t * LANES < count
        head = jnp.where((iota((16, LANES), 0) > 0) | kept, normed[:16], FLAG)
        stack_s[t * chans : (t + 1) * chans] = jnp.concatenate([head, normed[16:]], 0).astype(BF16)
    keep_first = pltpu.make_async_copy(first_s, first_hbm, stores.at[0])
    keep_first.start()
    moved = dot(stack_s[...], within(run))
    moved = swap_blocks([moved[t * chans : (t + 1) * chans] for t in range(tiles)])
    for t in range(tiles):
        sent_s[:, tile(t)] = moved[t].astype(BF16)
    send = pltpu.make_async_copy(sent_s, sent_hbm, stores.at[1])
    send.start()
    wait_all([keep_first, send])


def tables_kernel(
    cap, qkv_hbm, out_hbm, up_hbm, slot_hbm, owner_hbm, voxel_hbm, gain_hbm, weights_s, facts_s,
    gain_s, hot_s, qkv_ref, out_ref, up_ref, slot_ref, owner_ref, voxel_ref, gain_ref, sems
):
    loads = start_all(
        [
            (qkv_hbm, qkv_ref),
            (out_hbm, out_ref),
            (up_hbm, up_ref),
            (slot_hbm, slot_ref),
            (owner_hbm, owner_ref),
            (voxel_hbm, voxel_ref),
            (gain_hbm, gain_ref),
        ],
        sems,
    )
    wait_all(loads)
    gain = jnp.concatenate([gain_ref[...], jnp.zeros((7, gain_ref.shape[1]), F32)], 0)
    gain_s[...] = jnp.broadcast_to(gain.T[:, 0:1], gain_s.shape)
    votes = slot_ref.shape[1]
    codes = facts_s.shape[1]
    owners = codes // cap
    chans = out_ref.shape[0]
    src = head_order(chans)
    src = jnp.concatenate([src, src + chans, src + 2 * chans], 0)
    shuffle = (src == iota((3 * chans, 3 * chans), 1)).astype(BF16)
    weights_s[: 3 * chans] = dot_t(shuffle, qkv_ref[...]).astype(BF16)
    out_t = dot(shuffle[:chans, :chans], out_ref[...])
    weights_s[3 * chans : 4 * chans] = transposed(out_t)
    weights_s[4 * chans :] = transposed(up_ref[...])
    owner = jnp.bitwise_xor(owner_ref[...], lax.axis_index("tile"))
    hot = owner == iota((owners, votes), 0)
    upto = (iota((votes, votes), 0) <= iota((votes, votes), 1)).astype(BF16)
    rank = jnp.sum(jnp.where(hot, dot(hot.astype(BF16), upto), 0.0), 0, keepdims=True)
    code = owner * cap + rank.astype(jnp.int32) - 1
    member = place(code % LANES, code // LANES, codes // LANES)
    slot = slot_ref[...]
    row = iota((16, votes), 0)
    facts = jnp.where(
        row == 0,
        voxel_ref[...],
        jnp.where(row == 1, slot // LANES, jnp.where(row == 2, slot % LANES, 1)),
    )
    listed = dot_t(facts.astype(F32).astype(BF16), member)
    facts = jnp.where(listed[3:4] > 0.5, listed, -1.0)
    facts_s[...] = facts.astype(BF16)
    low, high = facts[2:3].astype(jnp.int32), facts[1:2].astype(jnp.int32)
    hot_s[...] = place(low, high, hot_s.shape[0] // LANES)


def clean(block):
    head = block[:16].astype(F32)
    gone = head[0:1] > 0.5 * FLAG
    head = jnp.where((iota(head.shape, 0) == 0) & gone, 0.0, head)
    return jnp.concatenate([head.astype(BF16), block[16:]], 0), gone


def add_keys(blocks, kv_t, k_s, v_s, m_s):
    chans = kv_t.shape[1]
    tiles = k_s.shape[1]
    for n, block in enumerate(blocks):
        block, gone = clean(block)
        kv = dot(kv_t, block)
        mask = jnp.where(gone, -1e9, 0.0)
        for t in range(tiles):
            k_s[n, t] = kv[:chans, tile(t)].reshape(chans // 8, 8, LANES)
            v_s[n, t] = kv[chans:, tile(t)].reshape(chans // 8, 8, LANES)
            m_s[n, t] = jnp.broadcast_to(mask[:, tile(t)], (8, LANES))


def attend_two(t, run, q_s, k_s, v_s, m_s, s_s, state_s, fresh):
    rows8 = q_s.shape[1]
    cut = 2 * rows8 // 3
    keys = k_s.shape[0] * run
    base = (t // run) * run
    both = range(2)
    query = [[q_s[t + n, i] for i in range(rows8)] for n in both]

    def score(key, top):
        block, at = key // run, base + key % run
        mask = m_s[block, at]
        sums = [[None, None], [None, None]]
        for i in range(rows8):
            part = int(i >= cut)
            row = k_s[block, at, i]
            for n in both:
                term = query[n][i] * row
                held = sums[n][part]
                sums[n][part] = term if held is None else held + term
        tops = []
        for n in both:
            a, b = sums[n]
            b = b + pltpu.roll(b, 4, 0)
            a = a + mask
            b = b + mask
            s_s[key, 2 * n] = a
            s_s[key, 2 * n + 1] = b
            tops += [jnp.maximum(top[2 * n], a), jnp.maximum(top[2 * n + 1], b)]
        return tuple(tops)

    if fresh:
        old = tuple(jnp.full((8, LANES), -3e38, F32) for _ in range(4))
    else:
        old = tuple(state_s[t + n, rows8 + part] for n in both for part in both)
    tops = lax.fori_loop(0, keys, score, old, unroll=8)
    if fresh:
        zero = jnp.zeros((8, LANES), F32)
        sums = tuple(zero for _ in range(4))
        accs = tuple(zero for _ in range(2 * rows8))
    else:
        fade = [jnp.exp2(old[n] - tops[n]) for n in range(4)]
        sums = tuple(
            state_s[t + n, rows8 + 2 + part] * fade[2 * n + part] for n in both for part in both
        )
        accs = tuple(
            state_s[t + n, i] * fade[2 * n + int(i >= cut)] for n in both for i in range(rows8)
        )

    def gather(key, carry):
        sums, accs = carry
        block, at = key // run, base + key % run
        weight = [jnp.exp2(s_s[key, n] - tops[n]) for n in range(4)]
        accs = list(accs)
        for i in range(rows8):
            row = v_s[block, at, i]
            for n in both:
                at_acc = n * rows8 + i
                accs[at_acc] = accs[at_acc] + weight[2 * n + int(i >= cut)] * row
        return tuple(sums[n] + weight[n] for n in range(4)), tuple(accs)

    sums, accs = lax.fori_loop(0, keys, gather, (sums, accs), unroll=8)
    return tops, sums, accs


def hold_two(n, state, state_s):
    tops, sums, accs = state
    rows8 = len(accs) // 2
    for m in range(2):
        for i in range(rows8):
            state_s[2 * n + m, i] = accs[m * rows8 + i]
        for part in range(2):
            state_s[2 * n + m, rows8 + part] = tops[2 * m + part]
            state_s[2 * n + m, rows8 + 2 + part] = sums[2 * m + part]


def near_kernel(run, own_ref, near_ref, weights_ref, q_s, state_s, k_s, v_s, m_s, s_s):
    chans, slots = own_ref.shape
    tiles = slots // LANES
    scale = (chans // HEADS) ** -0.5 * LOG2E
    own, _ = clean(own_ref[...])
    query = dot(weights_ref[:chans, :], own) * scale
    for t in range(tiles):
        q_s[t] = query[:, tile(t)].reshape(chans // 8, 8, LANES)
    add_keys([own_ref[...], near_ref[...]], weights_ref[chans : 3 * chans, :], k_s, v_s, m_s)

    def step(n, _):
        hold_two(n, attend_two(2 * n, run, q_s, k_s, v_s, m_s, s_s, state_s, True), state_s)
        return 0

    lax.fori_loop(0, tiles // 2, step, 0)


def middle_kernel(run, count, *refs):
    blocks, refs = refs[:count], refs[count:]
    q_s, old_s, weights_ref, state_s, k_s, v_s, m_s, s_s = refs
    chans = weights_ref.shape[1]
    kv_t = weights_ref[chans : 3 * chans, :]
    add_keys([block[...] for block in blocks], kv_t, k_s, v_s, m_s)

    def step(n, _):
        hold_two(n, attend_two(2 * n, run, q_s, k_s, v_s, m_s, s_s, old_s, False), state_s)
        return 0

    lax.fori_loop(0, q_s.shape[0] // 2, step, 0)


def second_kernel(run, cap, far, owners, count_ref, *refs):
    blocks, refs = refs[:far], refs[far:]
    q_s, state_s, weights_s, first_s, gain_s, down_s, facts_s, hot_s, feat_hbm = refs[:9]
    votes_s, refs = refs[9 : 9 + owners // 2], refs[9 + owners // 2 :]
    feat_s, store, k_s, v_s, m_s, s_s, ctx_s, bf_s, inner_s = refs
    chans, slots = first_s.shape
    tiles = slots // LANES
    count = count_ref[0]
    add_keys([block[...] for block in blocks], weights_s[chans : 3 * chans], k_s, v_s, m_s)
    rows8 = chans // 8

    def step(n, _):
        t = 2 * n
        _, sums, accs = attend_two(t, run, q_s, k_s, v_s, m_s, s_s, state_s, False)
        share = [1.0 / total for total in sums]
        cut = 2 * rows8 // 3
        for n in range(2):
            for i in range(rows8):
                ctx_s[t + n, i] = accs[n * rows8 + i] * share[2 * n + int(i >= cut)]
        return 0

    lax.fori_loop(0, tiles // 2, step, 0)
    ctx = swap_blocks([ctx_s[t].reshape(chans, LANES) for t in range(tiles)])
    ctx = dot_t(jnp.concatenate(ctx, 0).astype(BF16), within(run)).astype(BF16)
    ctx = jnp.concatenate([ctx[t * chans : (t + 1) * chans] for t in range(tiles)], 1)
    gain = gain_s[...]
    moved = dot(weights_s[3 * chans : 4 * chans], ctx)
    for t in range(tiles):
        at = tile(t)
        second = first_s[:, at].astype(F32) + moved[:, at]
        feat_s[:, at] = second
        inner_s[:, at] = norm_t(second, gain).astype(BF16)
    kept = iota((1, slots), 1) < count
    wide = 2 * LANES
    cuts = [slice(at, at + wide) for at in range(0, slots, wide)]
    up_t = weights_s[4 * chans :]
    raised = dot(up_t, inner_s[:, cuts[0]])
    for n, at in enumerate(cuts):
        now = raised
        if n + 1 < len(cuts):
            raised = dot(up_t, inner_s[:, cuts[n + 1]])
        hidden = gelu(now).astype(BF16)
        third = feat_s[:, at] + dot(down_s[...], hidden)
        third = jnp.where(kept[:, at], third, 0.0)
        feat_s[:, at] = third
        bf_s[:, at] = third.astype(BF16)
    keep = pltpu.make_async_copy(feat_s, feat_hbm, store)
    keep.start()
    picked = dot(bf_s[...], hot_s[...]).astype(BF16)
    for o in range(owners):
        at = slice(o * cap, (o + 1) * cap)
        ballot = jnp.concatenate([picked[:, at], facts_s[:8, at]], 0)
        votes_s[o % len(votes_s)][o // len(votes_s)] = ballot
    keep.wait()


def sums_kernel(*refs):
    ballots, outs = refs[:-2], refs[-2:]
    cap = ballots[0].shape[2]
    for kind, out_ref in enumerate(outs):
        chans, voxels = out_ref.shape
        total = jnp.zeros(out_ref.shape, F32)
        for ref in ballots:
            ballot = ref[kind]
            label = ballot[chans:].astype(F32)[0:1]
            hot = (label == iota((voxels, cap), 0).astype(F32)).astype(BF16)
            total = total + dot_t(ballot[:chans], hot)
        out_ref[...] = total.astype(out_ref.dtype)


def total_kernel(here_ref, there_ref, out_ref):
    out_ref[...] = here_ref[...] + there_ref[...].astype(F32)


def call(kernel, outs, scratch, flops, spaces, out_spaces, limit=VMEM):
    place_of = {"s": pltpu.SMEM, "v": pltpu.VMEM, "a": pl.ANY}
    return pl.pallas_call(
        kernel,
        out_shape=outs,
        in_specs=[pl.BlockSpec(memory_space=place_of[c]) for c in spaces],
        out_specs=[pl.BlockSpec(memory_space=place_of[c]) for c in out_spaces],
        scratch_shapes=scratch,
        compiler_params=pltpu.CompilerParams(vmem_limit_bytes=limit),
        cost_estimate=pl.CostEstimate(flops=flops, bytes_accessed=2 << 20, transcendentals=0),
    )


def turned(x, axis, bit):
    n = lax.axis_size(axis)
    return lax.ppermute(x, axis, [(i, i ^ bit) for i in range(n)])


def body(
    nodes,
    node_ids,
    node_count,
    pos_weight,
    gain_one,
    qkv_one,
    out_one,
    gain_two,
    qkv_two,
    out_two,
    gain_three,
    w_up,
    w_down,
    vote_slot,
    vote_owner,
    vote_voxel,
):
    slots, chans = nodes.shape
    groups, owners = lax.axis_size("grp"), lax.axis_size("tile")
    run = WIN // groups
    votes = vote_slot.shape[0]
    cap = 2 * votes // owners
    codes = owners * cap
    tiles = slots // LANES
    rows8 = chans // 8
    hidden = w_up.shape[1]
    per = LANES // WIN
    sds = jax.ShapeDtypeStruct
    vmem = pltpu.VMEM
    dma = pltpu.SemaphoreType.DMA

    first, sent = call(
        functools.partial(first_kernel, run),
        [sds((chans, slots), BF16), sds((chans, slots), BF16)],
        [
            vmem((chans, slots), BF16),
            vmem((1, slots), jnp.int32),
            vmem((3, chans), F32),
            vmem((1, chans), F32),
            vmem((1, chans), F32),
            vmem((chans, 3 * chans), BF16),
            vmem((chans, chans), BF16),
            dma((7,)),
            vmem((3 * chans, slots), BF16),
            vmem((tiles, chans, 2 * LANES), BF16),
            vmem((tiles, LANES, chans), BF16),
            vmem((tiles, chans, LANES), BF16),
            vmem((tiles, chans, LANES), BF16),
            vmem((chans, slots), BF16),
            vmem((tiles * chans, LANES), BF16),
            vmem((chans, slots), BF16),
            vmem((chans, slots), BF16),
            dma((2,)),
        ],
        2_000_000_000,
        "saaaaaaa",
        "aa",
    )(
        node_count,
        nodes.T,
        node_ids.reshape(1, slots),
        pos_weight,
        gain_one.reshape(1, chans),
        gain_two.reshape(1, chans),
        qkv_one,
        out_one,
    )
    bit = groups // 2
    mid = []
    while bit > 1:
        mid += [turned(block, "grp", bit) for block in [sent] + mid]
        bit //= 2
    near = turned(sent, "grp", 1)
    weights, facts, gain, hot = call(
        functools.partial(tables_kernel, cap),
        [
            sds((4 * chans + hidden, chans), BF16),
            sds((16, codes), BF16),
            sds((chans, LANES), F32),
            sds((slots, codes), BF16),
        ],
        [
            vmem((chans, 3 * chans), BF16),
            vmem((chans, chans), BF16),
            vmem((chans, hidden), BF16),
            vmem((1, votes), jnp.int32),
            vmem((1, votes), jnp.int32),
            vmem((1, votes), jnp.int32),
            vmem((1, chans), F32),
            dma((7,)),
        ],
        2_000_000_000,
        "aaaaaaa",
        "vvvv",
        limit=TIGHT,
    )(
        qkv_two,
        out_two,
        w_up,
        vote_slot.reshape(1, votes),
        vote_owner.reshape(1, votes),
        vote_voxel.reshape(1, votes),
        gain_three.reshape(1, chans),
    )
    q_like = ((tiles, rows8, 8, LANES), F32)
    state_like = ((tiles, rows8 + 4, 8, LANES), F32)

    def key_scratch(blocks):
        return [
            vmem((blocks, tiles, rows8, 8, LANES), F32),
            vmem((blocks, tiles, rows8, 8, LANES), F32),
            vmem((blocks, tiles, 8, LANES), F32),
            vmem((blocks * run, 4, 8, LANES), F32),
        ]

    query, state = call(
        functools.partial(near_kernel, run),
        [sds(*q_like), sds(*state_like)],
        key_scratch(2),
        3_000_000_000,
        "vvv",
        "vv",
        limit=ROOMY,
    )(sent, near, weights)
    mid, query = lax.optimization_barrier((mid, query))
    far = [turned(block, "grp", 1) for block in mid]
    (state,) = call(
        functools.partial(middle_kernel, run, len(mid)),
        [sds(*state_like)],
        key_scratch(len(mid)),
        2_000_000_000,
        "v" * len(mid) + "vvv",
        "v",
        limit=ROOMY,
    )(*mid, query, state, weights)
    features_t, *ballots = call(
        functools.partial(second_kernel, run, cap, len(far), owners),
        [sds((chans, slots), F32)] + [sds((2, chans + 8, cap), BF16)] * (owners // 2),
        [vmem((chans, slots), F32), dma]
        + key_scratch(len(far))
        + [vmem(*q_like), vmem((chans, slots), BF16), vmem((chans, slots), BF16)],
        3_000_000_000,
        "s" + "v" * (len(far) + 8),
        "a" + "v" * (owners // 2),
        limit=ROOMY,
    )(
        node_count,
        *far,
        query,
        state,
        weights,
        first,
        gain,
        w_down.T,
        facts,
        hot,
    )
    half = owners // 2
    got = [ballots[0]] + [turned(ballots[k], "tile", k) for k in range(1, half)]
    here, there = call(
        sums_kernel,
        [sds((chans, VOX_DEV), F32), sds((chans, VOX_DEV), BF16)],
        [],
        200_000_000,
        "v" * half,
        "vv",
        limit=ROOMY,
    )(*got)
    (sums_t,) = call(
        total_kernel, [sds((chans, VOX_DEV), F32)], [], 1_000_000, "vv", "v", limit=ROOMY
    )(here, turned(there, "tile", half))
    return (features_t.T, sums_t.T)


def solution(mesh):
    in_specs = (
        P(("grp", "tile"), None),
        P(("grp", "tile")),
        P(("grp", "tile")),
        P(),
        P(),
        P(),
        P(),
        P(),
        P(),
        P(),
        P(),
        P(),
        P(),
        P(("grp", "tile")),
        P(("grp", "tile"), None),
        P(("grp", "tile")),
    )
    out_specs = (P(("grp", "tile"), None), P(("grp", "tile"), None))
    return jax.shard_map(body, mesh=mesh, in_specs=in_specs, out_specs=out_specs, check_vma=False)
```

```python
import functools
import math

import jax
import jax.numpy as jnp
from jax import lax
from jax.experimental import pallas as pl
from jax.experimental.pallas import tpu as pltpu
from jax.sharding import PartitionSpec as P

HEADS = 12
WIN = 32
VOX_DEV = 256
LANES = 128
FLAG = 16384.0
VMEM = 64 * 1024 * 1024 - 65536
TIGHT = VMEM - 2 * 1024 * 1024
ROOMY = 24 * 1024 * 1024
F32 = jnp.float32
BF16 = jnp.bfloat16
LOG2E = math.log2(math.e)


def iota(shape, dim):
    return lax.broadcasted_iota(jnp.int32, shape, dim)


def dot(a, b):
    return jnp.dot(a, b, preferred_element_type=F32)


def dot_t(a, b):
    return lax.dot_general(a, b, (((1,), (1,)), ((), ())), preferred_element_type=F32)


def eye(n):
    return (iota((n, n), 0) == iota((n, n), 1)).astype(BF16)


def transposed(a):
    return a.astype(F32).T.astype(BF16)


def tile(t):
    return slice(t * LANES, (t + 1) * LANES)


def head_order(chans):
    size = chans // HEADS
    cut = 8 * size
    j = iota((chans, 1), 0)
    high = j - cut
    low_src = (j % 8) * size + j // 8
    high_src = (8 + high % 4) * size + high // 8 + (size // 2) * ((high % 8) // 4)
    return jnp.where(j < cut, low_src, high_src)


def within(run):
    lane = iota((1, LANES), 1)
    q, e = lane // 16, lane % 16
    p = (4 * (q // run) + e // 4) * run + q % run
    return ((e % 4) * WIN + p == iota((LANES, LANES), 0)).astype(BF16)


def swap_blocks(tiles):
    tiles = list(tiles)
    block = iota(tiles[0].shape, 1) // 16
    step = len(tiles) // 2
    while step:
        for n in range(len(tiles)):
            if n & step:
                continue
            a, b = tiles[n], tiles[n + step]
            low = block // step % 2 == 0
            tiles[n] = jnp.where(low, a, pltpu.roll(b, 16 * step, 1))
            tiles[n + step] = jnp.where(low, pltpu.roll(a, LANES - 16 * step, 1), b)
        step //= 2
    return tiles


def place(low, high, blocks):
    base = jnp.where(low == iota((LANES, low.shape[1]), 0), 1.0, 0.0).astype(BF16)
    high = jnp.broadcast_to(high, base.shape).astype(F32).astype(BF16)
    nil = jnp.zeros_like(base)
    parts = [jnp.where(high == jnp.asarray(n, BF16), base, nil) for n in range(blocks)]
    return jnp.concatenate(parts, 0)


def norm_t(x, gain):
    inv = 1.0 / x.shape[0]
    mean = jnp.sum(x, 0, keepdims=True) * inv
    cent = x - mean
    var = jnp.sum(cent * cent, 0, keepdims=True) * inv
    return cent * lax.rsqrt(var + 1e-05) * gain


def gelu(x):
    half = 0.5 * x
    scale = math.sqrt(2 / math.pi)
    return half + half * jnp.tanh(x * (scale + (0.044715 * scale) * (x * x)))


def start_all(pairs, sems):
    copies = [pltpu.make_async_copy(a, b, sems.at[n]) for n, (a, b) in enumerate(pairs)]
    for copy in copies:
        copy.start()
    return copies


def wait_all(copies):
    for copy in copies:
        copy.wait()


def fold8(x, op):
    y = x[0]
    for n in range(1, x.shape[0]):
        y = op(y, x[n])
    for shift in (4, 2, 1):
        y = op(y, pltpu.roll(y, shift, 0))
    return y


def first_kernel(
    run, count_ref, nodes_hbm, ids_hbm, pos_hbm, gain_one_hbm, gain_two_hbm, qkv_hbm, out_hbm,
    first_hbm, sent_hbm, nodes_ref, ids_ref, pos_ref, gain_one_ref, gain_two_ref, qkv_ref, out_ref,
    sems, qkv_s, q_s, k_s, v_s, ctx_s, n_s, first_s, sent_s, stores
):
    loads = start_all(
        [
            (nodes_hbm, nodes_ref),
            (ids_hbm, ids_ref),
            (pos_hbm, pos_ref),
            (gain_one_hbm, gain_one_ref),
            (gain_two_hbm, gain_two_ref),
            (qkv_hbm, qkv_ref),
            (out_hbm, out_ref),
        ],
        sems,
    )
    chans, slots = nodes_ref.shape
    tiles = slots // LANES
    size = chans // HEADS
    per = LANES // WIN
    count = count_ref[0]
    wait_all(loads)
    cols = jnp.concatenate(
        [pos_ref[...], gain_one_ref[...], gain_two_ref[...], jnp.zeros((3, chans), F32)], 0
    ).T
    ids = ids_ref[...]
    coords = []
    for axis in range(3):
        total = jnp.zeros(ids.shape, jnp.int32)
        for level in range(6):
            bit = jnp.bitwise_and(jnp.right_shift(ids, 3 * level + axis), 1)
            total = total + bit * 2**level
        coords.append(total.astype(F32) / 64.0 - 0.5)
    for t in range(tiles):
        at = tile(t)
        start = cols[:, 0:1] * coords[0][:, at]
        for axis in range(1, 3):
            start = start + cols[:, axis : axis + 1] * coords[axis][:, at]
        start = (nodes_ref[:, at].astype(F32) + start).astype(BF16)
        nodes_ref[:, at] = start
        n_s[:, at] = norm_t(start.astype(F32), cols[:, 3:4]).astype(BF16)
    qkv_t = transposed(qkv_ref[...])
    out_t = transposed(out_ref[...])
    qkv_s[...] = dot(qkv_t, n_s[...]).astype(BF16)
    side = eye(LANES)
    row_head = iota((chans, LANES), 0) // size
    even_row = row_head % 2 == 0
    for t in range(tiles):
        query = qkv_s[:chans, tile(t)].astype(F32) * size**-0.5
        q_s[t, :, :LANES] = jnp.where(even_row, query, 0.0).astype(BF16)
        q_s[t, :, LANES:] = jnp.where(even_row, 0.0, query).astype(BF16)
        k_s[t] = dot_t(side, qkv_s[chans : 2 * chans, tile(t)]).astype(BF16)
        v_s[t] = qkv_s[2 * chans :, tile(t)]

    lane_pair = iota((WIN, chans), 1) // (2 * size)
    window = iota((8, LANES), 1) // WIN
    wide_window = iota((WIN, LANES), 1) // WIN
    rank = iota((WIN, LANES), 0) + WIN * (iota((WIN, LANES), 1) // WIN)

    def group(t, _):
        query = q_s[t]
        even, odd = None, None
        for w in range(per):
            keys = k_s[t, w * WIN : (w + 1) * WIN, :]
            by_pair = jnp.concatenate(
                [jnp.where(lane_pair == m, keys, jnp.zeros_like(keys)) for m in range(HEADS // 2)],
                0,
            )
            got = dot(by_pair, query)
            left = got[:, :LANES].reshape(-1, 8, LANES)
            right = got[:, LANES:].reshape(-1, 8, LANES)
            even = left if w == 0 else jnp.where(window[None] == w, left, even)
            odd = right if w == 0 else jnp.where(window[None] == w, right, odd)
        mask = jnp.where(rank + t * LANES < count, 0.0, -1e9).astype(F32)
        mask = mask.reshape(WIN // 8, 8, LANES)
        probs, inverse = [], []
        for h in range(HEADS):
            scores = (even, odd)[h % 2]
            mine = scores[h // 2 * (WIN // 8) : (h // 2 + 1) * (WIN // 8)] + mask
            top = fold8(mine, jnp.maximum)
            weight = jnp.exp(mine - top[None])
            inverse.append(1.0 / fold8(weight, jnp.add))
            probs.append(weight.reshape(WIN, LANES).astype(BF16))
        parts = []
        for m in range(HEADS // 2):
            both = []
            for h in (2 * m, 2 * m + 1):
                nil = jnp.zeros_like(probs[h])
                both.append(
                    jnp.concatenate(
                        [jnp.where(wide_window == w, probs[h], nil) for w in range(per)], 0
                    )
                )
            rows = slice(2 * m * size, 2 * (m + 1) * size)
            got = dot(v_s[t, rows, :], jnp.concatenate(both, 1))
            for n in range(2):
                block = got[n * size : (n + 1) * size, tile(n)].reshape(-1, 8, LANES)
                block = block * inverse[2 * m + n][None]
                parts.append(block.reshape(size, LANES))
        ctx_s[t] = jnp.concatenate(parts, 0).astype(BF16)
        return 0

    lax.fori_loop(0, tiles, group, 0, unroll=8)
    ctx = jnp.concatenate([ctx_s[t] for t in range(tiles)], 1)
    moved = dot(out_t, ctx)
    for t in range(tiles):
        at = tile(t)
        first = (nodes_ref[:, at].astype(F32) + moved[:, at]).astype(BF16)
        first_s[:, at] = first
        normed = norm_t(first.astype(F32), cols[:, 4:5])
        kept = iota((1, LANES), 1) + t * LANES < count
        head = jnp.where((iota((16, LANES), 0) > 0) | kept, normed[:16], FLAG)
        n_s[:, at] = jnp.concatenate([head, normed[16:]], 0).astype(BF16)
    keep_first = pltpu.make_async_copy(first_s, first_hbm, stores.at[0])
    keep_first.start()
    inside = within(run)
    for t, block in enumerate(swap_blocks([dot(n_s[:, tile(t)], inside) for t in range(tiles)])):
        sent_s[:, tile(t)] = block.astype(BF16)
    send = pltpu.make_async_copy(sent_s, sent_hbm, stores.at[1])
    send.start()
    wait_all([keep_first, send])


def tables_kernel(
    cap, qkv_hbm, out_hbm, up_hbm, slot_hbm, owner_hbm, voxel_hbm, gain_hbm, weights_s, facts_s,
    gain_s, qkv_ref, out_ref, up_ref, slot_ref, owner_ref, voxel_ref, gain_ref, sems
):
    loads = start_all(
        [
            (qkv_hbm, qkv_ref),
            (out_hbm, out_ref),
            (up_hbm, up_ref),
            (slot_hbm, slot_ref),
            (owner_hbm, owner_ref),
            (voxel_hbm, voxel_ref),
            (gain_hbm, gain_ref),
        ],
        sems,
    )
    wait_all(loads)
    gain = jnp.concatenate([gain_ref[...], jnp.zeros((7, gain_ref.shape[1]), F32)], 0)
    gain_s[...] = jnp.broadcast_to(gain.T[:, 0:1], gain_s.shape)
    votes = slot_ref.shape[1]
    codes = facts_s.shape[1]
    owners = codes // cap
    chans = out_ref.shape[0]
    src = head_order(chans)
    src = jnp.concatenate([src, src + chans, src + 2 * chans], 0)
    shuffle = (src == iota((3 * chans, 3 * chans), 1)).astype(BF16)
    weights_s[: 3 * chans] = dot_t(shuffle, qkv_ref[...]).astype(BF16)
    out_t = dot(shuffle[:chans, :chans], out_ref[...])
    weights_s[3 * chans : 4 * chans] = transposed(out_t)
    weights_s[4 * chans :] = transposed(up_ref[...])
    owner = jnp.bitwise_xor(owner_ref[...], lax.axis_index("tile"))
    hot = owner == iota((owners, votes), 0)
    upto = (iota((votes, votes), 0) <= iota((votes, votes), 1)).astype(BF16)
    rank = jnp.sum(jnp.where(hot, dot(hot.astype(BF16), upto), 0.0), 0, keepdims=True)
    code = owner * cap + rank.astype(jnp.int32) - 1
    member = place(code % LANES, code // LANES, codes // LANES)
    slot = slot_ref[...]
    row = iota((16, votes), 0)
    facts = jnp.where(
        row == 0,
        voxel_ref[...],
        jnp.where(row == 1, slot // LANES, jnp.where(row == 2, slot % LANES, 1)),
    )
    listed = dot_t(facts.astype(F32).astype(BF16), member)
    facts_s[...] = jnp.where(listed[3:4] > 0.5, listed, -1.0).astype(BF16)


def clean(block):
    head = block[:16].astype(F32)
    gone = head[0:1] > 0.5 * FLAG
    head = jnp.where((iota(head.shape, 0) == 0) & gone, 0.0, head)
    return jnp.concatenate([head.astype(BF16), block[16:]], 0), gone


def add_keys(blocks, kv_t, k_s, v_s, m_s):
    chans = kv_t.shape[1]
    tiles = k_s.shape[1]
    for n, block in enumerate(blocks):
        block, gone = clean(block)
        kv = dot(kv_t, block)
        mask = jnp.where(gone, -1e9, 0.0)
        for t in range(tiles):
            k_s[n, t] = kv[:chans, tile(t)].reshape(chans // 8, 8, LANES)
            v_s[n, t] = kv[chans:, tile(t)].reshape(chans // 8, 8, LANES)
            m_s[n, t] = jnp.broadcast_to(mask[:, tile(t)], (8, LANES))


def attend_two(t, run, q_s, k_s, v_s, m_s, s_s, state_s, fresh):
    rows8 = q_s.shape[1]
    cut = 2 * rows8 // 3
    keys = k_s.shape[0] * run
    base = (t // run) * run
    both = range(2)
    query = [[q_s[t + n, i] for i in range(rows8)] for n in both]

    def score(key, top):
        block, at = key // run, base + key % run
        mask = m_s[block, at]
        sums = [[None, None], [None, None]]
        for i in range(rows8):
            part = int(i >= cut)
            row = k_s[block, at, i]
            for n in both:
                term = query[n][i] * row
                held = sums[n][part]
                sums[n][part] = term if held is None else held + term
        tops = []
        for n in both:
            a, b = sums[n]
            b = b + pltpu.roll(b, 4, 0)
            a = a + mask
            b = b + mask
            s_s[key, 2 * n] = a
            s_s[key, 2 * n + 1] = b
            tops += [jnp.maximum(top[2 * n], a), jnp.maximum(top[2 * n + 1], b)]
        return tuple(tops)

    if fresh:
        old = tuple(jnp.full((8, LANES), -3e38, F32) for _ in range(4))
    else:
        old = tuple(state_s[t + n, rows8 + part] for n in both for part in both)
    tops = lax.fori_loop(0, keys, score, old, unroll=8)
    if fresh:
        zero = jnp.zeros((8, LANES), F32)
        sums = tuple(zero for _ in range(4))
        accs = tuple(zero for _ in range(2 * rows8))
    else:
        fade = [jnp.exp2(old[n] - tops[n]) for n in range(4)]
        sums = tuple(
            state_s[t + n, rows8 + 2 + part] * fade[2 * n + part] for n in both for part in both
        )
        accs = tuple(
            state_s[t + n, i] * fade[2 * n + int(i >= cut)] for n in both for i in range(rows8)
        )

    def gather(key, carry):
        sums, accs = carry
        block, at = key // run, base + key % run
        weight = [jnp.exp2(s_s[key, n] - tops[n]) for n in range(4)]
        accs = list(accs)
        for i in range(rows8):
            row = v_s[block, at, i]
            for n in both:
                at_acc = n * rows8 + i
                accs[at_acc] = accs[at_acc] + weight[2 * n + int(i >= cut)] * row
        return tuple(sums[n] + weight[n] for n in range(4)), tuple(accs)

    sums, accs = lax.fori_loop(0, keys, gather, (sums, accs), unroll=8)
    return tops, sums, accs


def hold_two(n, state, state_s):
    tops, sums, accs = state
    rows8 = len(accs) // 2
    for m in range(2):
        for i in range(rows8):
            state_s[2 * n + m, i] = accs[m * rows8 + i]
        for part in range(2):
            state_s[2 * n + m, rows8 + part] = tops[2 * m + part]
            state_s[2 * n + m, rows8 + 2 + part] = sums[2 * m + part]


def near_kernel(run, own_ref, near_ref, weights_ref, q_s, state_s, k_s, v_s, m_s, s_s):
    chans, slots = own_ref.shape
    tiles = slots // LANES
    scale = (chans // HEADS) ** -0.5 * LOG2E
    own, _ = clean(own_ref[...])
    query = dot(weights_ref[:chans, :], own) * scale
    for t in range(tiles):
        q_s[t] = query[:, tile(t)].reshape(chans // 8, 8, LANES)
    add_keys([own_ref[...], near_ref[...]], weights_ref[chans : 3 * chans, :], k_s, v_s, m_s)

    def step(n, _):
        hold_two(n, attend_two(2 * n, run, q_s, k_s, v_s, m_s, s_s, state_s, True), state_s)
        return 0

    lax.fori_loop(0, tiles // 2, step, 0)


def middle_kernel(run, count, *refs):
    blocks, refs = refs[:count], refs[count:]
    q_s, old_s, weights_ref, state_s, k_s, v_s, m_s, s_s = refs
    chans = weights_ref.shape[1]
    kv_t = weights_ref[chans : 3 * chans, :]
    add_keys([block[...] for block in blocks], kv_t, k_s, v_s, m_s)

    def step(n, _):
        hold_two(n, attend_two(2 * n, run, q_s, k_s, v_s, m_s, s_s, old_s, False), state_s)
        return 0

    lax.fori_loop(0, q_s.shape[0] // 2, step, 0)


def second_kernel(run, cap, far, owners, count_ref, *refs):
    blocks, refs = refs[:far], refs[far:]
    q_s, state_s, weights_s, first_s, gain_s, down_s, facts_s, feat_hbm = refs[:8]
    votes_s, refs = refs[8 : 8 + owners // 2], refs[8 + owners // 2 :]
    feat_s, store, k_s, v_s, m_s, s_s, ctx_s, bf_s, inner_s = refs
    chans, slots = first_s.shape
    tiles = slots // LANES
    count = count_ref[0]
    add_keys([block[...] for block in blocks], weights_s[chans : 3 * chans], k_s, v_s, m_s)
    rows8 = chans // 8

    def step(n, _):
        t = 2 * n
        _, sums, accs = attend_two(t, run, q_s, k_s, v_s, m_s, s_s, state_s, False)
        share = [1.0 / total for total in sums]
        cut = 2 * rows8 // 3
        for n in range(2):
            for i in range(rows8):
                ctx_s[t + n, i] = accs[n * rows8 + i] * share[2 * n + int(i >= cut)]
        return 0

    lax.fori_loop(0, tiles // 2, step, 0)
    ctx = swap_blocks([ctx_s[t].reshape(chans, LANES) for t in range(tiles)])
    ctx = dot_t(jnp.concatenate(ctx, 0).astype(BF16), within(run)).astype(BF16)
    ctx = jnp.concatenate([ctx[t * chans : (t + 1) * chans] for t in range(tiles)], 1)
    gain = gain_s[...]
    moved = dot(weights_s[3 * chans : 4 * chans], ctx)
    for t in range(tiles):
        at = tile(t)
        second = first_s[:, at].astype(F32) + moved[:, at]
        feat_s[:, at] = second
        inner_s[:, at] = norm_t(second, gain).astype(BF16)
    kept = iota((1, slots), 1) < count
    wide = 4 * LANES
    cuts = [slice(at, at + wide) for at in range(0, slots, wide)]
    up_t = weights_s[4 * chans :]
    raised = dot(up_t, inner_s[:, cuts[0]])
    for n, at in enumerate(cuts):
        now = raised
        if n + 1 < len(cuts):
            raised = dot(up_t, inner_s[:, cuts[n + 1]])
        hidden = gelu(now).astype(BF16)
        third = feat_s[:, at] + dot(down_s[...], hidden)
        third = jnp.where(kept[:, at], third, 0.0)
        feat_s[:, at] = third
        bf_s[:, at] = third.astype(BF16)
    keep = pltpu.make_async_copy(feat_s, feat_hbm, store)
    keep.start()
    facts = facts_s[...].astype(F32)
    low, high = facts[2:3].astype(jnp.int32), facts[1:2].astype(jnp.int32)
    picked = dot(bf_s[...], place(low, high, tiles)).astype(BF16)
    for o in range(owners):
        at = slice(o * cap, (o + 1) * cap)
        ballot = jnp.concatenate([picked[:, at], facts_s[:8, at]], 0)
        votes_s[o % len(votes_s)][o // len(votes_s)] = ballot
    keep.wait()


def sums_kernel(*refs):
    ballots, outs = refs[:-2], refs[-2:]
    cap = ballots[0].shape[2]
    for kind, out_ref in enumerate(outs):
        chans, voxels = out_ref.shape
        total = jnp.zeros(out_ref.shape, F32)
        for ref in ballots:
            ballot = ref[kind]
            label = ballot[chans:].astype(F32)[0:1]
            hot = (label == iota((voxels, cap), 0).astype(F32)).astype(BF16)
            total = total + dot_t(ballot[:chans], hot)
        out_ref[...] = total.astype(out_ref.dtype)


def total_kernel(here_ref, there_ref, out_ref):
    out_ref[...] = here_ref[...] + there_ref[...].astype(F32)


def call(kernel, outs, scratch, flops, spaces, out_spaces, limit=VMEM):
    place_of = {"s": pltpu.SMEM, "v": pltpu.VMEM, "a": pl.ANY}
    return pl.pallas_call(
        kernel,
        out_shape=outs,
        in_specs=[pl.BlockSpec(memory_space=place_of[c]) for c in spaces],
        out_specs=[pl.BlockSpec(memory_space=place_of[c]) for c in out_spaces],
        scratch_shapes=scratch,
        compiler_params=pltpu.CompilerParams(vmem_limit_bytes=limit),
        cost_estimate=pl.CostEstimate(flops=flops, bytes_accessed=2 << 20, transcendentals=0),
    )


def turned(x, axis, bit):
    n = lax.axis_size(axis)
    return lax.ppermute(x, axis, [(i, i ^ bit) for i in range(n)])


def body(
    nodes,
    node_ids,
    node_count,
    pos_weight,
    gain_one,
    qkv_one,
    out_one,
    gain_two,
    qkv_two,
    out_two,
    gain_three,
    w_up,
    w_down,
    vote_slot,
    vote_owner,
    vote_voxel,
):
    slots, chans = nodes.shape
    groups, owners = lax.axis_size("grp"), lax.axis_size("tile")
    run = WIN // groups
    votes = vote_slot.shape[0]
    cap = 2 * votes // owners
    codes = owners * cap
    tiles = slots // LANES
    rows8 = chans // 8
    hidden = w_up.shape[1]
    per = LANES // WIN
    sds = jax.ShapeDtypeStruct
    vmem = pltpu.VMEM
    dma = pltpu.SemaphoreType.DMA

    first, sent = call(
        functools.partial(first_kernel, run),
        [sds((chans, slots), BF16), sds((chans, slots), BF16)],
        [
            vmem((chans, slots), BF16),
            vmem((1, slots), jnp.int32),
            vmem((3, chans), F32),
            vmem((1, chans), F32),
            vmem((1, chans), F32),
            vmem((chans, 3 * chans), BF16),
            vmem((chans, chans), BF16),
            dma((7,)),
            vmem((3 * chans, slots), BF16),
            vmem((tiles, chans, 2 * LANES), BF16),
            vmem((tiles, LANES, chans), BF16),
            vmem((tiles, chans, LANES), BF16),
            vmem((tiles, chans, LANES), BF16),
            vmem((chans, slots), BF16),
            vmem((chans, slots), BF16),
            vmem((chans, slots), BF16),
            dma((2,)),
        ],
        2_000_000_000,
        "saaaaaaa",
        "aa",
    )(
        node_count,
        nodes.T,
        node_ids.reshape(1, slots),
        pos_weight,
        gain_one.reshape(1, chans),
        gain_two.reshape(1, chans),
        qkv_one,
        out_one,
    )
    bit = groups // 2
    mid = []
    while bit > 1:
        mid += [turned(block, "grp", bit) for block in [sent] + mid]
        bit //= 2
    near = turned(sent, "grp", 1)
    weights, facts, gain = call(
        functools.partial(tables_kernel, cap),
        [
            sds((4 * chans + hidden, chans), BF16),
            sds((16, codes), BF16),
            sds((chans, LANES), F32),
        ],
        [
            vmem((chans, 3 * chans), BF16),
            vmem((chans, chans), BF16),
            vmem((chans, hidden), BF16),
            vmem((1, votes), jnp.int32),
            vmem((1, votes), jnp.int32),
            vmem((1, votes), jnp.int32),
            vmem((1, chans), F32),
            dma((7,)),
        ],
        2_000_000_000,
        "aaaaaaa",
        "vvv",
        limit=TIGHT,
    )(
        qkv_two,
        out_two,
        w_up,
        vote_slot.reshape(1, votes),
        vote_owner.reshape(1, votes),
        vote_voxel.reshape(1, votes),
        gain_three.reshape(1, chans),
    )
    q_like = ((tiles, rows8, 8, LANES), F32)
    state_like = ((tiles, rows8 + 4, 8, LANES), F32)

    def key_scratch(blocks):
        return [
            vmem((blocks, tiles, rows8, 8, LANES), F32),
            vmem((blocks, tiles, rows8, 8, LANES), F32),
            vmem((blocks, tiles, 8, LANES), F32),
            vmem((blocks * run, 4, 8, LANES), F32),
        ]

    query, state = call(
        functools.partial(near_kernel, run),
        [sds(*q_like), sds(*state_like)],
        key_scratch(2),
        3_000_000_000,
        "vvv",
        "vv",
        limit=ROOMY,
    )(sent, near, weights)
    mid, query = lax.optimization_barrier((mid, query))
    far = [turned(block, "grp", 1) for block in mid]
    (state,) = call(
        functools.partial(middle_kernel, run, len(mid)),
        [sds(*state_like)],
        key_scratch(len(mid)),
        2_000_000_000,
        "v" * len(mid) + "vvv",
        "v",
        limit=ROOMY,
    )(*mid, query, state, weights)
    features_t, *ballots = call(
        functools.partial(second_kernel, run, cap, len(far), owners),
        [sds((chans, slots), F32)] + [sds((2, chans + 8, cap), BF16)] * (owners // 2),
        [vmem((chans, slots), F32), dma]
        + key_scratch(len(far))
        + [vmem(*q_like), vmem((chans, slots), BF16), vmem((chans, slots), BF16)],
        3_000_000_000,
        "s" + "v" * (len(far) + 7),
        "a" + "v" * (owners // 2),
        limit=ROOMY,
    )(
        node_count,
        *far,
        query,
        state,
        weights,
        first,
        gain,
        w_down.T,
        facts,
    )
    half = owners // 2
    got = [ballots[0]] + [turned(ballots[k], "tile", k) for k in range(half - 1, 0, -1)]
    here, there = call(
        sums_kernel,
        [sds((chans, VOX_DEV), F32), sds((chans, VOX_DEV), BF16)],
        [],
        200_000_000,
        "v" * half,
        "vv",
        limit=ROOMY,
    )(*got)
    (sums_t,) = call(
        total_kernel, [sds((chans, VOX_DEV), F32)], [], 1_000_000, "vv", "v", limit=ROOMY
    )(here, turned(there, "tile", half))
    return (features_t.T, sums_t.T)


def solution(mesh):
    in_specs = (
        P(("grp", "tile"), None),
        P(("grp", "tile")),
        P(("grp", "tile")),
        P(),
        P(),
        P(),
        P(),
        P(),
        P(),
        P(),
        P(),
        P(),
        P(),
        P(("grp", "tile")),
        P(("grp", "tile"), None),
        P(("grp", "tile")),
    )
    out_specs = (P(("grp", "tile"), None), P(("grp", "tile"), None))
    return jax.shard_map(body, mesh=mesh, in_specs=in_specs, out_specs=out_specs, check_vma=False)
```

```python
import functools
import math

import jax
import jax.numpy as jnp
from jax import lax
from jax.experimental import pallas as pl
from jax.experimental.pallas import tpu as pltpu
from jax.sharding import PartitionSpec as P

HEADS = 12
WIN = 32
VOX_DEV = 256
LANES = 128
FLAG = 16384.0
VMEM = 64 * 1024 * 1024 - 65536
TIGHT = VMEM - 2 * 1024 * 1024
ROOMY = 24 * 1024 * 1024
F32 = jnp.float32
BF16 = jnp.bfloat16
LOG2E = math.log2(math.e)


def iota(shape, dim):
    return lax.broadcasted_iota(jnp.int32, shape, dim)


def dot(a, b):
    return jnp.dot(a, b, preferred_element_type=F32)


def dot_t(a, b):
    return lax.dot_general(a, b, (((1,), (1,)), ((), ())), preferred_element_type=F32)


def eye(n):
    return (iota((n, n), 0) == iota((n, n), 1)).astype(BF16)


def transposed(a):
    return a.astype(F32).T.astype(BF16)


def tile(t):
    return slice(t * LANES, (t + 1) * LANES)


def head_order(chans):
    size = chans // HEADS
    cut = 8 * size
    j = iota((chans, 1), 0)
    high = j - cut
    low_src = (j % 8) * size + j // 8
    high_src = (8 + high % 4) * size + high // 8 + (size // 2) * ((high % 8) // 4)
    return jnp.where(j < cut, low_src, high_src)


def within(run):
    lane = iota((1, LANES), 1)
    q, e = lane // 16, lane % 16
    p = (4 * (q // run) + e // 4) * run + q % run
    return ((e % 4) * WIN + p == iota((LANES, LANES), 0)).astype(BF16)


def swap_blocks(tiles):
    tiles = list(tiles)
    block = iota(tiles[0].shape, 1) // 16
    step = len(tiles) // 2
    while step:
        for n in range(len(tiles)):
            if n & step:
                continue
            a, b = tiles[n], tiles[n + step]
            low = block // step % 2 == 0
            tiles[n] = jnp.where(low, a, pltpu.roll(b, 16 * step, 1))
            tiles[n + step] = jnp.where(low, pltpu.roll(a, LANES - 16 * step, 1), b)
        step //= 2
    return tiles


def place(low, high, blocks):
    base = jnp.where(low == iota((LANES, low.shape[1]), 0), 1.0, 0.0).astype(BF16)
    high = jnp.broadcast_to(high, base.shape).astype(F32).astype(BF16)
    nil = jnp.zeros_like(base)
    parts = [jnp.where(high == jnp.asarray(n, BF16), base, nil) for n in range(blocks)]
    return jnp.concatenate(parts, 0)


def norm_t(x, gain):
    inv = 1.0 / x.shape[0]
    mean = jnp.sum(x, 0, keepdims=True) * inv
    cent = x - mean
    var = jnp.sum(cent * cent, 0, keepdims=True) * inv
    return cent * lax.rsqrt(var + 1e-05) * gain


def gelu(x):
    half = 0.5 * x
    scale = math.sqrt(2 / math.pi)
    return half + half * jnp.tanh(x * (scale + (0.044715 * scale) * (x * x)))


def start_all(pairs, sems):
    copies = [pltpu.make_async_copy(a, b, sems.at[n]) for n, (a, b) in enumerate(pairs)]
    for copy in copies:
        copy.start()
    return copies


def wait_all(copies):
    for copy in copies:
        copy.wait()


def fold8(x, op):
    y = x[0]
    for n in range(1, x.shape[0]):
        y = op(y, x[n])
    for shift in (4, 2, 1):
        y = op(y, pltpu.roll(y, shift, 0))
    return y


def first_kernel(
    run, count_ref, nodes_hbm, ids_hbm, pos_hbm, gain_one_hbm, gain_two_hbm, qkv_hbm, out_hbm,
    first_hbm, sent_hbm, nodes_ref, ids_ref, pos_ref, gain_one_ref, gain_two_ref, qkv_ref, out_ref,
    sems, qkv_s, q_s, k_s, v_s, ctx_s, n_s, first_s, sent_s, stores
):
    loads = start_all(
        [
            (nodes_hbm, nodes_ref),
            (ids_hbm, ids_ref),
            (pos_hbm, pos_ref),
            (gain_one_hbm, gain_one_ref),
            (gain_two_hbm, gain_two_ref),
            (qkv_hbm, qkv_ref),
            (out_hbm, out_ref),
        ],
        sems,
    )
    chans, slots = nodes_ref.shape
    tiles = slots // LANES
    size = chans // HEADS
    per = LANES // WIN
    count = count_ref[0]
    wait_all(loads)
    cols = jnp.concatenate(
        [pos_ref[...], gain_one_ref[...], gain_two_ref[...], jnp.zeros((3, chans), F32)], 0
    ).T
    ids = ids_ref[...]
    coords = []
    for axis in range(3):
        total = jnp.zeros(ids.shape, jnp.int32)
        for level in range(6):
            bit = jnp.bitwise_and(jnp.right_shift(ids, 3 * level + axis), 1)
            total = total + bit * 2**level
        coords.append(total.astype(F32) / 64.0 - 0.5)
    for t in range(tiles):
        at = tile(t)
        start = cols[:, 0:1] * coords[0][:, at]
        for axis in range(1, 3):
            start = start + cols[:, axis : axis + 1] * coords[axis][:, at]
        start = (nodes_ref[:, at].astype(F32) + start).astype(BF16)
        nodes_ref[:, at] = start
        n_s[:, at] = norm_t(start.astype(F32), cols[:, 3:4]).astype(BF16)
    qkv_t = transposed(qkv_ref[...])
    out_t = transposed(out_ref[...])
    qkv_s[...] = dot(qkv_t, n_s[...]).astype(BF16)
    side = eye(LANES)
    row_head = iota((chans, LANES), 0) // size
    even_row = row_head % 2 == 0
    for t in range(tiles):
        query = qkv_s[:chans, tile(t)].astype(F32) * size**-0.5
        q_s[t, :, :LANES] = jnp.where(even_row, query, 0.0).astype(BF16)
        q_s[t, :, LANES:] = jnp.where(even_row, 0.0, query).astype(BF16)
        k_s[t] = dot_t(side, qkv_s[chans : 2 * chans, tile(t)]).astype(BF16)
        v_s[t] = qkv_s[2 * chans :, tile(t)]

    lane_pair = iota((WIN, chans), 1) // (2 * size)
    window = iota((8, LANES), 1) // WIN
    wide_window = iota((WIN, LANES), 1) // WIN
    ones = jnp.ones((16, LANES), BF16)
    rank = iota((WIN, LANES), 0) + WIN * (iota((WIN, LANES), 1) // WIN)

    def group(t, _):
        query = q_s[t]
        even, odd = None, None
        for w in range(per):
            keys = k_s[t, w * WIN : (w + 1) * WIN, :]
            by_pair = jnp.concatenate(
                [jnp.where(lane_pair == m, keys, jnp.zeros_like(keys)) for m in range(HEADS // 2)],
                0,
            )
            got = dot(by_pair, query)
            left = got[:, :LANES].reshape(-1, 8, LANES)
            right = got[:, LANES:].reshape(-1, 8, LANES)
            even = left if w == 0 else jnp.where(window[None] == w, left, even)
            odd = right if w == 0 else jnp.where(window[None] == w, right, odd)
        mask = jnp.where(rank + t * LANES < count, 0.0, -1e9).astype(F32)
        mask = mask.reshape(WIN // 8, 8, LANES)
        probs = []
        for h in range(HEADS):
            scores = (even, odd)[h % 2]
            mine = scores[h // 2 * (WIN // 8) : (h // 2 + 1) * (WIN // 8)] + mask
            top = fold8(mine, jnp.maximum)
            weight = jnp.exp(mine - top[None])
            probs.append(weight.reshape(WIN, LANES).astype(BF16))
        parts = []
        for m in range(HEADS // 2):
            both = []
            for h in (2 * m, 2 * m + 1):
                nil = jnp.zeros_like(probs[h])
                both.append(
                    jnp.concatenate(
                        [jnp.where(wide_window == w, probs[h], nil) for w in range(per)], 0
                    )
                )
            rows = slice(2 * m * size, 2 * (m + 1) * size)
            value = jnp.concatenate([v_s[t, rows, :], ones], 0)
            got = dot(value, jnp.concatenate(both, 1))
            for n in range(2):
                block = got[n * size : (n + 1) * size, tile(n)].reshape(-1, 8, LANES)
                block = block * (1.0 / got[2 * size : 2 * size + 8, tile(n)])[None]
                parts.append(block.reshape(size, LANES))
        ctx_s[t] = jnp.concatenate(parts, 0).astype(BF16)
        return 0

    lax.fori_loop(0, tiles, group, 0, unroll=8)
    ctx = jnp.concatenate([ctx_s[t] for t in range(tiles)], 1)
    moved = dot(out_t, ctx)
    for t in range(tiles):
        at = tile(t)
        first = (nodes_ref[:, at].astype(F32) + moved[:, at]).astype(BF16)
        first_s[:, at] = first
        normed = norm_t(first.astype(F32), cols[:, 4:5])
        kept = iota((1, LANES), 1) + t * LANES < count
        head = jnp.where((iota((16, LANES), 0) > 0) | kept, normed[:16], FLAG)
        n_s[:, at] = jnp.concatenate([head, normed[16:]], 0).astype(BF16)
    keep_first = pltpu.make_async_copy(first_s, first_hbm, stores.at[0])
    keep_first.start()
    inside = within(run)
    for t, block in enumerate(swap_blocks([dot(n_s[:, tile(t)], inside) for t in range(tiles)])):
        sent_s[:, tile(t)] = block.astype(BF16)
    send = pltpu.make_async_copy(sent_s, sent_hbm, stores.at[1])
    send.start()
    wait_all([keep_first, send])


def tables_kernel(
    cap, qkv_hbm, out_hbm, up_hbm, slot_hbm, owner_hbm, voxel_hbm, gain_hbm, weights_s, facts_s,
    gain_s, qkv_ref, out_ref, up_ref, slot_ref, owner_ref, voxel_ref, gain_ref, sems
):
    loads = start_all(
        [
            (qkv_hbm, qkv_ref),
            (out_hbm, out_ref),
            (up_hbm, up_ref),
            (slot_hbm, slot_ref),
            (owner_hbm, owner_ref),
            (voxel_hbm, voxel_ref),
            (gain_hbm, gain_ref),
        ],
        sems,
    )
    wait_all(loads)
    gain = jnp.concatenate([gain_ref[...], jnp.zeros((7, gain_ref.shape[1]), F32)], 0)
    gain_s[...] = jnp.broadcast_to(gain.T[:, 0:1], gain_s.shape)
    votes = slot_ref.shape[1]
    codes = facts_s.shape[1]
    owners = codes // cap
    chans = out_ref.shape[0]
    src = head_order(chans)
    src = jnp.concatenate([src, src + chans, src + 2 * chans], 0)
    shuffle = (src == iota((3 * chans, 3 * chans), 1)).astype(BF16)
    weights_s[: 3 * chans] = dot_t(shuffle, qkv_ref[...]).astype(BF16)
    out_t = dot(shuffle[:chans, :chans], out_ref[...])
    weights_s[3 * chans : 4 * chans] = transposed(out_t)
    weights_s[4 * chans :] = transposed(up_ref[...])
    owner = jnp.bitwise_xor(owner_ref[...], lax.axis_index("tile"))
    hot = owner == iota((owners, votes), 0)
    upto = (iota((votes, votes), 0) <= iota((votes, votes), 1)).astype(BF16)
    rank = jnp.sum(jnp.where(hot, dot(hot.astype(BF16), upto), 0.0), 0, keepdims=True)
    code = owner * cap + rank.astype(jnp.int32) - 1
    member = place(code % LANES, code // LANES, codes // LANES)
    slot = slot_ref[...]
    row = iota((16, votes), 0)
    facts = jnp.where(
        row == 0,
        voxel_ref[...],
        jnp.where(row == 1, slot // LANES, jnp.where(row == 2, slot % LANES, 1)),
    )
    listed = dot_t(facts.astype(F32).astype(BF16), member)
    facts_s[...] = jnp.where(listed[3:4] > 0.5, listed, -1.0).astype(BF16)


def clean(block):
    head = block[:16].astype(F32)
    gone = head[0:1] > 0.5 * FLAG
    head = jnp.where((iota(head.shape, 0) == 0) & gone, 0.0, head)
    return jnp.concatenate([head.astype(BF16), block[16:]], 0), gone


def add_keys(blocks, kv_t, k_s, v_s, m_s):
    chans = kv_t.shape[1]
    tiles = k_s.shape[1]
    for n, block in enumerate(blocks):
        block, gone = clean(block)
        kv = dot(kv_t, block)
        mask = jnp.where(gone, -1e9, 0.0)
        for t in range(tiles):
            k_s[n, t] = kv[:chans, tile(t)].reshape(chans // 8, 8, LANES)
            v_s[n, t] = kv[chans:, tile(t)].reshape(chans // 8, 8, LANES)
            m_s[n, t] = jnp.broadcast_to(mask[:, tile(t)], (8, LANES))


def attend_two(t, run, q_s, k_s, v_s, m_s, s_s, state_s, fresh):
    rows8 = q_s.shape[1]
    cut = 2 * rows8 // 3
    keys = k_s.shape[0] * run
    base = (t // run) * run
    both = range(2)
    query = [[q_s[t + n, i] for i in range(rows8)] for n in both]

    def score(key, top):
        block, at = key // run, base + key % run
        mask = m_s[block, at]
        sums = [[None, None], [None, None]]
        for i in range(rows8):
            part = int(i >= cut)
            row = k_s[block, at, i]
            for n in both:
                term = query[n][i] * row
                held = sums[n][part]
                sums[n][part] = term if held is None else held + term
        tops = []
        for n in both:
            a, b = sums[n]
            b = b + pltpu.roll(b, 4, 0)
            a = a + mask
            b = b + mask
            s_s[key, 2 * n] = a
            s_s[key, 2 * n + 1] = b
            tops += [jnp.maximum(top[2 * n], a), jnp.maximum(top[2 * n + 1], b)]
        return tuple(tops)

    if fresh:
        old = tuple(jnp.full((8, LANES), -3e38, F32) for _ in range(4))
    else:
        old = tuple(state_s[t + n, rows8 + part] for n in both for part in both)
    tops = lax.fori_loop(0, keys, score, old, unroll=8)
    if fresh:
        zero = jnp.zeros((8, LANES), F32)
        sums = tuple(zero for _ in range(4))
        accs = tuple(zero for _ in range(2 * rows8))
    else:
        fade = [jnp.exp2(old[n] - tops[n]) for n in range(4)]
        sums = tuple(
            state_s[t + n, rows8 + 2 + part] * fade[2 * n + part] for n in both for part in both
        )
        accs = tuple(
            state_s[t + n, i] * fade[2 * n + int(i >= cut)] for n in both for i in range(rows8)
        )

    def gather(key, carry):
        sums, accs = carry
        block, at = key // run, base + key % run
        weight = [jnp.exp2(s_s[key, n] - tops[n]) for n in range(4)]
        accs = list(accs)
        for i in range(rows8):
            row = v_s[block, at, i]
            for n in both:
                at_acc = n * rows8 + i
                accs[at_acc] = accs[at_acc] + weight[2 * n + int(i >= cut)] * row
        return tuple(sums[n] + weight[n] for n in range(4)), tuple(accs)

    sums, accs = lax.fori_loop(0, keys, gather, (sums, accs), unroll=8)
    return tops, sums, accs


def hold_two(n, state, state_s):
    tops, sums, accs = state
    rows8 = len(accs) // 2
    for m in range(2):
        for i in range(rows8):
            state_s[2 * n + m, i] = accs[m * rows8 + i]
        for part in range(2):
            state_s[2 * n + m, rows8 + part] = tops[2 * m + part]
            state_s[2 * n + m, rows8 + 2 + part] = sums[2 * m + part]


def near_kernel(run, own_ref, near_ref, weights_ref, q_s, state_s, k_s, v_s, m_s, s_s):
    chans, slots = own_ref.shape
    tiles = slots // LANES
    scale = (chans // HEADS) ** -0.5 * LOG2E
    own, _ = clean(own_ref[...])
    query = dot(weights_ref[:chans, :], own) * scale
    for t in range(tiles):
        q_s[t] = query[:, tile(t)].reshape(chans // 8, 8, LANES)
    add_keys([own_ref[...], near_ref[...]], weights_ref[chans : 3 * chans, :], k_s, v_s, m_s)

    def step(n, _):
        hold_two(n, attend_two(2 * n, run, q_s, k_s, v_s, m_s, s_s, state_s, True), state_s)
        return 0

    lax.fori_loop(0, tiles // 2, step, 0)


def middle_kernel(run, count, *refs):
    blocks, refs = refs[:count], refs[count:]
    q_s, old_s, weights_ref, state_s, k_s, v_s, m_s, s_s = refs
    chans = weights_ref.shape[1]
    kv_t = weights_ref[chans : 3 * chans, :]
    add_keys([block[...] for block in blocks], kv_t, k_s, v_s, m_s)

    def step(n, _):
        hold_two(n, attend_two(2 * n, run, q_s, k_s, v_s, m_s, s_s, old_s, False), state_s)
        return 0

    lax.fori_loop(0, q_s.shape[0] // 2, step, 0)


def second_kernel(run, cap, far, owners, count_ref, *refs):
    blocks, refs = refs[:far], refs[far:]
    q_s, state_s, weights_s, first_s, gain_s, down_s, facts_s, feat_hbm = refs[:8]
    votes_s, refs = refs[8 : 8 + owners // 2], refs[8 + owners // 2 :]
    feat_s, store, k_s, v_s, m_s, s_s, ctx_s, bf_s, inner_s = refs
    chans, slots = first_s.shape
    tiles = slots // LANES
    count = count_ref[0]
    add_keys([block[...] for block in blocks], weights_s[chans : 3 * chans], k_s, v_s, m_s)
    rows8 = chans // 8

    def step(n, _):
        t = 2 * n
        _, sums, accs = attend_two(t, run, q_s, k_s, v_s, m_s, s_s, state_s, False)
        share = [1.0 / total for total in sums]
        cut = 2 * rows8 // 3
        for n in range(2):
            for i in range(rows8):
                ctx_s[t + n, i] = accs[n * rows8 + i] * share[2 * n + int(i >= cut)]
        return 0

    lax.fori_loop(0, tiles // 2, step, 0)
    ctx = swap_blocks([ctx_s[t].reshape(chans, LANES) for t in range(tiles)])
    ctx = dot_t(jnp.concatenate(ctx, 0).astype(BF16), within(run)).astype(BF16)
    ctx = jnp.concatenate([ctx[t * chans : (t + 1) * chans] for t in range(tiles)], 1)
    gain = gain_s[...]
    moved = dot(weights_s[3 * chans : 4 * chans], ctx)
    for t in range(tiles):
        at = tile(t)
        second = first_s[:, at].astype(F32) + moved[:, at]
        feat_s[:, at] = second
        inner_s[:, at] = norm_t(second, gain).astype(BF16)
    kept = iota((1, slots), 1) < count
    wide = 2 * LANES
    cuts = [slice(at, at + wide) for at in range(0, slots, wide)]
    up_t = weights_s[4 * chans :]
    raised = dot(up_t, inner_s[:, cuts[0]])
    for n, at in enumerate(cuts):
        now = raised
        if n + 1 < len(cuts):
            raised = dot(up_t, inner_s[:, cuts[n + 1]])
        hidden = gelu(now).astype(BF16)
        third = feat_s[:, at] + dot(down_s[...], hidden)
        third = jnp.where(kept[:, at], third, 0.0)
        feat_s[:, at] = third
        bf_s[:, at] = third.astype(BF16)
    keep = pltpu.make_async_copy(feat_s, feat_hbm, store)
    keep.start()
    facts = facts_s[...].astype(F32)
    low, high = facts[2:3].astype(jnp.int32), facts[1:2].astype(jnp.int32)
    picked = dot(bf_s[...], place(low, high, tiles)).astype(BF16)
    for o in range(owners):
        at = slice(o * cap, (o + 1) * cap)
        ballot = jnp.concatenate([picked[:, at], facts_s[:8, at]], 0)
        votes_s[o % len(votes_s)][o // len(votes_s)] = ballot
    keep.wait()


def sums_kernel(*refs):
    ballots, outs = refs[:-2], refs[-2:]
    cap = ballots[0].shape[2]
    for kind, out_ref in enumerate(outs):
        chans, voxels = out_ref.shape
        total = jnp.zeros(out_ref.shape, F32)
        for ref in ballots:
            ballot = ref[kind]
            label = ballot[chans:].astype(F32)[0:1]
            hot = (label == iota((voxels, cap), 0).astype(F32)).astype(BF16)
            total = total + dot_t(ballot[:chans], hot)
        out_ref[...] = total.astype(out_ref.dtype)


def total_kernel(here_ref, there_ref, out_ref):
    out_ref[...] = here_ref[...] + there_ref[...].astype(F32)


def call(kernel, outs, scratch, flops, spaces, out_spaces, limit=VMEM):
    place_of = {"s": pltpu.SMEM, "v": pltpu.VMEM, "a": pl.ANY}
    return pl.pallas_call(
        kernel,
        out_shape=outs,
        in_specs=[pl.BlockSpec(memory_space=place_of[c]) for c in spaces],
        out_specs=[pl.BlockSpec(memory_space=place_of[c]) for c in out_spaces],
        scratch_shapes=scratch,
        compiler_params=pltpu.CompilerParams(vmem_limit_bytes=limit),
        cost_estimate=pl.CostEstimate(flops=flops, bytes_accessed=2 << 20, transcendentals=0),
    )


def turned(x, axis, bit):
    n = lax.axis_size(axis)
    return lax.ppermute(x, axis, [(i, i ^ bit) for i in range(n)])


def body(
    nodes,
    node_ids,
    node_count,
    pos_weight,
    gain_one,
    qkv_one,
    out_one,
    gain_two,
    qkv_two,
    out_two,
    gain_three,
    w_up,
    w_down,
    vote_slot,
    vote_owner,
    vote_voxel,
):
    slots, chans = nodes.shape
    groups, owners = lax.axis_size("grp"), lax.axis_size("tile")
    run = WIN // groups
    votes = vote_slot.shape[0]
    cap = 2 * votes // owners
    codes = owners * cap
    tiles = slots // LANES
    rows8 = chans // 8
    hidden = w_up.shape[1]
    per = LANES // WIN
    sds = jax.ShapeDtypeStruct
    vmem = pltpu.VMEM
    dma = pltpu.SemaphoreType.DMA

    first, sent = call(
        functools.partial(first_kernel, run),
        [sds((chans, slots), BF16), sds((chans, slots), BF16)],
        [
            vmem((chans, slots), BF16),
            vmem((1, slots), jnp.int32),
            vmem((3, chans), F32),
            vmem((1, chans), F32),
            vmem((1, chans), F32),
            vmem((chans, 3 * chans), BF16),
            vmem((chans, chans), BF16),
            dma((7,)),
            vmem((3 * chans, slots), BF16),
            vmem((tiles, chans, 2 * LANES), BF16),
            vmem((tiles, LANES, chans), BF16),
            vmem((tiles, chans, LANES), BF16),
            vmem((tiles, chans, LANES), BF16),
            vmem((chans, slots), BF16),
            vmem((chans, slots), BF16),
            vmem((chans, slots), BF16),
            dma((2,)),
        ],
        2_000_000_000,
        "saaaaaaa",
        "aa",
    )(
        node_count,
        nodes.T,
        node_ids.reshape(1, slots),
        pos_weight,
        gain_one.reshape(1, chans),
        gain_two.reshape(1, chans),
        qkv_one,
        out_one,
    )
    bit = groups // 2
    mid = []
    while bit > 1:
        mid += [turned(block, "grp", bit) for block in [sent] + mid]
        bit //= 2
    near = turned(sent, "grp", 1)
    weights, facts, gain = call(
        functools.partial(tables_kernel, cap),
        [
            sds((4 * chans + hidden, chans), BF16),
            sds((16, codes), BF16),
            sds((chans, LANES), F32),
        ],
        [
            vmem((chans, 3 * chans), BF16),
            vmem((chans, chans), BF16),
            vmem((chans, hidden), BF16),
            vmem((1, votes), jnp.int32),
            vmem((1, votes), jnp.int32),
            vmem((1, votes), jnp.int32),
            vmem((1, chans), F32),
            dma((7,)),
        ],
        2_000_000_000,
        "aaaaaaa",
        "vvv",
        limit=TIGHT,
    )(
        qkv_two,
        out_two,
        w_up,
        vote_slot.reshape(1, votes),
        vote_owner.reshape(1, votes),
        vote_voxel.reshape(1, votes),
        gain_three.reshape(1, chans),
    )
    q_like = ((tiles, rows8, 8, LANES), F32)
    state_like = ((tiles, rows8 + 4, 8, LANES), F32)

    def key_scratch(blocks):
        return [
            vmem((blocks, tiles, rows8, 8, LANES), F32),
            vmem((blocks, tiles, rows8, 8, LANES), F32),
            vmem((blocks, tiles, 8, LANES), F32),
            vmem((blocks * run, 4, 8, LANES), F32),
        ]

    query, state = call(
        functools.partial(near_kernel, run),
        [sds(*q_like), sds(*state_like)],
        key_scratch(2),
        3_000_000_000,
        "vvv",
        "vv",
        limit=ROOMY,
    )(sent, near, weights)
    mid, query = lax.optimization_barrier((mid, query))
    far = [turned(block, "grp", 1) for block in mid]
    (state,) = call(
        functools.partial(middle_kernel, run, len(mid)),
        [sds(*state_like)],
        key_scratch(len(mid)),
        2_000_000_000,
        "v" * len(mid) + "vvv",
        "v",
        limit=ROOMY,
    )(*mid, query, state, weights)
    features_t, *ballots = call(
        functools.partial(second_kernel, run, cap, len(far), owners),
        [sds((chans, slots), F32)] + [sds((2, chans + 8, cap), BF16)] * (owners // 2),
        [vmem((chans, slots), F32), dma]
        + key_scratch(len(far))
        + [vmem(*q_like), vmem((chans, slots), BF16), vmem((chans, slots), BF16)],
        3_000_000_000,
        "s" + "v" * (len(far) + 7),
        "a" + "v" * (owners // 2),
        limit=ROOMY,
    )(
        node_count,
        *far,
        query,
        state,
        weights,
        first,
        gain,
        w_down.T,
        facts,
    )
    half = owners // 2
    got = [ballots[0]] + [turned(ballots[k], "tile", k) for k in range(1, half)]
    here, there = call(
        sums_kernel,
        [sds((chans, VOX_DEV), F32), sds((chans, VOX_DEV), BF16)],
        [],
        200_000_000,
        "v" * half,
        "vv",
        limit=ROOMY,
    )(*got)
    (sums_t,) = call(
        total_kernel, [sds((chans, VOX_DEV), F32)], [], 1_000_000, "vv", "v", limit=ROOMY
    )(here, turned(there, "tile", half))
    return (features_t.T, sums_t.T)


def solution(mesh):
    in_specs = (
        P(("grp", "tile"), None),
        P(("grp", "tile")),
        P(("grp", "tile")),
        P(),
        P(),
        P(),
        P(),
        P(),
        P(),
        P(),
        P(),
        P(),
        P(),
        P(("grp", "tile")),
        P(("grp", "tile"), None),
        P(("grp", "tile")),
    )
    out_specs = (P(("grp", "tile"), None), P(("grp", "tile"), None))
    return jax.shard_map(body, mesh=mesh, in_specs=in_specs, out_specs=out_specs, check_vma=False)
```
